32 devices in a mesh: sub: 2 (over y), rng: 16 (over z, x, core).
Axes of the slice: x: 2, y: 2, z: 4, core: 2. Of those that a mesh axis runs over, the one named last changes fastest.
Arguments:
- echoes: bfloat16 [2, 1024, 8192], P(None, ('sub', 'rng')), may hold values from -6 to 6
- fore_flag: int32 [1, 2, 16], P(None, None, 'rng'), may hold values from 0 to 1, as said below
- band_offset: int32 [1, 2, 16], P(None, None, 'rng'), may hold values from -16 to 16, as said below
- angle_interp: bfloat16 [1, 2, 512, 256], replicated, may hold values from -1 to 1
- range_kernel: bfloat16 [1, 544, 512], replicated, may hold values from -1 to 2, as said below
- center_shift: float32 [1, 2], replicated, may hold values from -6 to 6
Outputs:
- focused_image: float32 [2, 1024, 8192], P(None, 'sub', 'rng')
The draws below stay inside these ranges and needn't reach their ends.
Inputs may be any that keep to these rules, and one draw needn't show every extreme that they name: fore_flag[l, g, b] + fore_flag[l, g XOR 2**l, b] = 1 for every level l, group g and block b. `band_offset`: in every level both -16 and 16 occur. range_kernel[l, w, r] = 0 wherever |w - 16 - r| > 16.
All inputs are finite; a program needn't handle non-finite values.
Results may differ from the reference program's by a relative error of at most 0.0076.
Values may be sent and summed in bfloat16 or wider, within the bound.
No kernel may reach another device: no remote copies, remote signals or barrier semaphores. Data moves between devices by JAX's collectives and lax.ppermute only.
A program may use at most 64 MiB of HBM per device.

```python
import math
import jax
import jax.numpy as jnp

ANGLES = 512
PULSES = 512
BLOCK_BINS = 512
BAND_HALF = 16
MAX_SHIFT = 16
RIM_WIDTH = 32
HALF_ANGLES = 256
LEVELS = 1
ALL_PULSES = 1024
ALL_BINS = 8192
N_SUB = 2
N_RNG = 16


def draw_fore_flag(key, part):
    sub_key = jax.random.fold_in(key, 5)
    coin_flips = jax.random.randint(sub_key, (LEVELS, N_SUB, N_RNG), 0, 2)
    group_ids = jnp.arange(N_SUB)
    level_rows = []
    for tree_level in range(LEVELS):
        stride = 2 ** tree_level
        upper_side = group_ids // stride % 2
        lower_group = group_ids - upper_side * stride
        level_rows.append((coin_flips[tree_level][lower_group] + upper_side[:, None]) % 2)
    return jnp.stack(level_rows).astype(jnp.int32)


def draw_band_offset(key, part):
    first_key, second_key, third_key = jax.random.split(jax.random.fold_in(key, 11), 3)
    cell_count = N_SUB * N_RNG
    shifts = jax.random.randint(first_key, (LEVELS, cell_count), -MAX_SHIFT, MAX_SHIFT + 1)
    top_pos = jax.random.randint(second_key, (LEVELS, 1), 0, cell_count)
    spacing = jax.random.randint(third_key, (LEVELS, 1), 1, cell_count)
    bottom_pos = (top_pos + spacing) % cell_count
    positions = jnp.arange(cell_count)[None, :]
    shifts = jnp.where(positions == top_pos, MAX_SHIFT, shifts)
    shifts = jnp.where(positions == bottom_pos, -MAX_SHIFT, shifts)
    return shifts.reshape(LEVELS, N_SUB, N_RNG).astype(jnp.int32)


def draw_angle_interp(key, part):
    sub_key = jax.random.fold_in(key, 23)
    parent = jnp.arange(ANGLES)[:, None]
    child_ids = jnp.arange(HALF_ANGLES)[None, :]
    nearest = jnp.where(child_ids == parent // 2, 0.55, 0.0).astype(jnp.float32)
    shape = (LEVELS, 2, ANGLES, HALF_ANGLES)
    jitter = 0.35 * jnp.clip(jax.random.normal(sub_key, shape, jnp.float32), -4.0, 4.0)
    return (nearest + jitter / math.sqrt(HALF_ANGLES)).astype(jnp.bfloat16)


def draw_range_kernel(key, part):
    sub_key = jax.random.fold_in(key, 37)
    row_ids = jnp.arange(BLOCK_BINS + 2 * BAND_HALF)[:, None]
    col_ids = jnp.arange(BLOCK_BINS)[None, :]
    offset = row_ids - BAND_HALF - col_ids
    inband = (jnp.abs(offset) <= BAND_HALF).astype(jnp.float32)
    diagonal = (offset == 0).astype(jnp.float32)
    shape = (LEVELS, BLOCK_BINS + 2 * BAND_HALF, BLOCK_BINS)
    jitter = 0.35 * jnp.clip(jax.random.normal(sub_key, shape, jnp.float32), -4.0, 4.0)
    return (diagonal + inband * jitter / math.sqrt(2 * BAND_HALF + 1)).astype(jnp.bfloat16)


def shard_levels(stream_key, shape, cuts, low, top_value):
    def one(position, parts):
        heights = jax.random.uniform(jax.random.fold_in(jax.random.fold_in(stream_key, 6), position), (parts,), jnp.float32, low / len(cuts), top_value / len(cuts))
        return jnp.repeat(jnp.exp(heights), shape[position] // parts).reshape((-1,) + (1,) * (len(shape) - position - 1))

    factor_of = one(*cuts[0])
    for cut in cuts[1:]:
        factor_of = factor_of * one(*cut)
    return factor_of


def bell_draw(own_key, shape, width, reach, cuts=(), kind=jnp.bfloat16):
    result = jax.random.normal(own_key, shape, jnp.float32) * width
    if len(cuts) > 0:
        result = shard_levels(own_key, shape, cuts, -0.22, 0.18) * result
    return jnp.clip(result, min=-reach, max=reach).astype(kind)


def setup_inputs(seed: int = 0) -> dict:
    seeds = jax.random.split(jax.random.key(seed), 7)
    return {
        "echoes": bell_draw(seeds[0], (2, ALL_PULSES, ALL_BINS), 1.0, 6.0, ((1, 32),)),
        "fore_flag": draw_fore_flag(jax.random.fold_in(seeds[6], 71), 0),
        "band_offset": draw_band_offset(jax.random.fold_in(seeds[6], 71), 0),
        "angle_interp": draw_angle_interp(jax.random.fold_in(seeds[6], 71), 0),
        "range_kernel": draw_range_kernel(jax.random.fold_in(seeds[6], 71), 0),
        "center_shift": jnp.clip(jax.random.uniform(seeds[5], (LEVELS, N_SUB), jnp.float32, -6.0, 6.0), -6.0, 6.0),
    }


def doppler_matrix(angles, pulses):
    angle_ids = jnp.arange(angles, dtype=jnp.int32)[:, None]
    pulse_ids = jnp.arange(pulses, dtype=jnp.int32)[None, :]
    cycles = (2 * angle_ids + 1 - angles) * pulse_ids % (2 * angles)
    phase_angle = math.pi / angles * cycles.astype(jnp.float32)
    cosine = jnp.cos(phase_angle) / math.sqrt(pulses)
    sine_part = jnp.sin(phase_angle) / math.sqrt(pulses)
    upper_rows = jnp.concatenate([cosine, sine_part], axis=1)
    bottom = jnp.concatenate([-sine_part, cosine], axis=1)
    return jnp.concatenate([upper_rows, bottom], axis=0).astype(jnp.bfloat16)

def phase_turn(real_imag, shift_rate, block_start, total_bins):
    angles = real_imag.shape[1]
    bin_count = real_imag.shape[2]
    angle_pos = (jnp.arange(angles).astype(jnp.float32)[:, None] + 0.5) / angles - 0.5
    range_pos = 1.0 + (block_start + jnp.arange(bin_count)).astype(jnp.float32)[None, :] / total_bins
    phase_angle = math.pi * shift_rate * angle_pos * range_pos
    cosine = jnp.cos(phase_angle)
    sine_part = jnp.sin(phase_angle)
    real_part = real_imag[0] * cosine - real_imag[1] * sine_part
    imag_part = real_imag[0] * sine_part + real_imag[1] * cosine
    return jnp.stack([real_part, imag_part])

def block_term(image, upper_sel, matrix_zero, matrix_one, use_one):
    blocks = image.reshape(2, ANGLES, N_RNG, BLOCK_BINS)
    rows = jnp.where(upper_sel, blocks[:, HALF_ANGLES:], blocks[:, :HALF_ANGLES]).astype(jnp.float32)
    term_zero = jnp.einsum('pa,cabr->cpbr', matrix_zero, rows)
    term_one = jnp.einsum('pa,cabr->cpbr', matrix_one, rows)
    return jnp.where(use_one, term_one, term_zero).reshape(2, ANGLES, ALL_BINS)

def reference(echoes, fore_flag, band_offset, angle_interp, range_kernel, center_shift):
    filter_matrix = doppler_matrix(ANGLES, PULSES)
    images = []
    for group_id in range(N_SUB):
        pulse_block = echoes[:, group_id * PULSES:(group_id + 1) * PULSES, :].reshape(2 * PULSES, ALL_BINS)
        filtered = jnp.dot(filter_matrix, pulse_block, preferred_element_type=jnp.float32)
        images.append(filtered.astype(jnp.bfloat16).reshape(2, ANGLES, ALL_BINS))
    window_ids = jnp.arange(BLOCK_BINS + 2 * BAND_HALF, dtype=jnp.int32)
    block_starts = jnp.arange(N_RNG, dtype=jnp.int32) * BLOCK_BINS + RIM_WIDTH - BAND_HALF
    for tree_level in range(LEVELS):
        kernel = range_kernel[tree_level].astype(jnp.float32)
        resampled = []
        for group_id in range(N_SUB):
            padded = jnp.pad(images[group_id], ((0, 0), (0, 0), (RIM_WIDTH, RIM_WIDTH)))
            starts = (block_starts + band_offset[tree_level, group_id]).astype(jnp.int32)
            window_index = (starts[:, None] + window_ids[None, :]).astype(jnp.int32)
            windows = padded[:, :, window_index].astype(jnp.float32)
            values = jnp.einsum('cabw,wr->cabr', windows, kernel)
            resampled.append(values.reshape(2, ANGLES, ALL_BINS).astype(jnp.bfloat16))
        matrix_zero = angle_interp[tree_level, 0].astype(jnp.float32)
        matrix_one = angle_interp[tree_level, 1].astype(jnp.float32)
        merged_list = []
        for group_id in range(N_SUB):
            partner = group_id ^ 1 << tree_level
            own_flag = fore_flag[tree_level, group_id]
            partner_flag = fore_flag[tree_level, partner]
            upper_sel = (own_flag == 1)[None, None, :, None]
            own_one = (own_flag == 1)[None, None, :, None]
            partner_one = (partner_flag == 1)[None, None, :, None]
            own_term = block_term(resampled[group_id], upper_sel, matrix_zero, matrix_one, own_one)
            partner_term = block_term(resampled[partner], upper_sel, matrix_zero, matrix_one, partner_one)
            merged = phase_turn(own_term, center_shift[tree_level, group_id], 0, ALL_BINS)
            merged = merged + phase_turn(partner_term, center_shift[tree_level, partner], 0, ALL_BINS)
            if tree_level + 1 < LEVELS:
                merged = merged.astype(jnp.bfloat16)
            merged_list.append(merged)
        images = merged_list
    return jnp.concatenate(images, axis=1)
```

```python
import functools
import math

import jax
import jax.numpy as jnp
from jax import lax
from jax.experimental import pallas as pl
from jax.experimental.pallas import tpu as pltpu
from jax.sharding import PartitionSpec as P

MAX_SHIFT = 16
LANES = 128
VMEM = pltpu.VMEM
MIB = 2**20


def half_turn_parts(v):
    turns = jnp.floor(v + 0.5)
    rest = v - turns
    sign = 1.0 - 2.0 * (turns - 2.0 * jnp.floor(turns * 0.5))
    return rest * rest, rest, sign


def series(square, first, count):
    coefs = [
        (-1) ** i * math.pi ** (2 * i + first) / math.factorial(2 * i + first)
        for i in range(count)
    ]
    total = jnp.full_like(square, coefs[-1])
    for coef in coefs[-2::-1]:
        total = total * square + coef
    return total


def cos_pi(v):
    square, _, sign = half_turn_parts(v)
    return series(square, 0, 8) * sign


def cos_sin_pi(v):
    square, rest, sign = half_turn_parts(v)
    return series(square, 0, 8) * sign, series(square, 1, 7) * rest * sign


def table_kernel(level, stride, local_pulses, with_filter, flag_ref, offset_ref, shift_ref, range_ref, *refs):
    if with_filter:
        filter_ref, centre_ref, rim_ref, turn_ref, padded_ref, moved_ref = refs
    else:
        centre_ref, rim_ref, turn_ref, padded_ref, moved_ref = refs
    group = lax.axis_index("sub")
    block = lax.axis_index("rng")
    total_bins = lax.axis_size("rng") * centre_ref.shape[-1]
    angles, bins = turn_ref.shape[-2:]
    half = angles // 2
    rows = 16

    if with_filter:
        columns = filter_ref.shape[1]
        scale = 1.0 / math.sqrt(columns // 2)
        lane = lax.broadcasted_iota(jnp.int32, (1, columns), 1)
        second = lane // local_pulses % 2
        pulse = (lane // (2 * local_pulses) * local_pulses + lane % local_pulses).astype(jnp.float32)
        lag = second.astype(jnp.float32) * 0.5

        def filter_rows(i, carry):
            start = pl.multiple_of(i * rows, rows)
            angle = start + lax.broadcasted_iota(jnp.int32, (rows, 1), 0)
            twice = (2 * angle + 1 - angles).astype(jnp.float32)
            upper = cos_pi(twice * pulse / angles - lag) * scale
            ahead = pltpu.roll(upper, local_pulses, 1)
            behind = pltpu.roll(upper, columns - local_pulses, 1)
            lower = jnp.where(second == 1, ahead, -behind)
            filter_ref[pl.ds(start, rows), :] = upper.astype(jnp.bfloat16)
            filter_ref[pl.ds(angles + start, rows), :] = lower.astype(jnp.bfloat16)
            return carry

        lax.fori_loop(0, angles // rows, filter_rows, 0)

    own_flag = flag_ref[level, group, 0]
    taps = range_ref.shape[1]
    band = (taps - bins) // 2
    rim = MAX_SHIFT + band
    padded_ref[pl.ds(0, rim), :] = jnp.zeros((rim, bins), jnp.float32)
    padded_ref[pl.ds(rim + taps, rim), :] = jnp.zeros((rim, bins), jnp.float32)
    padded_ref[pl.ds(rim, taps), :] = range_ref[level].astype(jnp.float32)
    rim_ref[...] = jnp.zeros(rim_ref.shape, jnp.bfloat16)
    outer = bins // 4
    for child in range(2):
        member = group if child == 0 else group ^ stride
        offset = offset_ref[level, member, 0]
        shift = padded_ref.shape[0] - (band - offset)
        moved_ref[...] = pltpu.roll(padded_ref[...], shift, 0)

        def taps_of(bin_start, count):
            begin = rim + bin_start
            return moved_ref[begin : begin + count, :].astype(jnp.bfloat16)

        centre_ref[child, :outer, :] = taps_of(0, outer)
        centre_ref[child, outer : 2 * outer, :] = taps_of(bins - outer, outer)
        centre_ref[child, 2 * outer :, :] = taps_of(outer, bins - 2 * outer)
        before = taps_of(-rim, rim)
        after = taps_of(bins, rim)
        for part in range(2):
            place = pl.multiple_of((2 * part + own_flag) * rim, rim)
            rim_ref[child, part, pl.ds(place, rim), :] = before
            rim_ref[child, part, pl.ds(4 * rim + place, rim), :] = after

        rate = shift_ref[level, member]
        first_bin = block * bins
        bin_id = first_bin + lax.broadcasted_iota(jnp.int32, (1, bins), 1)
        reach = 1.0 + bin_id.astype(jnp.float32) / total_bins

        def turn_rows(i, carry):
            begin = pl.multiple_of(i * rows, rows)
            angle = begin + lax.broadcasted_iota(jnp.int32, (rows, 1), 0)
            place = (angle.astype(jnp.float32) + 0.5) / angles - 0.5
            cosine, sine = cos_sin_pi(rate * place * reach)
            turn_ref[child, 0, pl.ds(begin, rows), :] = cosine
            turn_ref[child, 1, pl.ds(begin, rows), :] = sine
            return carry

        lax.fori_loop(0, angles // rows, turn_rows, 0)


def tables(level, stride, local_pulses, with_filter, fore_flag, band_offset, center_shift, range_kernel, angles):
    taps, bins = range_kernel.shape[1:]
    rim = MAX_SHIFT + (taps - bins) // 2
    shapes = [
        jax.ShapeDtypeStruct((2, bins, bins), jnp.bfloat16),
        jax.ShapeDtypeStruct((2, 2, 8 * rim, bins), jnp.bfloat16),
        jax.ShapeDtypeStruct((2, 2, angles, bins), jnp.float32),
    ]
    if with_filter:
        side = 2 * local_pulses * lax.axis_size("rng")
        shapes.insert(0, jax.ShapeDtypeStruct((2 * angles, side), jnp.bfloat16))
    return pl.pallas_call(
        functools.partial(table_kernel, level, stride, local_pulses, with_filter),
        out_shape=shapes,
        in_specs=[pl.BlockSpec(memory_space=pltpu.SMEM)] * 3 + [pl.BlockSpec(memory_space=VMEM)],
        out_specs=[pl.BlockSpec(memory_space=VMEM)] * len(shapes),
        scratch_shapes=[VMEM((taps + 2 * rim, bins), jnp.float32)] * 2,
        compiler_params=pltpu.CompilerParams(vmem_limit_bytes=24 * MIB),
        cost_estimate=pl.CostEstimate(flops=40_000_000, bytes_accessed=9 * MIB, transcendentals=0),
    )(fore_flag, band_offset, center_shift, range_kernel)


def filter_kernel(level, piece, flag_ref, filter_ref, pulses_ref, *refs):
    own_flag = flag_ref[level, lax.axis_index("sub"), 0]
    own_ref, out_ref = refs[-4:-2] if piece == "outer" else refs[-2:]
    half = own_ref.shape[1]
    first = own_flag == 0
    edges = [0.0, 0.0]
    for part in range(2):
        pair = []
        for side in range(2):
            begin = (2 * part + side) * half
            image = jnp.dot(
                filter_ref[begin : begin + half, :],
                pulses_ref[...],
                preferred_element_type=jnp.float32,
            )
            pair.append(image)
            if piece == "outer":
                rim = LANES // 4
                group = 2 * part + side
                lane = lax.broadcasted_iota(jnp.int32, (1, LANES), 1)
                here = lane // rim == group
                last = image.shape[1] - LANES
                low = pltpu.roll(image[:, :LANES], group * rim, 1) if group else image[:, :LANES]
                turn = (group * rim + rim) % LANES
                high = pltpu.roll(image[:, last:], turn, 1) if turn else image[:, last:]
                edges[0] = edges[0] + jnp.where(here, low, 0.0)
                edges[1] = edges[1] + jnp.where(here, high, 0.0)
        own_ref[part] = jnp.where(first, pair[0], pair[1]).astype(jnp.bfloat16)
        out_ref[part] = jnp.where(first, pair[1], pair[0]).astype(jnp.bfloat16)
    if piece == "outer":
        refs[-2][...] = edges[0].astype(jnp.bfloat16)
        refs[-1][...] = edges[1].astype(jnp.bfloat16)
    if piece == "rims":
        out_ref[2] = refs[0][...]
        out_ref[3] = refs[1][...]


def filtered(level, piece, fore_flag, filter_matrix, pulses, rims=()):
    half = filter_matrix.shape[0] // 4
    columns = pulses.shape[1]
    shapes = [
        jax.ShapeDtypeStruct((2, half, columns), jnp.bfloat16),
        jax.ShapeDtypeStruct((4 if piece == "rims" else 2, half, columns), jnp.bfloat16),
    ]
    if piece == "outer":
        shapes += [jax.ShapeDtypeStruct((half, LANES), jnp.bfloat16)] * 2
    size = filter_matrix.shape[0] * filter_matrix.shape[1]
    return pl.pallas_call(
        functools.partial(filter_kernel, level, piece),
        out_shape=shapes,
        in_specs=[pl.BlockSpec(memory_space=pltpu.SMEM)]
        + [pl.BlockSpec(memory_space=VMEM)] * (2 + len(rims)),
        out_specs=[pl.BlockSpec(memory_space=VMEM)] * len(shapes),
        compiler_params=pltpu.CompilerParams(vmem_limit_bytes=16 * MIB),
        cost_estimate=pl.CostEstimate(
            flops=2 * size * columns, bytes_accessed=3 * MIB, transcendentals=0
        ),
    )(fore_flag, filter_matrix, pulses, *rims)


def merge_kernel(
    level, flag_ref, own_outer, own_mid, own_last, rim_low, rim_high, far_outer, far_mid, far_last,
    centre_ref, rim_ref, matrix_ref, turn_ref, out_ref,
):
    own_flag = flag_ref[level, lax.axis_index("sub"), 0]
    outer = own_outer.shape[-1]
    merged = [0.0, 0.0]
    for child in range(2):
        pieces = (own_outer, own_mid, own_last) if child == 0 else (far_outer, far_mid, far_last)
        if child == 0:
            rims = jnp.concatenate([rim_low[...], rim_high[...]], axis=1)
        else:
            rims = jnp.concatenate([far_mid[2], far_mid[3]], axis=1)
        matrix = matrix_ref[level, own_flag if child == 0 else 1 - own_flag]
        terms = []
        for part in range(2):
            inner = jnp.concatenate([pieces[1][part], pieces[2][part]], axis=1)
            value = jnp.dot(
                pieces[0][part], centre_ref[child, :outer, :], preferred_element_type=jnp.float32
            )
            value += jnp.dot(
                inner, centre_ref[child, outer:, :], preferred_element_type=jnp.float32
            )
            value += jnp.dot(rims, rim_ref[child, part], preferred_element_type=jnp.float32)
            terms.append(
                jnp.dot(matrix, value.astype(jnp.bfloat16), preferred_element_type=jnp.float32)
            )
        cosine, sine = turn_ref[child, 0], turn_ref[child, 1]
        merged[0] = merged[0] + (terms[0] * cosine - terms[1] * sine)
        merged[1] = merged[1] + (terms[0] * sine + terms[1] * cosine)
    out_ref[0] = merged[0].astype(out_ref.dtype)
    out_ref[1] = merged[1].astype(out_ref.dtype)


def merged_image(level, fore_flag, own, rims, far, centre, rim, angle_interp, turn, dtype):
    angles, bins = turn.shape[-2:]
    tile = bins // 2

    def whole(value):
        return pl.BlockSpec(value.shape, lambda n, r=value.ndim: (0,) * r)

    def by_columns(value):
        lead = value.ndim - 1
        return pl.BlockSpec(value.shape[:-1] + (tile,), lambda n, r=lead: (0,) * r + (n,))

    operands = (*own, *rims, *far)
    return pl.pallas_call(
        functools.partial(merge_kernel, level),
        out_shape=jax.ShapeDtypeStruct((2, angles, bins), dtype),
        grid=(bins // tile,),
        in_specs=[pl.BlockSpec(memory_space=pltpu.SMEM)]
        + [whole(value) for value in operands]
        + [by_columns(centre), by_columns(rim), whole(angle_interp), by_columns(turn)],
        out_specs=pl.BlockSpec((2, angles, tile), lambda n: (0, 0, n)),
        compiler_params=pltpu.CompilerParams(vmem_limit_bytes=32 * MIB),
        cost_estimate=pl.CostEstimate(
            flops=8 * angles * bins * bins, bytes_accessed=11 * MIB, transcendentals=0
        ),
    )(fore_flag, *operands, centre, rim, angle_interp, turn)


def neighbour_rims(low, high):
    devices = lax.axis_size("rng")
    up = [(i, i + 1) for i in range(devices - 1)]
    below = lax.ppermute(high, "rng", up)
    above = lax.ppermute(low, "rng", [(j, i) for i, j in up])
    return below, above


def from_partner(value, stride):
    pairs = [(source, source ^ stride) for source in range(lax.axis_size("sub"))]
    return lax.ppermute(value, "sub", pairs)


def split_image(level, image, fore_flag, rim):
    angles, bins = image.shape[1:]
    half, outer = angles // 2, bins // 4
    own_flag = fore_flag[level, lax.axis_index("sub"), 0]
    sides = image.reshape(2, 2, half, bins)

    def pieces(side):
        rows = lax.dynamic_index_in_dim(sides, side, 1, keepdims=False)
        ends = jnp.concatenate([rows[..., :outer], rows[..., -outer:]], axis=-1)
        return ends, rows[..., outer : 2 * outer], rows[..., 2 * outer : -outer]

    def packed(edge):
        return edge.transpose(2, 0, 1, 3).reshape(half, 4 * rim)

    low, high = packed(sides[..., :rim]), packed(sides[..., -rim:])
    return pieces(own_flag), pieces(1 - own_flag), low, high


def on_device(echoes, fore_flag, band_offset, angle_interp, range_kernel, center_shift):
    sub_count = lax.axis_size("sub")
    rng_count = lax.axis_size("rng")
    local_pulses = echoes.shape[1]
    block_bins = echoes.shape[2] // rng_count
    angles = angle_interp.shape[2]
    rim = MAX_SHIFT + (range_kernel.shape[1] - block_bins) // 2
    outer = block_bins // 4
    levels = range_kernel.shape[0]

    blocks = echoes.reshape(2 * local_pulses, rng_count, block_bins)

    def turned(columns):
        pulses = columns.transpose(1, 0, 2).reshape(2 * local_pulses * rng_count, -1)
        return lax.all_to_all(pulses, "rng", split_axis=0, concat_axis=0, tiled=True)

    ends = jnp.concatenate([blocks[..., :outer], blocks[..., -outer:]], axis=-1)
    got_outer = turned(ends)
    got_mid = turned(blocks[..., outer : 2 * outer])
    got_last = turned(blocks[..., 2 * outer : -outer])

    flags = (fore_flag, band_offset, center_shift, range_kernel, angles)
    filter_matrix, centre, rims_matrix, turn = tables(0, 1, local_pulses, True, *flags)
    own_outer, out_outer, low, high = filtered(0, "outer", fore_flag, filter_matrix, got_outer)
    rims = neighbour_rims(low, high)
    far_outer = from_partner(out_outer, 1)
    own_mid, out_mid = filtered(0, "rims", fore_flag, filter_matrix, got_mid, rims)
    far_mid = from_partner(out_mid, 1)
    own_last, out_last = filtered(0, "last", fore_flag, filter_matrix, got_last)
    far_last = from_partner(out_last, 1)
    own = (own_outer, own_mid, own_last)
    far = (far_outer, far_mid, far_last)
    for level in range(levels):
        if level > 0:
            stride = 2**level
            centre, rims_matrix, turn = tables(level, stride, local_pulses, False, *flags)
            own, out, low, high = split_image(level, image, fore_flag, rim)
            rims = neighbour_rims(low, high)
            out_mid = jnp.concatenate([out[1], jnp.stack(rims)], axis=0)
            far = [from_partner(value, stride) for value in (out[0], out_mid, out[2])]
        dtype = jnp.bfloat16 if level + 1 < levels else jnp.float32
        image = merged_image(
            level, fore_flag, own, rims, far, centre, rims_matrix, angle_interp, turn, dtype
        )
    return image


def solution(mesh):
    placed = (
        P(None, ("sub", "rng"), None),
        P(None, None, "rng"),
        P(None, None, "rng"),
        P(),
        P(),
        P(),
    )
    return jax.shard_map(
        on_device, mesh=mesh, in_specs=placed, out_specs=P(None, "sub", "rng"), check_vma=False
    )
```

```python
import functools
import math

import jax
import jax.numpy as jnp
from jax import lax
from jax.experimental import pallas as pl
from jax.experimental.pallas import tpu as pltpu
from jax.sharding import PartitionSpec as P

MAX_SHIFT = 16
LANES = 128
MIB = 2**20
VMEM = pl.BlockSpec(memory_space=pltpu.VMEM)
SMEM = pl.BlockSpec(memory_space=pltpu.SMEM)
ANY = pl.BlockSpec(memory_space=pl.ANY)
F32 = jnp.float32
BF16 = jnp.bfloat16


def dot(a, b):
    return jnp.dot(a, b, preferred_element_type=F32)


def params(mib):
    return pltpu.CompilerParams(vmem_limit_bytes=mib * MIB)


def series(square, first, count):
    coefs = [
        (-1) ** i * math.pi ** (2 * i + first) / math.factorial(2 * i + first)
        for i in range(count)
    ]
    total = jnp.full_like(square, coefs[-1])
    for coef in coefs[-2::-1]:
        total = total * square + coef
    return total


def cos_sin_pi(v):
    turns = jnp.floor(v + 0.5)
    rest = v - turns
    sign = 1.0 - 2.0 * (turns - 2.0 * jnp.floor(turns * 0.5))
    square = rest * rest
    return series(square, 0, 8) * sign, series(square, 1, 7) * rest * sign


def rotated(pair, step):
    return pair[0] * step[0] - pair[1] * step[1], pair[0] * step[1] + pair[1] * step[0]


def place_kernel(echoes_ref, direct_same, direct_cross, keep_ref, give_ref, sems):
    me = lax.axis_index("rng")
    chips = keep_ref.shape[0]
    bins = keep_ref.shape[-1]
    outer = bins // 4
    copies = []

    def take(device, target, first, count, at):
        start = pl.multiple_of(device * bins + first, LANES)
        copy = pltpu.make_async_copy(
            echoes_ref.at[:, pl.ds(start, count)], target.at[:, pl.ds(at, count)], sems.at[len(copies)]
        )
        copy.start()
        copies.append(copy)

    for target, flip in ((direct_same, 0), (direct_cross, 1)):
        device = me ^ (chips + flip)
        take(device, target, 0, outer, 0)
        take(device, target, bins - outer, outer, outer)
    for flip, ref in ((1, give_ref), (0, keep_ref)):
        for d in range(chips):
            device = me ^ (2 * d + flip)
            take(device, ref.at[d], 0, outer, 0)
            take(device, ref.at[d], bins - outer, outer, outer)
            take(device, ref.at[d], outer, bins - 2 * outer, 2 * outer)
    for copy in copies:
        copy.wait()


def placed(echoes, chips, bins):
    rows = echoes.shape[0]
    direct = jax.ShapeDtypeStruct((rows, bins // 2), BF16)
    whole = jax.ShapeDtypeStruct((chips, rows, bins), BF16)
    return pl.pallas_call(
        place_kernel,
        out_shape=[direct, direct, whole, whole],
        in_specs=[ANY],
        out_specs=[VMEM] * 4,
        scratch_shapes=[pltpu.SemaphoreType.DMA((4 + 6 * chips,))],
        compiler_params=params(8),
        cost_estimate=pl.CostEstimate(flops=0, bytes_accessed=3 * MIB, transcendentals=0),
    )(echoes)


def join_kernel(picks, after, keep_ref, got_ref, *refs):
    rows = keep_ref.shape[1]
    for (d, first, count), out_ref in zip(picks, refs[after:]):
        out_ref[:rows] = keep_ref[d, :, first : first + count]
        out_ref[rows:] = got_ref[d, :, first : first + count]


def joined(picks, keep, got, after=()):
    rows = keep.shape[1]
    return pl.pallas_call(
        functools.partial(join_kernel, picks, len(after)),
        out_shape=[jax.ShapeDtypeStruct((2 * rows, count), BF16) for _, _, count in picks],
        in_specs=[VMEM] * 2 + [ANY] * len(after),
        out_specs=[VMEM] * len(picks),
        compiler_params=params(8),
        cost_estimate=pl.CostEstimate(flops=0, bytes_accessed=2 * MIB, transcendentals=0),
    )(keep, got, *after)


def exchanged(value, devices, mask):
    return lax.ppermute(value, "rng", [(i, i ^ mask) for i in range(devices)])


def filter_table_kernel(local_pulses, after_ref, filter_ref, cos_ref, sin_ref):
    me = lax.axis_index("rng")
    columns = filter_ref.shape[1]
    angles = filter_ref.shape[0] // 2
    base = cos_ref.shape[0]
    scale = 1.0 / math.sqrt(columns // 2)
    lane = lax.broadcasted_iota(jnp.int32, (8, columns), 1)
    slot = lane // (2 * local_pulses)
    second = lane // local_pulses % 2
    pulse_id = (slot ^ me) * local_pulses + lane % local_pulses
    pulse = pulse_id.astype(F32)
    lag = second.astype(F32) * 0.5
    per_angle = pulse * (1.0 / angles)
    row = lax.broadcasted_iota(jnp.int32, (8, columns), 0)
    for i in range(base // 8):
        twice = (2 * (row + 8 * i) + 1 - angles).astype(F32)
        cosine, sine = cos_sin_pi(twice * per_angle - lag)
        cos_ref[8 * i : 8 * i + 8, :] = cosine * scale
        sin_ref[8 * i : 8 * i + 8, :] = sine * scale
    step = cos_sin_pi(per_angle * (2 * base))
    for j in range(angles // base):
        for i in range(base // 16):
            pair = [], []
            for k in (2 * i, 2 * i + 1):
                here = slice(8 * k, 8 * k + 8)
                now = cos_ref[here, :], sin_ref[here, :]
                pair[0].append(now[0])
                pair[1].append(-now[1])
                if j + 1 < angles // base:
                    cos_ref[here, :], sin_ref[here, :] = rotated(now, step)
            begin = j * base + 16 * i
            filter_ref[begin : begin + 16, :] = jnp.concatenate(pair[0]).astype(BF16)
            begin += angles
            filter_ref[begin : begin + 16, :] = jnp.concatenate(pair[1]).astype(BF16)


def filter_table(angles, local_pulses, after):
    side = 2 * local_pulses * lax.axis_size("rng")
    return pl.pallas_call(
        functools.partial(filter_table_kernel, local_pulses),
        out_shape=jax.ShapeDtypeStruct((2 * angles, side), BF16),
        in_specs=[ANY],
        out_specs=VMEM,
        scratch_shapes=[pltpu.VMEM((64, side), F32)] * 2,
        compiler_params=params(6),
        cost_estimate=pl.CostEstimate(flops=9_000_000, bytes_accessed=4 * MIB, transcendentals=0),
    )(after)


def merge_table_kernel(
    level, stride, flag_ref, offset_ref, shift_ref, range_ref, after_ref, centre_ref, rim_ref, turn_ref
):
    group = lax.axis_index("sub")
    block = lax.axis_index("rng")
    bins = centre_ref.shape[-1]
    angles = turn_ref.shape[-2]
    total_bins = lax.axis_size("rng") * bins
    own_flag = flag_ref[level, group, 0]
    taps = range_ref.shape[1]
    band = (taps - bins) // 2
    rim = MAX_SHIFT + band
    outer = bins // 4
    kernel = range_ref[level]

    def moved(bin_id):
        tap = lax.broadcasted_iota(jnp.int32, (bin_id.shape[0], taps), 1)
        return dot(jnp.where(tap == bin_id, 1.0, 0.0).astype(BF16), kernel).astype(BF16)

    row = lax.broadcasted_iota(jnp.int32, (2 * outer, 1), 0)
    rim_row = lax.broadcasted_iota(jnp.int32, (8 * rim, 1), 0)
    below = rim_row < 4 * rim
    rim_bin = rim_row % rim + jnp.where(below, -rim, bins)
    rim_group = rim_row % (4 * rim) // rim
    rows = 8
    for child in range(2):
        member = group if child == 0 else group ^ stride
        lead = band - offset_ref[level, member, 0]
        ends = jnp.where(row < outer, row, row + (bins - 2 * outer))
        centre_ref[child, : 2 * outer, :] = moved(ends + lead)
        centre_ref[child, 2 * outer :, :] = moved(row + outer + lead)
        for part in range(2):
            wanted = rim_group == 2 * part + own_flag
            rim_ref[child, part] = moved(jnp.where(wanted, rim_bin + lead, -1))

        rate = shift_ref[level, member]
        bin_id = block * bins + lax.broadcasted_iota(jnp.int32, (1, LANES), 1)
        reach = 1.0 + bin_id.astype(F32) * (1.0 / total_bins)

        def turn_rows(i, carry):
            begin = pl.multiple_of(i * rows, rows)
            angle = begin + lax.broadcasted_iota(jnp.int32, (rows, LANES), 0)
            place = ((angle.astype(F32) + 0.5) * (1.0 / angles) - 0.5) * rate
            now = cos_sin_pi(place * reach)
            step = cos_sin_pi(place * (LANES / total_bins))
            for tile in range(bins // LANES):
                lanes = slice(tile * LANES, tile * LANES + LANES)
                turn_ref[child, 0, pl.ds(begin, rows), lanes] = now[0]
                turn_ref[child, 1, pl.ds(begin, rows), lanes] = now[1]
                now = rotated(now, step)
            return carry

        lax.fori_loop(0, angles // rows, turn_rows, 0, unroll=4)


def merge_tables(level, stride, fore_flag, band_offset, center_shift, range_kernel, angles, after):
    taps, bins = range_kernel.shape[1:]
    rim = MAX_SHIFT + (taps - bins) // 2
    return pl.pallas_call(
        functools.partial(merge_table_kernel, level, stride),
        out_shape=[
            jax.ShapeDtypeStruct((2, bins, bins), BF16),
            jax.ShapeDtypeStruct((2, 2, 8 * rim, bins), BF16),
            jax.ShapeDtypeStruct((2, 2, angles, bins), F32),
        ],
        in_specs=[SMEM] * 3 + [VMEM, ANY],
        out_specs=[VMEM] * 3,
        compiler_params=params(12),
        cost_estimate=pl.CostEstimate(
            flops=2_300_000_000, bytes_accessed=7 * MIB, transcendentals=0
        ),
    )(fore_flag, band_offset, center_shift, range_kernel, after)


def filter_kernel(pieces, first, count, ends, flag_ref, filter_ref, *refs):
    own_flag = flag_ref[0, lax.axis_index("sub"), 0]
    pulses_ref = refs[-1]
    own_ref, out_ref = refs[pieces : pieces + 2]
    at = 0
    for ref in refs[:pieces]:
        begin = first if ref.shape[1] > count else 0
        pulses_ref[at : at + ref.shape[0], :] = ref[:, begin : begin + count]
        at += ref.shape[0]
    half = own_ref.shape[1]
    foremost = own_flag == 0
    edges = [0.0, 0.0]
    for part in range(2):
        pair = []
        for side in range(2):
            begin = (2 * part + side) * half
            image = dot(filter_ref[begin : begin + half, :], pulses_ref[...])
            pair.append(image)
            if ends:
                rim = LANES // 4
                group = 2 * part + side
                lane = lax.broadcasted_iota(jnp.int32, (1, LANES), 1)
                here = lane // rim == group
                low, high = image[:, :LANES], image[:, -LANES:]
                low = pltpu.roll(low, group * rim, 1) if group else low
                turn = (group * rim + rim) % LANES
                high = pltpu.roll(high, turn, 1) if turn else high
                edges[0] = edges[0] + jnp.where(here, low, 0.0)
                edges[1] = edges[1] + jnp.where(here, high, 0.0)
        own_ref[part] = jnp.where(foremost, pair[0], pair[1]).astype(BF16)
        out_ref[part] = jnp.where(foremost, pair[1], pair[0]).astype(BF16)
    if ends:
        refs[pieces + 2][...] = edges[0].astype(BF16)
        refs[pieces + 3][...] = edges[1].astype(BF16)


def filtered(fore_flag, filter_matrix, pieces, first, count, ends):
    half = filter_matrix.shape[0] // 4
    shapes = [jax.ShapeDtypeStruct((2, half, count), BF16)] * 2
    if ends:
        shapes += [jax.ShapeDtypeStruct((half, LANES), BF16)] * 2
    return pl.pallas_call(
        functools.partial(filter_kernel, len(pieces), first, count, ends),
        out_shape=shapes,
        in_specs=[SMEM] + [VMEM] * (1 + len(pieces)),
        out_specs=[VMEM] * len(shapes),
        scratch_shapes=[pltpu.VMEM((filter_matrix.shape[1], count), BF16)],
        compiler_params=params(10),
        cost_estimate=pl.CostEstimate(
            flops=2 * filter_matrix.size * count, bytes_accessed=4 * MIB, transcendentals=0
        ),
    )(fore_flag, filter_matrix, *pieces)


def early_kernel(
    level, flag_ref, own_outer, own_inner, rim_low, rim_high, far_outer, far_low, far_high,
    centre_ref, rim_ref, matrix_ref, turn_ref, merged_ref, partial_ref,
):
    own_flag = flag_ref[level, lax.axis_index("sub"), 0]
    count = own_outer.shape[-1]
    matrix = matrix_ref[level, own_flag]
    rims = jnp.concatenate([rim_low[...], rim_high[...]], axis=1)
    far_rims = jnp.concatenate([far_low[...], far_high[...]], axis=1)
    rows = []
    for part in range(2):
        value = dot(own_outer[part], centre_ref[0, :count, :])
        value += dot(own_inner[part], centre_ref[0, count:, :])
        value += dot(rims, rim_ref[0, part])
        rows.append(value.astype(BF16))
    block = LANES
    for begin in range(0, matrix.shape[0], block):
        here = slice(begin, begin + block)
        real, imag = dot(matrix[here], rows[0]), dot(matrix[here], rows[1])
        merged_ref[0, here], merged_ref[1, here] = rotated(
            (real, imag), (turn_ref[0, 0, here], turn_ref[0, 1, here])
        )
    for part in range(2):
        value = dot(far_outer[part], centre_ref[1, :count, :])
        partial_ref[part] = value + dot(far_rims, rim_ref[1, part])


def late_kernel(
    level, flag_ref, far_inner, merged_ref, partial_ref, centre_ref, matrix_ref, turn_ref, out_ref,
    buffer, sems,
):
    own_flag = flag_ref[level, lax.axis_index("sub"), 0]
    count = far_inner.shape[-1]
    matrix = matrix_ref[level, 1 - own_flag]
    rows = []
    for part in range(2):
        value = partial_ref[part] + dot(far_inner[part], centre_ref[1, count:, :])
        rows.append(value.astype(BF16))
    block = LANES
    copies = []
    for begin in range(0, matrix.shape[0], block):
        here = slice(begin, begin + block)
        real, imag = dot(matrix[here], rows[0]), dot(matrix[here], rows[1])
        real, imag = rotated((real, imag), (turn_ref[1, 0, here], turn_ref[1, 1, here]))
        buffer[0, here] = (merged_ref[0, here] + real).astype(buffer.dtype)
        buffer[1, here] = (merged_ref[1, here] + imag).astype(buffer.dtype)
        copy = pltpu.make_async_copy(
            buffer.at[:, here], out_ref.at[:, here], sems.at[begin // block]
        )
        copy.start()
        copies.append(copy)
    for copy in copies:
        copy.wait()


def merged_image(level, fore_flag, own, rims, far, far_rims, centre, rim, angle_interp, turn, dtype):
    angles, bins = turn.shape[-2:]
    cost = pl.CostEstimate(flops=4 * angles * bins * bins, bytes_accessed=8 * MIB, transcendentals=0)
    merged, partial = pl.pallas_call(
        functools.partial(early_kernel, level),
        out_shape=[
            jax.ShapeDtypeStruct((2, angles, bins), F32),
            jax.ShapeDtypeStruct((2, angles // 2, bins), F32),
        ],
        in_specs=[SMEM] + [VMEM] * 11,
        out_specs=[VMEM] * 2,
        compiler_params=params(20),
        cost_estimate=cost,
    )(fore_flag, *own, *rims, far[0], *far_rims, centre, rim, angle_interp, turn)
    return pl.pallas_call(
        functools.partial(late_kernel, level),
        out_shape=jax.ShapeDtypeStruct((2, angles, bins), dtype),
        in_specs=[SMEM] + [VMEM] * 6,
        out_specs=ANY,
        scratch_shapes=[
            pltpu.VMEM((2, angles, bins), dtype),
            pltpu.SemaphoreType.DMA((angles // LANES,)),
        ],
        compiler_params=params(20),
        cost_estimate=cost,
    )(fore_flag, far[1], merged, partial, centre, angle_interp, turn)


def neighbour_rims(low, high):
    devices = lax.axis_size("rng")
    up = [(i, i + 1) for i in range(devices - 1)]
    below = lax.ppermute(high, "rng", up)
    above = lax.ppermute(low, "rng", [(j, i) for i, j in up])
    return below, above


def from_partner(value, stride):
    pairs = [(source, source ^ stride) for source in range(lax.axis_size("sub"))]
    return lax.ppermute(value, "sub", pairs)


def split_image(level, image, fore_flag, rim):
    angles, bins = image.shape[1:]
    half, outer = angles // 2, bins // 4
    own_flag = fore_flag[level, lax.axis_index("sub"), 0]
    sides = image.reshape(2, 2, half, bins)

    def pieces(side):
        rows = lax.dynamic_index_in_dim(sides, side, 1, keepdims=False)
        ends = jnp.concatenate([rows[..., :outer], rows[..., -outer:]], axis=-1)
        return ends, rows[..., outer:-outer]

    def packed(edge):
        return edge.transpose(2, 0, 1, 3).reshape(half, 4 * rim)

    low, high = packed(sides[..., :rim]), packed(sides[..., -rim:])
    return pieces(own_flag), pieces(1 - own_flag), low, high


def on_device(echoes, fore_flag, band_offset, angle_interp, range_kernel, center_shift):
    devices = lax.axis_size("rng")
    chips = devices // 2
    far_chip = chips // 2
    local_pulses = echoes.shape[1]
    bins = echoes.shape[2] // devices
    count = bins // 2
    angles = angle_interp.shape[2]
    rim = MAX_SHIFT + (range_kernel.shape[1] - bins) // 2
    levels = range_kernel.shape[0]

    rows = echoes.reshape(2 * local_pulses, devices * bins)
    direct_same, direct_cross, keep, give = placed(rows, chips, bins)
    direct = (
        exchanged(direct_same, devices, chips),
        exchanged(direct_cross, devices, chips + 1),
    )
    got = exchanged(give, devices, 1)
    first_far = range(far_chip + 1, chips)
    near = range(1, far_chip)
    picks = [(d, 0, count) for d in first_far] + [(d, 0, bins) for d in (*near, 0)]
    sends = joined(picks, keep, got)
    outer_far = [
        exchanged(value, devices, 2 * d) for d, value in zip(first_far, sends)
    ]
    whole = [sends[-1]] + [
        exchanged(value, devices, 2 * d) for d, value in zip(near, sends[len(first_far) :])
    ]
    later = range(far_chip, chips)
    late_sends = joined([(d, count, count) for d in later], keep, got, (outer_far[0],))
    inner_far = [exchanged(value, devices, 2 * d) for d, value in zip(later, late_sends)]

    filter_matrix = filter_table(angles, local_pulses, sends[-1])
    settings = (fore_flag, band_offset, center_shift, range_kernel, angles)
    centre, rim_matrix, turn = merge_tables(0, 1, *settings, filter_matrix)

    own_outer, out_outer, low, high = filtered(
        fore_flag, filter_matrix, (*whole, *direct, *outer_far), 0, count, True
    )
    rims = neighbour_rims(low, high)
    far_outer = from_partner(out_outer, 1)
    far_rims = [from_partner(value, 1) for value in rims]
    own_inner, out_inner = filtered(
        fore_flag, filter_matrix, (*whole, *inner_far), count, count, False
    )
    far_inner = from_partner(out_inner, 1)
    own, far = (own_outer, own_inner), (far_outer, far_inner)
    for level in range(levels):
        if level > 0:
            stride = 2**level
            centre, rim_matrix, turn = merge_tables(level, stride, *settings, image)
            own, out, low, high = split_image(level, image, fore_flag, rim)
            rims = neighbour_rims(low, high)
            far = [from_partner(value, stride) for value in out]
            far_rims = [from_partner(value, stride) for value in rims]
        dtype = BF16 if level + 1 < levels else F32
        image = merged_image(
            level, fore_flag, own, rims, far, far_rims, centre, rim_matrix, angle_interp, turn, dtype
        )
    return image


def solution(mesh):
    placed_as = (
        P(None, ("sub", "rng"), None),
        P(None, None, "rng"),
        P(None, None, "rng"),
        P(),
        P(),
        P(),
    )
    return jax.shard_map(
        on_device, mesh=mesh, in_specs=placed_as, out_specs=P(None, "sub", "rng"), check_vma=False
    )
```

```python
import functools
import math

import jax
import jax.numpy as jnp
from jax import lax
from jax.experimental import pallas as pl
from jax.experimental.pallas import tpu as pltpu
from jax.sharding import PartitionSpec as P

MAX_SHIFT = 16
LANES = 128
MIB = 2**20
VMEM = pl.BlockSpec(memory_space=pltpu.VMEM)
SMEM = pl.BlockSpec(memory_space=pltpu.SMEM)
ANY = pl.BlockSpec(memory_space=pl.ANY)
F32 = jnp.float32
BF16 = jnp.bfloat16


def dot(a, b):
    return jnp.dot(a, b, preferred_element_type=F32)


def params(mib):
    return pltpu.CompilerParams(vmem_limit_bytes=mib * MIB)


def series(square, first, count):
    coefs = [
        (-1) ** i * math.pi ** (2 * i + first) / math.factorial(2 * i + first)
        for i in range(count)
    ]
    total = jnp.full_like(square, coefs[-1])
    for coef in coefs[-2::-1]:
        total = total * square + coef
    return total


def cos_sin_pi(v):
    turns = jnp.floor(v + 0.5)
    rest = v - turns
    sign = 1.0 - 2.0 * (turns - 2.0 * jnp.floor(turns * 0.5))
    square = rest * rest
    return series(square, 0, 8) * sign, series(square, 1, 7) * rest * sign


def rotated(pair, step):
    return pair[0] * step[0] - pair[1] * step[1], pair[0] * step[1] + pair[1] * step[0]


def place_kernel(order, echoes_ref, direct_ref, give_ref, keep_ref, sems):
    me = lax.axis_index("rng")
    bins = keep_ref.shape[-1]
    outer = bins // 4
    copies = []

    def take(device, target):
        for first, count, at in (
            (0, outer, 0),
            (bins - outer, outer, outer),
            (outer, bins - 2 * outer, 2 * outer),
        ):
            start = pl.multiple_of(device * bins + first, LANES)
            copy = pltpu.make_async_copy(
                echoes_ref.at[:, pl.ds(start, count)],
                target.at[:, pl.ds(at, count)],
                sems.at[len(copies)],
            )
            copy.start()
            copies.append(copy)

    take(me ^ (2 * order[-1]), direct_ref)
    for flip, ref in ((1, give_ref), (0, keep_ref)):
        for i, d in enumerate(order[: ref.shape[0]]):
            take(me ^ (2 * d + flip), ref.at[i])
    for copy in copies:
        copy.wait()


def placed(echoes, order, bins):
    rows = echoes.shape[0]
    shapes = [(rows, bins), (len(order), rows, bins), (len(order) - 1, rows, bins)]
    return pl.pallas_call(
        functools.partial(place_kernel, order),
        out_shape=[jax.ShapeDtypeStruct(shape, BF16) for shape in shapes],
        in_specs=[ANY],
        out_specs=[ANY] * 3,
        scratch_shapes=[pltpu.SemaphoreType.DMA((6 * len(order),))],
        compiler_params=params(56),
        cost_estimate=pl.CostEstimate(flops=0, bytes_accessed=2 * MIB, transcendentals=0),
    )(echoes)


def join_kernel(picks, keep_ref, got_ref, *refs):
    rows = keep_ref.shape[1]
    refs[0][...] = got_ref[keep_ref.shape[0]]
    for (i, first, count), out_ref in zip(picks, refs[1:]):
        out_ref[:rows] = keep_ref[i, :, first : first + count]
        out_ref[rows:] = got_ref[i, :, first : first + count]


def joined(picks, keep, got):
    _, rows, bins = keep.shape
    shapes = [(rows, bins)] + [(2 * rows, count) for _, _, count in picks]
    return pl.pallas_call(
        functools.partial(join_kernel, picks),
        out_shape=[jax.ShapeDtypeStruct(shape, BF16) for shape in shapes],
        in_specs=[VMEM] * 2,
        out_specs=[VMEM] * len(shapes),
        compiler_params=params(8),
        cost_estimate=pl.CostEstimate(flops=0, bytes_accessed=2 * MIB, transcendentals=0),
    )(keep, got)


def after(value, *earlier):
    return lax.optimization_barrier((value, *earlier))[0]


def exchanged(value, devices, mask):
    return lax.ppermute(value, "rng", [(i, i ^ mask) for i in range(devices)])


def filter_table_kernel(local_pulses, after_ref, filter_ref, cos_ref, sin_ref):
    me = lax.axis_index("rng")
    columns = filter_ref.shape[1]
    angles = filter_ref.shape[0] // 2
    base = cos_ref.shape[0]
    scale = 1.0 / math.sqrt(columns // 2)
    lane = lax.broadcasted_iota(jnp.int32, (8, columns), 1)
    slot = lane // (2 * local_pulses)
    second = lane // local_pulses % 2
    pulse_id = (slot ^ me) * local_pulses + lane % local_pulses
    pulse = pulse_id.astype(F32)
    lag = second.astype(F32) * 0.5
    per_angle = pulse * (1.0 / angles)
    row = lax.broadcasted_iota(jnp.int32, (8, columns), 0)
    for i in range(base // 8):
        twice = (2 * (row + 8 * i) + 1 - angles).astype(F32)
        cosine, sine = cos_sin_pi(twice * per_angle - lag)
        cos_ref[8 * i : 8 * i + 8, :] = cosine * scale
        sin_ref[8 * i : 8 * i + 8, :] = sine * scale
    step = cos_sin_pi(per_angle * (2 * base))
    for j in range(angles // base):
        for i in range(base // 16):
            pair = [], []
            for k in (2 * i, 2 * i + 1):
                here = slice(8 * k, 8 * k + 8)
                now = cos_ref[here, :], sin_ref[here, :]
                pair[0].append(now[0])
                pair[1].append(-now[1])
                if j + 1 < angles // base:
                    cos_ref[here, :], sin_ref[here, :] = rotated(now, step)
            begin = j * base + 16 * i
            filter_ref[begin : begin + 16, :] = jnp.concatenate(pair[0]).astype(BF16)
            begin += angles
            filter_ref[begin : begin + 16, :] = jnp.concatenate(pair[1]).astype(BF16)


def filter_table(angles, local_pulses, after):
    side = 2 * local_pulses * lax.axis_size("rng")
    return pl.pallas_call(
        functools.partial(filter_table_kernel, local_pulses),
        out_shape=jax.ShapeDtypeStruct((2 * angles, side), BF16),
        in_specs=[ANY],
        out_specs=VMEM,
        scratch_shapes=[pltpu.VMEM((64, side), F32)] * 2,
        compiler_params=params(6),
        cost_estimate=pl.CostEstimate(flops=9_000_000, bytes_accessed=4 * MIB, transcendentals=0),
    )(after)


def merge_table_kernel(
    level, stride, flag_ref, offset_ref, shift_ref, range_ref, after_ref, centre_ref, rim_ref, turn_ref
):
    group = lax.axis_index("sub")
    block = lax.axis_index("rng")
    bins = centre_ref.shape[-1]
    angles = turn_ref.shape[-2]
    total_bins = lax.axis_size("rng") * bins
    own_flag = flag_ref[level, group, 0]
    taps = range_ref.shape[1]
    band = (taps - bins) // 2
    rim = MAX_SHIFT + band
    outer = bins // 4
    kernel = range_ref[level]

    def moved(bin_id):
        tap = lax.broadcasted_iota(jnp.int32, (bin_id.shape[0], taps), 1)
        return dot(jnp.where(tap == bin_id, 1.0, 0.0).astype(BF16), kernel).astype(BF16)

    row = lax.broadcasted_iota(jnp.int32, (bins, 1), 0)
    own_bin = row - outer
    own_bin = jnp.where(row < 2 * outer, row + (bins - 2 * outer), own_bin)
    own_bin = jnp.where(row < outer, row, own_bin)
    rim_row = lax.broadcasted_iota(jnp.int32, (2 * rim, 1), 0)
    rim_bin = jnp.where(rim_row < rim, rim_row - rim, rim_row - rim + bins)
    rim_ref[...] = jnp.zeros(rim_ref.shape, BF16)
    bin_id = block * bins + lax.broadcasted_iota(jnp.int32, (1, LANES), 1)
    reach = 1.0 + bin_id.astype(F32) * (1.0 / total_bins)
    rows = 64
    for child in range(2):
        member = group if child == 0 else group ^ stride
        lead = band - offset_ref[level, member, 0]
        centre_ref[child] = moved(own_bin + lead)
        ends = moved(rim_bin + lead)
        for part in range(2):
            place = pl.multiple_of((2 * part + own_flag) * rim, rim)
            rim_ref[child, part, pl.ds(place, rim), :] = ends[:rim]
            rim_ref[child, part, pl.ds(4 * rim + place, rim), :] = ends[rim:]

        rate = shift_ref[level, member]

        def turn_rows(i, carry):
            begin = pl.multiple_of(i * rows, rows)
            angle = begin + lax.broadcasted_iota(jnp.int32, (rows, LANES), 0)
            place = ((angle.astype(F32) + 0.5) * (1.0 / angles) - 0.5) * rate
            now = cos_sin_pi(place * reach)
            step = cos_sin_pi(place * (LANES / total_bins))
            for tile in range(bins // LANES):
                lanes = slice(tile * LANES, tile * LANES + LANES)
                turn_ref[child, 0, pl.ds(begin, rows), lanes] = now[0]
                turn_ref[child, 1, pl.ds(begin, rows), lanes] = now[1]
                now = rotated(now, step)
            return carry

        lax.fori_loop(0, angles // rows, turn_rows, 0)


def merge_tables(level, stride, fore_flag, band_offset, center_shift, range_kernel, angles, after):
    taps, bins = range_kernel.shape[1:]
    rim = MAX_SHIFT + (taps - bins) // 2
    return pl.pallas_call(
        functools.partial(merge_table_kernel, level, stride),
        out_shape=[
            jax.ShapeDtypeStruct((2, bins, bins), BF16),
            jax.ShapeDtypeStruct((2, 2, 8 * rim, bins), BF16),
            jax.ShapeDtypeStruct((2, 2, angles, bins), F32),
        ],
        in_specs=[SMEM] * 3 + [VMEM, ANY],
        out_specs=[VMEM] * 3,
        compiler_params=params(12),
        cost_estimate=pl.CostEstimate(
            flops=2_300_000_000, bytes_accessed=7 * MIB, transcendentals=0
        ),
    )(fore_flag, band_offset, center_shift, range_kernel, after)


def filter_kernel(pieces, first, count, ends, flag_ref, filter_ref, *refs):
    own_flag = flag_ref[0, lax.axis_index("sub"), 0]
    pulses_ref, image_ref = refs[-2:]
    own_ref, out_ref = refs[pieces : pieces + 2]
    at = 0
    for ref in refs[:pieces]:
        begin = first if ref.shape[1] > count else 0
        pulses_ref[at : at + ref.shape[0], :] = ref[:, begin : begin + count]
        at += ref.shape[0]
    image_ref[...] = dot(filter_ref[...], pulses_ref[...])
    half = own_ref.shape[1]
    foremost = own_flag == 0
    for part in range(2):
        upper = image_ref[2 * part * half : (2 * part + 1) * half, :]
        lower = image_ref[(2 * part + 1) * half : (2 * part + 2) * half, :]
        own_ref[part] = jnp.where(foremost, upper, lower).astype(BF16)
        out_ref[part] = jnp.where(foremost, lower, upper).astype(BF16)
    if ends:
        rim = LANES // 4
        lane = lax.broadcasted_iota(jnp.int32, (1, LANES), 1)

        def packed(lanes, edge):
            total = jnp.zeros((half, LANES), F32)
            for group in range(4):
                value = image_ref[group * half : (group + 1) * half, lanes]
                turn = (group * rim - edge) % LANES
                value = pltpu.roll(value, turn, 1) if turn else value
                total = jnp.where(lane // rim == group, value, total)
            return total.astype(BF16)

        low = packed(slice(0, LANES), 0)
        high = packed(slice(count - LANES, count), LANES - rim)
        even = lax.axis_index("rng") % 2 == 0
        refs[pieces + 2][...] = jnp.where(even, high, low)
        refs[pieces + 3][...] = jnp.where(even, low, high)


def filtered(fore_flag, filter_matrix, pieces, first, count, ends):
    angles = filter_matrix.shape[0]
    half = angles // 4
    shapes = [jax.ShapeDtypeStruct((2, half, count), BF16)] * 2
    if ends:
        shapes += [jax.ShapeDtypeStruct((half, LANES), BF16)] * 2
    return pl.pallas_call(
        functools.partial(filter_kernel, len(pieces), first, count, ends),
        out_shape=shapes,
        in_specs=[SMEM] + [VMEM] * (1 + len(pieces)),
        out_specs=[VMEM] * len(shapes),
        scratch_shapes=[
            pltpu.VMEM((filter_matrix.shape[1], count), BF16),
            pltpu.VMEM((angles, count), F32),
        ],
        compiler_params=params(10),
        cost_estimate=pl.CostEstimate(
            flops=2 * filter_matrix.size * count, bytes_accessed=4 * MIB, transcendentals=0
        ),
    )(fore_flag, filter_matrix, *pieces)


def rims_of(first, second):
    even = lax.axis_index("rng") % 2 == 0
    below = jnp.where(even, second, first)
    above = jnp.where(even, first, second)
    return jnp.concatenate([below, above], axis=1)


def early_kernel(
    level, flag_ref, own_outer, own_inner, rim_first, rim_second, far_outer, far_first, far_second,
    centre_ref, rim_ref, matrix_ref, turn_ref, merged_ref, partial_ref, value_ref, term_ref,
):
    own_flag = flag_ref[level, lax.axis_index("sub"), 0]
    parts, half, count = own_outer.shape
    bins = centre_ref.shape[-1]
    own_rims = rims_of(rim_first[...], rim_second[...])
    far_rims = rims_of(far_first[...], far_second[...])
    image = jnp.concatenate([own_outer[...], own_inner[...]], axis=2)
    value_ref[...] = dot(image.reshape(parts * half, 2 * count), centre_ref[0])
    matrix = matrix_ref[level, own_flag]
    for part in range(parts):
        value = value_ref[part * half : (part + 1) * half, :] + dot(own_rims, rim_ref[0, part])
        term_ref[part] = dot(matrix, value.astype(BF16))
    merged_ref[0], merged_ref[1] = rotated(
        (term_ref[0], term_ref[1]), (turn_ref[0, 0], turn_ref[0, 1])
    )
    outer = far_outer[...].reshape(parts * half, count)
    value_ref[...] = dot(outer, centre_ref[1, :count, :])
    for part in range(parts):
        value = value_ref[part * half : (part + 1) * half, :]
        partial_ref[part] = value + dot(far_rims, rim_ref[1, part])


def late_kernel(
    level, flag_ref, far_inner, merged_ref, partial_ref, centre_ref, matrix_ref, turn_ref, out_ref,
    buffer, value_ref, sems,
):
    own_flag = flag_ref[level, lax.axis_index("sub"), 0]
    parts, half, count = far_inner.shape
    inner = far_inner[...].reshape(parts * half, count)
    value_ref[...] = dot(inner, centre_ref[1, count:, :])
    rows = []
    for part in range(parts):
        value = value_ref[part * half : (part + 1) * half, :] + partial_ref[part]
        rows.append(value.astype(BF16))
    matrix = matrix_ref.at[level, 1 - own_flag]
    block = 2 * LANES
    copies = []
    for begin in range(0, matrix.shape[0], block):
        here = slice(begin, begin + block)
        turned = rotated(
            (dot(matrix[here], rows[0]), dot(matrix[here], rows[1])),
            (turn_ref[1, 0, here], turn_ref[1, 1, here]),
        )
        for part in range(parts):
            buffer[part, here] = (merged_ref[part, here] + turned[part]).astype(buffer.dtype)
            copy = pltpu.make_async_copy(
                buffer.at[part, here], out_ref.at[part, here], sems.at[len(copies)]
            )
            copy.start()
            copies.append(copy)
    for copy in copies:
        copy.wait()


def merged_image(level, fore_flag, own, rims, far, far_rims, centre, rim, angle_interp, turn, dtype):
    angles, bins = turn.shape[-2:]
    cost = pl.CostEstimate(flops=4 * angles * bins * bins, bytes_accessed=8 * MIB, transcendentals=0)
    merged, partial = pl.pallas_call(
        functools.partial(early_kernel, level),
        out_shape=[
            jax.ShapeDtypeStruct((2, angles, bins), F32),
            jax.ShapeDtypeStruct((2, angles // 2, bins), F32),
        ],
        in_specs=[SMEM] + [VMEM] * 11,
        out_specs=[VMEM] * 2,
        scratch_shapes=[pltpu.VMEM((angles, bins), F32), pltpu.VMEM((2, angles, bins), F32)],
        compiler_params=params(20),
        cost_estimate=cost,
    )(fore_flag, *own, *rims, far[0], *far_rims, centre, rim, angle_interp, turn)
    return pl.pallas_call(
        functools.partial(late_kernel, level),
        out_shape=jax.ShapeDtypeStruct((2, angles, bins), dtype),
        in_specs=[SMEM] + [VMEM] * 6,
        out_specs=ANY,
        scratch_shapes=[
            pltpu.VMEM((2, angles, bins), dtype),
            pltpu.VMEM((angles, bins), F32),
            pltpu.SemaphoreType.DMA((angles // LANES,)),
        ],
        compiler_params=params(20),
        cost_estimate=cost,
    )(fore_flag, far[1], merged, partial, centre, angle_interp, turn)


def neighbour_rims(first, second):
    devices = lax.axis_size("rng")
    pairs = [(i, i + 1) for i in range(1, devices - 1, 2)]
    return (
        exchanged(first, devices, 1),
        lax.ppermute(second, "rng", pairs + [(j, i) for i, j in pairs]),
    )


def from_partner(value, stride):
    pairs = [(source, source ^ stride) for source in range(lax.axis_size("sub"))]
    return lax.ppermute(value, "sub", pairs)


def split_image(level, image, fore_flag, rim):
    angles, bins = image.shape[1:]
    half, outer = angles // 2, bins // 4
    own_flag = fore_flag[level, lax.axis_index("sub"), 0]
    sides = image.reshape(2, 2, half, bins)

    def pieces(side):
        rows = lax.dynamic_index_in_dim(sides, side, 1, keepdims=False)
        ends = jnp.concatenate([rows[..., :outer], rows[..., -outer:]], axis=-1)
        return ends, rows[..., outer:-outer]

    def packed(edge):
        return edge.transpose(2, 0, 1, 3).reshape(half, 4 * rim)

    low, high = packed(sides[..., :rim]), packed(sides[..., -rim:])
    even = lax.axis_index("rng") % 2 == 0
    edges = jnp.where(even, high, low), jnp.where(even, low, high)
    return pieces(own_flag), pieces(1 - own_flag), edges


def on_device(echoes, fore_flag, band_offset, angle_interp, range_kernel, center_shift):
    devices = lax.axis_size("rng")
    chips = devices // 2
    far_chip = chips // 2
    local_pulses = echoes.shape[1]
    bins = echoes.shape[2] // devices
    count = bins // 2
    angles = angle_interp.shape[2]
    rim = MAX_SHIFT + (range_kernel.shape[1] - bins) // 2
    levels = range_kernel.shape[0]

    rows = echoes.reshape(2 * local_pulses, devices * bins)
    near, far = list(range(1, far_chip)), list(range(far_chip + 1, chips))
    order = [*far, *near, 0, far_chip]
    direct, give, keep = placed(rows, order, bins)
    got = exchanged(give, devices, 1)
    first_far = [exchanged(direct, devices, 2 * far_chip)]
    picks = [(i, 0, count) for i in range(len(far))]
    picks += [(i, count, count) for i in range(len(far))]
    picks += [(i, 0, bins) for i in range(len(far), chips - 1)]
    relay, *sends = joined(picks, keep, got)
    outer_sends, inner_sends = sends[: len(far)], sends[len(far) : 2 * len(far)]
    whole_sends = sends[2 * len(far) :]
    first_far.append(exchanged(relay, devices, 2 * far_chip))
    outer_far, inner_far = [], []
    for i, d in enumerate(far):
        earlier = (got, *first_far, *outer_far)[i]
        outer_far.append(exchanged(after(outer_sends[i], earlier), devices, 2 * d))
    whole = [whole_sends[-1]]
    for i, d in enumerate(near):
        whole.append(exchanged(after(whole_sends[i], first_far[1]), devices, 2 * d))
    whole += first_far

    filter_matrix = filter_table(angles, local_pulses, whole_sends[-1])
    own_outer, out_outer, *edges = filtered(
        fore_flag, filter_matrix, (*whole, *outer_far), 0, count, True
    )
    for i, d in enumerate(far):
        earlier = (own_outer,) if i else (outer_far[1],)
        inner_far.append(exchanged(after(inner_sends[i], *earlier), devices, 2 * d))
    far_outer = from_partner(out_outer, 1)
    rims = neighbour_rims(*(after(edge, inner_far[0]) for edge in edges))
    far_rims = [from_partner(value, 1) for value in rims]
    own_inner, out_inner = filtered(
        fore_flag, filter_matrix, (*whole, *inner_far), count, count, False
    )
    far_inner = from_partner(out_inner, 1)
    settings = (fore_flag, band_offset, center_shift, range_kernel, angles)
    centre, rim_matrix, turn = merge_tables(0, 1, *settings, own_inner)
    own, far = (own_outer, own_inner), (far_outer, far_inner)
    for level in range(levels):
        if level > 0:
            stride = 2**level
            centre, rim_matrix, turn = merge_tables(level, stride, *settings, image)
            own, out, edges = split_image(level, image, fore_flag, rim)
            rims = neighbour_rims(*edges)
            far = [from_partner(value, stride) for value in out]
            far_rims = [from_partner(value, stride) for value in rims]
        dtype = BF16 if level + 1 < levels else F32
        image = merged_image(
            level, fore_flag, own, rims, far, far_rims, centre, rim_matrix, angle_interp, turn, dtype
        )
    return image


def solution(mesh):
    placed_as = (
        P(None, ("sub", "rng"), None),
        P(None, None, "rng"),
        P(None, None, "rng"),
        P(),
        P(),
        P(),
    )
    return jax.shard_map(
        on_device, mesh=mesh, in_specs=placed_as, out_specs=P(None, "sub", "rng"), check_vma=False
    )
```

```python
import functools
import math

import jax
import jax.numpy as jnp
from jax import lax
from jax.experimental import pallas as pl
from jax.experimental.pallas import tpu as pltpu
from jax.sharding import PartitionSpec as P

MAX_SHIFT = 16
LANES = 128
MIB = 2**20
VMEM = pl.BlockSpec(memory_space=pltpu.VMEM)
SMEM = pl.BlockSpec(memory_space=pltpu.SMEM)
ANY = pl.BlockSpec(memory_space=pl.ANY)
F32 = jnp.float32
BF16 = jnp.bfloat16


def dot(a, b):
    return jnp.dot(a, b, preferred_element_type=F32)


def params(mib):
    return pltpu.CompilerParams(vmem_limit_bytes=mib * MIB)


def series(square, first, count):
    coefs = [
        (-1) ** i * math.pi ** (2 * i + first) / math.factorial(2 * i + first)
        for i in range(count)
    ]
    total = jnp.full_like(square, coefs[-1])
    for coef in coefs[-2::-1]:
        total = total * square + coef
    return total


def cos_sin_pi(v):
    turns = jnp.floor(v + 0.5)
    rest = v - turns
    sign = 1.0 - 2.0 * (turns - 2.0 * jnp.floor(turns * 0.5))
    square = rest * rest
    return series(square, 0, 8) * sign, series(square, 1, 7) * rest * sign


def rotated(pair, step):
    return pair[0] * step[0] - pair[1] * step[1], pair[0] * step[1] + pair[1] * step[0]


def place_kernel(order, echoes_ref, turn_ref, give_ref, keep_ref, sems):
    me = lax.axis_index("rng")
    outer = turn_ref.shape[-1] // 2
    bins = 4 * outer
    copies = []

    def take(device, first, count, target):
        start = pl.multiple_of(device * bins + first, LANES)
        copy = pltpu.make_async_copy(
            echoes_ref.at[:, pl.ds(start, count)], target, sems.at[len(copies)]
        )
        copy.start()
        copies.append(copy)

    for flip, ref in ((1, give_ref), (0, keep_ref)):
        for i, d in enumerate(order):
            take(me ^ (2 * d + flip), outer, bins - 2 * outer, ref.at[i])
    for device in range(turn_ref.shape[0]):
        take(device, 0, outer, turn_ref.at[device, :, pl.ds(0, outer)])
        take(device, bins - outer, outer, turn_ref.at[device, :, pl.ds(outer, outer)])
    for copy in copies:
        copy.wait()


def placed(echoes, order, bins):
    rows = echoes.shape[0]
    chips = len(order)
    shapes = [(2 * chips, rows, bins // 2), (chips, rows, bins // 2), (chips, rows, bins // 2)]
    return pl.pallas_call(
        functools.partial(place_kernel, order),
        out_shape=[jax.ShapeDtypeStruct(shape, BF16) for shape in shapes],
        in_specs=[ANY],
        out_specs=[VMEM] * 3,
        scratch_shapes=[pltpu.SemaphoreType.DMA((6 * chips,))],
        compiler_params=params(8),
        cost_estimate=pl.CostEstimate(flops=0, bytes_accessed=2 * MIB, transcendentals=0),
    )(echoes)


def join_kernel(keep_ref, got_ref, *refs):
    rows = keep_ref.shape[1]
    for i, out_ref in enumerate(refs):
        out_ref[:rows] = keep_ref[i]
        out_ref[rows:] = got_ref[i]


def joined(keep, got):
    chips, rows, count = keep.shape
    return pl.pallas_call(
        join_kernel,
        out_shape=[jax.ShapeDtypeStruct((2 * rows, count), BF16)] * chips,
        in_specs=[VMEM] * 2,
        out_specs=[VMEM] * chips,
        compiler_params=params(8),
        cost_estimate=pl.CostEstimate(flops=0, bytes_accessed=MIB, transcendentals=0),
    )(keep, got)


def after(value, *earlier):
    return lax.optimization_barrier((value, *earlier))[0]


def exchanged(value, devices, mask):
    return lax.ppermute(value, "rng", [(i, i ^ mask) for i in range(devices)])


def filter_table_kernel(local_pulses, after_ref, filter_ref, cos_ref, sin_ref):
    me = lax.axis_index("rng")
    columns = filter_ref.shape[1]
    angles = filter_ref.shape[0] // 2
    base = cos_ref.shape[0]
    scale = 1.0 / math.sqrt(columns // 2)
    lane = lax.broadcasted_iota(jnp.int32, (8, columns), 1)
    slot = lane // (2 * local_pulses)
    second = lane // local_pulses % 2
    pulse_id = (slot ^ me) * local_pulses + lane % local_pulses
    pulse = pulse_id.astype(F32)
    lag = second.astype(F32) * 0.5
    per_angle = pulse * (1.0 / angles)
    row = lax.broadcasted_iota(jnp.int32, (8, columns), 0)
    for i in range(base // 8):
        twice = (2 * (row + 8 * i) + 1 - angles).astype(F32)
        cosine, sine = cos_sin_pi(twice * per_angle - lag)
        cos_ref[8 * i : 8 * i + 8, :] = cosine * scale
        sin_ref[8 * i : 8 * i + 8, :] = sine * scale
    step = cos_sin_pi(per_angle * (2 * base))
    for j in range(angles // base):
        for i in range(base // 16):
            pair = [], []
            for k in (2 * i, 2 * i + 1):
                here = slice(8 * k, 8 * k + 8)
                now = cos_ref[here, :], sin_ref[here, :]
                pair[0].append(now[0])
                pair[1].append(-now[1])
                if j + 1 < angles // base:
                    cos_ref[here, :], sin_ref[here, :] = rotated(now, step)
            begin = j * base + 16 * i
            filter_ref[begin : begin + 16, :] = jnp.concatenate(pair[0]).astype(BF16)
            begin += angles
            filter_ref[begin : begin + 16, :] = jnp.concatenate(pair[1]).astype(BF16)


def filter_table(angles, local_pulses, after):
    side = 2 * local_pulses * lax.axis_size("rng")
    return pl.pallas_call(
        functools.partial(filter_table_kernel, local_pulses),
        out_shape=jax.ShapeDtypeStruct((2 * angles, side), BF16),
        in_specs=[ANY],
        out_specs=VMEM,
        scratch_shapes=[pltpu.VMEM((64, side), F32)] * 2,
        compiler_params=params(6),
        cost_estimate=pl.CostEstimate(flops=9_000_000, bytes_accessed=4 * MIB, transcendentals=0),
    )(after)


def merge_table_kernel(
    level, stride, flag_ref, offset_ref, shift_ref, range_ref, after_ref, centre_ref, rim_ref, turn_ref
):
    group = lax.axis_index("sub")
    block = lax.axis_index("rng")
    bins = centre_ref.shape[-1]
    angles = turn_ref.shape[-2]
    total_bins = lax.axis_size("rng") * bins
    own_flag = flag_ref[level, group, 0]
    taps = range_ref.shape[1]
    band = (taps - bins) // 2
    rim = MAX_SHIFT + band
    outer = bins // 4
    kernel = range_ref[level]

    def moved(bin_id):
        tap = lax.broadcasted_iota(jnp.int32, (bin_id.shape[0], taps), 1)
        return dot(jnp.where(tap == bin_id, 1.0, 0.0).astype(BF16), kernel).astype(BF16)

    row = lax.broadcasted_iota(jnp.int32, (bins, 1), 0)
    own_bin = row - outer
    own_bin = jnp.where(row < 2 * outer, row + (bins - 2 * outer), own_bin)
    own_bin = jnp.where(row < outer, row, own_bin)
    rim_row = lax.broadcasted_iota(jnp.int32, (2 * rim, 1), 0)
    rim_bin = jnp.where(rim_row < rim, rim_row - rim, rim_row - rim + bins)
    rim_ref[...] = jnp.zeros(rim_ref.shape, BF16)
    bin_id = block * bins + lax.broadcasted_iota(jnp.int32, (1, LANES), 1)
    reach = 1.0 + bin_id.astype(F32) * (1.0 / total_bins)
    rows = 64
    for child in range(2):
        member = group if child == 0 else group ^ stride
        lead = band - offset_ref[level, member, 0]
        centre_ref[child] = moved(own_bin + lead)
        ends = moved(rim_bin + lead)
        for part in range(2):
            place = pl.multiple_of((2 * part + own_flag) * rim, rim)
            rim_ref[child, part, pl.ds(place, rim), :] = ends[:rim]
            rim_ref[child, part, pl.ds(4 * rim + place, rim), :] = ends[rim:]

        rate = shift_ref[level, member]

        def turn_rows(i, carry):
            begin = pl.multiple_of(i * rows, rows)
            angle = begin + lax.broadcasted_iota(jnp.int32, (rows, LANES), 0)
            place = ((angle.astype(F32) + 0.5) * (1.0 / angles) - 0.5) * rate
            now = cos_sin_pi(place * reach)
            step = cos_sin_pi(place * (LANES / total_bins))
            for tile in range(bins // LANES):
                lanes = slice(tile * LANES, tile * LANES + LANES)
                turn_ref[child, 0, pl.ds(begin, rows), lanes] = now[0]
                turn_ref[child, 1, pl.ds(begin, rows), lanes] = now[1]
                now = rotated(now, step)
            return carry

        lax.fori_loop(0, angles // rows, turn_rows, 0)


def merge_tables(level, stride, fore_flag, band_offset, center_shift, range_kernel, angles, after):
    taps, bins = range_kernel.shape[1:]
    rim = MAX_SHIFT + (taps - bins) // 2
    return pl.pallas_call(
        functools.partial(merge_table_kernel, level, stride),
        out_shape=[
            jax.ShapeDtypeStruct((2, bins, bins), BF16),
            jax.ShapeDtypeStruct((2, 2, 8 * rim, bins), BF16),
            jax.ShapeDtypeStruct((2, 2, angles, bins), F32),
        ],
        in_specs=[SMEM] * 3 + [VMEM, ANY],
        out_specs=[VMEM] * 3,
        compiler_params=params(12),
        cost_estimate=pl.CostEstimate(
            flops=2_300_000_000, bytes_accessed=7 * MIB, transcendentals=0
        ),
    )(fore_flag, band_offset, center_shift, range_kernel, after)


def filter_kernel(pieces, ends, flag_ref, filter_ref, *refs):
    own_flag = flag_ref[0, lax.axis_index("sub"), 0]
    me = lax.axis_index("rng")
    pulses_ref, image_ref = refs[-2:]
    own_ref, out_ref = refs[pieces : pieces + 2]
    count = own_ref.shape[-1]
    if ends:
        devices, rows, _ = refs[0].shape
        for slot in range(devices):
            pulses_ref[slot * rows : (slot + 1) * rows, :] = refs[0][me ^ slot]
    else:
        at = 0
        for ref in refs[:pieces]:
            pulses_ref[at : at + ref.shape[0], :] = ref[...]
            at += ref.shape[0]
    image_ref[...] = dot(filter_ref[...], pulses_ref[...])
    half = own_ref.shape[1]
    foremost = own_flag == 0
    for part in range(2):
        upper = image_ref[2 * part * half : (2 * part + 1) * half, :]
        lower = image_ref[(2 * part + 1) * half : (2 * part + 2) * half, :]
        own_ref[part] = jnp.where(foremost, upper, lower).astype(BF16)
        out_ref[part] = jnp.where(foremost, lower, upper).astype(BF16)
    if ends:
        rim = LANES // 4
        lane = lax.broadcasted_iota(jnp.int32, (1, LANES), 1)

        def packed(lanes, edge):
            total = jnp.zeros((half, LANES), F32)
            for group in range(4):
                value = image_ref[group * half : (group + 1) * half, lanes]
                turn = (group * rim - edge) % LANES
                value = pltpu.roll(value, turn, 1) if turn else value
                total = jnp.where(lane // rim == group, value, total)
            return total.astype(BF16)

        low = packed(slice(0, LANES), 0)
        high = packed(slice(count - LANES, count), LANES - rim)
        even = lax.axis_index("rng") % 2 == 0
        refs[pieces + 2][...] = jnp.where(even, high, low)
        refs[pieces + 3][...] = jnp.where(even, low, high)


def filtered(fore_flag, filter_matrix, pieces, ends):
    angles = filter_matrix.shape[0]
    count = pieces[0].shape[-1]
    half = angles // 4
    shapes = [jax.ShapeDtypeStruct((2, half, count), BF16)] * 2
    if ends:
        shapes += [jax.ShapeDtypeStruct((half, LANES), BF16)] * 2
    return pl.pallas_call(
        functools.partial(filter_kernel, len(pieces), ends),
        out_shape=shapes,
        in_specs=[SMEM] + [VMEM] * (1 + len(pieces)),
        out_specs=[VMEM] * len(shapes),
        scratch_shapes=[
            pltpu.VMEM((filter_matrix.shape[1], count), BF16),
            pltpu.VMEM((angles, count), F32),
        ],
        compiler_params=params(10),
        cost_estimate=pl.CostEstimate(
            flops=2 * filter_matrix.size * count, bytes_accessed=4 * MIB, transcendentals=0
        ),
    )(fore_flag, filter_matrix, *pieces)


def rims_of(first, second):
    even = lax.axis_index("rng") % 2 == 0
    below = jnp.where(even, second, first)
    above = jnp.where(even, first, second)
    return jnp.concatenate([below, above], axis=1)


def early_kernel(
    level, flag_ref, own_outer, own_inner, rim_first, rim_second, far_outer, far_first, far_second,
    centre_ref, rim_ref, matrix_ref, turn_ref, merged_ref, partial_ref, value_ref, term_ref,
):
    own_flag = flag_ref[level, lax.axis_index("sub"), 0]
    parts, half, count = own_outer.shape
    bins = centre_ref.shape[-1]
    own_rims = rims_of(rim_first[...], rim_second[...])
    far_rims = rims_of(far_first[...], far_second[...])
    image = jnp.concatenate([own_outer[...], own_inner[...]], axis=2)
    value_ref[...] = dot(image.reshape(parts * half, 2 * count), centre_ref[0])
    matrix = matrix_ref[level, own_flag]
    for part in range(parts):
        value = value_ref[part * half : (part + 1) * half, :] + dot(own_rims, rim_ref[0, part])
        term_ref[part] = dot(matrix, value.astype(BF16))
    merged_ref[0], merged_ref[1] = rotated(
        (term_ref[0], term_ref[1]), (turn_ref[0, 0], turn_ref[0, 1])
    )
    outer = far_outer[...].reshape(parts * half, count)
    value_ref[...] = dot(outer, centre_ref[1, :count, :])
    for part in range(parts):
        value = value_ref[part * half : (part + 1) * half, :]
        partial_ref[part] = value + dot(far_rims, rim_ref[1, part])


def late_kernel(
    level, flag_ref, far_inner, merged_ref, partial_ref, centre_ref, matrix_ref, turn_ref, out_ref,
    buffer, value_ref, sems,
):
    own_flag = flag_ref[level, lax.axis_index("sub"), 0]
    parts, half, count = far_inner.shape
    inner = far_inner[...].reshape(parts * half, count)
    value_ref[...] = dot(inner, centre_ref[1, count:, :])
    rows = []
    for part in range(parts):
        value = value_ref[part * half : (part + 1) * half, :] + partial_ref[part]
        rows.append(value.astype(BF16))
    matrix = matrix_ref.at[level, 1 - own_flag]
    block = 2 * LANES
    copies = []
    for begin in range(0, matrix.shape[0], block):
        here = slice(begin, begin + block)
        turned = rotated(
            (dot(matrix[here], rows[0]), dot(matrix[here], rows[1])),
            (turn_ref[1, 0, here], turn_ref[1, 1, here]),
        )
        for part in range(parts):
            buffer[part, here] = (merged_ref[part, here] + turned[part]).astype(buffer.dtype)
            copy = pltpu.make_async_copy(
                buffer.at[part, here], out_ref.at[part, here], sems.at[len(copies)]
            )
            copy.start()
            copies.append(copy)
    for copy in copies:
        copy.wait()


def merged_image(level, fore_flag, own, rims, far, far_rims, centre, rim, angle_interp, turn, dtype):
    angles, bins = turn.shape[-2:]
    cost = pl.CostEstimate(flops=4 * angles * bins * bins, bytes_accessed=8 * MIB, transcendentals=0)
    merged, partial = pl.pallas_call(
        functools.partial(early_kernel, level),
        out_shape=[
            jax.ShapeDtypeStruct((2, angles, bins), F32),
            jax.ShapeDtypeStruct((2, angles // 2, bins), F32),
        ],
        in_specs=[SMEM] + [VMEM] * 11,
        out_specs=[VMEM] * 2,
        scratch_shapes=[pltpu.VMEM((angles, bins), F32), pltpu.VMEM((2, angles, bins), F32)],
        compiler_params=params(20),
        cost_estimate=cost,
    )(fore_flag, *own, *rims, far[0], *far_rims, centre, rim, angle_interp, turn)
    return pl.pallas_call(
        functools.partial(late_kernel, level),
        out_shape=jax.ShapeDtypeStruct((2, angles, bins), dtype),
        in_specs=[SMEM] + [VMEM] * 6,
        out_specs=ANY,
        scratch_shapes=[
            pltpu.VMEM((2, angles, bins), dtype),
            pltpu.VMEM((angles, bins), F32),
            pltpu.SemaphoreType.DMA((angles // LANES,)),
        ],
        compiler_params=params(20),
        cost_estimate=cost,
    )(fore_flag, far[1], merged, partial, centre, angle_interp, turn)


def neighbour_rims(first, second):
    devices = lax.axis_size("rng")
    pairs = [(i, i + 1) for i in range(1, devices - 1, 2)]
    return (
        exchanged(first, devices, 1),
        lax.ppermute(second, "rng", pairs + [(j, i) for i, j in pairs]),
    )


def from_partner(value, stride):
    pairs = [(source, source ^ stride) for source in range(lax.axis_size("sub"))]
    return lax.ppermute(value, "sub", pairs)


def split_image(level, image, fore_flag, rim):
    angles, bins = image.shape[1:]
    half, outer = angles // 2, bins // 4
    own_flag = fore_flag[level, lax.axis_index("sub"), 0]
    sides = image.reshape(2, 2, half, bins)

    def pieces(side):
        rows = lax.dynamic_index_in_dim(sides, side, 1, keepdims=False)
        ends = jnp.concatenate([rows[..., :outer], rows[..., -outer:]], axis=-1)
        return ends, rows[..., outer:-outer]

    def packed(edge):
        return edge.transpose(2, 0, 1, 3).reshape(half, 4 * rim)

    low, high = packed(sides[..., :rim]), packed(sides[..., -rim:])
    even = lax.axis_index("rng") % 2 == 0
    edges = jnp.where(even, high, low), jnp.where(even, low, high)
    return pieces(own_flag), pieces(1 - own_flag), edges


def on_device(echoes, fore_flag, band_offset, angle_interp, range_kernel, center_shift):
    devices = lax.axis_size("rng")
    chips = devices // 2
    far_chip = chips // 2
    local_pulses = echoes.shape[1]
    bins = echoes.shape[2] // devices
    angles = angle_interp.shape[2]
    rim = MAX_SHIFT + (range_kernel.shape[1] - bins) // 2
    levels = range_kernel.shape[0]

    rows = echoes.reshape(2 * local_pulses, devices * bins)
    order = [*range(far_chip, chips), *range(1, far_chip), 0]
    turn, give, keep = placed(rows, order, bins)
    got = exchanged(give, devices, 1)
    outer_pulses = lax.all_to_all(turn, "rng", split_axis=0, concat_axis=0, tiled=True)
    sends = joined(keep, got)
    inner_pulses = [
        exchanged(value, devices, 2 * d) if d else value for d, value in zip(order, sends)
    ]
    inner_pulses = inner_pulses[-1:] + inner_pulses[far_chip:-1] + inner_pulses[:far_chip]

    filter_matrix = filter_table(angles, local_pulses, sends[-1])
    outer_pulses = after(outer_pulses, *inner_pulses[1 : far_chip + 2])
    own_outer, out_outer, *edges = filtered(fore_flag, filter_matrix, (outer_pulses,), True)
    far_outer = from_partner(out_outer, 1)
    rims = neighbour_rims(*edges)
    far_rims = [from_partner(after(value, far_outer), 1) for value in rims]
    own_inner, out_inner = filtered(fore_flag, filter_matrix, inner_pulses, False)
    far_inner = from_partner(out_inner, 1)
    settings = (fore_flag, band_offset, center_shift, range_kernel, angles)
    centre, rim_matrix, turn = merge_tables(0, 1, *settings, own_inner)
    own, far = (own_outer, own_inner), (far_outer, far_inner)
    for level in range(levels):
        if level > 0:
            stride = 2**level
            centre, rim_matrix, turn = merge_tables(level, stride, *settings, image)
            own, out, edges = split_image(level, image, fore_flag, rim)
            rims = neighbour_rims(*edges)
            far = [from_partner(value, stride) for value in out]
            far_rims = [from_partner(value, stride) for value in rims]
        dtype = BF16 if level + 1 < levels else F32
        image = merged_image(
            level, fore_flag, own, rims, far, far_rims, centre, rim_matrix, angle_interp, turn, dtype
        )
    return image


def solution(mesh):
    placed_as = (
        P(None, ("sub", "rng"), None),
        P(None, None, "rng"),
        P(None, None, "rng"),
        P(),
        P(),
        P(),
    )
    return jax.shard_map(
        on_device, mesh=mesh, in_specs=placed_as, out_specs=P(None, "sub", "rng"), check_vma=False
    )
```

```python
import functools
import math

import jax
import jax.numpy as jnp
from jax import lax
from jax.experimental import pallas as pl
from jax.experimental.pallas import tpu as pltpu
from jax.sharding import PartitionSpec as P

MAX_SHIFT = 16
LANES = 128
MIB = 2**20
VMEM = pl.BlockSpec(memory_space=pltpu.VMEM)
SMEM = pl.BlockSpec(memory_space=pltpu.SMEM)
ANY = pl.BlockSpec(memory_space=pl.ANY)
F32 = jnp.float32
BF16 = jnp.bfloat16


def dot(a, b):
    return jnp.dot(a, b, preferred_element_type=F32)


def params(mib):
    return pltpu.CompilerParams(vmem_limit_bytes=mib * MIB)


def series(square, first, count):
    coefs = [
        (-1) ** i * math.pi ** (2 * i + first) / math.factorial(2 * i + first)
        for i in range(count)
    ]
    total = jnp.full_like(square, coefs[-1])
    for coef in coefs[-2::-1]:
        total = total * square + coef
    return total


def cos_sin_pi(v):
    turns = jnp.floor(v + 0.5)
    rest = v - turns
    sign = 1.0 - 2.0 * (turns - 2.0 * jnp.floor(turns * 0.5))
    square = rest * rest
    return series(square, 0, 8) * sign, series(square, 1, 7) * rest * sign


def rotated(pair, step):
    return pair[0] * step[0] - pair[1] * step[1], pair[0] * step[1] + pair[1] * step[0]


def place_kernel(order, echoes_ref, direct_ref, give_ref, keep_ref, sems):
    me = lax.axis_index("rng")
    bins = keep_ref.shape[-1]
    outer = bins // 4
    copies = []

    def take(device, target):
        for first, count, at in (
            (0, outer, 0),
            (bins - outer, outer, outer),
            (outer, bins - 2 * outer, 2 * outer),
        ):
            start = pl.multiple_of(device * bins + first, LANES)
            copy = pltpu.make_async_copy(
                echoes_ref.at[:, pl.ds(start, count)],
                target.at[:, pl.ds(at, count)],
                sems.at[len(copies)],
            )
            copy.start()
            copies.append(copy)

    take(me ^ (2 * order[-1]), direct_ref)
    for flip, ref in ((1, give_ref), (0, keep_ref)):
        for i, d in enumerate(order[: ref.shape[0]]):
            take(me ^ (2 * d + flip), ref.at[i])
    for copy in copies:
        copy.wait()


def placed(echoes, order, bins):
    rows = echoes.shape[0]
    shapes = [(rows, bins), (len(order), rows, bins), (len(order) - 1, rows, bins)]
    return pl.pallas_call(
        functools.partial(place_kernel, order),
        out_shape=[jax.ShapeDtypeStruct(shape, BF16) for shape in shapes],
        in_specs=[ANY],
        out_specs=[VMEM] * 3,
        scratch_shapes=[pltpu.SemaphoreType.DMA((6 * len(order),))],
        compiler_params=params(8),
        cost_estimate=pl.CostEstimate(flops=0, bytes_accessed=2 * MIB, transcendentals=0),
    )(echoes)


def join_kernel(picks, keep_ref, got_ref, *refs):
    rows = keep_ref.shape[1]
    refs[0][...] = got_ref[keep_ref.shape[0]]
    for (i, first, count), out_ref in zip(picks, refs[1:]):
        out_ref[:rows] = keep_ref[i, :, first : first + count]
        out_ref[rows:] = got_ref[i, :, first : first + count]


def joined(picks, keep, got):
    _, rows, bins = keep.shape
    shapes = [(rows, bins)] + [(2 * rows, count) for _, _, count in picks]
    return pl.pallas_call(
        functools.partial(join_kernel, picks),
        out_shape=[jax.ShapeDtypeStruct(shape, BF16) for shape in shapes],
        in_specs=[VMEM] * 2,
        out_specs=[VMEM] * len(shapes),
        compiler_params=params(8),
        cost_estimate=pl.CostEstimate(flops=0, bytes_accessed=2 * MIB, transcendentals=0),
    )(keep, got)


def after(value, *earlier):
    return lax.optimization_barrier((value, *earlier))[0]


def exchanged(value, devices, mask):
    return lax.ppermute(value, "rng", [(i, i ^ mask) for i in range(devices)])


def filter_table_kernel(local_pulses, after_ref, filter_ref, cos_ref, sin_ref):
    me = lax.axis_index("rng")
    columns = filter_ref.shape[1]
    angles = filter_ref.shape[0] // 2
    base = cos_ref.shape[0]
    scale = 1.0 / math.sqrt(columns // 2)
    lane = lax.broadcasted_iota(jnp.int32, (8, columns), 1)
    slot = lane // (2 * local_pulses)
    second = lane // local_pulses % 2
    pulse_id = (slot ^ me) * local_pulses + lane % local_pulses
    pulse = pulse_id.astype(F32)
    lag = second.astype(F32) * 0.5
    per_angle = pulse * (1.0 / angles)
    row = lax.broadcasted_iota(jnp.int32, (8, columns), 0)
    for i in range(base // 8):
        twice = (2 * (row + 8 * i) + 1 - angles).astype(F32)
        cosine, sine = cos_sin_pi(twice * per_angle - lag)
        cos_ref[8 * i : 8 * i + 8, :] = cosine * scale
        sin_ref[8 * i : 8 * i + 8, :] = sine * scale
    step = cos_sin_pi(per_angle * (2 * base))
    for j in range(angles // base):
        for i in range(base // 16):
            pair = [], []
            for k in (2 * i, 2 * i + 1):
                here = slice(8 * k, 8 * k + 8)
                now = cos_ref[here, :], sin_ref[here, :]
                pair[0].append(now[0])
                pair[1].append(-now[1])
                if j + 1 < angles // base:
                    cos_ref[here, :], sin_ref[here, :] = rotated(now, step)
            begin = j * base + 16 * i
            filter_ref[begin : begin + 16, :] = jnp.concatenate(pair[0]).astype(BF16)
            begin += angles
            filter_ref[begin : begin + 16, :] = jnp.concatenate(pair[1]).astype(BF16)


def filter_table(angles, local_pulses, after):
    side = 2 * local_pulses * lax.axis_size("rng")
    return pl.pallas_call(
        functools.partial(filter_table_kernel, local_pulses),
        out_shape=jax.ShapeDtypeStruct((2 * angles, side), BF16),
        in_specs=[ANY],
        out_specs=VMEM,
        scratch_shapes=[pltpu.VMEM((64, side), F32)] * 2,
        compiler_params=params(6),
        cost_estimate=pl.CostEstimate(flops=9_000_000, bytes_accessed=4 * MIB, transcendentals=0),
    )(after)


def merge_table_kernel(
    level, stride, flag_ref, offset_ref, shift_ref, range_ref, after_ref, centre_ref, rim_ref, turn_ref
):
    group = lax.axis_index("sub")
    block = lax.axis_index("rng")
    bins = centre_ref.shape[-1]
    angles = turn_ref.shape[-2]
    total_bins = lax.axis_size("rng") * bins
    own_flag = flag_ref[level, group, 0]
    taps = range_ref.shape[1]
    band = (taps - bins) // 2
    rim = MAX_SHIFT + band
    outer = bins // 4
    kernel = range_ref[level]

    def moved(bin_id):
        tap = lax.broadcasted_iota(jnp.int32, (bin_id.shape[0], taps), 1)
        return dot(jnp.where(tap == bin_id, 1.0, 0.0).astype(BF16), kernel).astype(BF16)

    row = lax.broadcasted_iota(jnp.int32, (bins, 1), 0)
    own_bin = row - outer
    own_bin = jnp.where(row < 2 * outer, row + (bins - 2 * outer), own_bin)
    own_bin = jnp.where(row < outer, row, own_bin)
    rim_row = lax.broadcasted_iota(jnp.int32, (2 * rim, 1), 0)
    rim_bin = jnp.where(rim_row < rim, rim_row - rim, rim_row - rim + bins)
    rim_ref[...] = jnp.zeros(rim_ref.shape, BF16)
    bin_id = block * bins + lax.broadcasted_iota(jnp.int32, (1, LANES), 1)
    reach = 1.0 + bin_id.astype(F32) * (1.0 / total_bins)
    rows = 64
    for child in range(2):
        member = group if child == 0 else group ^ stride
        lead = band - offset_ref[level, member, 0]
        centre_ref[child] = moved(own_bin + lead)
        ends = moved(rim_bin + lead)
        for part in range(2):
            place = pl.multiple_of((2 * part + own_flag) * rim, rim)
            rim_ref[child, part, pl.ds(place, rim), :] = ends[:rim]
            rim_ref[child, part, pl.ds(4 * rim + place, rim), :] = ends[rim:]

        rate = shift_ref[level, member]

        def turn_rows(i, carry):
            begin = pl.multiple_of(i * rows, rows)
            angle = begin + lax.broadcasted_iota(jnp.int32, (rows, LANES), 0)
            place = ((angle.astype(F32) + 0.5) * (1.0 / angles) - 0.5) * rate
            now = cos_sin_pi(place * reach)
            step = cos_sin_pi(place * (LANES / total_bins))
            for tile in range(bins // LANES):
                lanes = slice(tile * LANES, tile * LANES + LANES)
                turn_ref[child, 0, pl.ds(begin, rows), lanes] = now[0]
                turn_ref[child, 1, pl.ds(begin, rows), lanes] = now[1]
                now = rotated(now, step)
            return carry

        lax.fori_loop(0, angles // rows, turn_rows, 0)


def merge_tables(level, stride, fore_flag, band_offset, center_shift, range_kernel, angles, after):
    taps, bins = range_kernel.shape[1:]
    rim = MAX_SHIFT + (taps - bins) // 2
    return pl.pallas_call(
        functools.partial(merge_table_kernel, level, stride),
        out_shape=[
            jax.ShapeDtypeStruct((2, bins, bins), BF16),
            jax.ShapeDtypeStruct((2, 2, 8 * rim, bins), BF16),
            jax.ShapeDtypeStruct((2, 2, angles, bins), F32),
        ],
        in_specs=[SMEM] * 3 + [VMEM, ANY],
        out_specs=[VMEM] * 3,
        compiler_params=params(12),
        cost_estimate=pl.CostEstimate(
            flops=2_300_000_000, bytes_accessed=7 * MIB, transcendentals=0
        ),
    )(fore_flag, band_offset, center_shift, range_kernel, after)


def filter_kernel(pieces, first, count, ends, flag_ref, filter_ref, *refs):
    own_flag = flag_ref[0, lax.axis_index("sub"), 0]
    pulses_ref, image_ref = refs[-2:]
    own_ref, out_ref = refs[pieces : pieces + 2]
    at = 0
    for ref in refs[:pieces]:
        begin = first if ref.shape[1] > count else 0
        pulses_ref[at : at + ref.shape[0], :] = ref[:, begin : begin + count]
        at += ref.shape[0]
    image_ref[...] = dot(filter_ref[...], pulses_ref[...])
    half = own_ref.shape[1]
    foremost = own_flag == 0
    for part in range(2):
        upper = image_ref[2 * part * half : (2 * part + 1) * half, :]
        lower = image_ref[(2 * part + 1) * half : (2 * part + 2) * half, :]
        own_ref[part] = jnp.where(foremost, upper, lower).astype(BF16)
        out_ref[part] = jnp.where(foremost, lower, upper).astype(BF16)
    if ends:
        rim = LANES // 4
        lane = lax.broadcasted_iota(jnp.int32, (1, LANES), 1)

        def packed(lanes, edge):
            total = jnp.zeros((half, LANES), F32)
            for group in range(4):
                value = image_ref[group * half : (group + 1) * half, lanes]
                turn = (group * rim - edge) % LANES
                value = pltpu.roll(value, turn, 1) if turn else value
                total = jnp.where(lane // rim == group, value, total)
            return total.astype(BF16)

        low = packed(slice(0, LANES), 0)
        high = packed(slice(count - LANES, count), LANES - rim)
        even = lax.axis_index("rng") % 2 == 0
        refs[pieces + 2][...] = jnp.where(even, high, low)
        refs[pieces + 3][...] = jnp.where(even, low, high)


def filtered(fore_flag, filter_matrix, pieces, first, count, ends):
    angles = filter_matrix.shape[0]
    half = angles // 4
    shapes = [jax.ShapeDtypeStruct((2, half, count), BF16)] * 2
    if ends:
        shapes += [jax.ShapeDtypeStruct((half, LANES), BF16)] * 2
    return pl.pallas_call(
        functools.partial(filter_kernel, len(pieces), first, count, ends),
        out_shape=shapes,
        in_specs=[SMEM] + [VMEM] * (1 + len(pieces)),
        out_specs=[VMEM] * len(shapes),
        scratch_shapes=[
            pltpu.VMEM((filter_matrix.shape[1], count), BF16),
            pltpu.VMEM((angles, count), F32),
        ],
        compiler_params=params(10),
        cost_estimate=pl.CostEstimate(
            flops=2 * filter_matrix.size * count, bytes_accessed=4 * MIB, transcendentals=0
        ),
    )(fore_flag, filter_matrix, *pieces)


def rims_of(first, second):
    even = lax.axis_index("rng") % 2 == 0
    below = jnp.where(even, second, first)
    above = jnp.where(even, first, second)
    return jnp.concatenate([below, above], axis=1)


def early_kernel(
    level, flag_ref, own_outer, own_inner, rim_first, rim_second, far_outer, far_first, far_second,
    centre_ref, rim_ref, matrix_ref, turn_ref, merged_ref, partial_ref, value_ref, term_ref,
):
    own_flag = flag_ref[level, lax.axis_index("sub"), 0]
    parts, half, count = own_outer.shape
    bins = centre_ref.shape[-1]
    own_rims = rims_of(rim_first[...], rim_second[...])
    far_rims = rims_of(far_first[...], far_second[...])
    image = jnp.concatenate([own_outer[...], own_inner[...]], axis=2)
    value_ref[...] = dot(image.reshape(parts * half, 2 * count), centre_ref[0])
    matrix = matrix_ref[level, own_flag]
    for part in range(parts):
        value = value_ref[part * half : (part + 1) * half, :] + dot(own_rims, rim_ref[0, part])
        term_ref[part] = dot(matrix, value.astype(BF16))
    merged_ref[0], merged_ref[1] = rotated(
        (term_ref[0], term_ref[1]), (turn_ref[0, 0], turn_ref[0, 1])
    )
    outer = far_outer[...].reshape(parts * half, count)
    value_ref[...] = dot(outer, centre_ref[1, :count, :])
    for part in range(parts):
        value = value_ref[part * half : (part + 1) * half, :]
        partial_ref[part] = value + dot(far_rims, rim_ref[1, part])


def late_kernel(
    level, flag_ref, far_inner, merged_ref, partial_ref, centre_ref, matrix_ref, turn_ref, out_ref,
    buffer, value_ref, sems,
):
    own_flag = flag_ref[level, lax.axis_index("sub"), 0]
    parts, half, count = far_inner.shape
    inner = far_inner[...].reshape(parts * half, count)
    value_ref[...] = dot(inner, centre_ref[1, count:, :])
    rows = []
    for part in range(parts):
        value = value_ref[part * half : (part + 1) * half, :] + partial_ref[part]
        rows.append(value.astype(BF16))
    matrix = matrix_ref.at[level, 1 - own_flag]
    block = 2 * LANES
    copies = []
    for begin in range(0, matrix.shape[0], block):
        here = slice(begin, begin + block)
        turned = rotated(
            (dot(matrix[here], rows[0]), dot(matrix[here], rows[1])),
            (turn_ref[1, 0, here], turn_ref[1, 1, here]),
        )
        for part in range(parts):
            buffer[part, here] = (merged_ref[part, here] + turned[part]).astype(buffer.dtype)
            copy = pltpu.make_async_copy(
                buffer.at[part, here], out_ref.at[part, here], sems.at[len(copies)]
            )
            copy.start()
            copies.append(copy)
    for copy in copies:
        copy.wait()


def merged_image(level, fore_flag, own, rims, far, far_rims, centre, rim, angle_interp, turn, dtype):
    angles, bins = turn.shape[-2:]
    cost = pl.CostEstimate(flops=4 * angles * bins * bins, bytes_accessed=8 * MIB, transcendentals=0)
    merged, partial = pl.pallas_call(
        functools.partial(early_kernel, level),
        out_shape=[
            jax.ShapeDtypeStruct((2, angles, bins), F32),
            jax.ShapeDtypeStruct((2, angles // 2, bins), F32),
        ],
        in_specs=[SMEM] + [VMEM] * 11,
        out_specs=[VMEM] * 2,
        scratch_shapes=[pltpu.VMEM((angles, bins), F32), pltpu.VMEM((2, angles, bins), F32)],
        compiler_params=params(20),
        cost_estimate=cost,
    )(fore_flag, *own, *rims, far[0], *far_rims, centre, rim, angle_interp, turn)
    return pl.pallas_call(
        functools.partial(late_kernel, level),
        out_shape=jax.ShapeDtypeStruct((2, angles, bins), dtype),
        in_specs=[SMEM] + [VMEM] * 6,
        out_specs=ANY,
        scratch_shapes=[
            pltpu.VMEM((2, angles, bins), dtype),
            pltpu.VMEM((angles, bins), F32),
            pltpu.SemaphoreType.DMA((angles // LANES,)),
        ],
        compiler_params=params(20),
        cost_estimate=cost,
    )(fore_flag, far[1], merged, partial, centre, angle_interp, turn)


def neighbour_rims(first, second, flip=0):
    groups, devices = lax.axis_size("sub"), lax.axis_size("rng")

    def swapped(value, begin):
        ups = [(i, i + 1) for i in range(begin, devices - 1, 2)]
        pairs = [
            (g * devices + i, (g ^ flip) * devices + j)
            for g in range(groups)
            for up in ups
            for i, j in (up, up[::-1])
        ]
        return lax.ppermute(value, ("sub", "rng"), pairs)

    return swapped(first, 0), swapped(second, 1)


def from_partner(value, stride):
    pairs = [(source, source ^ stride) for source in range(lax.axis_size("sub"))]
    return lax.ppermute(value, "sub", pairs)


def split_image(level, image, fore_flag, rim):
    angles, bins = image.shape[1:]
    half, outer = angles // 2, bins // 4
    own_flag = fore_flag[level, lax.axis_index("sub"), 0]
    sides = image.reshape(2, 2, half, bins)

    def pieces(side):
        rows = lax.dynamic_index_in_dim(sides, side, 1, keepdims=False)
        ends = jnp.concatenate([rows[..., :outer], rows[..., -outer:]], axis=-1)
        return ends, rows[..., outer:-outer]

    def packed(edge):
        return edge.transpose(2, 0, 1, 3).reshape(half, 4 * rim)

    low, high = packed(sides[..., :rim]), packed(sides[..., -rim:])
    even = lax.axis_index("rng") % 2 == 0
    edges = jnp.where(even, high, low), jnp.where(even, low, high)
    return pieces(own_flag), pieces(1 - own_flag), edges


def on_device(echoes, fore_flag, band_offset, angle_interp, range_kernel, center_shift):
    devices = lax.axis_size("rng")
    chips = devices // 2
    far_chip = chips // 2
    local_pulses = echoes.shape[1]
    bins = echoes.shape[2] // devices
    count = bins // 2
    angles = angle_interp.shape[2]
    rim = MAX_SHIFT + (range_kernel.shape[1] - bins) // 2
    levels = range_kernel.shape[0]

    rows = echoes.reshape(2 * local_pulses, devices * bins)
    near, far = list(range(1, far_chip)), list(range(far_chip + 1, chips))
    order = [*far, *near, 0, far_chip]
    direct, give, keep = placed(rows, order, bins)
    got = exchanged(give, devices, 1)
    first_far = [exchanged(direct, devices, 2 * far_chip)]
    picks = [(i, 0, count) for i in range(len(far))]
    picks += [(i, count, count) for i in range(len(far))]
    picks += [(i, 0, bins) for i in range(len(far), chips - 1)]
    relay, *sends = joined(picks, keep, got)
    outer_sends, inner_sends = sends[: len(far)], sends[len(far) : 2 * len(far)]
    whole_sends = sends[2 * len(far) :]
    first_far.append(exchanged(relay, devices, 2 * far_chip))
    outer_far, inner_far = [], []
    for i, d in enumerate(far):
        earlier = (got, first_far[0], first_far[1], *outer_far)[i]
        outer_far.append(exchanged(after(outer_sends[i], earlier), devices, 2 * d))
    whole = [whole_sends[-1]]
    for i, d in enumerate(near):
        whole.append(exchanged(whole_sends[i], devices, 2 * d))
    whole += first_far

    filter_matrix = filter_table(angles, local_pulses, whole_sends[-1])
    own_outer, out_outer, *edges = filtered(
        fore_flag, filter_matrix, (*whole, *outer_far), 0, count, True
    )
    for i, d in enumerate(far):
        earlier = (own_outer,) if i else (outer_far[1],)
        inner_far.append(exchanged(after(inner_sends[i], *earlier), devices, 2 * d))
    far_outer = from_partner(after(out_outer, inner_far[0]), 1)
    edges = [after(edge, inner_far[0]) for edge in edges]
    rims, far_rims = neighbour_rims(*edges), neighbour_rims(*edges, 1)
    inner_far[0] = after(inner_far[0], far_outer)
    own_inner, out_inner = filtered(
        fore_flag, filter_matrix, (*whole, *inner_far), count, count, False
    )
    far_inner = from_partner(out_inner, 1)
    settings = (fore_flag, band_offset, center_shift, range_kernel, angles)
    centre, rim_matrix, turn = merge_tables(0, 1, *settings, own_inner)
    own, far = (own_outer, own_inner), (far_outer, far_inner)
    for level in range(levels):
        if level > 0:
            stride = 2**level
            centre, rim_matrix, turn = merge_tables(level, stride, *settings, image)
            own, out, edges = split_image(level, image, fore_flag, rim)
            rims = neighbour_rims(*edges)
            far = [from_partner(value, stride) for value in out]
            far_rims = neighbour_rims(*edges, stride)
        dtype = BF16 if level + 1 < levels else F32
        image = merged_image(
            level, fore_flag, own, rims, far, far_rims, centre, rim_matrix, angle_interp, turn, dtype
        )
    return image


def solution(mesh):
    placed_as = (
        P(None, ("sub", "rng"), None),
        P(None, None, "rng"),
        P(None, None, "rng"),
        P(),
        P(),
        P(),
    )
    return jax.shard_map(
        on_device, mesh=mesh, in_specs=placed_as, out_specs=P(None, "sub", "rng"), check_vma=False
    )
```

```python
import functools
import math

import jax
import jax.numpy as jnp
from jax import lax
from jax.experimental import pallas as pl
from jax.experimental.pallas import tpu as pltpu
from jax.sharding import PartitionSpec as P

MAX_SHIFT = 16
LANES = 128
MIB = 2**20
VMEM = pl.BlockSpec(memory_space=pltpu.VMEM)
SMEM = pl.BlockSpec(memory_space=pltpu.SMEM)
ANY = pl.BlockSpec(memory_space=pl.ANY)
F32 = jnp.float32
BF16 = jnp.bfloat16


def dot(a, b):
    return jnp.dot(a, b, preferred_element_type=F32)


def params(mib):
    return pltpu.CompilerParams(vmem_limit_bytes=mib * MIB)


def series(square, first, count):
    coefs = [
        (-1) ** i * math.pi ** (2 * i + first) / math.factorial(2 * i + first)
        for i in range(count)
    ]
    total = jnp.full_like(square, coefs[-1])
    for coef in coefs[-2::-1]:
        total = total * square + coef
    return total


def cos_sin_pi(v):
    turns = jnp.floor(v + 0.5)
    rest = v - turns
    sign = 1.0 - 2.0 * (turns - 2.0 * jnp.floor(turns * 0.5))
    square = rest * rest
    return series(square, 0, 8) * sign, series(square, 1, 7) * rest * sign


def rotated(pair, step):
    return pair[0] * step[0] - pair[1] * step[1], pair[0] * step[1] + pair[1] * step[0]


def place_kernel(echoes_ref, blocks_ref, sems):
    bins = blocks_ref.shape[-1]
    copies = []
    for device in range(blocks_ref.shape[0]):
        copy = pltpu.make_async_copy(
            echoes_ref.at[:, pl.ds(device * bins, bins)], blocks_ref.at[device], sems.at[device]
        )
        copy.start()
        copies.append(copy)
    for copy in copies:
        copy.wait()


def placed(echoes, devices):
    rows, columns = echoes.shape
    return pl.pallas_call(
        place_kernel,
        out_shape=jax.ShapeDtypeStruct((devices, rows, columns // devices), BF16),
        in_specs=[ANY],
        out_specs=VMEM,
        scratch_shapes=[pltpu.SemaphoreType.DMA((devices,))],
        compiler_params=params(8),
        cost_estimate=pl.CostEstimate(flops=0, bytes_accessed=2 * MIB, transcendentals=0),
    )(echoes)


def filter_table_kernel(local_pulses, after_ref, filter_ref, cos_ref, sin_ref):
    columns = filter_ref.shape[1]
    angles = filter_ref.shape[0] // 2
    base = cos_ref.shape[0]
    scale = 1.0 / math.sqrt(columns // 2)
    lane = lax.broadcasted_iota(jnp.int32, (8, columns), 1)
    slot = lane // (2 * local_pulses)
    second = lane // local_pulses % 2
    pulse_id = slot * local_pulses + lane % local_pulses
    pulse = pulse_id.astype(F32)
    lag = second.astype(F32) * 0.5
    per_angle = pulse * (1.0 / angles)
    row = lax.broadcasted_iota(jnp.int32, (8, columns), 0)
    for i in range(base // 8):
        twice = (2 * (row + 8 * i) + 1 - angles).astype(F32)
        cosine, sine = cos_sin_pi(twice * per_angle - lag)
        cos_ref[8 * i : 8 * i + 8, :] = cosine * scale
        sin_ref[8 * i : 8 * i + 8, :] = sine * scale
    step = cos_sin_pi(per_angle * (2 * base))
    for j in range(angles // base):
        for i in range(base // 16):
            pair = [], []
            for k in (2 * i, 2 * i + 1):
                here = slice(8 * k, 8 * k + 8)
                now = cos_ref[here, :], sin_ref[here, :]
                pair[0].append(now[0])
                pair[1].append(-now[1])
                if j + 1 < angles // base:
                    cos_ref[here, :], sin_ref[here, :] = rotated(now, step)
            begin = j * base + 16 * i
            filter_ref[begin : begin + 16, :] = jnp.concatenate(pair[0]).astype(BF16)
            begin += angles
            filter_ref[begin : begin + 16, :] = jnp.concatenate(pair[1]).astype(BF16)


def filter_table(angles, local_pulses, after):
    side = 2 * local_pulses * lax.axis_size("rng")
    return pl.pallas_call(
        functools.partial(filter_table_kernel, local_pulses),
        out_shape=jax.ShapeDtypeStruct((2 * angles, side), BF16),
        in_specs=[ANY],
        out_specs=VMEM,
        scratch_shapes=[pltpu.VMEM((64, side), F32)] * 2,
        compiler_params=params(6),
        cost_estimate=pl.CostEstimate(flops=9_000_000, bytes_accessed=4 * MIB, transcendentals=0),
    )(after)


def merge_table_kernel(
    level, stride, offset_ref, shift_ref, range_ref, after_ref, centre_ref, rim_ref, turn_ref
):
    group = lax.axis_index("sub")
    block = lax.axis_index("rng")
    bins = centre_ref.shape[-1]
    angles = turn_ref.shape[-2]
    total_bins = lax.axis_size("rng") * bins
    taps = range_ref.shape[1]
    band = (taps - bins) // 2
    rim = MAX_SHIFT + band
    kernel = range_ref[level]

    def moved(bin_id):
        tap = lax.broadcasted_iota(jnp.int32, (bin_id.shape[0], taps), 1)
        return dot(jnp.where(tap == bin_id, 1.0, 0.0).astype(BF16), kernel).astype(BF16)

    row = lax.broadcasted_iota(jnp.int32, (bins, 1), 0)
    rim_row = lax.broadcasted_iota(jnp.int32, (2 * rim, 1), 0)
    rim_bin = jnp.where(rim_row < rim, rim_row - rim, rim_row - rim + bins)
    rim_ref[...] = jnp.zeros(rim_ref.shape, BF16)
    bin_id = block * bins + lax.broadcasted_iota(jnp.int32, (1, LANES), 1)
    reach = 1.0 + bin_id.astype(F32) * (1.0 / total_bins)
    rows = 64
    for child in range(2):
        member = group if child == 0 else group ^ stride
        lead = band - offset_ref[level, member, 0]
        centre_ref[child] = moved(row + lead)
        ends = moved(rim_bin + lead)
        for part in range(2):
            for side in range(2):
                place = (2 * side + part) * rim
                rim_ref[child, part, place : place + rim, :] = ends[side * rim : (side + 1) * rim]

        rate = shift_ref[level, member]

        def turn_rows(i, carry):
            begin = pl.multiple_of(i * rows, rows)
            angle = begin + lax.broadcasted_iota(jnp.int32, (rows, LANES), 0)
            place = ((angle.astype(F32) + 0.5) * (1.0 / angles) - 0.5) * rate
            now = cos_sin_pi(place * reach)
            step = cos_sin_pi(place * (LANES / total_bins))
            for tile in range(bins // LANES):
                lanes = slice(tile * LANES, tile * LANES + LANES)
                turn_ref[child, 0, pl.ds(begin, rows), lanes] = now[0]
                turn_ref[child, 1, pl.ds(begin, rows), lanes] = now[1]
                now = rotated(now, step)
            return carry

        lax.fori_loop(0, angles // rows, turn_rows, 0)


def merge_tables(level, stride, band_offset, center_shift, range_kernel, angles, after):
    taps, bins = range_kernel.shape[1:]
    rim = MAX_SHIFT + (taps - bins) // 2
    return pl.pallas_call(
        functools.partial(merge_table_kernel, level, stride),
        out_shape=[
            jax.ShapeDtypeStruct((2, bins, bins), BF16),
            jax.ShapeDtypeStruct((2, 2, 4 * rim, bins), BF16),
            jax.ShapeDtypeStruct((2, 2, angles, bins), F32),
        ],
        in_specs=[SMEM] * 2 + [VMEM, ANY],
        out_specs=[VMEM] * 3,
        compiler_params=params(12),
        cost_estimate=pl.CostEstimate(
            flops=2_300_000_000, bytes_accessed=7 * MIB, transcendentals=0
        ),
    )(band_offset, center_shift, range_kernel, after)


def sector(filter_ref, part, side):
    half = filter_ref.shape[0] // 4
    return filter_ref[pl.ds(pl.multiple_of((2 * part + side) * half, half), half), :]


def partner_rows_kernel(flag_ref, filter_ref, pulses_ref, *out_refs):
    own_flag = flag_ref[0, lax.axis_index("sub"), 0]
    for part in range(2):
        rows = dot(sector(filter_ref, part, 1 - own_flag), pulses_ref[...]).astype(BF16)
        at = 0
        for ref in out_refs:
            count = ref.shape[-1]
            ref[part] = rows[:, at : at + count]
            at += count


def partner_rows(fore_flag, filter_matrix, pulses, cut):
    half, bins = filter_matrix.shape[0] // 4, pulses.shape[1]
    return pl.pallas_call(
        partner_rows_kernel,
        out_shape=[jax.ShapeDtypeStruct((2, half, n), BF16) for n in (cut, bins - cut)],
        in_specs=[SMEM] + [VMEM] * 2,
        out_specs=[VMEM] * 2,
        compiler_params=params(10),
        cost_estimate=pl.CostEstimate(
            flops=filter_matrix.size * bins, bytes_accessed=4 * MIB, transcendentals=0
        ),
    )(fore_flag, filter_matrix, pulses)


def own_rows_kernel(flag_ref, filter_ref, pulses_ref, first_ref, last_ref, own_ref, *edge_refs):
    own_flag = flag_ref[0, lax.axis_index("sub"), 0]
    rim = LANES // 4
    lane = lax.broadcasted_iota(jnp.int32, (1, LANES), 1)
    edges = [0.0, 0.0]
    for part in range(2):
        rows = dot(sector(filter_ref, part, own_flag), pulses_ref[...])
        own_ref[part] = rows.astype(BF16)
        ends = (
            (rows[:, :LANES], first_ref[part, :, :LANES].astype(F32)),
            (rows[:, -LANES:], last_ref[part, :, -LANES:].astype(F32)),
        )
        for end, (own, out) in enumerate(ends):
            for side in range(2):
                group = 2 * part + side
                value = jnp.where(own_flag == side, own, out)
                turn = (group + end) * rim % LANES
                value = pltpu.roll(value, turn, 1) if turn else value
                edges[end] = edges[end] + jnp.where(lane // rim == group, value, 0.0)
    even = lax.axis_index("rng") % 2 == 0
    edge_refs[0][...] = jnp.where(even, edges[1], edges[0]).astype(BF16)
    edge_refs[1][...] = jnp.where(even, edges[0], edges[1]).astype(BF16)


def own_rows(fore_flag, filter_matrix, pulses, out):
    half, bins = filter_matrix.shape[0] // 4, pulses.shape[1]
    return pl.pallas_call(
        own_rows_kernel,
        out_shape=[jax.ShapeDtypeStruct((2, half, bins), BF16)]
        + [jax.ShapeDtypeStruct((half, LANES), BF16)] * 2,
        in_specs=[SMEM] + [VMEM] * 4,
        out_specs=[VMEM] * 3,
        compiler_params=params(10),
        cost_estimate=pl.CostEstimate(
            flops=filter_matrix.size * bins, bytes_accessed=4 * MIB, transcendentals=0
        ),
    )(fore_flag, filter_matrix, pulses, *out)


def exchanged(value, begin):
    devices = lax.axis_size("rng")
    pairs = [(i, i + 1) for i in range(begin, devices - 1, 2)]
    return lax.ppermute(value, "rng", pairs + [(j, i) for i, j in pairs])


def rims_kernel(level, flag_ref, first_ref, second_ref, own_ref, out_ref):
    own_flag = flag_ref[level, lax.axis_index("sub"), 0]
    rim = LANES // 4
    even = lax.axis_index("rng") % 2 == 0
    first, second = first_ref[...].astype(F32), second_ref[...].astype(F32)
    ends = jnp.where(even, second, first), jnp.where(even, first, second)
    group = lax.broadcasted_iota(jnp.int32, (1, LANES), 1) // rim
    packed = [0.0, 0.0]
    for end, value in enumerate(ends):
        for part in range(2):
            place = 2 * end + part
            for side in range(2):
                turn = (place - (2 * part + side)) * rim % LANES
                moved = pltpu.roll(value, turn, 1) if turn else value
                packed[side] = packed[side] + jnp.where(group == place, moved, 0.0)
    own_ref[...] = jnp.where(own_flag == 0, packed[0], packed[1]).astype(BF16)
    out_ref[...] = jnp.where(own_flag == 0, packed[1], packed[0]).astype(BF16)


def sorted_rims(level, fore_flag, first, second):
    return pl.pallas_call(
        functools.partial(rims_kernel, level),
        out_shape=[jax.ShapeDtypeStruct(first.shape, BF16)] * 2,
        in_specs=[SMEM] + [VMEM] * 2,
        out_specs=[VMEM] * 2,
        compiler_params=params(4),
        cost_estimate=pl.CostEstimate(flops=1_000_000, bytes_accessed=MIB // 4, transcendentals=0),
    )(fore_flag, first, second)


def own_term_kernel(
    level, flag_ref, own_ref, rims_ref, centre_ref, rim_ref, matrix_ref, turn_ref, merged_ref,
    value_ref,
):
    own_flag = flag_ref[level, lax.axis_index("sub"), 0]
    parts, half, bins = own_ref.shape
    value_ref[...] = dot(own_ref[...].reshape(parts * half, bins), centre_ref[0])
    rows = []
    for part in range(parts):
        value = value_ref[part * half : (part + 1) * half, :]
        rows.append((value + dot(rims_ref[...], rim_ref[0, part])).astype(BF16))
    matrix = matrix_ref[level, own_flag]
    merged_ref[0], merged_ref[1] = rotated(
        (dot(matrix, rows[0]), dot(matrix, rows[1])), (turn_ref[0, 0], turn_ref[0, 1])
    )


def far_term_kernel(
    level, flag_ref, far_ref, rims_ref, merged_ref, centre_ref, rim_ref, matrix_ref, turn_ref,
    out_ref, partial_ref, value_ref, buffer, sems,
):
    own_flag = flag_ref[level, lax.axis_index("sub"), 0]
    parts, half, cut = far_ref.shape
    bins = centre_ref.shape[-1]
    middle = bins // 2
    value_ref[...] = dot(far_ref[...].reshape(parts * half, cut), centre_ref[1, :cut, :])
    rows = []
    for part in range(parts):
        value = value_ref[part * half : (part + 1) * half, :]
        value = value + dot(rims_ref[...], rim_ref[1, part])
        partial_ref[part] = value[:, middle:]
        rows.append(value[:, :middle].astype(BF16))
    terms = [dot(matrix_ref[level, 1 - own_flag], value) for value in rows]
    finish(terms, turn_ref, merged_ref, buffer, out_ref, sems, 0, middle)


def finish(terms, turn_ref, merged_ref, buffer, out_ref, sems, begin, end):
    lanes = slice(begin, end)
    block = LANES
    copies = []
    for first in range(0, terms[0].shape[0], block):
        here = slice(first, first + block)
        turned = rotated(
            (terms[0][here], terms[1][here]),
            (turn_ref[1, 0, here, lanes], turn_ref[1, 1, here, lanes]),
        )
        for part in range(2):
            buffer[part, here] = (merged_ref[part, here, lanes] + turned[part]).astype(buffer.dtype)
        copy = pltpu.make_async_copy(
            buffer.at[:, pl.ds(first, block)],
            out_ref.at[:, pl.ds(first, block), pl.ds(begin, end - begin)],
            sems.at[len(copies)],
        )
        copy.start()
        copies.append(copy)
    for copy in copies:
        copy.wait()


def last_term_kernel(
    level, flag_ref, far_ref, partial_ref, merged_ref, centre_ref, matrix_ref, turn_ref, begun_ref,
    out_ref, buffer, sems,
):
    own_flag = flag_ref[level, lax.axis_index("sub"), 0]
    parts, half, count = far_ref.shape
    bins = centre_ref.shape[-1]
    middle = bins // 2
    far = far_ref[...].reshape(parts * half, count)
    value = dot(far, centre_ref[1, bins - count :, middle:])
    terms = []
    for part in range(parts):
        rows = (partial_ref[part] + value[part * half : (part + 1) * half]).astype(BF16)
        terms.append(dot(matrix_ref[level, 1 - own_flag], rows))
    finish(terms, turn_ref, merged_ref, buffer, out_ref, sems, middle, bins)


def own_term(level, fore_flag, own, rims, centre, rim, angle_interp, turn):
    angles, bins = turn.shape[-2:]
    return pl.pallas_call(
        functools.partial(own_term_kernel, level),
        out_shape=jax.ShapeDtypeStruct((2, angles, bins), F32),
        in_specs=[SMEM] + [VMEM] * 6,
        out_specs=VMEM,
        scratch_shapes=[pltpu.VMEM((angles, bins), F32)],
        compiler_params=params(20),
        cost_estimate=pl.CostEstimate(
            flops=4 * angles * bins * bins, bytes_accessed=4 * MIB, transcendentals=0
        ),
    )(fore_flag, own, rims, centre, rim, angle_interp, turn)


def merged_image(level, fore_flag, merged, far, far_rims, centre, rim, angle_interp, turn, dtype):
    angles, bins = turn.shape[-2:]
    cost = pl.CostEstimate(flops=2 * angles * bins * bins, bytes_accessed=4 * MIB, transcendentals=0)
    image = jax.ShapeDtypeStruct((2, angles, bins), dtype)
    buffers = [
        pltpu.VMEM((2, angles, bins // 2), dtype),
        pltpu.SemaphoreType.DMA((angles // LANES,)),
    ]
    begun, partial = pl.pallas_call(
        functools.partial(far_term_kernel, level),
        out_shape=[image, jax.ShapeDtypeStruct((2, angles // 2, bins // 2), F32)],
        in_specs=[SMEM] + [VMEM] * 7,
        out_specs=[ANY, VMEM],
        scratch_shapes=[pltpu.VMEM((angles, bins), F32)] + buffers,
        compiler_params=params(20),
        cost_estimate=cost,
    )(fore_flag, far[0], far_rims, merged, centre, rim, angle_interp, turn)
    return pl.pallas_call(
        functools.partial(last_term_kernel, level),
        out_shape=image,
        in_specs=[SMEM] + [VMEM] * 6 + [ANY],
        out_specs=ANY,
        scratch_shapes=buffers,
        input_output_aliases={7: 0},
        compiler_params=params(20),
        cost_estimate=cost,
    )(fore_flag, far[1], partial, merged, centre, angle_interp, turn, begun)


def after(value, *earlier):
    return lax.optimization_barrier((value, *earlier))[0]


def from_partner(value, stride):
    pairs = [(source, source ^ stride) for source in range(lax.axis_size("sub"))]
    return lax.ppermute(value, "sub", pairs)


def split_image(level, image, fore_flag, rim, cut):
    angles, bins = image.shape[1:]
    half = angles // 2
    own_flag = fore_flag[level, lax.axis_index("sub"), 0]
    sides = image.reshape(2, 2, half, bins)
    own = lax.dynamic_index_in_dim(sides, own_flag, 1, keepdims=False)
    out = lax.dynamic_index_in_dim(sides, 1 - own_flag, 1, keepdims=False)

    def packed(edge):
        return edge.transpose(2, 0, 1, 3).reshape(half, 4 * rim)

    low, high = packed(sides[..., :rim]), packed(sides[..., -rim:])
    even = lax.axis_index("rng") % 2 == 0
    edges = jnp.where(even, high, low), jnp.where(even, low, high)
    return own, (out[..., :cut], out[..., cut:]), edges


def on_device(echoes, fore_flag, band_offset, angle_interp, range_kernel, center_shift):
    devices = lax.axis_size("rng")
    local_pulses = echoes.shape[1]
    bins = echoes.shape[2] // devices
    cut = 3 * bins // 4
    angles = angle_interp.shape[2]
    rim = MAX_SHIFT + (range_kernel.shape[1] - bins) // 2
    levels = range_kernel.shape[0]
    settings = (band_offset, center_shift, range_kernel, angles)

    blocks = placed(echoes.reshape(2 * local_pulses, devices * bins), devices)
    pulses = lax.all_to_all(blocks, "rng", split_axis=0, concat_axis=0, tiled=True)
    pulses = pulses.reshape(2 * local_pulses * devices, bins)
    filter_matrix = filter_table(angles, local_pulses, blocks)
    centre, rim_matrix, turn = merge_tables(0, 1, *settings, filter_matrix)
    pulses = after(pulses, centre)
    out = partner_rows(fore_flag, filter_matrix, pulses, cut)
    own, *edges = own_rows(fore_flag, filter_matrix, pulses, out)
    for level in range(levels):
        stride = 2**level
        if level > 0:
            centre, rim_matrix, turn = merge_tables(level, stride, *settings, image)
            own, out, edges = split_image(level, image, fore_flag, rim, cut)
        far_first = from_partner(out[0], stride)
        edges = exchanged(edges[0], 0), exchanged(edges[1], 1)
        rims, out_rims = sorted_rims(level, fore_flag, *edges)
        far_rims = from_partner(out_rims, stride)
        far_last = from_partner(after(out[1], out_rims), stride)
        merged = own_term(level, fore_flag, own, rims, centre, rim_matrix, angle_interp, turn)
        dtype = BF16 if level + 1 < levels else F32
        image = merged_image(
            level, fore_flag, merged, (far_first, far_last), far_rims, centre, rim_matrix,
            angle_interp, turn, dtype,
        )
    return image


def solution(mesh):
    placed_as = (
        P(None, ("sub", "rng"), None),
        P(None, None, "rng"),
        P(None, None, "rng"),
        P(),
        P(),
        P(),
    )
    return jax.shard_map(
        on_device, mesh=mesh, in_specs=placed_as, out_specs=P(None, "sub", "rng"), check_vma=False
    )
```

```python
import functools
import math

import jax
import jax.numpy as jnp
from jax import lax
from jax.experimental import pallas as pl
from jax.experimental.pallas import tpu as pltpu
from jax.sharding import PartitionSpec as P

MAX_SHIFT = 16
LANES = 128
MIB = 2**20
JOIN_COST = 10**11
VMEM = pl.BlockSpec(memory_space=pltpu.VMEM)
SMEM = pl.BlockSpec(memory_space=pltpu.SMEM)
ANY = pl.BlockSpec(memory_space=pl.ANY)
F32 = jnp.float32
BF16 = jnp.bfloat16


def dot(a, b):
    return jnp.dot(a, b, preferred_element_type=F32)


def params(mib):
    return pltpu.CompilerParams(vmem_limit_bytes=mib * MIB)


def series(square, first, count):
    coefs = [
        (-1) ** i * math.pi ** (2 * i + first) / math.factorial(2 * i + first)
        for i in range(count)
    ]
    total = jnp.full_like(square, coefs[-1])
    for coef in coefs[-2::-1]:
        total = total * square + coef
    return total


def cos_sin_pi(v):
    turns = jnp.floor(v + 0.5)
    rest = v - turns
    sign = 1.0 - 2.0 * (turns - 2.0 * jnp.floor(turns * 0.5))
    square = rest * rest
    return series(square, 0, 8) * sign, series(square, 1, 7) * rest * sign


def rotated(pair, step):
    return pair[0] * step[0] - pair[1] * step[1], pair[0] * step[1] + pair[1] * step[0]


def mixed(left, right):
    lane = lax.broadcasted_iota(jnp.int32, left.shape, 1)
    return jnp.where(lane < LANES // 2, left.astype(F32), right.astype(F32)).astype(BF16)


def place_kernel(echoes_ref, far_ref, near_ref, inner_ref):
    devices, _, count = inner_ref.shape
    bins = count + LANES
    half = devices // 2
    base = lax.axis_index("rng") // half * half

    def tile(device, first):
        return echoes_ref[:, pl.ds(pl.multiple_of(device * bins + first, LANES), LANES)]

    for ref, start in ((far_ref, half - base), (near_ref, base)):
        for i in range(half):
            ref[i] = mixed(tile(start + i, 0), tile(start + i, bins - LANES))
    for device in range(devices):
        begin = device * bins
        inner_ref[device, :, :LANES] = mixed(tile(device, bins - LANES), tile(device, 0))
        inner_ref[device, :, LANES:] = echoes_ref[:, begin + LANES : begin + bins - LANES]


def placed(echoes, devices):
    rows, columns = echoes.shape
    outer = jax.ShapeDtypeStruct((devices // 2, rows, LANES), BF16)
    inner = jax.ShapeDtypeStruct((devices, rows, columns // devices - LANES), BF16)
    return pl.pallas_call(
        place_kernel,
        out_shape=[outer, outer, inner],
        in_specs=[VMEM],
        out_specs=[VMEM] * 3,
        compiler_params=params(8),
        cost_estimate=pl.CostEstimate(flops=0, bytes_accessed=2 * MIB, transcendentals=0),
    )(echoes)


def join_kernel(near_ref, relay_ref, *refs):
    me = lax.axis_index("rng") % len(refs)
    rows = near_ref.shape[1]
    for d, out_ref in enumerate(refs):
        out_ref[:rows] = near_ref[me ^ d]
        out_ref[rows:] = relay_ref[me ^ d]


def joined(near, relay):
    half, rows, count = near.shape
    return pl.pallas_call(
        join_kernel,
        out_shape=[jax.ShapeDtypeStruct((2 * rows, count), BF16)] * half,
        in_specs=[VMEM] * 2,
        out_specs=[VMEM] * half,
        compiler_params=params(4),
        cost_estimate=pl.CostEstimate(flops=JOIN_COST, bytes_accessed=MIB, transcendentals=0),
    )(near, relay)


def across(value, mask):
    devices = lax.axis_size("rng")
    return lax.ppermute(value, "rng", [(i, i ^ mask) for i in range(devices)])


def filter_table_kernel(local_pulses, flag_ref, after_ref, own_ref, out_ref, cos_ref, sin_ref):
    own_flag = flag_ref[0, lax.axis_index("sub"), 0]
    rows, columns = own_ref.shape
    half, angles = rows // 2, rows
    base = cos_ref.shape[0]
    scale = 1.0 / math.sqrt(columns // 2)
    lane = lax.broadcasted_iota(jnp.int32, (8, columns), 1)
    slot = lane // (2 * local_pulses)
    second = lane // local_pulses % 2
    pulse = (slot * local_pulses + lane % local_pulses).astype(F32)
    lag = second.astype(F32) * 0.5
    per_angle = pulse * (1.0 / angles)
    row = lax.broadcasted_iota(jnp.int32, (8, columns), 0)
    step = cos_sin_pi(per_angle * (2 * base))
    for ref, side in ((out_ref, 1 - own_flag), (own_ref, own_flag)):
        first = side * half
        for i in range(base // 8):
            twice = (2 * (row + 8 * i + first) + 1 - angles).astype(F32)
            cosine, sine = cos_sin_pi(twice * per_angle - lag)
            cos_ref[8 * i : 8 * i + 8, :] = cosine * scale
            sin_ref[8 * i : 8 * i + 8, :] = sine * scale
        for j in range(half // base):
            for i in range(base // 16):
                pair = [], []
                for k in (2 * i, 2 * i + 1):
                    here = slice(8 * k, 8 * k + 8)
                    now = cos_ref[here, :], sin_ref[here, :]
                    pair[0].append(now[0])
                    pair[1].append(-now[1])
                    if j + 1 < half // base:
                        cos_ref[here, :], sin_ref[here, :] = rotated(now, step)
                begin = j * base + 16 * i
                ref[begin : begin + 16, :] = jnp.concatenate(pair[0]).astype(BF16)
                begin += half
                ref[begin : begin + 16, :] = jnp.concatenate(pair[1]).astype(BF16)


def filter_table(fore_flag, angles, local_pulses, earlier):
    side = 2 * local_pulses * lax.axis_size("rng")
    return pl.pallas_call(
        functools.partial(filter_table_kernel, local_pulses),
        out_shape=[jax.ShapeDtypeStruct((angles, side), BF16)] * 2,
        in_specs=[SMEM, ANY],
        out_specs=[VMEM] * 2,
        scratch_shapes=[pltpu.VMEM((64, side), F32)] * 2,
        compiler_params=params(6),
        cost_estimate=pl.CostEstimate(flops=9_000_000, bytes_accessed=4 * MIB, transcendentals=0),
    )(fore_flag, earlier)


def merge_table_kernel(
    level, stride, flag_ref, offset_ref, shift_ref, range_ref, interp_ref, after_ref, centre_ref,
    rim_ref, turn_ref, matrix_ref,
):
    group = lax.axis_index("sub")
    block = lax.axis_index("rng")
    bins = centre_ref.shape[-1]
    angles = turn_ref.shape[-2]
    total_bins = lax.axis_size("rng") * bins
    taps = range_ref.shape[1]
    band = (taps - bins) // 2
    rim = MAX_SHIFT + band
    kernel = range_ref[level]

    def moved(bin_id):
        tap = lax.broadcasted_iota(jnp.int32, (bin_id.shape[0], taps), 1)
        return dot(jnp.where(tap == bin_id, 1.0, 0.0).astype(BF16), kernel).astype(BF16)

    row = lax.broadcasted_iota(jnp.int32, (bins, 1), 0)
    upper = row + (bins - 2 * LANES)
    own_bin = jnp.where(row % LANES < LANES // 2, row, upper + LANES)
    own_bin = jnp.where(row >= LANES, jnp.where(row % LANES < LANES // 2, upper, row - LANES), own_bin)
    own_bin = jnp.where(row >= 2 * LANES, row - LANES, own_bin)
    own_flag = flag_ref[level, group, 0]
    matrix_ref[0] = interp_ref[level, own_flag]
    matrix_ref[1] = interp_ref[level, 1 - own_flag]
    rim_row = lax.broadcasted_iota(jnp.int32, (2 * rim, 1), 0)
    rim_bin = jnp.where(rim_row < rim, rim_row - rim, rim_row - rim + bins)
    rim_ref[...] = jnp.zeros(rim_ref.shape, BF16)
    bin_id = block * bins + lax.broadcasted_iota(jnp.int32, (1, LANES), 1)
    reach = 1.0 + bin_id.astype(F32) * (1.0 / total_bins)
    rows = 64
    for child in range(2):
        member = group if child == 0 else group ^ stride
        lead = band - offset_ref[level, member, 0]
        centre_ref[child] = moved(own_bin + lead)
        ends = moved(rim_bin + lead)
        for part in range(2):
            for side in range(2):
                place = (2 * side + part) * rim
                rim_ref[child, part, place : place + rim, :] = ends[side * rim : (side + 1) * rim]

        rate = shift_ref[level, member]

        def turn_rows(i, carry):
            begin = pl.multiple_of(i * rows, rows)
            angle = begin + lax.broadcasted_iota(jnp.int32, (rows, LANES), 0)
            place = ((angle.astype(F32) + 0.5) * (1.0 / angles) - 0.5) * rate
            now = cos_sin_pi(place * reach)
            step = cos_sin_pi(place * (LANES / total_bins))
            for tile in range(bins // LANES):
                lanes = slice(tile * LANES, tile * LANES + LANES)
                turn_ref[child, 0, pl.ds(begin, rows), lanes] = now[0]
                turn_ref[child, 1, pl.ds(begin, rows), lanes] = now[1]
                now = rotated(now, step)
            return carry

        lax.fori_loop(0, angles // rows, turn_rows, 0)


def merge_tables(
    level, stride, fore_flag, band_offset, center_shift, range_kernel, angle_interp, earlier
):
    taps, bins = range_kernel.shape[1:]
    angles = angle_interp.shape[2]
    rim = MAX_SHIFT + (taps - bins) // 2
    return pl.pallas_call(
        functools.partial(merge_table_kernel, level, stride),
        out_shape=[
            jax.ShapeDtypeStruct((2, bins, bins), BF16),
            jax.ShapeDtypeStruct((2, 2, 4 * rim, bins), BF16),
            jax.ShapeDtypeStruct((2, 2, angles, bins), F32),
            jax.ShapeDtypeStruct((2, *angle_interp.shape[2:]), BF16),
        ],
        in_specs=[SMEM] * 3 + [VMEM] * 2 + [ANY],
        out_specs=[VMEM] * 4,
        compiler_params=params(12),
        cost_estimate=pl.CostEstimate(
            flops=2_300_000_000, bytes_accessed=7 * MIB, transcendentals=0
        ),
    )(fore_flag, band_offset, center_shift, range_kernel, angle_interp, earlier)


def outer_kernel(pieces, flag_ref, own_rows, out_rows, *refs):
    own_flag = flag_ref[0, lax.axis_index("sub"), 0]
    me = lax.axis_index("rng")
    own_ref, out_ref, *edge_refs = refs[pieces:-1]
    pulses_ref = refs[-1]
    rows = refs[0].shape[0] // 2
    for d, ref in enumerate(refs[:pieces]):
        for t in range(2):
            place = pl.multiple_of((me ^ (d + t * pieces)) * rows, rows)
            pulses_ref[pl.ds(place, rows), :] = ref[t * rows : (t + 1) * rows, :]
    images = dot(own_rows[...], pulses_ref[...]), dot(out_rows[...], pulses_ref[...])
    half = own_ref.shape[1]
    rim = LANES // 4
    lane = lax.broadcasted_iota(jnp.int32, (1, LANES), 1)
    edges = [0.0, 0.0]
    for part in range(2):
        own, out = (image[part * half : (part + 1) * half] for image in images)
        own_ref[part] = own.astype(BF16)
        out_ref[part] = out.astype(BF16)
        for side in range(2):
            value = jnp.where(own_flag == side, own, out)
            group = 2 * part + side
            for end in range(2):
                turn = (group + end) * rim % LANES
                moved = pltpu.roll(value, turn, 1) if turn else value
                edges[end] = edges[end] + jnp.where(lane // rim == group, moved, 0.0)
    even = me % 2 == 0
    edge_refs[0][...] = jnp.where(even, edges[1], edges[0]).astype(BF16)
    edge_refs[1][...] = jnp.where(even, edges[0], edges[1]).astype(BF16)


def outer_image(fore_flag, own_rows, out_rows, pieces):
    angles, side = own_rows.shape
    image = jax.ShapeDtypeStruct((2, angles // 2, LANES), BF16)
    edge = jax.ShapeDtypeStruct((angles // 2, LANES), BF16)
    return pl.pallas_call(
        functools.partial(outer_kernel, len(pieces)),
        out_shape=[image, image, edge, edge],
        in_specs=[SMEM] + [VMEM] * (2 + len(pieces)),
        out_specs=[VMEM] * 4,
        scratch_shapes=[pltpu.VMEM((side, LANES), BF16)],
        compiler_params=params(10),
        cost_estimate=pl.CostEstimate(
            flops=4 * angles * side * LANES, bytes_accessed=3 * MIB, transcendentals=0
        ),
    )(fore_flag, own_rows, out_rows, *pieces)


def exchanged(value, begin):
    devices = lax.axis_size("rng")
    pairs = [(i, i + 1) for i in range(begin, devices - 1, 2)]
    return lax.ppermute(value, "rng", pairs + [(j, i) for i, j in pairs])


def rims_kernel(level, flag_ref, first_ref, second_ref, own_ref, out_ref):
    own_flag = flag_ref[level, lax.axis_index("sub"), 0]
    rim = LANES // 4
    even = lax.axis_index("rng") % 2 == 0
    first, second = first_ref[...].astype(F32), second_ref[...].astype(F32)
    ends = jnp.where(even, second, first), jnp.where(even, first, second)
    group = lax.broadcasted_iota(jnp.int32, (1, LANES), 1) // rim
    packed = [0.0, 0.0]
    for end, value in enumerate(ends):
        for part in range(2):
            place = 2 * end + part
            for side in range(2):
                turn = (place - (2 * part + side)) * rim % LANES
                moved = pltpu.roll(value, turn, 1) if turn else value
                packed[side] = packed[side] + jnp.where(group == place, moved, 0.0)
    own_ref[...] = jnp.where(own_flag == 0, packed[0], packed[1]).astype(BF16)
    out_ref[...] = jnp.where(own_flag == 0, packed[1], packed[0]).astype(BF16)


def sorted_rims(level, fore_flag, first, second):
    return pl.pallas_call(
        functools.partial(rims_kernel, level),
        out_shape=[jax.ShapeDtypeStruct(first.shape, BF16)] * 2,
        in_specs=[SMEM] + [VMEM] * 2,
        out_specs=[VMEM] * 2,
        compiler_params=params(4),
        cost_estimate=pl.CostEstimate(flops=1_000_000, bytes_accessed=MIB // 4, transcendentals=0),
    )(fore_flag, first, second)


def early_kernel(
    own_outer, own_inner, rims_ref, far_outer, far_rims, centre_ref, rim_ref, matrix_ref, turn_ref,
    merged_ref, partial_ref, value_ref,
):
    parts, half, count = own_outer.shape
    image = jnp.concatenate([own_outer[...], own_inner[...]], axis=2)
    value_ref[...] = dot(image.reshape(parts * half, image.shape[2]), centre_ref[0])
    rows = []
    for part in range(parts):
        value = value_ref[part * half : (part + 1) * half, :]
        rows.append((value + dot(rims_ref[...], rim_ref[0, part])).astype(BF16))
    merged_ref[0], merged_ref[1] = rotated(
        (dot(matrix_ref[0], rows[0]), dot(matrix_ref[0], rows[1])), (turn_ref[0, 0], turn_ref[0, 1])
    )
    for part in range(parts):
        value = dot(far_outer[part], centre_ref[1, :count, :])
        here = slice(part * half, (part + 1) * half)
        partial_ref[here, :] = value + dot(far_rims[...], rim_ref[1, part])


def late_kernel(
    far_inner, merged_ref, partial_ref, centre_ref, matrix_ref, turn_ref, out_ref, buffer, sems
):
    parts, half, count = far_inner.shape
    bins = centre_ref.shape[-1]
    inner = far_inner[...].reshape(parts * half, count)
    value = partial_ref[...] + dot(inner, centre_ref[1, bins - count :, :])
    rows = [value[part * half : (part + 1) * half].astype(BF16) for part in range(parts)]
    block = LANES
    copies = []
    for first in range(0, matrix_ref.shape[1], 2 * block):
        matrix = matrix_ref[1, first : first + 2 * block]
        terms = dot(matrix, rows[0]), dot(matrix, rows[1])
        for step in range(2):
            here = slice(first + step * block, first + (step + 1) * block)
            there = slice(step * block, (step + 1) * block)
            turned = rotated(
                (terms[0][there], terms[1][there]), (turn_ref[1, 0, here], turn_ref[1, 1, here])
            )
            for part in range(parts):
                buffer[part, here] = (merged_ref[part, here] + turned[part]).astype(buffer.dtype)
            copy = pltpu.make_async_copy(
                buffer.at[:, here], out_ref.at[:, here], sems.at[len(copies)]
            )
            copy.start()
            copies.append(copy)
    for copy in copies:
        copy.wait()


def merged_image(own, rims, far, far_rims, tables, dtype):
    centre, rim, turn, matrices = tables
    angles, bins = turn.shape[-2:]
    cost = pl.CostEstimate(flops=4 * angles * bins * bins, bytes_accessed=8 * MIB, transcendentals=0)
    merged, partial = pl.pallas_call(
        early_kernel,
        out_shape=[
            jax.ShapeDtypeStruct((2, angles, bins), F32),
            jax.ShapeDtypeStruct((angles, bins), F32),
        ],
        in_specs=[VMEM] * 9,
        out_specs=[VMEM] * 2,
        scratch_shapes=[pltpu.VMEM((angles, bins), F32)],
        compiler_params=params(20),
        cost_estimate=cost,
    )(*own, rims, far[0], far_rims, centre, rim, matrices, turn)
    return pl.pallas_call(
        late_kernel,
        out_shape=jax.ShapeDtypeStruct((2, angles, bins), dtype),
        in_specs=[VMEM] * 6,
        out_specs=ANY,
        scratch_shapes=[
            pltpu.VMEM((2, angles, bins), dtype),
            pltpu.SemaphoreType.DMA((angles // LANES,)),
        ],
        compiler_params=params(20),
        cost_estimate=cost,
    )(far[1], merged, partial, centre, matrices, turn)


def after(value, *earlier):
    return lax.optimization_barrier((value, *earlier))[0]


def from_partner(value, stride):
    pairs = [(source, source ^ stride) for source in range(lax.axis_size("sub"))]
    return lax.ppermute(value, "sub", pairs)


def split_image(level, image, fore_flag, rim):
    angles, bins = image.shape[1:]
    half, step = angles // 2, LANES // 2
    own_flag = fore_flag[level, lax.axis_index("sub"), 0]
    sides = image.reshape(2, 2, half, bins)

    def pieces(side):
        rows = lax.dynamic_index_in_dim(sides, side, 1, keepdims=False)
        ends = [rows[..., :step], rows[..., -step:]]
        rest = [rows[..., -2 * step : -step], rows[..., step : -2 * step]]
        return jnp.concatenate(ends, axis=-1), jnp.concatenate(rest, axis=-1)

    def packed(edge):
        return edge.transpose(2, 0, 1, 3).reshape(half, 4 * rim)

    low, high = packed(sides[..., :rim]), packed(sides[..., -rim:])
    even = lax.axis_index("rng") % 2 == 0
    edges = jnp.where(even, high, low), jnp.where(even, low, high)
    return pieces(own_flag), pieces(1 - own_flag), edges


def on_device(echoes, fore_flag, band_offset, angle_interp, range_kernel, center_shift):
    devices = lax.axis_size("rng")
    half = devices // 2
    local_pulses = echoes.shape[1]
    bins = echoes.shape[2] // devices
    angles = angle_interp.shape[2]
    rim = MAX_SHIFT + (range_kernel.shape[1] - bins) // 2
    levels = range_kernel.shape[0]
    settings = (fore_flag, band_offset, center_shift, range_kernel, angle_interp)

    far_blocks, near_blocks, blocks = placed(
        echoes.reshape(2 * local_pulses, devices * bins), devices
    )
    relay = across(far_blocks, half)
    pulses = lax.all_to_all(blocks, "rng", split_axis=0, concat_axis=0, tiled=True)
    sends = joined(near_blocks, relay)
    pieces = [across(value, d) if d else value for d, value in enumerate(sends)]
    own_matrix, out_matrix = filter_table(fore_flag, angles, local_pulses, sends[0])
    own_outer, out_outer, *edges = outer_image(fore_flag, own_matrix, out_matrix, pieces)

    pulses = after(pulses, out_outer).reshape(2 * local_pulses * devices, bins - LANES)
    out_inner = dot(out_matrix, pulses).astype(BF16).reshape(2, angles // 2, -1)
    own_inner = dot(own_matrix, pulses).astype(BF16).reshape(2, angles // 2, -1)
    tables = merge_tables(0, 1, *settings, own_inner)
    own, out = (own_outer, own_inner), (out_outer, out_inner)
    for level in range(levels):
        stride = 2**level
        if level > 0:
            tables = merge_tables(level, stride, *settings, image)
            own, out, edges = split_image(level, image, fore_flag, rim)
        far = [from_partner(value, stride) for value in out]
        edges = exchanged(edges[0], 0), exchanged(edges[1], 1)
        rims, out_rims = sorted_rims(level, fore_flag, *edges)
        far_rims = from_partner(out_rims, stride)
        image = merged_image(own, rims, far, far_rims, tables, BF16 if level + 1 < levels else F32)
    return image


def solution(mesh):
    placed_as = (
        P(None, ("sub", "rng"), None),
        P(None, None, "rng"),
        P(None, None, "rng"),
        P(),
        P(),
        P(),
    )
    return jax.shard_map(
        on_device, mesh=mesh, in_specs=placed_as, out_specs=P(None, "sub", "rng"), check_vma=False
    )
```

```python
import functools
import math

import jax
import jax.numpy as jnp
from jax import lax
from jax.experimental import pallas as pl
from jax.experimental.pallas import tpu as pltpu
from jax.sharding import PartitionSpec as P

MAX_SHIFT = 16
LANES = 128
MIB = 2**20
JOIN_COST = 10**11
SIDE = jax.ShapeDtypeStruct((8, LANES), jnp.float32)
VMEM = pl.BlockSpec(memory_space=pltpu.VMEM)
SMEM = pl.BlockSpec(memory_space=pltpu.SMEM)
ANY = pl.BlockSpec(memory_space=pl.ANY)
F32 = jnp.float32
BF16 = jnp.bfloat16


def dot(a, b):
    return jnp.dot(a, b, preferred_element_type=F32)


def params(mib):
    return pltpu.CompilerParams(vmem_limit_bytes=mib * MIB)


def series(square, first, count):
    coefs = [
        (-1) ** i * math.pi ** (2 * i + first) / math.factorial(2 * i + first)
        for i in range(count)
    ]
    total = jnp.full_like(square, coefs[-1])
    for coef in coefs[-2::-1]:
        total = total * square + coef
    return total


def cos_sin_pi(v):
    turns = jnp.floor(v + 0.5)
    rest = v - turns
    sign = 1.0 - 2.0 * (turns - 2.0 * jnp.floor(turns * 0.5))
    square = rest * rest
    return series(square, 0, 8) * sign, series(square, 1, 7) * rest * sign


def rotated(pair, step):
    return pair[0] * step[0] - pair[1] * step[1], pair[0] * step[1] + pair[1] * step[0]


def mixed(left, right):
    lane = lax.broadcasted_iota(jnp.int32, left.shape, 1)
    return jnp.where(lane < LANES // 2, left.astype(F32), right.astype(F32)).astype(BF16)


def place_kernel(echoes_ref, far_ref, near_ref, inner_ref):
    devices, _, count = inner_ref.shape
    bins = count + LANES
    half = devices // 2
    base = lax.axis_index("rng") // half * half

    def tile(device, first):
        return echoes_ref[:, pl.ds(pl.multiple_of(device * bins + first, LANES), LANES)]

    for ref, start in ((far_ref, half - base), (near_ref, base)):
        for i in range(half):
            ref[i] = mixed(tile(start + i, 0), tile(start + i, bins - LANES))
    for device in range(devices):
        begin = device * bins
        inner_ref[device, :, :LANES] = mixed(tile(device, bins - LANES), tile(device, 0))
        inner_ref[device, :, LANES:] = echoes_ref[:, begin + LANES : begin + bins - LANES]


def placed(echoes, devices):
    rows, columns = echoes.shape
    outer = jax.ShapeDtypeStruct((devices // 2, rows, LANES), BF16)
    inner = jax.ShapeDtypeStruct((devices, rows, columns // devices - LANES), BF16)
    return pl.pallas_call(
        place_kernel,
        out_shape=[outer, outer, inner],
        in_specs=[VMEM],
        out_specs=[VMEM] * 3,
        compiler_params=params(8),
        cost_estimate=pl.CostEstimate(flops=0, bytes_accessed=2 * MIB, transcendentals=0),
    )(echoes)


def join_kernel(near_ref, relay_ref, *refs):
    me = lax.axis_index("rng") % len(refs)
    rows = near_ref.shape[1]
    for d, out_ref in enumerate(refs):
        out_ref[:rows] = near_ref[me ^ d]
        out_ref[rows:] = relay_ref[me ^ d]


def joined(near, relay):
    half, rows, count = near.shape
    return pl.pallas_call(
        join_kernel,
        out_shape=[jax.ShapeDtypeStruct((2 * rows, count), BF16)] * half,
        in_specs=[VMEM] * 2,
        out_specs=[VMEM] * half,
        compiler_params=params(4),
        cost_estimate=pl.CostEstimate(flops=JOIN_COST, bytes_accessed=MIB, transcendentals=0),
    )(near, relay)


def across(value, mask):
    devices = lax.axis_size("rng")
    return lax.ppermute(value, "rng", [(i, i ^ mask) for i in range(devices)])


def filter_table_kernel(
    local_pulses, flag_ref, after_ref, own_ref, out_ref, side_ref, cos_ref, sin_ref
):
    own_flag = flag_ref[0, lax.axis_index("sub"), 0]
    side_ref[...] = jnp.full(side_ref.shape, own_flag.astype(F32))
    rows, columns = own_ref.shape
    half, angles = rows // 2, rows
    base = cos_ref.shape[0]
    scale = 1.0 / math.sqrt(columns // 2)
    lane = lax.broadcasted_iota(jnp.int32, (8, columns), 1)
    slot = lane // (2 * local_pulses)
    second = lane // local_pulses % 2
    pulse = (slot * local_pulses + lane % local_pulses).astype(F32)
    lag = second.astype(F32) * 0.5
    per_angle = pulse * (1.0 / angles)
    row = lax.broadcasted_iota(jnp.int32, (8, columns), 0)
    step = cos_sin_pi(per_angle * (2 * base))
    for ref, side in ((out_ref, 1 - own_flag), (own_ref, own_flag)):
        first = side * half
        for i in range(base // 8):
            twice = (2 * (row + 8 * i + first) + 1 - angles).astype(F32)
            cosine, sine = cos_sin_pi(twice * per_angle - lag)
            cos_ref[8 * i : 8 * i + 8, :] = cosine * scale
            sin_ref[8 * i : 8 * i + 8, :] = sine * scale
        for j in range(half // base):
            for i in range(base // 16):
                pair = [], []
                for k in (2 * i, 2 * i + 1):
                    here = slice(8 * k, 8 * k + 8)
                    now = cos_ref[here, :], sin_ref[here, :]
                    pair[0].append(now[0])
                    pair[1].append(-now[1])
                    if j + 1 < half // base:
                        cos_ref[here, :], sin_ref[here, :] = rotated(now, step)
                begin = j * base + 16 * i
                ref[begin : begin + 16, :] = jnp.concatenate(pair[0]).astype(BF16)
                begin += half
                ref[begin : begin + 16, :] = jnp.concatenate(pair[1]).astype(BF16)


def filter_table(fore_flag, angles, local_pulses, earlier):
    side = 2 * local_pulses * lax.axis_size("rng")
    return pl.pallas_call(
        functools.partial(filter_table_kernel, local_pulses),
        out_shape=[jax.ShapeDtypeStruct((angles, side), BF16)] * 2 + [SIDE],
        in_specs=[SMEM, ANY],
        out_specs=[VMEM] * 3,
        scratch_shapes=[pltpu.VMEM((64, side), F32)] * 2,
        compiler_params=params(6),
        cost_estimate=pl.CostEstimate(flops=9_000_000, bytes_accessed=4 * MIB, transcendentals=0),
    )(fore_flag, earlier)


def merge_table_kernel(
    level, stride, flag_ref, offset_ref, shift_ref, range_ref, interp_ref, after_ref, centre_ref,
    rim_ref, turn_ref, matrix_ref, side_ref,
):
    group = lax.axis_index("sub")
    block = lax.axis_index("rng")
    bins = centre_ref.shape[-1]
    angles = turn_ref.shape[-2]
    total_bins = lax.axis_size("rng") * bins
    taps = range_ref.shape[1]
    band = (taps - bins) // 2
    rim = MAX_SHIFT + band
    kernel = range_ref[level]

    def moved(bin_id):
        tap = lax.broadcasted_iota(jnp.int32, (bin_id.shape[0], taps), 1)
        return dot(jnp.where(tap == bin_id, 1.0, 0.0).astype(BF16), kernel).astype(BF16)

    row = lax.broadcasted_iota(jnp.int32, (bins, 1), 0)
    upper = row + (bins - 2 * LANES)
    own_bin = jnp.where(row % LANES < LANES // 2, row, upper + LANES)
    own_bin = jnp.where(row >= LANES, jnp.where(row % LANES < LANES // 2, upper, row - LANES), own_bin)
    own_bin = jnp.where(row >= 2 * LANES, row - LANES, own_bin)
    own_flag = flag_ref[level, group, 0]
    side_ref[...] = jnp.full(side_ref.shape, own_flag.astype(F32))
    matrix_ref[0] = interp_ref[level, own_flag]
    matrix_ref[1] = interp_ref[level, 1 - own_flag]
    rim_row = lax.broadcasted_iota(jnp.int32, (2 * rim, 1), 0)
    rim_bin = jnp.where(rim_row < rim, rim_row - rim, rim_row - rim + bins)
    rim_ref[...] = jnp.zeros(rim_ref.shape, BF16)
    bin_id = block * bins + lax.broadcasted_iota(jnp.int32, (1, LANES), 1)
    reach = 1.0 + bin_id.astype(F32) * (1.0 / total_bins)
    rows = 64
    for child in range(2):
        member = group if child == 0 else group ^ stride
        lead = band - offset_ref[level, member, 0]
        centre_ref[child] = moved(own_bin + lead)
        ends = moved(rim_bin + lead)
        for part in range(2):
            for side in range(2):
                place = (2 * side + part) * rim
                rim_ref[child, part, place : place + rim, :] = ends[side * rim : (side + 1) * rim]

        rate = shift_ref[level, member]

        def turn_rows(i, carry):
            begin = pl.multiple_of(i * rows, rows)
            angle = begin + lax.broadcasted_iota(jnp.int32, (rows, LANES), 0)
            place = ((angle.astype(F32) + 0.5) * (1.0 / angles) - 0.5) * rate
            now = cos_sin_pi(place * reach)
            step = cos_sin_pi(place * (LANES / total_bins))
            for tile in range(bins // LANES):
                lanes = slice(tile * LANES, tile * LANES + LANES)
                turn_ref[child, 0, pl.ds(begin, rows), lanes] = now[0]
                turn_ref[child, 1, pl.ds(begin, rows), lanes] = now[1]
                now = rotated(now, step)
            return carry

        lax.fori_loop(0, angles // rows, turn_rows, 0)


def merge_tables(
    level, stride, fore_flag, band_offset, center_shift, range_kernel, angle_interp, earlier
):
    taps, bins = range_kernel.shape[1:]
    angles = angle_interp.shape[2]
    rim = MAX_SHIFT + (taps - bins) // 2
    return pl.pallas_call(
        functools.partial(merge_table_kernel, level, stride),
        out_shape=[
            jax.ShapeDtypeStruct((2, bins, bins), BF16),
            jax.ShapeDtypeStruct((2, 2, 4 * rim, bins), BF16),
            jax.ShapeDtypeStruct((2, 2, angles, bins), F32),
            jax.ShapeDtypeStruct((2, *angle_interp.shape[2:]), BF16),
            SIDE,
        ],
        in_specs=[SMEM] * 3 + [VMEM] * 2 + [ANY],
        out_specs=[VMEM] * 5,
        compiler_params=params(12),
        cost_estimate=pl.CostEstimate(
            flops=2_300_000_000, bytes_accessed=7 * MIB, transcendentals=0
        ),
    )(fore_flag, band_offset, center_shift, range_kernel, angle_interp, earlier)


def outer_kernel(pieces, side_ref, own_rows, out_rows, *refs):
    own_side = side_ref[:1, :]
    me = lax.axis_index("rng")
    own_ref, out_ref, *edge_refs = refs[pieces:-1]
    pulses_ref = refs[-1]
    rows = refs[0].shape[0] // 2
    for d, ref in enumerate(refs[:pieces]):
        for t in range(2):
            place = pl.multiple_of((me ^ (d + t * pieces)) * rows, rows)
            pulses_ref[pl.ds(place, rows), :] = ref[t * rows : (t + 1) * rows, :]
    images = dot(own_rows[...], pulses_ref[...]), dot(out_rows[...], pulses_ref[...])
    half = own_ref.shape[1]
    rim = LANES // 4
    lane = lax.broadcasted_iota(jnp.int32, (1, LANES), 1)
    edges = [0.0, 0.0]
    for part in range(2):
        own, out = (image[part * half : (part + 1) * half] for image in images)
        own_ref[part] = own.astype(BF16)
        out_ref[part] = out.astype(BF16)
        for side in range(2):
            value = jnp.where(own_side == side, own, out)
            group = 2 * part + side
            for end in range(2):
                turn = (group + end) * rim % LANES
                moved = pltpu.roll(value, turn, 1) if turn else value
                edges[end] = edges[end] + jnp.where(lane // rim == group, moved, 0.0)
    even = me % 2 == 0
    edge_refs[0][...] = jnp.where(even, edges[1], edges[0]).astype(BF16)
    edge_refs[1][...] = jnp.where(even, edges[0], edges[1]).astype(BF16)


def outer_image(own_side, own_rows, out_rows, pieces):
    angles, side = own_rows.shape
    image = jax.ShapeDtypeStruct((2, angles // 2, LANES), BF16)
    edge = jax.ShapeDtypeStruct((angles // 2, LANES), BF16)
    return pl.pallas_call(
        functools.partial(outer_kernel, len(pieces)),
        out_shape=[image, image, edge, edge],
        in_specs=[VMEM] * (3 + len(pieces)),
        out_specs=[VMEM] * 4,
        scratch_shapes=[pltpu.VMEM((side, LANES), BF16)],
        compiler_params=params(10),
        cost_estimate=pl.CostEstimate(
            flops=4 * angles * side * LANES, bytes_accessed=3 * MIB, transcendentals=0
        ),
    )(own_side, own_rows, out_rows, *pieces)


def inner_kernel(rows_ref, pulses_ref, image_ref):
    image = dot(rows_ref[...], pulses_ref[...])
    image_ref[...] = image.astype(BF16).reshape(image_ref.shape)


def inner_image(rows, pulses):
    angles, count = rows.shape[0], pulses.shape[1]
    return pl.pallas_call(
        inner_kernel,
        out_shape=jax.ShapeDtypeStruct((2, angles // 2, count), BF16),
        in_specs=[VMEM] * 2,
        out_specs=VMEM,
        compiler_params=params(8),
        cost_estimate=pl.CostEstimate(
            flops=2 * rows.size * count, bytes_accessed=3 * MIB, transcendentals=0
        ),
    )(rows, pulses)


def exchanged(value, begin):
    devices = lax.axis_size("rng")
    pairs = [(i, (i + 1) % devices) for i in range(begin, devices, 2)]
    return lax.ppermute(value, "rng", pairs + [(j, i) for i, j in pairs])


def rims_kernel(side_ref, first_ref, second_ref, own_ref, out_ref):
    own_side = side_ref[:1, :]
    rim = LANES // 4
    me, devices = lax.axis_index("rng"), lax.axis_size("rng")
    even = me % 2 == 0
    first, second = first_ref[...].astype(F32), second_ref[...].astype(F32)
    below = jnp.where(me == 0, 0.0, jnp.where(even, second, first))
    above = jnp.where(me == devices - 1, 0.0, jnp.where(even, first, second))
    group = lax.broadcasted_iota(jnp.int32, (1, LANES), 1) // rim
    packed = [0.0, 0.0]
    for end, value in enumerate((below, above)):
        for part in range(2):
            place = 2 * end + part
            for side in range(2):
                turn = (place - (2 * part + side)) * rim % LANES
                moved = pltpu.roll(value, turn, 1) if turn else value
                packed[side] = packed[side] + jnp.where(group == place, moved, 0.0)
    own_ref[...] = jnp.where(own_side == 0, packed[0], packed[1]).astype(BF16)
    out_ref[...] = jnp.where(own_side == 0, packed[1], packed[0]).astype(BF16)


def sorted_rims(own_side, first, second):
    return pl.pallas_call(
        rims_kernel,
        out_shape=[jax.ShapeDtypeStruct(first.shape, BF16)] * 2,
        in_specs=[VMEM] * 3,
        out_specs=[VMEM] * 2,
        compiler_params=params(4),
        cost_estimate=pl.CostEstimate(flops=1_000_000, bytes_accessed=MIB // 4, transcendentals=0),
    )(own_side, first, second)


def early_kernel(
    own_outer, own_inner, rims_ref, far_outer, far_rims, centre_ref, rim_ref, matrix_ref, turn_ref,
    merged_ref, partial_ref, value_ref,
):
    parts, half, count = own_outer.shape
    image = jnp.concatenate([own_outer[...], own_inner[...]], axis=2)
    value_ref[...] = dot(image.reshape(parts * half, image.shape[2]), centre_ref[0])
    rows = []
    for part in range(parts):
        value = value_ref[part * half : (part + 1) * half, :]
        rows.append((value + dot(rims_ref[...], rim_ref[0, part])).astype(BF16))
    merged_ref[0], merged_ref[1] = rotated(
        (dot(matrix_ref[0], rows[0]), dot(matrix_ref[0], rows[1])), (turn_ref[0, 0], turn_ref[0, 1])
    )
    for part in range(parts):
        value = dot(far_outer[part], centre_ref[1, :count, :])
        here = slice(part * half, (part + 1) * half)
        partial_ref[here, :] = value + dot(far_rims[...], rim_ref[1, part])


def late_kernel(
    far_inner, merged_ref, partial_ref, centre_ref, matrix_ref, turn_ref, out_ref, buffer, sems
):
    parts, half, count = far_inner.shape
    bins = centre_ref.shape[-1]
    inner = far_inner[...].reshape(parts * half, count)
    value = partial_ref[...] + dot(inner, centre_ref[1, bins - count :, :])
    rows = [value[part * half : (part + 1) * half].astype(BF16) for part in range(parts)]
    block = LANES
    copies = []
    for first in range(0, matrix_ref.shape[1], 2 * block):
        matrix = matrix_ref[1, first : first + 2 * block]
        terms = dot(matrix, rows[0]), dot(matrix, rows[1])
        for step in range(2):
            here = slice(first + step * block, first + (step + 1) * block)
            there = slice(step * block, (step + 1) * block)
            turned = rotated(
                (terms[0][there], terms[1][there]), (turn_ref[1, 0, here], turn_ref[1, 1, here])
            )
            for part in range(parts):
                buffer[part, here] = (merged_ref[part, here] + turned[part]).astype(buffer.dtype)
            copy = pltpu.make_async_copy(
                buffer.at[:, here], out_ref.at[:, here], sems.at[len(copies)]
            )
            copy.start()
            copies.append(copy)
    for copy in copies:
        copy.wait()


def merged_image(own, rims, far, far_rims, tables, dtype):
    centre, rim, turn, matrices, _ = tables
    angles, bins = turn.shape[-2:]
    cost = pl.CostEstimate(flops=4 * angles * bins * bins, bytes_accessed=8 * MIB, transcendentals=0)
    merged, partial = pl.pallas_call(
        early_kernel,
        out_shape=[
            jax.ShapeDtypeStruct((2, angles, bins), F32),
            jax.ShapeDtypeStruct((angles, bins), F32),
        ],
        in_specs=[VMEM] * 9,
        out_specs=[VMEM] * 2,
        scratch_shapes=[pltpu.VMEM((angles, bins), F32)],
        compiler_params=params(20),
        cost_estimate=cost,
    )(*own, rims, far[0], far_rims, centre, rim, matrices, turn)
    return pl.pallas_call(
        late_kernel,
        out_shape=jax.ShapeDtypeStruct((2, angles, bins), dtype),
        in_specs=[VMEM] * 6,
        out_specs=ANY,
        scratch_shapes=[
            pltpu.VMEM((2, angles, bins), dtype),
            pltpu.SemaphoreType.DMA((angles // LANES,)),
        ],
        compiler_params=params(20),
        cost_estimate=cost,
    )(far[1], merged, partial, centre, matrices, turn)


def after(value, *earlier):
    return lax.optimization_barrier((value, *earlier))[0]


def from_partner(value, stride):
    pairs = [(source, source ^ stride) for source in range(lax.axis_size("sub"))]
    return lax.ppermute(value, "sub", pairs)


def split_image(level, image, fore_flag, rim):
    angles, bins = image.shape[1:]
    half, step = angles // 2, LANES // 2
    own_flag = fore_flag[level, lax.axis_index("sub"), 0]
    sides = image.reshape(2, 2, half, bins)

    def pieces(side):
        rows = lax.dynamic_index_in_dim(sides, side, 1, keepdims=False)
        ends = [rows[..., :step], rows[..., -step:]]
        rest = [rows[..., -2 * step : -step], rows[..., step : -2 * step]]
        return jnp.concatenate(ends, axis=-1), jnp.concatenate(rest, axis=-1)

    def packed(edge):
        return edge.transpose(2, 0, 1, 3).reshape(half, 4 * rim)

    low, high = packed(sides[..., :rim]), packed(sides[..., -rim:])
    even = lax.axis_index("rng") % 2 == 0
    edges = jnp.where(even, high, low), jnp.where(even, low, high)
    return pieces(own_flag), pieces(1 - own_flag), edges


def on_device(echoes, fore_flag, band_offset, angle_interp, range_kernel, center_shift):
    devices = lax.axis_size("rng")
    half = devices // 2
    local_pulses = echoes.shape[1]
    bins = echoes.shape[2] // devices
    angles = angle_interp.shape[2]
    rim = MAX_SHIFT + (range_kernel.shape[1] - bins) // 2
    levels = range_kernel.shape[0]
    settings = (fore_flag, band_offset, center_shift, range_kernel, angle_interp)

    far_blocks, near_blocks, blocks = placed(
        echoes.reshape(2 * local_pulses, devices * bins), devices
    )
    relay = across(far_blocks, half)
    pulses = lax.all_to_all(blocks, "rng", split_axis=0, concat_axis=0, tiled=True)
    sends = joined(near_blocks, relay)
    pieces = [across(value, d) if d else value for d, value in enumerate(sends)]
    own_matrix, out_matrix, own_side = filter_table(fore_flag, angles, local_pulses, sends[0])
    tables = merge_tables(0, 1, *settings, own_matrix)
    pieces[0] = after(pieces[0], tables[0])
    own_outer, out_outer, *edges = outer_image(own_side, own_matrix, out_matrix, pieces)

    pulses = after(pulses, out_outer).reshape(2 * local_pulses * devices, bins - LANES)
    out_inner = inner_image(out_matrix, pulses)
    own_inner = inner_image(own_matrix, pulses)
    far = [from_partner(value, 1) for value in (out_outer, out_inner)]
    edges = [after(edge, out_inner, far[0]) for edge in edges]
    own = own_outer, own_inner
    for level in range(levels):
        stride = 2**level
        if level > 0:
            tables = merge_tables(level, stride, *settings, image)
            own, out, edges = split_image(level, image, fore_flag, rim)
            far = [from_partner(value, stride) for value in out]
        edges = exchanged(edges[0], 0), exchanged(edges[1], 1)
        rims, out_rims = sorted_rims(tables[-1], *edges)
        far_rims = from_partner(out_rims, stride)
        image = merged_image(own, rims, far, far_rims, tables, BF16 if level + 1 < levels else F32)
    return image


def solution(mesh):
    placed_as = (
        P(None, ("sub", "rng"), None),
        P(None, None, "rng"),
        P(None, None, "rng"),
        P(),
        P(),
        P(),
    )
    return jax.shard_map(
        on_device, mesh=mesh, in_specs=placed_as, out_specs=P(None, "sub", "rng"), check_vma=False
    )
```

```python
import functools
import math

import jax
import jax.numpy as jnp
from jax import lax
from jax.experimental import pallas as pl
from jax.experimental.pallas import tpu as pltpu
from jax.sharding import PartitionSpec as P

MAX_SHIFT = 16
LANES = 128
MIB = 2**20
JOIN_COST = 10**11
SIDE = jax.ShapeDtypeStruct((8, LANES), jnp.float32)
VMEM = pl.BlockSpec(memory_space=pltpu.VMEM)
SMEM = pl.BlockSpec(memory_space=pltpu.SMEM)
ANY = pl.BlockSpec(memory_space=pl.ANY)
F32 = jnp.float32
BF16 = jnp.bfloat16


def dot(a, b):
    return jnp.dot(a, b, preferred_element_type=F32)


def params(mib):
    return pltpu.CompilerParams(vmem_limit_bytes=mib * MIB)


def series(square, first, count):
    coefs = [
        (-1) ** i * math.pi ** (2 * i + first) / math.factorial(2 * i + first)
        for i in range(count)
    ]
    total = jnp.full_like(square, coefs[-1])
    for coef in coefs[-2::-1]:
        total = total * square + coef
    return total


def cos_sin_pi(v):
    turns = jnp.floor(v + 0.5)
    rest = v - turns
    sign = 1.0 - 2.0 * (turns - 2.0 * jnp.floor(turns * 0.5))
    square = rest * rest
    return series(square, 0, 8) * sign, series(square, 1, 7) * rest * sign


def rotated(pair, step):
    return pair[0] * step[0] - pair[1] * step[1], pair[0] * step[1] + pair[1] * step[0]


def mixed(left, right):
    lane = lax.broadcasted_iota(jnp.int32, left.shape, 1)
    return jnp.where(lane < LANES // 2, left.astype(F32), right.astype(F32)).astype(BF16)


def place_kernel(echoes_ref, far_ref, near_ref, inner_ref):
    devices, _, count = inner_ref.shape
    bins = count + LANES
    half = devices // 2
    base = lax.axis_index("rng") // half * half

    def tile(device, first):
        return echoes_ref[:, pl.ds(pl.multiple_of(device * bins + first, LANES), LANES)]

    for ref, start in ((far_ref, half - base), (near_ref, base)):
        for i in range(half):
            ref[i] = mixed(tile(start + i, 0), tile(start + i, bins - LANES))
    for device in range(devices):
        begin = device * bins
        inner_ref[device, :, :LANES] = mixed(tile(device, bins - LANES), tile(device, 0))
        inner_ref[device, :, LANES:] = echoes_ref[:, begin + LANES : begin + bins - LANES]


def placed(echoes, devices):
    rows, columns = echoes.shape
    outer = jax.ShapeDtypeStruct((devices // 2, rows, LANES), BF16)
    inner = jax.ShapeDtypeStruct((devices, rows, columns // devices - LANES), BF16)
    return pl.pallas_call(
        place_kernel,
        out_shape=[outer, outer, inner],
        in_specs=[VMEM],
        out_specs=[VMEM] * 3,
        compiler_params=params(8),
        cost_estimate=pl.CostEstimate(flops=0, bytes_accessed=2 * MIB, transcendentals=0),
    )(echoes)


def join_kernel(near_ref, relay_ref, *refs):
    me = lax.axis_index("rng") % len(refs)
    rows = near_ref.shape[1]
    for d, out_ref in enumerate(refs):
        out_ref[:rows] = near_ref[me ^ d]
        out_ref[rows:] = relay_ref[me ^ d]


def joined(near, relay):
    half, rows, count = near.shape
    return pl.pallas_call(
        join_kernel,
        out_shape=[jax.ShapeDtypeStruct((2 * rows, count), BF16)] * half,
        in_specs=[VMEM] * 2,
        out_specs=[VMEM] * half,
        compiler_params=params(4),
        cost_estimate=pl.CostEstimate(flops=JOIN_COST, bytes_accessed=MIB, transcendentals=0),
    )(near, relay)


def across(value, mask):
    devices = lax.axis_size("rng")
    return lax.ppermute(value, "rng", [(i, i ^ mask) for i in range(devices)])


def filter_table_kernel(
    local_pulses, flag_ref, after_ref, own_ref, out_ref, side_ref, cos_ref, sin_ref
):
    own_flag = flag_ref[0, lax.axis_index("sub"), 0]
    side_ref[...] = jnp.full(side_ref.shape, own_flag.astype(F32))
    rows, columns = own_ref.shape
    half, angles = rows // 2, rows
    base = cos_ref.shape[0]
    scale = 1.0 / math.sqrt(columns // 2)
    lane = lax.broadcasted_iota(jnp.int32, (8, columns), 1)
    slot = lane // (2 * local_pulses)
    second = lane // local_pulses % 2
    pulse = (slot * local_pulses + lane % local_pulses).astype(F32)
    lag = second.astype(F32) * 0.5
    per_angle = pulse * (1.0 / angles)
    row = lax.broadcasted_iota(jnp.int32, (8, columns), 0)
    step = cos_sin_pi(per_angle * (2 * base))
    for ref, side in ((out_ref, 1 - own_flag), (own_ref, own_flag)):
        first = side * half
        for i in range(base // 8):
            twice = (2 * (row + 8 * i + first) + 1 - angles).astype(F32)
            cosine, sine = cos_sin_pi(twice * per_angle - lag)
            cos_ref[8 * i : 8 * i + 8, :] = cosine * scale
            sin_ref[8 * i : 8 * i + 8, :] = sine * scale
        for j in range(half // base):
            for i in range(base // 16):
                pair = [], []
                for k in (2 * i, 2 * i + 1):
                    here = slice(8 * k, 8 * k + 8)
                    now = cos_ref[here, :], sin_ref[here, :]
                    pair[0].append(now[0])
                    pair[1].append(-now[1])
                    if j + 1 < half // base:
                        cos_ref[here, :], sin_ref[here, :] = rotated(now, step)
                begin = j * base + 16 * i
                ref[begin : begin + 16, :] = jnp.concatenate(pair[0]).astype(BF16)
                begin += half
                ref[begin : begin + 16, :] = jnp.concatenate(pair[1]).astype(BF16)


def filter_table(fore_flag, angles, local_pulses, earlier):
    side = 2 * local_pulses * lax.axis_size("rng")
    return pl.pallas_call(
        functools.partial(filter_table_kernel, local_pulses),
        out_shape=[jax.ShapeDtypeStruct((angles, side), BF16)] * 2 + [SIDE],
        in_specs=[SMEM, ANY],
        out_specs=[VMEM] * 3,
        scratch_shapes=[pltpu.VMEM((64, side), F32)] * 2,
        compiler_params=params(6),
        cost_estimate=pl.CostEstimate(flops=9_000_000, bytes_accessed=4 * MIB, transcendentals=0),
    )(fore_flag, earlier)


def merge_table_kernel(
    level, stride, flag_ref, offset_ref, shift_ref, range_ref, interp_ref, after_ref, centre_ref,
    rim_ref, turn_ref, matrix_ref, side_ref,
):
    group = lax.axis_index("sub")
    block = lax.axis_index("rng")
    bins = centre_ref.shape[-1]
    angles = turn_ref.shape[-2]
    total_bins = lax.axis_size("rng") * bins
    taps = range_ref.shape[1]
    band = (taps - bins) // 2
    rim = MAX_SHIFT + band
    kernel = range_ref[level]

    def moved(bin_id):
        tap = lax.broadcasted_iota(jnp.int32, (bin_id.shape[0], taps), 1)
        return dot(jnp.where(tap == bin_id, 1.0, 0.0).astype(BF16), kernel).astype(BF16)

    row = lax.broadcasted_iota(jnp.int32, (bins, 1), 0)
    upper = row + (bins - 2 * LANES)
    own_bin = jnp.where(row % LANES < LANES // 2, row, upper + LANES)
    own_bin = jnp.where(row >= LANES, jnp.where(row % LANES < LANES // 2, upper, row - LANES), own_bin)
    own_bin = jnp.where(row >= 2 * LANES, row - LANES, own_bin)
    own_flag = flag_ref[level, group, 0]
    side_ref[...] = jnp.full(side_ref.shape, own_flag.astype(F32))
    matrix_ref[0] = interp_ref[level, own_flag]
    matrix_ref[1] = interp_ref[level, 1 - own_flag]
    rim_row = lax.broadcasted_iota(jnp.int32, (2 * rim, 1), 0)
    rim_bin = jnp.where(rim_row < rim, rim_row - rim, rim_row - rim + bins)
    rim_ref[...] = jnp.zeros(rim_ref.shape, BF16)
    bin_id = block * bins + lax.broadcasted_iota(jnp.int32, (1, LANES), 1)
    reach = 1.0 + bin_id.astype(F32) * (1.0 / total_bins)
    rows = 64
    for child in range(2):
        member = group if child == 0 else group ^ stride
        lead = band - offset_ref[level, member, 0]
        centre_ref[child] = moved(own_bin + lead)
        ends = moved(rim_bin + lead)
        for part in range(2):
            for side in range(2):
                place = (2 * side + part) * rim
                rim_ref[child, part, place : place + rim, :] = ends[side * rim : (side + 1) * rim]

        rate = shift_ref[level, member]

        def turn_rows(i, carry):
            begin = pl.multiple_of(i * rows, rows)
            angle = begin + lax.broadcasted_iota(jnp.int32, (rows, LANES), 0)
            place = ((angle.astype(F32) + 0.5) * (1.0 / angles) - 0.5) * rate
            now = cos_sin_pi(place * reach)
            step = cos_sin_pi(place * (LANES / total_bins))
            for tile in range(bins // LANES):
                lanes = slice(tile * LANES, tile * LANES + LANES)
                turn_ref[child, 0, pl.ds(begin, rows), lanes] = now[0]
                turn_ref[child, 1, pl.ds(begin, rows), lanes] = now[1]
                now = rotated(now, step)
            return carry

        lax.fori_loop(0, angles // rows, turn_rows, 0)


def merge_tables(
    level, stride, fore_flag, band_offset, center_shift, range_kernel, angle_interp, earlier
):
    taps, bins = range_kernel.shape[1:]
    angles = angle_interp.shape[2]
    rim = MAX_SHIFT + (taps - bins) // 2
    return pl.pallas_call(
        functools.partial(merge_table_kernel, level, stride),
        out_shape=[
            jax.ShapeDtypeStruct((2, bins, bins), BF16),
            jax.ShapeDtypeStruct((2, 2, 4 * rim, bins), BF16),
            jax.ShapeDtypeStruct((2, 2, angles, bins), F32),
            jax.ShapeDtypeStruct((2, *angle_interp.shape[2:]), BF16),
            SIDE,
        ],
        in_specs=[SMEM] * 3 + [VMEM] * 2 + [ANY],
        out_specs=[VMEM] * 5,
        compiler_params=params(12),
        cost_estimate=pl.CostEstimate(
            flops=2_300_000_000, bytes_accessed=7 * MIB, transcendentals=0
        ),
    )(fore_flag, band_offset, center_shift, range_kernel, angle_interp, earlier)


def outer_kernel(pieces, side_ref, own_rows, out_rows, *refs):
    own_side = side_ref[:1, :]
    me = lax.axis_index("rng")
    own_ref, out_ref, *edge_refs = refs[pieces:-1]
    pulses_ref = refs[-1]
    rows = refs[0].shape[0] // 2
    for d, ref in enumerate(refs[:pieces]):
        for t in range(2):
            place = pl.multiple_of((me ^ (d + t * pieces)) * rows, rows)
            pulses_ref[pl.ds(place, rows), :] = ref[t * rows : (t + 1) * rows, :]
    images = dot(own_rows[...], pulses_ref[...]), dot(out_rows[...], pulses_ref[...])
    half = own_ref.shape[1]
    rim = LANES // 4
    lane = lax.broadcasted_iota(jnp.int32, (1, LANES), 1)
    edges = [0.0, 0.0]
    for part in range(2):
        own, out = (image[part * half : (part + 1) * half] for image in images)
        own_ref[part] = own.astype(BF16)
        out_ref[part] = out.astype(BF16)
        for side in range(2):
            value = jnp.where(own_side == side, own, out)
            group = 2 * part + side
            for end in range(2):
                turn = (group + end) * rim % LANES
                moved = pltpu.roll(value, turn, 1) if turn else value
                edges[end] = edges[end] + jnp.where(lane // rim == group, moved, 0.0)
    even = me % 2 == 0
    edge_refs[0][...] = jnp.where(even, edges[1], edges[0]).astype(BF16)
    edge_refs[1][...] = jnp.where(even, edges[0], edges[1]).astype(BF16)


def outer_image(own_side, own_rows, out_rows, pieces):
    angles, side = own_rows.shape
    image = jax.ShapeDtypeStruct((2, angles // 2, LANES), BF16)
    edge = jax.ShapeDtypeStruct((angles // 2, LANES), BF16)
    return pl.pallas_call(
        functools.partial(outer_kernel, len(pieces)),
        out_shape=[image, image, edge, edge],
        in_specs=[VMEM] * (3 + len(pieces)),
        out_specs=[VMEM] * 4,
        scratch_shapes=[pltpu.VMEM((side, LANES), BF16)],
        compiler_params=params(10),
        cost_estimate=pl.CostEstimate(
            flops=4 * angles * side * LANES, bytes_accessed=3 * MIB, transcendentals=0
        ),
    )(own_side, own_rows, out_rows, *pieces)


def inner_kernel(rows_ref, pulses_ref, outer_ref, image_ref):
    image = dot(rows_ref[...], pulses_ref[...])
    parts, half, count = outer_ref.shape
    image_ref[:, :, :count] = outer_ref[...]
    image_ref[:, :, count:] = image.astype(BF16).reshape(parts, half, image.shape[1])


def whole_image(rows, pulses, outer):
    parts, half, count = outer.shape
    return pl.pallas_call(
        inner_kernel,
        out_shape=jax.ShapeDtypeStruct((parts, half, count + pulses.shape[1]), BF16),
        in_specs=[VMEM] * 3,
        out_specs=VMEM,
        compiler_params=params(8),
        cost_estimate=pl.CostEstimate(
            flops=2 * rows.size * pulses.shape[1], bytes_accessed=3 * MIB, transcendentals=0
        ),
    )(rows, pulses, outer)


def exchanged(value, begin):
    devices = lax.axis_size("rng")
    pairs = [(i, (i + 1) % devices) for i in range(begin, devices, 2)]
    return lax.ppermute(value, "rng", pairs + [(j, i) for i, j in pairs])


def rims_kernel(side_ref, first_ref, second_ref, own_ref, out_ref):
    own_side = side_ref[:1, :]
    rim = LANES // 4
    me, devices = lax.axis_index("rng"), lax.axis_size("rng")
    even = me % 2 == 0
    first, second = first_ref[...].astype(F32), second_ref[...].astype(F32)
    below = jnp.where(me == 0, 0.0, jnp.where(even, second, first))
    above = jnp.where(me == devices - 1, 0.0, jnp.where(even, first, second))
    group = lax.broadcasted_iota(jnp.int32, (1, LANES), 1) // rim
    packed = [0.0, 0.0]
    for end, value in enumerate((below, above)):
        for part in range(2):
            place = 2 * end + part
            for side in range(2):
                turn = (place - (2 * part + side)) * rim % LANES
                moved = pltpu.roll(value, turn, 1) if turn else value
                packed[side] = packed[side] + jnp.where(group == place, moved, 0.0)
    own_ref[...] = jnp.where(own_side == 0, packed[0], packed[1]).astype(BF16)
    out_ref[...] = jnp.where(own_side == 0, packed[1], packed[0]).astype(BF16)


def sorted_rims(own_side, first, second):
    return pl.pallas_call(
        rims_kernel,
        out_shape=[jax.ShapeDtypeStruct(first.shape, BF16)] * 2,
        in_specs=[VMEM] * 3,
        out_specs=[VMEM] * 2,
        compiler_params=params(4),
        cost_estimate=pl.CostEstimate(flops=1_000_000, bytes_accessed=MIB // 4, transcendentals=0),
    )(own_side, first, second)


def resampled(image_ref, rims_ref, centre_ref, rim_ref, value_ref, child):
    parts, half, bins = image_ref.shape
    value_ref[...] = dot(image_ref[...].reshape(parts * half, bins), centre_ref[child])
    rims = rims_ref[...]
    return [
        (value_ref[part * half : (part + 1) * half, :] + dot(rims, rim_ref[child, part])).astype(BF16)
        for part in range(parts)
    ]


def early_kernel(
    own_ref, rims_ref, centre_ref, rim_ref, matrix_ref, turn_ref, merged_ref, value_ref
):
    rows = resampled(own_ref, rims_ref, centre_ref, rim_ref, value_ref, 0)
    merged_ref[0], merged_ref[1] = rotated(
        (dot(matrix_ref[0], rows[0]), dot(matrix_ref[0], rows[1])), (turn_ref[0, 0], turn_ref[0, 1])
    )


def late_kernel(
    far_ref, rims_ref, merged_ref, centre_ref, rim_ref, matrix_ref, turn_ref, out_ref, buffer,
    value_ref, sems,
):
    rows = resampled(far_ref, rims_ref, centre_ref, rim_ref, value_ref, 1)
    parts = len(rows)
    block = LANES
    copies = []
    for first in range(0, matrix_ref.shape[1], 2 * block):
        matrix = matrix_ref[1, first : first + 2 * block]
        terms = dot(matrix, rows[0]), dot(matrix, rows[1])
        for step in range(2):
            here = slice(first + step * block, first + (step + 1) * block)
            there = slice(step * block, (step + 1) * block)
            turned = rotated(
                (terms[0][there], terms[1][there]), (turn_ref[1, 0, here], turn_ref[1, 1, here])
            )
            for part in range(parts):
                buffer[part, here] = (merged_ref[part, here] + turned[part]).astype(buffer.dtype)
            copy = pltpu.make_async_copy(
                buffer.at[:, here], out_ref.at[:, here], sems.at[len(copies)]
            )
            copy.start()
            copies.append(copy)
    for copy in copies:
        copy.wait()


def merged_image(own, rims, far, far_rims, tables, dtype):
    centre, rim, turn, matrices, _ = tables
    angles, bins = turn.shape[-2:]
    cost = pl.CostEstimate(flops=4 * angles * bins * bins, bytes_accessed=8 * MIB, transcendentals=0)
    value = pltpu.VMEM((angles, bins), F32)
    merged = pl.pallas_call(
        early_kernel,
        out_shape=jax.ShapeDtypeStruct((2, angles, bins), F32),
        in_specs=[VMEM] * 6,
        out_specs=VMEM,
        scratch_shapes=[value],
        compiler_params=params(16),
        cost_estimate=cost,
    )(own, rims, centre, rim, matrices, turn)
    return pl.pallas_call(
        late_kernel,
        out_shape=jax.ShapeDtypeStruct((2, angles, bins), dtype),
        in_specs=[VMEM] * 7,
        out_specs=ANY,
        scratch_shapes=[
            pltpu.VMEM((2, angles, bins), dtype),
            value,
            pltpu.SemaphoreType.DMA((angles // LANES,)),
        ],
        compiler_params=params(16),
        cost_estimate=cost,
    )(far, far_rims, merged, centre, rim, matrices, turn)


def after(value, *earlier):
    return lax.optimization_barrier((value, *earlier))[0]


def from_partner(value, stride):
    pairs = [(source, source ^ stride) for source in range(lax.axis_size("sub"))]
    return lax.ppermute(value, "sub", pairs)


def split_image(level, image, fore_flag, rim):
    angles, bins = image.shape[1:]
    half, step = angles // 2, LANES // 2
    own_flag = fore_flag[level, lax.axis_index("sub"), 0]
    sides = image.reshape(2, 2, half, bins)

    def pieces(side):
        rows = lax.dynamic_index_in_dim(sides, side, 1, keepdims=False)
        ends = [rows[..., :step], rows[..., -step:]]
        rest = [rows[..., -2 * step : -step], rows[..., step : -2 * step]]
        return jnp.concatenate(ends + rest, axis=-1)

    def packed(edge):
        return edge.transpose(2, 0, 1, 3).reshape(half, 4 * rim)

    low, high = packed(sides[..., :rim]), packed(sides[..., -rim:])
    even = lax.axis_index("rng") % 2 == 0
    edges = jnp.where(even, high, low), jnp.where(even, low, high)
    return pieces(own_flag), pieces(1 - own_flag), edges


def on_device(echoes, fore_flag, band_offset, angle_interp, range_kernel, center_shift):
    devices = lax.axis_size("rng")
    half = devices // 2
    local_pulses = echoes.shape[1]
    bins = echoes.shape[2] // devices
    angles = angle_interp.shape[2]
    rim = MAX_SHIFT + (range_kernel.shape[1] - bins) // 2
    levels = range_kernel.shape[0]
    settings = (fore_flag, band_offset, center_shift, range_kernel, angle_interp)

    far_blocks, near_blocks, blocks = placed(
        echoes.reshape(2 * local_pulses, devices * bins), devices
    )
    relay = across(far_blocks, half)
    pulses = lax.all_to_all(blocks, "rng", split_axis=0, concat_axis=0, tiled=True)
    sends = joined(near_blocks, relay)
    pieces = [across(value, d) if d else value for d, value in enumerate(sends)]
    own_matrix, out_matrix, own_side = filter_table(fore_flag, angles, local_pulses, sends[0])
    own_outer, out_outer, *edges = outer_image(own_side, own_matrix, out_matrix, pieces)

    pulses = after(pulses, out_outer).reshape(2 * local_pulses * devices, bins - LANES)
    out = whole_image(out_matrix, pulses, out_outer)
    own = whole_image(own_matrix, pulses, own_outer)
    edges = [after(edge, out) for edge in edges]
    tables = merge_tables(0, 1, *settings, own)
    for level in range(levels):
        stride = 2**level
        if level > 0:
            tables = merge_tables(level, stride, *settings, image)
            own, out, edges = split_image(level, image, fore_flag, rim)
            own_side = tables[-1]
        far = from_partner(out, stride)
        edges = exchanged(edges[0], 0), exchanged(edges[1], 1)
        rims, out_rims = sorted_rims(own_side, *edges)
        far_rims = from_partner(out_rims, stride)
        image = merged_image(own, rims, far, far_rims, tables, BF16 if level + 1 < levels else F32)
    return image


def solution(mesh):
    placed_as = (
        P(None, ("sub", "rng"), None),
        P(None, None, "rng"),
        P(None, None, "rng"),
        P(),
        P(),
        P(),
    )
    return jax.shard_map(
        on_device, mesh=mesh, in_specs=placed_as, out_specs=P(None, "sub", "rng"), check_vma=False
    )
```

```python
import functools
import math

import jax
import jax.numpy as jnp
from jax import lax
from jax.experimental import pallas as pl
from jax.experimental.pallas import tpu as pltpu
from jax.sharding import PartitionSpec as P

MAX_SHIFT = 16
LANES = 128
MIB = 2**20
JOIN_COST = 10**11
SIDE = jax.ShapeDtypeStruct((8, LANES), jnp.float32)
VMEM = pl.BlockSpec(memory_space=pltpu.VMEM)
SMEM = pl.BlockSpec(memory_space=pltpu.SMEM)
ANY = pl.BlockSpec(memory_space=pl.ANY)
F32 = jnp.float32
BF16 = jnp.bfloat16


def dot(a, b):
    return jnp.dot(a, b, preferred_element_type=F32)


def params(mib):
    return pltpu.CompilerParams(vmem_limit_bytes=mib * MIB)


def series(square, first, count):
    coefs = [
        (-1) ** i * math.pi ** (2 * i + first) / math.factorial(2 * i + first)
        for i in range(count)
    ]
    total = jnp.full_like(square, coefs[-1])
    for coef in coefs[-2::-1]:
        total = total * square + coef
    return total


def cos_sin_pi(v):
    turns = jnp.floor(v + 0.5)
    rest = v - turns
    sign = 1.0 - 2.0 * (turns - 2.0 * jnp.floor(turns * 0.5))
    square = rest * rest
    return series(square, 0, 8) * sign, series(square, 1, 7) * rest * sign


def rotated(pair, step):
    return pair[0] * step[0] - pair[1] * step[1], pair[0] * step[1] + pair[1] * step[0]


def mixed(left, right):
    lane = lax.broadcasted_iota(jnp.int32, left.shape, 1)
    return jnp.where(lane < LANES // 2, left.astype(F32), right.astype(F32)).astype(BF16)


def place_kernel(echoes_ref, far_ref, near_ref, inner_ref):
    devices, _, count = inner_ref.shape
    bins = count + LANES
    half = devices // 2
    base = lax.axis_index("rng") // half * half

    def tile(device, first):
        return echoes_ref[:, pl.ds(pl.multiple_of(device * bins + first, LANES), LANES)]

    for ref, start in ((far_ref, half - base), (near_ref, base)):
        for i in range(half):
            ref[i] = mixed(tile(start + i, 0), tile(start + i, bins - LANES))
    for device in range(devices):
        begin = device * bins
        inner_ref[device, :, :LANES] = mixed(tile(device, bins - LANES), tile(device, 0))
        inner_ref[device, :, LANES:] = echoes_ref[:, begin + LANES : begin + bins - LANES]


def placed(echoes, devices):
    rows, columns = echoes.shape
    outer = jax.ShapeDtypeStruct((devices // 2, rows, LANES), BF16)
    inner = jax.ShapeDtypeStruct((devices, rows, columns // devices - LANES), BF16)
    return pl.pallas_call(
        place_kernel,
        out_shape=[outer, outer, inner],
        in_specs=[VMEM],
        out_specs=[VMEM] * 3,
        compiler_params=params(8),
        cost_estimate=pl.CostEstimate(flops=0, bytes_accessed=2 * MIB, transcendentals=0),
    )(echoes)


def join_kernel(near_ref, relay_ref, send_ref, keep_ref):
    devices = near_ref.shape[0]
    me = lax.axis_index("rng") % devices
    rows = near_ref.shape[1]
    for d in range(devices):
        ref = keep_ref if d < devices // 2 else send_ref
        ref[0, d % (devices // 2), :rows] = near_ref[me ^ d]
        ref[0, d % (devices // 2), rows:] = relay_ref[me ^ d]


def split_kernel(keep_ref, got_ref, send_ref, next_ref):
    sources, targets = keep_ref.shape[:2]
    for i, ref in enumerate((keep_ref, got_ref)):
        here = slice(i * sources, (i + 1) * sources)
        next_ref[here] = ref[:, : targets // 2]
        send_ref[here] = ref[:, targets // 2 :]


def halved(kernel, shape, flops, *operands):
    return pl.pallas_call(
        kernel,
        out_shape=[jax.ShapeDtypeStruct(shape, BF16)] * 2,
        in_specs=[VMEM] * 2,
        out_specs=[VMEM] * 2,
        compiler_params=params(4),
        cost_estimate=pl.CostEstimate(flops=flops, bytes_accessed=MIB, transcendentals=0),
    )(*operands)


def spread(near, relay):
    devices, rows, count = near.shape
    shape = (1, devices // 2, 2 * rows, count)
    send, keep = halved(join_kernel, shape, JOIN_COST, near, relay)
    sources, bit = [0], devices // 2
    while True:
        got = across(send, bit)
        if bit == 1:
            return (keep, got), (sources, [d ^ bit for d in sources])
        sources = sources + [d ^ bit for d in sources]
        bit //= 2
        shape = (2 * shape[0], shape[1] // 2, *shape[2:])
        send, keep = halved(split_kernel, shape, 1_000_000, keep, got)


def across(value, mask):
    devices = lax.axis_size("rng")
    return lax.ppermute(value, "rng", [(i, i ^ mask) for i in range(devices)])


def filter_table_kernel(
    local_pulses, flag_ref, after_ref, own_ref, out_ref, side_ref, cos_ref, sin_ref
):
    own_flag = flag_ref[0, lax.axis_index("sub"), 0]
    side_ref[...] = jnp.full(side_ref.shape, own_flag.astype(F32))
    angles, columns = out_ref.shape
    half = angles // 2
    base = cos_ref.shape[0]
    scale = 1.0 / math.sqrt(columns // 2)
    lane = lax.broadcasted_iota(jnp.int32, (8, columns), 1)
    slot = lane // (2 * local_pulses)
    second = lane // local_pulses % 2
    pulse = (slot * local_pulses + lane % local_pulses).astype(F32)
    lag = second.astype(F32) * 0.5
    per_angle = pulse * (1.0 / angles)
    row = lax.broadcasted_iota(jnp.int32, (8, columns), 0)
    step = cos_sin_pi(per_angle * (2 * base))
    for ref, side in ((out_ref, 1 - own_flag), (own_ref, own_flag)):
        first = side * half
        for i in range(base // 8):
            twice = (2 * (row + 8 * i + first) + 1 - angles).astype(F32)
            cosine, sine = cos_sin_pi(twice * per_angle - lag)
            cos_ref[8 * i : 8 * i + 8, :] = cosine * scale
            sin_ref[8 * i : 8 * i + 8, :] = sine * scale
        for j in range(half // base):
            for i in range(base // 16):
                pair = [], []
                for k in (2 * i, 2 * i + 1):
                    here = slice(8 * k, 8 * k + 8)
                    now = cos_ref[here, :], sin_ref[here, :]
                    pair[0].append(now[0])
                    pair[1].append(-now[1])
                    if j + 1 < half // base:
                        cos_ref[here, :], sin_ref[here, :] = rotated(now, step)
                begin = j * base + 16 * i
                ref[begin : begin + 16, :] = jnp.concatenate(pair[0]).astype(BF16)
                if ref is out_ref:
                    begin += half
                    ref[begin : begin + 16, :] = jnp.concatenate(pair[1]).astype(BF16)


def filter_table(fore_flag, angles, local_pulses, earlier):
    side = 2 * local_pulses * lax.axis_size("rng")
    return pl.pallas_call(
        functools.partial(filter_table_kernel, local_pulses),
        out_shape=[
            jax.ShapeDtypeStruct((angles // 2, side), BF16),
            jax.ShapeDtypeStruct((angles, side), BF16),
            SIDE,
        ],
        in_specs=[SMEM, ANY],
        out_specs=[VMEM] * 3,
        scratch_shapes=[pltpu.VMEM((64, side), F32)] * 2,
        compiler_params=params(6),
        cost_estimate=pl.CostEstimate(flops=9_000_000, bytes_accessed=4 * MIB, transcendentals=0),
    )(fore_flag, earlier)


def merge_table_kernel(
    level, stride, flag_ref, offset_ref, shift_ref, range_ref, interp_ref, after_ref, centre_ref,
    rim_ref, turn_ref, matrix_ref, side_ref,
):
    group = lax.axis_index("sub")
    block = lax.axis_index("rng")
    bins = centre_ref.shape[-1]
    angles = turn_ref.shape[-2]
    total_bins = lax.axis_size("rng") * bins
    taps = range_ref.shape[1]
    band = (taps - bins) // 2
    rim = MAX_SHIFT + band
    kernel = range_ref[level]

    def moved(bin_id):
        tap = lax.broadcasted_iota(jnp.int32, (bin_id.shape[0], taps), 1)
        return dot(jnp.where(tap == bin_id, 1.0, 0.0).astype(BF16), kernel).astype(BF16)

    row = lax.broadcasted_iota(jnp.int32, (bins, 1), 0)
    upper = row + (bins - 2 * LANES)
    own_bin = jnp.where(row % LANES < LANES // 2, row, upper + LANES)
    own_bin = jnp.where(row >= LANES, jnp.where(row % LANES < LANES // 2, upper, row - LANES), own_bin)
    own_bin = jnp.where(row >= 2 * LANES, row - LANES, own_bin)
    own_flag = flag_ref[level, group, 0]
    side_ref[...] = jnp.full(side_ref.shape, own_flag.astype(F32))
    matrix_ref[0] = interp_ref[level, own_flag]
    matrix_ref[1] = interp_ref[level, 1 - own_flag]
    rim_row = lax.broadcasted_iota(jnp.int32, (2 * rim, 1), 0)
    rim_bin = jnp.where(rim_row < rim, rim_row - rim, rim_row - rim + bins)
    rim_ref[...] = jnp.zeros(rim_ref.shape, BF16)
    bin_id = block * bins + lax.broadcasted_iota(jnp.int32, (1, LANES), 1)
    reach = 1.0 + bin_id.astype(F32) * (1.0 / total_bins)
    rows = 64
    for child in range(2):
        member = group if child == 0 else group ^ stride
        lead = band - offset_ref[level, member, 0]
        centre_ref[child] = moved(own_bin + lead)
        ends = moved(rim_bin + lead)
        for part in range(2):
            for side in range(2):
                place = (2 * side + part) * rim
                rim_ref[child, part, place : place + rim, :] = ends[side * rim : (side + 1) * rim]

        rate = shift_ref[level, member]

        def turn_rows(i, carry):
            begin = pl.multiple_of(i * rows, rows)
            angle = begin + lax.broadcasted_iota(jnp.int32, (rows, LANES), 0)
            place = ((angle.astype(F32) + 0.5) * (1.0 / angles) - 0.5) * rate
            now = cos_sin_pi(place * reach)
            step = cos_sin_pi(place * (LANES / total_bins))
            for tile in range(bins // LANES):
                lanes = slice(tile * LANES, tile * LANES + LANES)
                turn_ref[child, 0, pl.ds(begin, rows), lanes] = now[0]
                turn_ref[child, 1, pl.ds(begin, rows), lanes] = now[1]
                now = rotated(now, step)
            return carry

        lax.fori_loop(0, angles // rows, turn_rows, 0)


def merge_tables(
    level, stride, fore_flag, band_offset, center_shift, range_kernel, angle_interp, earlier
):
    taps, bins = range_kernel.shape[1:]
    angles = angle_interp.shape[2]
    rim = MAX_SHIFT + (taps - bins) // 2
    return pl.pallas_call(
        functools.partial(merge_table_kernel, level, stride),
        out_shape=[
            jax.ShapeDtypeStruct((2, bins, bins), BF16),
            jax.ShapeDtypeStruct((2, 2, 4 * rim, bins), BF16),
            jax.ShapeDtypeStruct((2, 2, angles, bins), F32),
            jax.ShapeDtypeStruct((2, *angle_interp.shape[2:]), BF16),
            SIDE,
        ],
        in_specs=[SMEM] * 3 + [VMEM] * 2 + [ANY],
        out_specs=[VMEM] * 5,
        compiler_params=params(12),
        cost_estimate=pl.CostEstimate(
            flops=2_300_000_000, bytes_accessed=7 * MIB, transcendentals=0
        ),
    )(fore_flag, band_offset, center_shift, range_kernel, angle_interp, earlier)


def quarter_turned(pulses, local_pulses):
    value = pulses.astype(F32)
    count = value.shape[0]
    second = lax.broadcasted_iota(jnp.int32, (count, 1), 0) // local_pulses % 2 == 1
    ahead, behind = pltpu.roll(value, count - local_pulses, 0), pltpu.roll(value, local_pulses, 0)
    return jnp.where(second, -behind, ahead).astype(BF16)


def own_image(rows, pulses, local_pulses):
    return dot(rows, pulses), dot(rows, quarter_turned(pulses, local_pulses))


def outer_kernel(sources, side_ref, own_rows, out_rows, *refs):
    own_side = side_ref[:1, :]
    me = lax.axis_index("rng")
    own_ref, out_ref, *edge_refs = refs[2:-1]
    pulses_ref = refs[-1]
    rows = refs[0].shape[2] // 2
    across_half = 2 * len(sources[0])
    for ref, devices in zip(refs, sources):
        for i, d in enumerate(devices):
            for t in range(2):
                place = pl.multiple_of((me ^ (d + t * across_half)) * rows, rows)
                pulses_ref[pl.ds(place, rows), :] = ref[i, 0, t * rows : (t + 1) * rows, :]
    pulses = pulses_ref[...]
    own_parts = own_image(own_rows[...], pulses, rows // 2)
    out_parts = dot(out_rows[...], pulses)
    half = own_ref.shape[1]
    rim = LANES // 4
    lane = lax.broadcasted_iota(jnp.int32, (1, LANES), 1)
    edges = [0.0, 0.0]
    for part in range(2):
        own, out = own_parts[part], out_parts[part * half : (part + 1) * half]
        own_ref[part] = own.astype(BF16)
        out_ref[part] = out.astype(BF16)
        for side in range(2):
            value = jnp.where(own_side == side, own, out)
            group = 2 * part + side
            for end in range(2):
                turn = (group + end) * rim % LANES
                moved = pltpu.roll(value, turn, 1) if turn else value
                edges[end] = edges[end] + jnp.where(lane // rim == group, moved, 0.0)
    even = me % 2 == 0
    edge_refs[0][...] = jnp.where(even, edges[1], edges[0]).astype(BF16)
    edge_refs[1][...] = jnp.where(even, edges[0], edges[1]).astype(BF16)


def outer_image(own_side, own_rows, out_rows, pieces, sources):
    angles, side = out_rows.shape
    image = jax.ShapeDtypeStruct((2, angles // 2, LANES), BF16)
    edge = jax.ShapeDtypeStruct((angles // 2, LANES), BF16)
    return pl.pallas_call(
        functools.partial(outer_kernel, sources),
        out_shape=[image, image, edge, edge],
        in_specs=[VMEM] * (3 + len(pieces)),
        out_specs=[VMEM] * 4,
        scratch_shapes=[pltpu.VMEM((side, LANES), BF16)],
        compiler_params=params(10),
        cost_estimate=pl.CostEstimate(
            flops=4 * angles * side * LANES, bytes_accessed=3 * MIB, transcendentals=0
        ),
    )(own_side, own_rows, out_rows, *pieces)


def partner_rows_kernel(rows_ref, pulses_ref, image_ref):
    image = dot(rows_ref[...], pulses_ref[...])
    image_ref[...] = image.astype(BF16).reshape(image_ref.shape)


def own_rows_kernel(local_pulses, rows_ref, pulses_ref, outer_ref, image_ref):
    parts = own_image(rows_ref[...], pulses_ref[...], local_pulses)
    count = outer_ref.shape[2]
    image_ref[:, :, :count] = outer_ref[...]
    for part, image in enumerate(parts):
        image_ref[part, :, count:] = image.astype(BF16)


def inner_image(kernel, angles, rows, pulses, outer=()):
    count = pulses.shape[1]
    whole = count + (outer[0].shape[2] if outer else 0)
    return pl.pallas_call(
        kernel,
        out_shape=jax.ShapeDtypeStruct((2, angles // 2, whole), BF16),
        in_specs=[VMEM] * (2 + len(outer)),
        out_specs=VMEM,
        compiler_params=params(10),
        cost_estimate=pl.CostEstimate(
            flops=2 * angles * rows.shape[1] * count, bytes_accessed=3 * MIB, transcendentals=0
        ),
    )(rows, pulses, *outer)


def exchanged(value, begin):
    devices = lax.axis_size("rng")
    pairs = [(i, (i + 1) % devices) for i in range(begin, devices, 2)]
    return lax.ppermute(value, "rng", pairs + [(j, i) for i, j in pairs])


def rims_kernel(side_ref, first_ref, second_ref, own_ref, out_ref):
    own_side = side_ref[:1, :]
    rim = LANES // 4
    me, devices = lax.axis_index("rng"), lax.axis_size("rng")
    even = me % 2 == 0
    first, second = first_ref[...].astype(F32), second_ref[...].astype(F32)
    below = jnp.where(me == 0, 0.0, jnp.where(even, second, first))
    above = jnp.where(me == devices - 1, 0.0, jnp.where(even, first, second))
    group = lax.broadcasted_iota(jnp.int32, (1, LANES), 1) // rim
    packed = [0.0, 0.0]
    for end, value in enumerate((below, above)):
        for part in range(2):
            place = 2 * end + part
            for side in range(2):
                turn = (place - (2 * part + side)) * rim % LANES
                moved = pltpu.roll(value, turn, 1) if turn else value
                packed[side] = packed[side] + jnp.where(group == place, moved, 0.0)
    own_ref[...] = jnp.where(own_side == 0, packed[0], packed[1]).astype(BF16)
    out_ref[...] = jnp.where(own_side == 0, packed[1], packed[0]).astype(BF16)


def sorted_rims(own_side, first, second):
    return pl.pallas_call(
        rims_kernel,
        out_shape=[jax.ShapeDtypeStruct(first.shape, BF16)] * 2,
        in_specs=[VMEM] * 3,
        out_specs=[VMEM] * 2,
        compiler_params=params(4),
        cost_estimate=pl.CostEstimate(flops=1_000_000, bytes_accessed=MIB // 4, transcendentals=0),
    )(own_side, first, second)


def resampled(image, rims_ref, centre_ref, rim_ref, value_ref, child):
    parts, half, bins = image.shape
    value_ref[...] = dot(image.reshape(parts * half, bins), centre_ref[child])
    rims = rims_ref[...]
    return [
        (value_ref[part * half : (part + 1) * half, :] + dot(rims, rim_ref[child, part])).astype(BF16)
        for part in range(parts)
    ]


def early_kernel(
    own_ref, rims_ref, centre_ref, rim_ref, matrix_ref, turn_ref, merged_ref, value_ref
):
    rows = resampled(own_ref[...], rims_ref, centre_ref, rim_ref, value_ref, 0)
    merged_ref[0], merged_ref[1] = rotated(
        (dot(matrix_ref[0], rows[0]), dot(matrix_ref[0], rows[1])), (turn_ref[0, 0], turn_ref[0, 1])
    )


def late_kernel(
    far_outer, far_inner, rims_ref, merged_ref, centre_ref, rim_ref, matrix_ref, turn_ref, out_ref,
    buffer, value_ref, sems,
):
    image = jnp.concatenate([far_outer[...], far_inner[...]], axis=2)
    rows = resampled(image, rims_ref, centre_ref, rim_ref, value_ref, 1)
    parts = len(rows)
    block = LANES
    copies = []
    for first in range(0, matrix_ref.shape[1], 2 * block):
        matrix = matrix_ref[1, first : first + 2 * block]
        terms = dot(matrix, rows[0]), dot(matrix, rows[1])
        for step in range(2):
            here = slice(first + step * block, first + (step + 1) * block)
            there = slice(step * block, (step + 1) * block)
            turned = rotated(
                (terms[0][there], terms[1][there]), (turn_ref[1, 0, here], turn_ref[1, 1, here])
            )
            for part in range(parts):
                buffer[part, here] = (merged_ref[part, here] + turned[part]).astype(buffer.dtype)
            copy = pltpu.make_async_copy(
                buffer.at[:, here], out_ref.at[:, here], sems.at[len(copies)]
            )
            copy.start()
            copies.append(copy)
    for copy in copies:
        copy.wait()


def merged_image(own, rims, far, far_rims, tables, dtype):
    centre, rim, turn, matrices, _ = tables
    angles, bins = turn.shape[-2:]
    cost = pl.CostEstimate(flops=4 * angles * bins * bins, bytes_accessed=8 * MIB, transcendentals=0)
    value = pltpu.VMEM((angles, bins), F32)
    merged = pl.pallas_call(
        early_kernel,
        out_shape=jax.ShapeDtypeStruct((2, angles, bins), F32),
        in_specs=[VMEM] * 6,
        out_specs=VMEM,
        scratch_shapes=[value],
        compiler_params=params(16),
        cost_estimate=cost,
    )(own, rims, centre, rim, matrices, turn)
    return pl.pallas_call(
        late_kernel,
        out_shape=jax.ShapeDtypeStruct((2, angles, bins), dtype),
        in_specs=[VMEM] * 8,
        out_specs=ANY,
        scratch_shapes=[
            pltpu.VMEM((2, angles, bins), dtype),
            value,
            pltpu.SemaphoreType.DMA((angles // LANES,)),
        ],
        compiler_params=params(16),
        cost_estimate=cost,
    )(*far, far_rims, merged, centre, rim, matrices, turn)


def after(value, *earlier):
    return lax.optimization_barrier((value, *earlier))[0]


def from_partner(value, stride):
    pairs = [(source, source ^ stride) for source in range(lax.axis_size("sub"))]
    return lax.ppermute(value, "sub", pairs)


def split_image(level, image, fore_flag, rim):
    angles, bins = image.shape[1:]
    half, step = angles // 2, LANES // 2
    own_flag = fore_flag[level, lax.axis_index("sub"), 0]
    sides = image.reshape(2, 2, half, bins)

    def pieces(side):
        rows = lax.dynamic_index_in_dim(sides, side, 1, keepdims=False)
        ends = [rows[..., :step], rows[..., -step:]]
        rest = [rows[..., -2 * step : -step], rows[..., step : -2 * step]]
        return jnp.concatenate(ends + rest, axis=-1)

    def packed(edge):
        return edge.transpose(2, 0, 1, 3).reshape(half, 4 * rim)

    low, high = packed(sides[..., :rim]), packed(sides[..., -rim:])
    even = lax.axis_index("rng") % 2 == 0
    edges = jnp.where(even, high, low), jnp.where(even, low, high)
    return pieces(own_flag), pieces(1 - own_flag), edges


def on_device(echoes, fore_flag, band_offset, angle_interp, range_kernel, center_shift):
    devices = lax.axis_size("rng")
    half = devices // 2
    local_pulses = echoes.shape[1]
    bins = echoes.shape[2] // devices
    angles = angle_interp.shape[2]
    rim = MAX_SHIFT + (range_kernel.shape[1] - bins) // 2
    levels = range_kernel.shape[0]
    settings = (fore_flag, band_offset, center_shift, range_kernel, angle_interp)

    far_blocks, near_blocks, blocks = placed(
        echoes.reshape(2 * local_pulses, devices * bins), devices
    )
    relay = across(far_blocks, half)
    pulses = lax.all_to_all(blocks, "rng", split_axis=0, concat_axis=0, tiled=True)
    pieces, sources = spread(near_blocks, relay)
    own_matrix, out_matrix, own_side = filter_table(fore_flag, angles, local_pulses, pieces[0])
    own_outer, out_outer, *edges = outer_image(own_side, own_matrix, out_matrix, pieces, sources)

    def halos(side, edges, stride):
        rims, out_rims = sorted_rims(side, exchanged(edges[0], 0), exchanged(edges[1], 1))
        return rims, from_partner(out_rims, stride)

    far_outer = from_partner(out_outer, 1)
    rims, far_rims = halos(own_side, edges, 1)
    pulses = after(pulses, far_outer, far_rims)
    pulses = pulses.reshape(2 * local_pulses * devices, bins - LANES)
    out_inner = inner_image(partner_rows_kernel, angles, out_matrix, pulses)
    far = far_outer, from_partner(out_inner, 1)
    own_kernel = functools.partial(own_rows_kernel, local_pulses)
    own = inner_image(own_kernel, angles, own_matrix, pulses, (own_outer,))
    tables = merge_tables(0, 1, *settings, own)
    for level in range(levels):
        stride = 2**level
        if level > 0:
            tables = merge_tables(level, stride, *settings, image)
            own, out, edges = split_image(level, image, fore_flag, rim)
            far = [from_partner(value, stride) for value in (out[..., :LANES], out[..., LANES:])]
            rims, far_rims = halos(tables[-1], edges, stride)
        image = merged_image(own, rims, far, far_rims, tables, BF16 if level + 1 < levels else F32)
    return image


def solution(mesh):
    placed_as = (
        P(None, ("sub", "rng"), None),
        P(None, None, "rng"),
        P(None, None, "rng"),
        P(),
        P(),
        P(),
    )
    return jax.shard_map(
        on_device, mesh=mesh, in_specs=placed_as, out_specs=P(None, "sub", "rng"), check_vma=False
    )
```

```python
import functools
import math

import jax
import jax.numpy as jnp
from jax import lax
from jax.experimental import pallas as pl
from jax.experimental.pallas import tpu as pltpu
from jax.sharding import PartitionSpec as P

MAX_SHIFT = 16
LANES = 128
MIB = 2**20
JOIN_COST = 10**11
SIDE = jax.ShapeDtypeStruct((8, LANES), jnp.float32)
VMEM = pl.BlockSpec(memory_space=pltpu.VMEM)
SMEM = pl.BlockSpec(memory_space=pltpu.SMEM)
ANY = pl.BlockSpec(memory_space=pl.ANY)
F32 = jnp.float32
BF16 = jnp.bfloat16


def dot(a, b):
    return jnp.dot(a, b, preferred_element_type=F32)


def params(mib):
    return pltpu.CompilerParams(vmem_limit_bytes=mib * MIB)


def series(square, first, count):
    coefs = [
        (-1) ** i * math.pi ** (2 * i + first) / math.factorial(2 * i + first)
        for i in range(count)
    ]
    total = jnp.full_like(square, coefs[-1])
    for coef in coefs[-2::-1]:
        total = total * square + coef
    return total


def cos_sin_pi(v):
    turns = jnp.floor(v + 0.5)
    rest = v - turns
    sign = 1.0 - 2.0 * (turns - 2.0 * jnp.floor(turns * 0.5))
    square = rest * rest
    return series(square, 0, 8) * sign, series(square, 1, 7) * rest * sign


def rotated(pair, step):
    return pair[0] * step[0] - pair[1] * step[1], pair[0] * step[1] + pair[1] * step[0]


def mixed(left, right):
    lane = lax.broadcasted_iota(jnp.int32, left.shape, 1)
    return jnp.where(lane < LANES // 2, left.astype(F32), right.astype(F32)).astype(BF16)


def place_kernel(echoes_ref, far_ref, near_ref, inner_ref):
    devices, _, count = inner_ref.shape
    bins = count + LANES
    half = devices // 2
    base = lax.axis_index("rng") // half * half

    def tile(device, first):
        return echoes_ref[:, pl.ds(pl.multiple_of(device * bins + first, LANES), LANES)]

    for ref, start in ((far_ref, half - base), (near_ref, base)):
        for i in range(half):
            ref[i] = mixed(tile(start + i, 0), tile(start + i, bins - LANES))
    for device in range(devices):
        begin = device * bins
        inner_ref[device, :, :LANES] = mixed(tile(device, bins - LANES), tile(device, 0))
        inner_ref[device, :, LANES:] = echoes_ref[:, begin + LANES : begin + bins - LANES]


def placed(echoes, devices):
    rows, columns = echoes.shape
    outer = jax.ShapeDtypeStruct((devices // 2, rows, LANES), BF16)
    inner = jax.ShapeDtypeStruct((devices, rows, columns // devices - LANES), BF16)
    return pl.pallas_call(
        place_kernel,
        out_shape=[outer, outer, inner],
        in_specs=[VMEM],
        out_specs=[VMEM] * 3,
        compiler_params=params(8),
        cost_estimate=pl.CostEstimate(flops=0, bytes_accessed=2 * MIB, transcendentals=0),
    )(echoes)


def join_kernel(near_ref, relay_ref, *refs):
    me = lax.axis_index("rng") % len(refs)
    rows = near_ref.shape[1]
    for d, out_ref in enumerate(refs):
        out_ref[:rows] = near_ref[me ^ d]
        out_ref[rows:] = relay_ref[me ^ d]


def joined(near, relay):
    half, rows, count = near.shape
    return pl.pallas_call(
        join_kernel,
        out_shape=[jax.ShapeDtypeStruct((2 * rows, count), BF16)] * half,
        in_specs=[VMEM] * 2,
        out_specs=[VMEM] * half,
        compiler_params=params(4),
        cost_estimate=pl.CostEstimate(flops=JOIN_COST, bytes_accessed=MIB, transcendentals=0),
    )(near, relay)


def across(value, mask):
    devices = lax.axis_size("rng")
    return lax.ppermute(value, "rng", [(i, i ^ mask) for i in range(devices)])


def filter_table_kernel(
    local_pulses, flag_ref, after_ref, own_ref, out_ref, side_ref, cos_ref, sin_ref
):
    own_flag = flag_ref[0, lax.axis_index("sub"), 0]
    side_ref[...] = jnp.full(side_ref.shape, own_flag.astype(F32))
    angles, columns = out_ref.shape
    half = angles // 2
    base = cos_ref.shape[0]
    scale = 1.0 / math.sqrt(columns // 2)
    lane = lax.broadcasted_iota(jnp.int32, (8, columns), 1)
    slot = lane // (2 * local_pulses)
    second = lane // local_pulses % 2
    pulse = (slot * local_pulses + lane % local_pulses).astype(F32)
    lag = second.astype(F32) * 0.5
    per_angle = pulse * (1.0 / angles)
    row = lax.broadcasted_iota(jnp.int32, (8, columns), 0)
    step = cos_sin_pi(per_angle * (2 * base))
    for ref, side in ((out_ref, 1 - own_flag), (own_ref, own_flag)):
        first = side * half
        for i in range(base // 8):
            twice = (2 * (row + 8 * i + first) + 1 - angles).astype(F32)
            cosine, sine = cos_sin_pi(twice * per_angle - lag)
            cos_ref[8 * i : 8 * i + 8, :] = cosine * scale
            sin_ref[8 * i : 8 * i + 8, :] = sine * scale
        for j in range(half // base):
            for i in range(base // 16):
                pair = [], []
                for k in (2 * i, 2 * i + 1):
                    here = slice(8 * k, 8 * k + 8)
                    now = cos_ref[here, :], sin_ref[here, :]
                    pair[0].append(now[0])
                    pair[1].append(-now[1])
                    if j + 1 < half // base:
                        cos_ref[here, :], sin_ref[here, :] = rotated(now, step)
                begin = j * base + 16 * i
                ref[begin : begin + 16, :] = jnp.concatenate(pair[0]).astype(BF16)
                if ref is out_ref:
                    begin += half
                    ref[begin : begin + 16, :] = jnp.concatenate(pair[1]).astype(BF16)


def filter_table(fore_flag, angles, local_pulses, earlier):
    side = 2 * local_pulses * lax.axis_size("rng")
    return pl.pallas_call(
        functools.partial(filter_table_kernel, local_pulses),
        out_shape=[
            jax.ShapeDtypeStruct((angles // 2, side), BF16),
            jax.ShapeDtypeStruct((angles, side), BF16),
            SIDE,
        ],
        in_specs=[SMEM, ANY],
        out_specs=[VMEM] * 3,
        scratch_shapes=[pltpu.VMEM((64, side), F32)] * 2,
        compiler_params=params(6),
        cost_estimate=pl.CostEstimate(flops=9_000_000, bytes_accessed=4 * MIB, transcendentals=0),
    )(fore_flag, earlier)


def merge_table_kernel(
    level, stride, flag_ref, offset_ref, shift_ref, range_ref, interp_ref, after_ref, centre_ref,
    rim_ref, turn_ref, matrix_ref, side_ref,
):
    group = lax.axis_index("sub")
    block = lax.axis_index("rng")
    bins = centre_ref.shape[-1]
    angles = turn_ref.shape[-2]
    total_bins = lax.axis_size("rng") * bins
    taps = range_ref.shape[1]
    band = (taps - bins) // 2
    rim = MAX_SHIFT + band
    kernel = range_ref[level]

    def moved(bin_id):
        tap = lax.broadcasted_iota(jnp.int32, (bin_id.shape[0], taps), 1)
        return dot(jnp.where(tap == bin_id, 1.0, 0.0).astype(BF16), kernel).astype(BF16)

    row = lax.broadcasted_iota(jnp.int32, (bins, 1), 0)
    upper = row + (bins - 2 * LANES)
    own_bin = jnp.where(row % LANES < LANES // 2, row, upper + LANES)
    own_bin = jnp.where(row >= LANES, jnp.where(row % LANES < LANES // 2, upper, row - LANES), own_bin)
    own_bin = jnp.where(row >= 2 * LANES, row - LANES, own_bin)
    own_flag = flag_ref[level, group, 0]
    side_ref[...] = jnp.full(side_ref.shape, own_flag.astype(F32))
    matrix_ref[0] = interp_ref[level, own_flag]
    matrix_ref[1] = interp_ref[level, 1 - own_flag]
    rim_row = lax.broadcasted_iota(jnp.int32, (2 * rim, 1), 0)
    rim_bin = jnp.where(rim_row < rim, rim_row - rim, rim_row - rim + bins)
    rim_ref[...] = jnp.zeros(rim_ref.shape, BF16)
    bin_id = block * bins + lax.broadcasted_iota(jnp.int32, (8, bins), 1)
    reach = 1.0 + bin_id.astype(F32) * (1.0 / total_bins)
    line = lax.broadcasted_iota(jnp.int32, (8, bins), 0)
    base = 64
    for child in range(2):
        member = group if child == 0 else group ^ stride
        lead = band - offset_ref[level, member, 0]
        centre_ref[child] = moved(own_bin + lead)
        ends = moved(rim_bin + lead)
        for part in range(2):
            for side in range(2):
                place = (2 * side + part) * rim
                rim_ref[child, part, place : place + rim, :] = ends[side * rim : (side + 1) * rim]

        rate = shift_ref[level, member]

        for first in range(0, base, 8):
            angle = (first + line).astype(F32)
            now = cos_sin_pi(rate * ((angle + 0.5) * (1.0 / angles) - 0.5) * reach)
            turn_ref[child, 0, first : first + 8, :] = now[0]
            turn_ref[child, 1, first : first + 8, :] = now[1]
        step = cos_sin_pi(rate * (base / angles) * reach)
        for first in range(base, angles, 8):
            here, last = slice(first, first + 8), slice(first - base, first - base + 8)
            now = rotated((turn_ref[child, 0, last, :], turn_ref[child, 1, last, :]), step)
            turn_ref[child, 0, here, :], turn_ref[child, 1, here, :] = now


def merge_tables(
    level, stride, fore_flag, band_offset, center_shift, range_kernel, angle_interp, earlier
):
    taps, bins = range_kernel.shape[1:]
    angles = angle_interp.shape[2]
    rim = MAX_SHIFT + (taps - bins) // 2
    return pl.pallas_call(
        functools.partial(merge_table_kernel, level, stride),
        out_shape=[
            jax.ShapeDtypeStruct((2, bins, bins), BF16),
            jax.ShapeDtypeStruct((2, 2, 4 * rim, bins), BF16),
            jax.ShapeDtypeStruct((2, 2, angles, bins), F32),
            jax.ShapeDtypeStruct((2, *angle_interp.shape[2:]), BF16),
            SIDE,
        ],
        in_specs=[SMEM] * 3 + [VMEM] * 2 + [ANY],
        out_specs=[VMEM] * 5,
        compiler_params=params(12),
        cost_estimate=pl.CostEstimate(
            flops=2_300_000_000, bytes_accessed=7 * MIB, transcendentals=0
        ),
    )(fore_flag, band_offset, center_shift, range_kernel, angle_interp, earlier)


def quarter_turned(pulses, local_pulses):
    value = pulses.astype(F32)
    count = value.shape[0]
    second = lax.broadcasted_iota(jnp.int32, (count, 1), 0) // local_pulses % 2 == 1
    ahead, behind = pltpu.roll(value, count - local_pulses, 0), pltpu.roll(value, local_pulses, 0)
    return jnp.where(second, -behind, ahead).astype(BF16)


def own_image(rows, pulses, local_pulses):
    return dot(rows, pulses), dot(rows, quarter_turned(pulses, local_pulses))


def outer_kernel(pieces, side_ref, own_rows, out_rows, *refs):
    own_side = side_ref[:1, :]
    me = lax.axis_index("rng")
    own_ref, out_ref, *edge_refs = refs[pieces:-1]
    pulses_ref = refs[-1]
    rows = refs[0].shape[0] // 2
    for d, ref in enumerate(refs[:pieces]):
        for t in range(2):
            place = pl.multiple_of((me ^ (d + t * pieces)) * rows, rows)
            pulses_ref[pl.ds(place, rows), :] = ref[t * rows : (t + 1) * rows, :]
    pulses = pulses_ref[...]
    own_parts = own_image(own_rows[...], pulses, rows // 2)
    out_parts = dot(out_rows[...], pulses)
    half = own_ref.shape[1]
    rim = LANES // 4
    lane = lax.broadcasted_iota(jnp.int32, (1, LANES), 1)
    edges = [0.0, 0.0]
    for part in range(2):
        own, out = own_parts[part], out_parts[part * half : (part + 1) * half]
        own_ref[part] = own.astype(BF16)
        out_ref[part] = out.astype(BF16)
        for side in range(2):
            value = jnp.where(own_side == side, own, out)
            group = 2 * part + side
            for end in range(2):
                turn = (group + end) * rim % LANES
                moved = pltpu.roll(value, turn, 1) if turn else value
                edges[end] = edges[end] + jnp.where(lane // rim == group, moved, 0.0)
    even = me % 2 == 0
    edge_refs[0][...] = jnp.where(even, edges[1], edges[0]).astype(BF16)
    edge_refs[1][...] = jnp.where(even, edges[0], edges[1]).astype(BF16)


def outer_image(own_side, own_rows, out_rows, pieces):
    angles, side = out_rows.shape
    image = jax.ShapeDtypeStruct((2, angles // 2, LANES), BF16)
    edge = jax.ShapeDtypeStruct((angles // 2, LANES), BF16)
    return pl.pallas_call(
        functools.partial(outer_kernel, len(pieces)),
        out_shape=[image, image, edge, edge],
        in_specs=[VMEM] * (3 + len(pieces)),
        out_specs=[VMEM] * 4,
        scratch_shapes=[pltpu.VMEM((side, LANES), BF16)],
        compiler_params=params(10),
        cost_estimate=pl.CostEstimate(
            flops=4 * angles * side * LANES, bytes_accessed=3 * MIB, transcendentals=0
        ),
    )(own_side, own_rows, out_rows, *pieces)


def partner_rows_kernel(rows_ref, pulses_ref, image_ref):
    image = dot(rows_ref[...], pulses_ref[...])
    image_ref[...] = image.astype(BF16).reshape(image_ref.shape)


def own_rows_kernel(local_pulses, rows_ref, pulses_ref, outer_ref, image_ref):
    parts = own_image(rows_ref[...], pulses_ref[...], local_pulses)
    count = outer_ref.shape[2]
    image_ref[:, :, :count] = outer_ref[...]
    for part, image in enumerate(parts):
        image_ref[part, :, count:] = image.astype(BF16)


def inner_image(kernel, angles, rows, pulses, outer=()):
    count = pulses.shape[1]
    whole = count + (outer[0].shape[2] if outer else 0)
    return pl.pallas_call(
        kernel,
        out_shape=jax.ShapeDtypeStruct((2, angles // 2, whole), BF16),
        in_specs=[VMEM] * (2 + len(outer)),
        out_specs=VMEM,
        compiler_params=params(10),
        cost_estimate=pl.CostEstimate(
            flops=2 * angles * rows.shape[1] * count, bytes_accessed=3 * MIB, transcendentals=0
        ),
    )(rows, pulses, *outer)


def exchanged(value, begin):
    devices = lax.axis_size("rng")
    pairs = [(i, (i + 1) % devices) for i in range(begin, devices, 2)]
    return lax.ppermute(value, "rng", pairs + [(j, i) for i, j in pairs])


def rims_kernel(side_ref, first_ref, second_ref, own_ref, out_ref):
    own_side = side_ref[:1, :]
    rim = LANES // 4
    me, devices = lax.axis_index("rng"), lax.axis_size("rng")
    even = me % 2 == 0
    first, second = first_ref[...].astype(F32), second_ref[...].astype(F32)
    below = jnp.where(me == 0, 0.0, jnp.where(even, second, first))
    above = jnp.where(me == devices - 1, 0.0, jnp.where(even, first, second))
    group = lax.broadcasted_iota(jnp.int32, (1, LANES), 1) // rim
    packed = [0.0, 0.0]
    for end, value in enumerate((below, above)):
        for part in range(2):
            place = 2 * end + part
            for side in range(2):
                turn = (place - (2 * part + side)) * rim % LANES
                moved = pltpu.roll(value, turn, 1) if turn else value
                packed[side] = packed[side] + jnp.where(group == place, moved, 0.0)
    own_ref[...] = jnp.where(own_side == 0, packed[0], packed[1]).astype(BF16)
    out_ref[...] = jnp.where(own_side == 0, packed[1], packed[0]).astype(BF16)


def sorted_rims(own_side, first, second):
    return pl.pallas_call(
        rims_kernel,
        out_shape=[jax.ShapeDtypeStruct(first.shape, BF16)] * 2,
        in_specs=[VMEM] * 3,
        out_specs=[VMEM] * 2,
        compiler_params=params(4),
        cost_estimate=pl.CostEstimate(flops=1_000_000, bytes_accessed=MIB // 4, transcendentals=0),
    )(own_side, first, second)


def resampled(image, rims_ref, centre_ref, rim_ref, value_ref, child):
    parts, half, bins = image.shape
    value_ref[...] = dot(image.reshape(parts * half, bins), centre_ref[child])
    rims = rims_ref[...]
    return [
        (value_ref[part * half : (part + 1) * half, :] + dot(rims, rim_ref[child, part])).astype(BF16)
        for part in range(parts)
    ]


def early_kernel(
    own_ref, rims_ref, centre_ref, rim_ref, matrix_ref, turn_ref, merged_ref, value_ref
):
    rows = resampled(own_ref[...], rims_ref, centre_ref, rim_ref, value_ref, 0)
    merged_ref[0], merged_ref[1] = rotated(
        (dot(matrix_ref[0], rows[0]), dot(matrix_ref[0], rows[1])), (turn_ref[0, 0], turn_ref[0, 1])
    )


def finish(values, lanes, merged_ref, matrix_ref, turn_ref, out_ref, buffer, sems):
    rows = [value.astype(BF16) for value in values]
    terms = dot(matrix_ref[1], rows[0]), dot(matrix_ref[1], rows[1])
    block = 2 * LANES
    copies = []
    for first in range(0, matrix_ref.shape[1], block):
        here = slice(first, first + block)
        at = 0
        for begin, end in lanes:
            there = slice(at, at + end - begin)
            turned = rotated(
                (terms[0][here, there], terms[1][here, there]),
                (turn_ref[1, 0, here, begin:end], turn_ref[1, 1, here, begin:end]),
            )
            for part in range(2):
                total = merged_ref[part, here, begin:end] + turned[part]
                buffer[part, here, there] = total.astype(buffer.dtype)
            copy = pltpu.make_async_copy(
                buffer.at[:, here, there], out_ref.at[:, here, pl.ds(begin, end - begin)],
                sems.at[len(copies)],
            )
            copy.start()
            copies.append(copy)
            at += end - begin
    for copy in copies:
        copy.wait()


def middle_kernel(
    far_inner, merged_ref, centre_ref, matrix_ref, turn_ref, out_ref, value_ref, buffer, sems
):
    parts, half, count = far_inner.shape
    bins = centre_ref.shape[2]
    lanes = slice(LANES, bins - LANES)
    inner = far_inner[...].reshape(parts * half, count)
    value_ref[...] = dot(inner, centre_ref[1, bins - count :, lanes])
    values = [value_ref[part * half : (part + 1) * half, :] for part in range(parts)]
    finish(
        values, [(LANES, bins - LANES)], merged_ref, matrix_ref, turn_ref, out_ref, buffer, sems
    )


def end_kernel(
    far_outer, far_inner, rims_ref, merged_ref, centre_ref, rim_ref, matrix_ref, turn_ref,
    begun_ref, out_ref, value_ref, buffer, sems,
):
    bins = centre_ref.shape[2]
    lanes = [(0, LANES), (bins - LANES, bins)]

    def ends(value):
        return jnp.concatenate([value[:, :LANES], value[:, bins - LANES :]], axis=1)

    image = jnp.concatenate([far_outer[...], far_inner[...]], axis=2)
    parts, half, count = image.shape
    value_ref[...] = dot(image.reshape(parts * half, count), ends(centre_ref[1]))
    values = [
        value_ref[part * half : (part + 1) * half, :] + dot(rims_ref[...], ends(rim_ref[1, part]))
        for part in range(parts)
    ]
    finish(values, lanes, merged_ref, matrix_ref, turn_ref, out_ref, buffer, sems)


def merged_image(own, rims, far, far_rims, tables, dtype):
    centre, rim, turn, matrices, _ = tables
    angles, bins = turn.shape[-2:]
    cost = pl.CostEstimate(flops=4 * angles * bins * bins, bytes_accessed=8 * MIB, transcendentals=0)
    value = pltpu.VMEM((angles, bins), F32)
    merged = pl.pallas_call(
        early_kernel,
        out_shape=jax.ShapeDtypeStruct((2, angles, bins), F32),
        in_specs=[VMEM] * 6,
        out_specs=VMEM,
        scratch_shapes=[value],
        compiler_params=params(16),
        cost_estimate=cost,
    )(own, rims, centre, rim, matrices, turn)
    image = jax.ShapeDtypeStruct((2, angles, bins), dtype)
    scratch = [
        pltpu.VMEM((angles, bins - 2 * LANES), F32),
        pltpu.VMEM((2, angles, bins - 2 * LANES), dtype),
        pltpu.SemaphoreType.DMA((angles // LANES,)),
    ]
    begun = pl.pallas_call(
        middle_kernel,
        out_shape=image,
        in_specs=[VMEM] * 5,
        out_specs=ANY,
        scratch_shapes=scratch,
        compiler_params=params(16),
        cost_estimate=cost,
    )(far[1], merged, centre, matrices, turn)
    scratch[0] = pltpu.VMEM((angles, 2 * LANES), F32)
    scratch[1] = pltpu.VMEM((2, angles, 2 * LANES), dtype)
    return pl.pallas_call(
        end_kernel,
        out_shape=image,
        in_specs=[VMEM] * 8 + [ANY],
        out_specs=ANY,
        scratch_shapes=scratch,
        input_output_aliases={8: 0},
        compiler_params=params(16),
        cost_estimate=cost,
    )(*far, far_rims, merged, centre, rim, matrices, turn, begun)


def after(value, *earlier):
    return lax.optimization_barrier((value, *earlier))[0]


def from_partner(value, stride):
    pairs = [(source, source ^ stride) for source in range(lax.axis_size("sub"))]
    return lax.ppermute(value, "sub", pairs)


def split_image(level, image, fore_flag, rim):
    angles, bins = image.shape[1:]
    half, step = angles // 2, LANES // 2
    own_flag = fore_flag[level, lax.axis_index("sub"), 0]
    sides = image.reshape(2, 2, half, bins)

    def pieces(side):
        rows = lax.dynamic_index_in_dim(sides, side, 1, keepdims=False)
        ends = [rows[..., :step], rows[..., -step:]]
        rest = [rows[..., -2 * step : -step], rows[..., step : -2 * step]]
        return jnp.concatenate(ends + rest, axis=-1)

    def packed(edge):
        return edge.transpose(2, 0, 1, 3).reshape(half, 4 * rim)

    low, high = packed(sides[..., :rim]), packed(sides[..., -rim:])
    even = lax.axis_index("rng") % 2 == 0
    edges = jnp.where(even, high, low), jnp.where(even, low, high)
    return pieces(own_flag), pieces(1 - own_flag), edges


def on_device(echoes, fore_flag, band_offset, angle_interp, range_kernel, center_shift):
    devices = lax.axis_size("rng")
    half = devices // 2
    local_pulses = echoes.shape[1]
    bins = echoes.shape[2] // devices
    angles = angle_interp.shape[2]
    rim = MAX_SHIFT + (range_kernel.shape[1] - bins) // 2
    levels = range_kernel.shape[0]
    settings = (fore_flag, band_offset, center_shift, range_kernel, angle_interp)

    far_blocks, near_blocks, blocks = placed(
        echoes.reshape(2 * local_pulses, devices * bins), devices
    )
    relay = across(far_blocks, half)
    pulses = lax.all_to_all(blocks, "rng", split_axis=0, concat_axis=0, tiled=True)
    sends = joined(near_blocks, relay)
    pieces = [across(value, d) if d else value for d, value in enumerate(sends)]
    own_matrix, out_matrix, own_side = filter_table(fore_flag, angles, local_pulses, sends[0])
    own_outer, out_outer, *edges = outer_image(own_side, own_matrix, out_matrix, pieces)

    def halos(side, edges, stride):
        rims, out_rims = sorted_rims(side, exchanged(edges[0], 0), exchanged(edges[1], 1))
        return rims, from_partner(out_rims, stride)

    pulses = after(pulses, out_outer).reshape(2 * local_pulses * devices, bins - LANES)
    out_inner = inner_image(partner_rows_kernel, angles, out_matrix, pulses)
    far = [from_partner(value, 1) for value in (out_outer, out_inner)]
    rims, far_rims = halos(own_side, [after(edge, out_inner) for edge in edges], 1)
    pulses = after(pulses, far[0])
    own_kernel = functools.partial(own_rows_kernel, local_pulses)
    own = inner_image(own_kernel, angles, own_matrix, pulses, (own_outer,))
    tables = merge_tables(0, 1, *settings, own)
    for level in range(levels):
        stride = 2**level
        if level > 0:
            tables = merge_tables(level, stride, *settings, image)
            own, out, edges = split_image(level, image, fore_flag, rim)
            far = [from_partner(value, stride) for value in (out[..., :LANES], out[..., LANES:])]
            rims, far_rims = halos(tables[-1], edges, stride)
        image = merged_image(own, rims, far, far_rims, tables, BF16 if level + 1 < levels else F32)
    return image


def solution(mesh):
    placed_as = (
        P(None, ("sub", "rng"), None),
        P(None, None, "rng"),
        P(None, None, "rng"),
        P(),
        P(),
        P(),
    )
    return jax.shard_map(
        on_device, mesh=mesh, in_specs=placed_as, out_specs=P(None, "sub", "rng"), check_vma=False
    )
```

```python
import functools
import math

import jax
import jax.numpy as jnp
from jax import lax
from jax.experimental import pallas as pl
from jax.experimental.pallas import tpu as pltpu
from jax.sharding import PartitionSpec as P

MAX_SHIFT = 16
LANES = 128
MIB = 2**20
JOIN_COST = 10**11
SIDE = jax.ShapeDtypeStruct((8, LANES), jnp.float32)
VMEM = pl.BlockSpec(memory_space=pltpu.VMEM)
SMEM = pl.BlockSpec(memory_space=pltpu.SMEM)
ANY = pl.BlockSpec(memory_space=pl.ANY)
F32 = jnp.float32
BF16 = jnp.bfloat16


def dot(a, b):
    return jnp.dot(a, b, preferred_element_type=F32)


def params(mib):
    return pltpu.CompilerParams(vmem_limit_bytes=mib * MIB)


def series(square, first, count):
    coefs = [
        (-1) ** i * math.pi ** (2 * i + first) / math.factorial(2 * i + first)
        for i in range(count)
    ]
    total = jnp.full_like(square, coefs[-1])
    for coef in coefs[-2::-1]:
        total = total * square + coef
    return total


def cos_sin_pi(v):
    turns = jnp.floor(v + 0.5)
    rest = v - turns
    sign = 1.0 - 2.0 * (turns - 2.0 * jnp.floor(turns * 0.5))
    square = rest * rest
    return series(square, 0, 8) * sign, series(square, 1, 7) * rest * sign


def rotated(pair, step):
    return pair[0] * step[0] - pair[1] * step[1], pair[0] * step[1] + pair[1] * step[0]


def mixed(left, right):
    lane = lax.broadcasted_iota(jnp.int32, left.shape, 1)
    return jnp.where(lane < LANES // 2, left.astype(F32), right.astype(F32)).astype(BF16)


def place_kernel(echoes_ref, far_ref, near_ref, inner_ref):
    devices, _, count = inner_ref.shape
    bins = count + LANES
    half = devices // 2
    base = lax.axis_index("rng") // half * half

    def tile(device, first):
        return echoes_ref[:, pl.ds(pl.multiple_of(device * bins + first, LANES), LANES)]

    for ref, start in ((far_ref, half - base), (near_ref, base)):
        for i in range(half):
            ref[i] = mixed(tile(start + i, 0), tile(start + i, bins - LANES))
    for device in range(devices):
        begin = device * bins
        inner_ref[device, :, :LANES] = mixed(tile(device, bins - LANES), tile(device, 0))
        inner_ref[device, :, LANES:] = echoes_ref[:, begin + LANES : begin + bins - LANES]


def placed(echoes, devices):
    rows, columns = echoes.shape
    outer = jax.ShapeDtypeStruct((devices // 2, rows, LANES), BF16)
    inner = jax.ShapeDtypeStruct((devices, rows, columns // devices - LANES), BF16)
    return pl.pallas_call(
        place_kernel,
        out_shape=[outer, outer, inner],
        in_specs=[VMEM],
        out_specs=[VMEM] * 3,
        compiler_params=params(8),
        cost_estimate=pl.CostEstimate(flops=0, bytes_accessed=2 * MIB, transcendentals=0),
    )(echoes)


def join_kernel(near_ref, relay_ref, *refs):
    me = lax.axis_index("rng") % len(refs)
    rows = near_ref.shape[1]
    for d, out_ref in enumerate(refs):
        out_ref[:rows] = near_ref[me ^ d]
        out_ref[rows:] = relay_ref[me ^ d]


def joined(near, relay):
    half, rows, count = near.shape
    return pl.pallas_call(
        join_kernel,
        out_shape=[jax.ShapeDtypeStruct((2 * rows, count), BF16)] * half,
        in_specs=[VMEM] * 2,
        out_specs=[VMEM] * half,
        compiler_params=params(4),
        cost_estimate=pl.CostEstimate(flops=JOIN_COST, bytes_accessed=MIB, transcendentals=0),
    )(near, relay)


def across(value, mask):
    devices = lax.axis_size("rng")
    return lax.ppermute(value, "rng", [(i, i ^ mask) for i in range(devices)])


def filter_table_kernel(local_pulses, flag_ref, after_ref, rows_ref, side_ref, cos_ref, sin_ref):
    own_flag = flag_ref[0, lax.axis_index("sub"), 0]
    side_ref[...] = jnp.full(side_ref.shape, own_flag.astype(F32))
    angles, columns = rows_ref.shape
    half = angles // 2
    first = (1 - own_flag) * half
    base = cos_ref.shape[0]
    scale = 1.0 / math.sqrt(columns // 2)
    lane = lax.broadcasted_iota(jnp.int32, (8, columns), 1)
    slot = lane // (2 * local_pulses)
    second = lane // local_pulses % 2
    pulse = (slot * local_pulses + lane % local_pulses).astype(F32)
    lag = second.astype(F32) * 0.5
    per_angle = pulse * (1.0 / angles)
    row = lax.broadcasted_iota(jnp.int32, (8, columns), 0)
    for i in range(base // 8):
        twice = (2 * (row + 8 * i + first) + 1 - angles).astype(F32)
        cosine, sine = cos_sin_pi(twice * per_angle - lag)
        cos_ref[8 * i : 8 * i + 8, :] = cosine * scale
        sin_ref[8 * i : 8 * i + 8, :] = sine * scale
    step = cos_sin_pi(per_angle * (2 * base))
    for j in range(half // base):
        for i in range(base // 16):
            pair = [], []
            for k in (2 * i, 2 * i + 1):
                here = slice(8 * k, 8 * k + 8)
                now = cos_ref[here, :], sin_ref[here, :]
                pair[0].append(now[0])
                pair[1].append(-now[1])
                if j + 1 < half // base:
                    cos_ref[here, :], sin_ref[here, :] = rotated(now, step)
            begin = j * base + 16 * i
            rows_ref[begin : begin + 16, :] = jnp.concatenate(pair[0]).astype(BF16)
            begin += half
            rows_ref[begin : begin + 16, :] = jnp.concatenate(pair[1]).astype(BF16)


def filter_table(fore_flag, angles, local_pulses, earlier):
    side = 2 * local_pulses * lax.axis_size("rng")
    return pl.pallas_call(
        functools.partial(filter_table_kernel, local_pulses),
        out_shape=[jax.ShapeDtypeStruct((angles, side), BF16), SIDE],
        in_specs=[SMEM, ANY],
        out_specs=[VMEM] * 2,
        scratch_shapes=[pltpu.VMEM((64, side), F32)] * 2,
        compiler_params=params(6),
        cost_estimate=pl.CostEstimate(flops=9_000_000, bytes_accessed=4 * MIB, transcendentals=0),
    )(fore_flag, earlier)


def merge_table_kernel(
    level, stride, flag_ref, offset_ref, shift_ref, range_ref, interp_ref, after_ref, centre_ref,
    rim_ref, turn_ref, matrix_ref, side_ref, kernel_ref, sems,
):
    group = lax.axis_index("sub")
    block = lax.axis_index("rng")
    bins = centre_ref.shape[-1]
    angles = turn_ref.shape[-2]
    total_bins = lax.axis_size("rng") * bins
    taps = range_ref.shape[1]
    band = (taps - bins) // 2
    rim = MAX_SHIFT + band
    own_flag = flag_ref[level, group, 0]
    side_ref[...] = jnp.full(side_ref.shape, own_flag.astype(F32))
    copies = [
        pltpu.make_async_copy(source, target, sems.at[i])
        for i, (source, target) in enumerate(
            (
                (range_ref.at[level], kernel_ref),
                (interp_ref.at[level, own_flag], matrix_ref.at[0]),
                (interp_ref.at[level, 1 - own_flag], matrix_ref.at[1]),
            )
        )
    ]
    for copy in copies:
        copy.start()

    def moved(bin_id):
        tap = lax.broadcasted_iota(jnp.int32, (bin_id.shape[0], taps), 1)
        hot = jnp.where(tap == bin_id, 1.0, 0.0).astype(BF16)
        return dot(hot, kernel_ref[...]).astype(BF16)

    row = lax.broadcasted_iota(jnp.int32, (bins, 1), 0)
    upper = row + (bins - 2 * LANES)
    own_bin = jnp.where(row % LANES < LANES // 2, row, upper + LANES)
    own_bin = jnp.where(row >= LANES, jnp.where(row % LANES < LANES // 2, upper, row - LANES), own_bin)
    own_bin = jnp.where(row >= 2 * LANES, row - LANES, own_bin)
    rim_row = lax.broadcasted_iota(jnp.int32, (2 * rim, 1), 0)
    rim_bin = jnp.where(rim_row < rim, rim_row - rim, rim_row - rim + bins)
    rim_ref[...] = jnp.zeros(rim_ref.shape, BF16)
    bin_id = block * bins + lax.broadcasted_iota(jnp.int32, (8, bins), 1)
    reach = 1.0 + bin_id.astype(F32) * (1.0 / total_bins)
    line = lax.broadcasted_iota(jnp.int32, (8, bins), 0)
    base = 64
    members = group, group ^ stride
    for child, member in enumerate(members):
        rate = shift_ref[level, member]
        for first in range(0, base, 8):
            angle = (first + line).astype(F32)
            now = cos_sin_pi(rate * ((angle + 0.5) * (1.0 / angles) - 0.5) * reach)
            turn_ref[child, 0, first : first + 8, :] = now[0]
            turn_ref[child, 1, first : first + 8, :] = now[1]
        step = cos_sin_pi(rate * (base / angles) * reach)
        for first in range(base, angles, 8):
            here, last = slice(first, first + 8), slice(first - base, first - base + 8)
            now = rotated((turn_ref[child, 0, last, :], turn_ref[child, 1, last, :]), step)
            turn_ref[child, 0, here, :], turn_ref[child, 1, here, :] = now
    for copy in copies:
        copy.wait()
    for child, member in enumerate(members):
        lead = band - offset_ref[level, member, 0]
        centre_ref[child] = moved(own_bin + lead)
        ends = moved(rim_bin + lead)
        for part in range(2):
            for side in range(2):
                place = (2 * side + part) * rim
                rim_ref[child, part, place : place + rim, :] = ends[side * rim : (side + 1) * rim]


def merge_tables(
    level, stride, fore_flag, band_offset, center_shift, range_kernel, angle_interp, earlier
):
    taps, bins = range_kernel.shape[1:]
    angles = angle_interp.shape[2]
    rim = MAX_SHIFT + (taps - bins) // 2
    return pl.pallas_call(
        functools.partial(merge_table_kernel, level, stride),
        out_shape=[
            jax.ShapeDtypeStruct((2, bins, bins), BF16),
            jax.ShapeDtypeStruct((2, 2, 4 * rim, bins), BF16),
            jax.ShapeDtypeStruct((2, 2, angles, bins), F32),
            jax.ShapeDtypeStruct((2, *angle_interp.shape[2:]), BF16),
            SIDE,
        ],
        in_specs=[SMEM] * 3 + [ANY] * 3,
        out_specs=[VMEM] * 5,
        scratch_shapes=[pltpu.VMEM((taps, bins), BF16), pltpu.SemaphoreType.DMA((3,))],
        compiler_params=params(12),
        cost_estimate=pl.CostEstimate(
            flops=2_300_000_000, bytes_accessed=7 * MIB, transcendentals=0
        ),
    )(fore_flag, band_offset, center_shift, range_kernel, angle_interp, earlier)


def alternating(pulses, local_pulses):
    row = lax.broadcasted_iota(jnp.int32, (pulses.shape[0], 1), 0)
    pulse = row // (2 * local_pulses) * local_pulses + row % local_pulses
    return jnp.where(pulse % 2 == 1, -pulses.astype(F32), pulses.astype(F32)).astype(BF16)


def outer_kernel(pieces, side_ref, rows_ref, *refs):
    own_side = side_ref[:1, :]
    me = lax.axis_index("rng")
    own_ref, out_ref, *edge_refs = refs[pieces:-1]
    pulses_ref = refs[-1]
    rows = refs[0].shape[0] // 2
    for d, ref in enumerate(refs[:pieces]):
        for t in range(2):
            place = pl.multiple_of((me ^ (d + t * pieces)) * rows, rows)
            pulses_ref[pl.ds(place, rows), :] = ref[t * rows : (t + 1) * rows, :]
    pulses = pulses_ref[...]
    own_parts = dot(rows_ref[...], alternating(pulses, rows // 2))
    out_parts = dot(rows_ref[...], pulses)
    half = own_ref.shape[1]
    rim = LANES // 4
    lane = lax.broadcasted_iota(jnp.int32, (1, LANES), 1)
    edges = [0.0, 0.0]
    for part in range(2):
        own, out = (value[part * half : (part + 1) * half] for value in (own_parts, out_parts))
        own_ref[part] = own.astype(BF16)
        out_ref[part] = out.astype(BF16)
        for side in range(2):
            value = jnp.where(own_side == side, own, out)
            group = 2 * part + side
            for end in range(2):
                turn = (group + end) * rim % LANES
                moved = pltpu.roll(value, turn, 1) if turn else value
                edges[end] = edges[end] + jnp.where(lane // rim == group, moved, 0.0)
    even = me % 2 == 0
    edge_refs[0][...] = jnp.where(even, edges[1], edges[0]).astype(BF16)
    edge_refs[1][...] = jnp.where(even, edges[0], edges[1]).astype(BF16)


def outer_image(own_side, rows, pieces):
    angles, side = rows.shape
    image = jax.ShapeDtypeStruct((2, angles // 2, LANES), BF16)
    edge = jax.ShapeDtypeStruct((angles // 2, LANES), BF16)
    return pl.pallas_call(
        functools.partial(outer_kernel, len(pieces)),
        out_shape=[image, image, edge, edge],
        in_specs=[VMEM] * (2 + len(pieces)),
        out_specs=[VMEM] * 4,
        scratch_shapes=[pltpu.VMEM((side, LANES), BF16)],
        compiler_params=params(10),
        cost_estimate=pl.CostEstimate(
            flops=4 * angles * side * LANES, bytes_accessed=3 * MIB, transcendentals=0
        ),
    )(own_side, rows, *pieces)


def partner_rows_kernel(rows_ref, pulses_ref, image_ref):
    image = dot(rows_ref[...], pulses_ref[...])
    image_ref[...] = image.astype(BF16).reshape(image_ref.shape)


def own_rows_kernel(local_pulses, rows_ref, pulses_ref, outer_ref, image_ref):
    image = dot(rows_ref[...], alternating(pulses_ref[...], local_pulses))
    parts, half, count = outer_ref.shape
    image_ref[:, :, :count] = outer_ref[...]
    image_ref[:, :, count:] = image.astype(BF16).reshape(parts, half, image.shape[1])


def inner_image(kernel, angles, rows, pulses, outer=()):
    count = pulses.shape[1]
    whole = count + (outer[0].shape[2] if outer else 0)
    return pl.pallas_call(
        kernel,
        out_shape=jax.ShapeDtypeStruct((2, angles // 2, whole), BF16),
        in_specs=[VMEM] * (2 + len(outer)),
        out_specs=VMEM,
        compiler_params=params(10),
        cost_estimate=pl.CostEstimate(
            flops=2 * angles * rows.shape[1] * count, bytes_accessed=3 * MIB, transcendentals=0
        ),
    )(rows, pulses, *outer)


def exchanged(value, begin):
    devices = lax.axis_size("rng")
    pairs = [(i, (i + 1) % devices) for i in range(begin, devices, 2)]
    return lax.ppermute(value, "rng", pairs + [(j, i) for i, j in pairs])


def rims_kernel(side_ref, first_ref, second_ref, own_ref, out_ref):
    own_side = side_ref[:1, :]
    rim = LANES // 4
    me, devices = lax.axis_index("rng"), lax.axis_size("rng")
    even = me % 2 == 0
    first, second = first_ref[...].astype(F32), second_ref[...].astype(F32)
    below = jnp.where(me == 0, 0.0, jnp.where(even, second, first))
    above = jnp.where(me == devices - 1, 0.0, jnp.where(even, first, second))
    group = lax.broadcasted_iota(jnp.int32, (1, LANES), 1) // rim
    packed = [0.0, 0.0]
    for end, value in enumerate((below, above)):
        for part in range(2):
            place = 2 * end + part
            for side in range(2):
                turn = (place - (2 * part + side)) * rim % LANES
                moved = pltpu.roll(value, turn, 1) if turn else value
                packed[side] = packed[side] + jnp.where(group == place, moved, 0.0)
    own_ref[...] = jnp.where(own_side == 0, packed[0], packed[1]).astype(BF16)
    out_ref[...] = jnp.where(own_side == 0, packed[1], packed[0]).astype(BF16)


def sorted_rims(own_side, first, second):
    return pl.pallas_call(
        rims_kernel,
        out_shape=[jax.ShapeDtypeStruct(first.shape, BF16)] * 2,
        in_specs=[VMEM] * 3,
        out_specs=[VMEM] * 2,
        compiler_params=params(4),
        cost_estimate=pl.CostEstimate(flops=1_000_000, bytes_accessed=MIB // 4, transcendentals=0),
    )(own_side, first, second)


def resampled(image, rims_ref, centre_ref, rim_ref, value_ref, child):
    parts, half, bins = image.shape
    value_ref[...] = dot(image.reshape(parts * half, bins), centre_ref[child])
    rims = rims_ref[...]
    return [
        (value_ref[part * half : (part + 1) * half, :] + dot(rims, rim_ref[child, part])).astype(BF16)
        for part in range(parts)
    ]


def early_kernel(
    own_ref, rims_ref, centre_ref, rim_ref, matrix_ref, turn_ref, merged_ref, value_ref
):
    rows = resampled(own_ref[...], rims_ref, centre_ref, rim_ref, value_ref, 0)
    merged_ref[0], merged_ref[1] = rotated(
        (dot(matrix_ref[0], rows[0]), dot(matrix_ref[0], rows[1])), (turn_ref[0, 0], turn_ref[0, 1])
    )


def late_kernel(
    far_outer, far_inner, rims_ref, merged_ref, centre_ref, rim_ref, matrix_ref, turn_ref, out_ref,
    buffer, value_ref, sems,
):
    image = jnp.concatenate([far_outer[...], far_inner[...]], axis=2)
    rows = resampled(image, rims_ref, centre_ref, rim_ref, value_ref, 1)
    parts = len(rows)
    block = LANES
    copies = []
    for first in range(0, matrix_ref.shape[1], 2 * block):
        matrix = matrix_ref[1, first : first + 2 * block]
        terms = dot(matrix, rows[0]), dot(matrix, rows[1])
        for step in range(2):
            here = slice(first + step * block, first + (step + 1) * block)
            there = slice(step * block, (step + 1) * block)
            turned = rotated(
                (terms[0][there], terms[1][there]), (turn_ref[1, 0, here], turn_ref[1, 1, here])
            )
            for part in range(parts):
                buffer[part, here] = (merged_ref[part, here] + turned[part]).astype(buffer.dtype)
            copy = pltpu.make_async_copy(
                buffer.at[:, here], out_ref.at[:, here], sems.at[len(copies)]
            )
            copy.start()
            copies.append(copy)
    for copy in copies:
        copy.wait()


def merged_image(own, rims, far, far_rims, tables, dtype):
    centre, rim, turn, matrices, _ = tables
    angles, bins = turn.shape[-2:]
    cost = pl.CostEstimate(flops=4 * angles * bins * bins, bytes_accessed=8 * MIB, transcendentals=0)
    value = pltpu.VMEM((angles, bins), F32)
    merged = pl.pallas_call(
        early_kernel,
        out_shape=jax.ShapeDtypeStruct((2, angles, bins), F32),
        in_specs=[VMEM] * 6,
        out_specs=VMEM,
        scratch_shapes=[value],
        compiler_params=params(16),
        cost_estimate=cost,
    )(own, rims, centre, rim, matrices, turn)
    return pl.pallas_call(
        late_kernel,
        out_shape=jax.ShapeDtypeStruct((2, angles, bins), dtype),
        in_specs=[VMEM] * 8,
        out_specs=ANY,
        scratch_shapes=[
            pltpu.VMEM((2, angles, bins), dtype),
            value,
            pltpu.SemaphoreType.DMA((angles // LANES,)),
        ],
        compiler_params=params(16),
        cost_estimate=cost,
    )(*far, far_rims, merged, centre, rim, matrices, turn)


def after(value, *earlier):
    return lax.optimization_barrier((value, *earlier))[0]


def from_partner(value, stride):
    pairs = [(source, source ^ stride) for source in range(lax.axis_size("sub"))]
    return lax.ppermute(value, "sub", pairs)


def split_image(level, image, fore_flag, rim):
    angles, bins = image.shape[1:]
    half, step = angles // 2, LANES // 2
    own_flag = fore_flag[level, lax.axis_index("sub"), 0]
    sides = image.reshape(2, 2, half, bins)

    def pieces(side):
        rows = lax.dynamic_index_in_dim(sides, side, 1, keepdims=False)
        ends = [rows[..., :step], rows[..., -step:]]
        rest = [rows[..., -2 * step : -step], rows[..., step : -2 * step]]
        return jnp.concatenate(ends + rest, axis=-1)

    def packed(edge):
        return edge.transpose(2, 0, 1, 3).reshape(half, 4 * rim)

    low, high = packed(sides[..., :rim]), packed(sides[..., -rim:])
    even = lax.axis_index("rng") % 2 == 0
    edges = jnp.where(even, high, low), jnp.where(even, low, high)
    return pieces(own_flag), pieces(1 - own_flag), edges


def on_device(echoes, fore_flag, band_offset, angle_interp, range_kernel, center_shift):
    devices = lax.axis_size("rng")
    half = devices // 2
    local_pulses = echoes.shape[1]
    bins = echoes.shape[2] // devices
    angles = angle_interp.shape[2]
    rim = MAX_SHIFT + (range_kernel.shape[1] - bins) // 2
    levels = range_kernel.shape[0]
    settings = (fore_flag, band_offset, center_shift, range_kernel, angle_interp)

    far_blocks, near_blocks, blocks = placed(
        echoes.reshape(2 * local_pulses, devices * bins), devices
    )
    relay = across(far_blocks, half)
    pulses = lax.all_to_all(blocks, "rng", split_axis=0, concat_axis=0, tiled=True)
    sends = joined(near_blocks, relay)
    pieces = [across(value, d) if d else value for d, value in enumerate(sends)]
    matrix, own_side = filter_table(fore_flag, angles, local_pulses, sends[0])
    own_outer, out_outer, *edges = outer_image(own_side, matrix, pieces)

    def halos(side, edges, stride):
        rims, out_rims = sorted_rims(side, exchanged(edges[0], 0), exchanged(edges[1], 1))
        return rims, from_partner(out_rims, stride)

    pulses = after(pulses, out_outer).reshape(2 * local_pulses * devices, bins - LANES)
    out_inner = inner_image(partner_rows_kernel, angles, matrix, pulses)
    far = [from_partner(value, 1) for value in (out_outer, out_inner)]
    rims, far_rims = halos(own_side, [after(edge, out_inner) for edge in edges], 1)
    pulses = after(pulses, far[0])
    own_kernel = functools.partial(own_rows_kernel, local_pulses)
    own = inner_image(own_kernel, angles, matrix, pulses, (own_outer,))
    tables = merge_tables(0, 1, *settings, own)
    for level in range(levels):
        stride = 2**level
        if level > 0:
            tables = merge_tables(level, stride, *settings, image)
            own, out, edges = split_image(level, image, fore_flag, rim)
            far = [from_partner(value, stride) for value in (out[..., :LANES], out[..., LANES:])]
            rims, far_rims = halos(tables[-1], edges, stride)
        image = merged_image(own, rims, far, far_rims, tables, BF16 if level + 1 < levels else F32)
    return image


def solution(mesh):
    placed_as = (
        P(None, ("sub", "rng"), None),
        P(None, None, "rng"),
        P(None, None, "rng"),
        P(),
        P(),
        P(),
    )
    return jax.shard_map(
        on_device, mesh=mesh, in_specs=placed_as, out_specs=P(None, "sub", "rng"), check_vma=False
    )
```

```python
import functools
import math

import jax
import jax.numpy as jnp
from jax import lax
from jax.experimental import pallas as pl
from jax.experimental.pallas import tpu as pltpu
from jax.sharding import PartitionSpec as P

MAX_SHIFT = 16
LANES = 128
MIB = 2**20
JOIN_COST = 10**11
SIDE = jax.ShapeDtypeStruct((8, LANES), jnp.float32)
VMEM = pl.BlockSpec(memory_space=pltpu.VMEM)
SMEM = pl.BlockSpec(memory_space=pltpu.SMEM)
ANY = pl.BlockSpec(memory_space=pl.ANY)
F32 = jnp.float32
BF16 = jnp.bfloat16


def dot(a, b):
    return jnp.dot(a, b, preferred_element_type=F32)


def params(mib):
    return pltpu.CompilerParams(vmem_limit_bytes=mib * MIB)


def series(square, first, count):
    coefs = [
        (-1) ** i * math.pi ** (2 * i + first) / math.factorial(2 * i + first)
        for i in range(count)
    ]
    total = jnp.full_like(square, coefs[-1])
    for coef in coefs[-2::-1]:
        total = total * square + coef
    return total


def cos_sin_pi(v):
    turns = jnp.floor(v + 0.5)
    rest = v - turns
    sign = 1.0 - 2.0 * (turns - 2.0 * jnp.floor(turns * 0.5))
    square = rest * rest
    return series(square, 0, 8) * sign, series(square, 1, 7) * rest * sign


def rotated(pair, step):
    return pair[0] * step[0] - pair[1] * step[1], pair[0] * step[1] + pair[1] * step[0]


def mixed(left, right):
    lane = lax.broadcasted_iota(jnp.int32, left.shape, 1)
    return jnp.where(lane < LANES // 2, left.astype(F32), right.astype(F32)).astype(BF16)


def place_kernel(
    echoes_ref, far_ref, near_ref, inner_ref, held, outer, inner, held_sems, outer_sems, inner_sems
):
    devices, _, count = inner.shape
    bins = count + LANES
    half = devices // 2
    base = lax.axis_index("rng") // half * half
    reads, writes = [], []
    for i in range(devices):
        device = (i + half - base) if i < half else (i - half + base)
        start = pl.multiple_of(device * bins, bins)
        reads.append(
            pltpu.make_async_copy(echoes_ref.at[:, pl.ds(start, bins)], held.at[i], held_sems.at[i])
        )
        reads[-1].start()
    for i in range(devices):
        reads[i].wait()
        first, last = held[i, :, :LANES], held[i, :, bins - LANES :]
        outer[i] = mixed(first, last)
        inner[i, :, :LANES] = mixed(last, first)
        inner[i, :, LANES:] = held[i, :, LANES : bins - LANES]
        device = (i + half - base) if i < half else (i - half + base)
        writes.append(pltpu.make_async_copy(inner.at[i], inner_ref.at[device], inner_sems.at[i]))
        writes[-1].start()
        if i % half == half - 1:
            side = i // half
            target = (far_ref, near_ref)[side]
            source = outer.at[pl.ds(side * half, half)]
            writes.append(pltpu.make_async_copy(source, target, outer_sems.at[side]))
            writes[-1].start()
    for copy in writes:
        copy.wait()


def placed(echoes, devices):
    rows, columns = echoes.shape
    bins = columns // devices
    shapes = [(devices // 2, rows, LANES)] * 2 + [(devices, rows, bins - LANES)]
    return pl.pallas_call(
        place_kernel,
        out_shape=[jax.ShapeDtypeStruct(shape, BF16) for shape in shapes],
        in_specs=[ANY],
        out_specs=[ANY] * 3,
        scratch_shapes=[
            pltpu.VMEM((devices, rows, bins), BF16),
            pltpu.VMEM((devices, rows, LANES), BF16),
            pltpu.VMEM((devices, rows, bins - LANES), BF16),
            pltpu.SemaphoreType.DMA((devices,)),
            pltpu.SemaphoreType.DMA((2,)),
            pltpu.SemaphoreType.DMA((devices,)),
        ],
        compiler_params=params(56),
        cost_estimate=pl.CostEstimate(flops=0, bytes_accessed=2 * MIB, transcendentals=0),
    )(echoes)


def join_kernel(near_ref, relay_ref, *refs):
    me = lax.axis_index("rng") % len(refs)
    rows = near_ref.shape[1]
    for d, out_ref in enumerate(refs):
        out_ref[:rows] = near_ref[me ^ d]
        out_ref[rows:] = relay_ref[me ^ d]


def joined(near, relay):
    half, rows, count = near.shape
    return pl.pallas_call(
        join_kernel,
        out_shape=[jax.ShapeDtypeStruct((2 * rows, count), BF16)] * half,
        in_specs=[VMEM] * 2,
        out_specs=[VMEM] * half,
        compiler_params=params(4),
        cost_estimate=pl.CostEstimate(flops=JOIN_COST, bytes_accessed=MIB, transcendentals=0),
    )(near, relay)


def across(value, mask):
    devices = lax.axis_size("rng")
    return lax.ppermute(value, "rng", [(i, i ^ mask) for i in range(devices)])


def filter_table_kernel(local_pulses, flag_ref, after_ref, rows_ref, side_ref, cos_ref, sin_ref):
    own_flag = flag_ref[0, lax.axis_index("sub"), 0]
    side_ref[...] = jnp.full(side_ref.shape, own_flag.astype(F32))
    angles, columns = rows_ref.shape
    half = angles // 2
    first = (1 - own_flag) * half
    base = cos_ref.shape[0]
    scale = 1.0 / math.sqrt(columns // 2)
    lane = lax.broadcasted_iota(jnp.int32, (8, columns), 1)
    slot = lane // (2 * local_pulses)
    second = lane // local_pulses % 2
    pulse = (slot * local_pulses + lane % local_pulses).astype(F32)
    lag = second.astype(F32) * 0.5
    per_angle = pulse * (1.0 / angles)
    row = lax.broadcasted_iota(jnp.int32, (8, columns), 0)
    for i in range(base // 8):
        twice = (2 * (row + 8 * i + first) + 1 - angles).astype(F32)
        cosine, sine = cos_sin_pi(twice * per_angle - lag)
        cos_ref[8 * i : 8 * i + 8, :] = cosine * scale
        sin_ref[8 * i : 8 * i + 8, :] = sine * scale
    step = cos_sin_pi(per_angle * (2 * base))
    for j in range(half // base):
        for i in range(base // 16):
            pair = [], []
            for k in (2 * i, 2 * i + 1):
                here = slice(8 * k, 8 * k + 8)
                now = cos_ref[here, :], sin_ref[here, :]
                pair[0].append(now[0])
                pair[1].append(-now[1])
                if j + 1 < half // base:
                    cos_ref[here, :], sin_ref[here, :] = rotated(now, step)
            begin = j * base + 16 * i
            rows_ref[begin : begin + 16, :] = jnp.concatenate(pair[0]).astype(BF16)
            begin += half
            rows_ref[begin : begin + 16, :] = jnp.concatenate(pair[1]).astype(BF16)


def filter_table(fore_flag, angles, local_pulses, earlier):
    side = 2 * local_pulses * lax.axis_size("rng")
    return pl.pallas_call(
        functools.partial(filter_table_kernel, local_pulses),
        out_shape=[jax.ShapeDtypeStruct((angles, side), BF16), SIDE],
        in_specs=[SMEM, ANY],
        out_specs=[VMEM] * 2,
        scratch_shapes=[pltpu.VMEM((64, side), F32)] * 2,
        compiler_params=params(6),
        cost_estimate=pl.CostEstimate(flops=9_000_000, bytes_accessed=4 * MIB, transcendentals=0),
    )(fore_flag, earlier)


def merge_table_kernel(
    level, stride, flag_ref, offset_ref, shift_ref, range_ref, interp_ref, after_ref, centre_ref,
    rim_ref, turn_ref, matrix_ref, side_ref, kernel_ref, sems,
):
    group = lax.axis_index("sub")
    block = lax.axis_index("rng")
    bins = centre_ref.shape[-1]
    angles = turn_ref.shape[-2]
    total_bins = lax.axis_size("rng") * bins
    taps = range_ref.shape[1]
    band = (taps - bins) // 2
    rim = MAX_SHIFT + band
    own_flag = flag_ref[level, group, 0]
    side_ref[...] = jnp.full(side_ref.shape, own_flag.astype(F32))
    copies = [
        pltpu.make_async_copy(source, target, sems.at[i])
        for i, (source, target) in enumerate(
            (
                (range_ref.at[level], kernel_ref),
                (interp_ref.at[level, own_flag], matrix_ref.at[0]),
                (interp_ref.at[level, 1 - own_flag], matrix_ref.at[1]),
            )
        )
    ]
    for copy in copies:
        copy.start()

    def moved(bin_id):
        tap = lax.broadcasted_iota(jnp.int32, (bin_id.shape[0], taps), 1)
        hot = jnp.where(tap == bin_id, 1.0, 0.0).astype(BF16)
        return dot(hot, kernel_ref[...]).astype(BF16)

    row = lax.broadcasted_iota(jnp.int32, (bins, 1), 0)
    upper = row + (bins - 2 * LANES)
    own_bin = jnp.where(row % LANES < LANES // 2, row, upper + LANES)
    own_bin = jnp.where(row >= LANES, jnp.where(row % LANES < LANES // 2, upper, row - LANES), own_bin)
    own_bin = jnp.where(row >= 2 * LANES, row - LANES, own_bin)
    rim_row = lax.broadcasted_iota(jnp.int32, (2 * rim, 1), 0)
    rim_bin = jnp.where(rim_row < rim, rim_row - rim, rim_row - rim + bins)
    rim_ref[...] = jnp.zeros(rim_ref.shape, BF16)
    bin_id = block * bins + lax.broadcasted_iota(jnp.int32, (8, bins), 1)
    reach = 1.0 + bin_id.astype(F32) * (1.0 / total_bins)
    line = lax.broadcasted_iota(jnp.int32, (8, bins), 0)
    base = 64
    members = group, group ^ stride
    for child, member in enumerate(members):
        rate = shift_ref[level, member]
        for first in range(0, base, 8):
            angle = (first + line).astype(F32)
            now = cos_sin_pi(rate * ((angle + 0.5) * (1.0 / angles) - 0.5) * reach)
            turn_ref[child, 0, first : first + 8, :] = now[0]
            turn_ref[child, 1, first : first + 8, :] = now[1]
        step = cos_sin_pi(rate * (base / angles) * reach)
        for first in range(base, angles, 8):
            here, last = slice(first, first + 8), slice(first - base, first - base + 8)
            now = rotated((turn_ref[child, 0, last, :], turn_ref[child, 1, last, :]), step)
            turn_ref[child, 0, here, :], turn_ref[child, 1, here, :] = now
    for copy in copies:
        copy.wait()
    for child, member in enumerate(members):
        lead = band - offset_ref[level, member, 0]
        centre_ref[child] = moved(own_bin + lead)
        ends = moved(rim_bin + lead)
        for part in range(2):
            for side in range(2):
                place = (2 * side + part) * rim
                rim_ref[child, part, place : place + rim, :] = ends[side * rim : (side + 1) * rim]


def merge_tables(
    level, stride, fore_flag, band_offset, center_shift, range_kernel, angle_interp, earlier
):
    taps, bins = range_kernel.shape[1:]
    angles = angle_interp.shape[2]
    rim = MAX_SHIFT + (taps - bins) // 2
    return pl.pallas_call(
        functools.partial(merge_table_kernel, level, stride),
        out_shape=[
            jax.ShapeDtypeStruct((2, bins, bins), BF16),
            jax.ShapeDtypeStruct((2, 2, 4 * rim, bins), BF16),
            jax.ShapeDtypeStruct((2, 2, angles, bins), F32),
            jax.ShapeDtypeStruct((2, *angle_interp.shape[2:]), BF16),
            SIDE,
        ],
        in_specs=[SMEM] * 3 + [ANY] * 3,
        out_specs=[VMEM] * 5,
        scratch_shapes=[pltpu.VMEM((taps, bins), BF16), pltpu.SemaphoreType.DMA((3,))],
        compiler_params=params(12),
        cost_estimate=pl.CostEstimate(
            flops=2_300_000_000, bytes_accessed=7 * MIB, transcendentals=0
        ),
    )(fore_flag, band_offset, center_shift, range_kernel, angle_interp, earlier)


def alternating(pulses, local_pulses):
    row = lax.broadcasted_iota(jnp.int32, (pulses.shape[0], 1), 0)
    pulse = row // (2 * local_pulses) * local_pulses + row % local_pulses
    return jnp.where(pulse % 2 == 1, -pulses.astype(F32), pulses.astype(F32)).astype(BF16)


def outer_kernel(pieces, side_ref, rows_ref, *refs):
    own_side = side_ref[:1, :]
    me = lax.axis_index("rng")
    own_ref, out_ref, *edge_refs = refs[pieces:-1]
    pulses_ref = refs[-1]
    rows = refs[0].shape[0] // 2
    for d, ref in enumerate(refs[:pieces]):
        for t in range(2):
            place = pl.multiple_of((me ^ (d + t * pieces)) * rows, rows)
            pulses_ref[pl.ds(place, rows), :] = ref[t * rows : (t + 1) * rows, :]
    pulses = pulses_ref[...]
    own_parts = dot(rows_ref[...], alternating(pulses, rows // 2))
    out_parts = dot(rows_ref[...], pulses)
    half = own_ref.shape[1]
    rim = LANES // 4
    lane = lax.broadcasted_iota(jnp.int32, (1, LANES), 1)
    edges = [0.0, 0.0]
    for part in range(2):
        own, out = (value[part * half : (part + 1) * half] for value in (own_parts, out_parts))
        own_ref[part] = own.astype(BF16)
        out_ref[part] = out.astype(BF16)
        for side in range(2):
            value = jnp.where(own_side == side, own, out)
            group = 2 * part + side
            for end in range(2):
                turn = (group + end) * rim % LANES
                moved = pltpu.roll(value, turn, 1) if turn else value
                edges[end] = edges[end] + jnp.where(lane // rim == group, moved, 0.0)
    even = me % 2 == 0
    edge_refs[0][...] = jnp.where(even, edges[1], edges[0]).astype(BF16)
    edge_refs[1][...] = jnp.where(even, edges[0], edges[1]).astype(BF16)


def outer_image(own_side, rows, pieces):
    angles, side = rows.shape
    image = jax.ShapeDtypeStruct((2, angles // 2, LANES), BF16)
    edge = jax.ShapeDtypeStruct((angles // 2, LANES), BF16)
    return pl.pallas_call(
        functools.partial(outer_kernel, len(pieces)),
        out_shape=[image, image, edge, edge],
        in_specs=[VMEM] * (2 + len(pieces)),
        out_specs=[VMEM] * 4,
        scratch_shapes=[pltpu.VMEM((side, LANES), BF16)],
        compiler_params=params(10),
        cost_estimate=pl.CostEstimate(
            flops=4 * angles * side * LANES, bytes_accessed=3 * MIB, transcendentals=0
        ),
    )(own_side, rows, *pieces)


def partner_rows_kernel(rows_ref, pulses_ref, image_ref):
    image = dot(rows_ref[...], pulses_ref[...])
    image_ref[...] = image.astype(BF16).reshape(image_ref.shape)


def own_rows_kernel(local_pulses, rows_ref, pulses_ref, outer_ref, image_ref):
    image = dot(rows_ref[...], alternating(pulses_ref[...], local_pulses))
    parts, half, count = outer_ref.shape
    image_ref[:, :, :count] = outer_ref[...]
    image_ref[:, :, count:] = image.astype(BF16).reshape(parts, half, image.shape[1])


def inner_image(kernel, angles, rows, pulses, outer=()):
    count = pulses.shape[1]
    whole = count + (outer[0].shape[2] if outer else 0)
    return pl.pallas_call(
        kernel,
        out_shape=jax.ShapeDtypeStruct((2, angles // 2, whole), BF16),
        in_specs=[VMEM] * (2 + len(outer)),
        out_specs=VMEM,
        compiler_params=params(10),
        cost_estimate=pl.CostEstimate(
            flops=2 * angles * rows.shape[1] * count, bytes_accessed=3 * MIB, transcendentals=0
        ),
    )(rows, pulses, *outer)


def exchanged(value, begin):
    devices = lax.axis_size("rng")
    pairs = [(i, (i + 1) % devices) for i in range(begin, devices, 2)]
    return lax.ppermute(value, "rng", pairs + [(j, i) for i, j in pairs])


def rims_kernel(side_ref, first_ref, second_ref, own_ref, out_ref):
    own_side = side_ref[:1, :]
    rim = LANES // 4
    me, devices = lax.axis_index("rng"), lax.axis_size("rng")
    even = me % 2 == 0
    first, second = first_ref[...].astype(F32), second_ref[...].astype(F32)
    below = jnp.where(me == 0, 0.0, jnp.where(even, second, first))
    above = jnp.where(me == devices - 1, 0.0, jnp.where(even, first, second))
    group = lax.broadcasted_iota(jnp.int32, (1, LANES), 1) // rim
    packed = [0.0, 0.0]
    for end, value in enumerate((below, above)):
        for part in range(2):
            place = 2 * end + part
            for side in range(2):
                turn = (place - (2 * part + side)) * rim % LANES
                moved = pltpu.roll(value, turn, 1) if turn else value
                packed[side] = packed[side] + jnp.where(group == place, moved, 0.0)
    own_ref[...] = jnp.where(own_side == 0, packed[0], packed[1]).astype(BF16)
    out_ref[...] = jnp.where(own_side == 0, packed[1], packed[0]).astype(BF16)


def sorted_rims(own_side, first, second):
    return pl.pallas_call(
        rims_kernel,
        out_shape=[jax.ShapeDtypeStruct(first.shape, BF16)] * 2,
        in_specs=[VMEM] * 3,
        out_specs=[VMEM] * 2,
        compiler_params=params(4),
        cost_estimate=pl.CostEstimate(flops=1_000_000, bytes_accessed=MIB // 4, transcendentals=0),
    )(own_side, first, second)


def resampled(image, rims_ref, centre_ref, rim_ref, value_ref, child):
    parts, half, bins = image.shape
    value_ref[...] = dot(image.reshape(parts * half, bins), centre_ref[child])
    rims = rims_ref[...]
    return [
        (value_ref[part * half : (part + 1) * half, :] + dot(rims, rim_ref[child, part])).astype(BF16)
        for part in range(parts)
    ]


def early_kernel(
    own_ref, rims_ref, centre_ref, rim_ref, matrix_ref, turn_ref, merged_ref, value_ref
):
    rows = resampled(own_ref[...], rims_ref, centre_ref, rim_ref, value_ref, 0)
    merged_ref[0], merged_ref[1] = rotated(
        (dot(matrix_ref[0], rows[0]), dot(matrix_ref[0], rows[1])), (turn_ref[0, 0], turn_ref[0, 1])
    )


def late_kernel(
    far_outer, far_inner, rims_ref, merged_ref, centre_ref, rim_ref, matrix_ref, turn_ref, out_ref,
    buffer, value_ref, sems,
):
    image = jnp.concatenate([far_outer[...], far_inner[...]], axis=2)
    rows = resampled(image, rims_ref, centre_ref, rim_ref, value_ref, 1)
    parts = len(rows)
    block = LANES
    copies = []
    for first in range(0, matrix_ref.shape[1], 2 * block):
        matrix = matrix_ref[1, first : first + 2 * block]
        terms = dot(matrix, rows[0]), dot(matrix, rows[1])
        for step in range(2):
            here = slice(first + step * block, first + (step + 1) * block)
            there = slice(step * block, (step + 1) * block)
            turned = rotated(
                (terms[0][there], terms[1][there]), (turn_ref[1, 0, here], turn_ref[1, 1, here])
            )
            for part in range(parts):
                buffer[part, here] = (merged_ref[part, here] + turned[part]).astype(buffer.dtype)
            copy = pltpu.make_async_copy(
                buffer.at[:, here], out_ref.at[:, here], sems.at[len(copies)]
            )
            copy.start()
            copies.append(copy)
    for copy in copies:
        copy.wait()


def merged_image(own, rims, far, far_rims, tables, dtype):
    centre, rim, turn, matrices, _ = tables
    angles, bins = turn.shape[-2:]
    cost = pl.CostEstimate(flops=4 * angles * bins * bins, bytes_accessed=8 * MIB, transcendentals=0)
    value = pltpu.VMEM((angles, bins), F32)
    merged = pl.pallas_call(
        early_kernel,
        out_shape=jax.ShapeDtypeStruct((2, angles, bins), F32),
        in_specs=[VMEM] * 6,
        out_specs=VMEM,
        scratch_shapes=[value],
        compiler_params=params(16),
        cost_estimate=cost,
    )(own, rims, centre, rim, matrices, turn)
    return pl.pallas_call(
        late_kernel,
        out_shape=jax.ShapeDtypeStruct((2, angles, bins), dtype),
        in_specs=[VMEM] * 8,
        out_specs=ANY,
        scratch_shapes=[
            pltpu.VMEM((2, angles, bins), dtype),
            value,
            pltpu.SemaphoreType.DMA((angles // LANES,)),
        ],
        compiler_params=params(16),
        cost_estimate=cost,
    )(*far, far_rims, merged, centre, rim, matrices, turn)


def after(value, *earlier):
    return lax.optimization_barrier((value, *earlier))[0]


def from_partner(value, stride):
    pairs = [(source, source ^ stride) for source in range(lax.axis_size("sub"))]
    return lax.ppermute(value, "sub", pairs)


def split_image(level, image, fore_flag, rim):
    angles, bins = image.shape[1:]
    half, step = angles // 2, LANES // 2
    own_flag = fore_flag[level, lax.axis_index("sub"), 0]
    sides = image.reshape(2, 2, half, bins)

    def pieces(side):
        rows = lax.dynamic_index_in_dim(sides, side, 1, keepdims=False)
        ends = [rows[..., :step], rows[..., -step:]]
        rest = [rows[..., -2 * step : -step], rows[..., step : -2 * step]]
        return jnp.concatenate(ends + rest, axis=-1)

    def packed(edge):
        return edge.transpose(2, 0, 1, 3).reshape(half, 4 * rim)

    low, high = packed(sides[..., :rim]), packed(sides[..., -rim:])
    even = lax.axis_index("rng") % 2 == 0
    edges = jnp.where(even, high, low), jnp.where(even, low, high)
    return pieces(own_flag), pieces(1 - own_flag), edges


def on_device(echoes, fore_flag, band_offset, angle_interp, range_kernel, center_shift):
    devices = lax.axis_size("rng")
    half = devices // 2
    local_pulses = echoes.shape[1]
    bins = echoes.shape[2] // devices
    angles = angle_interp.shape[2]
    rim = MAX_SHIFT + (range_kernel.shape[1] - bins) // 2
    levels = range_kernel.shape[0]
    settings = (fore_flag, band_offset, center_shift, range_kernel, angle_interp)

    far_blocks, near_blocks, blocks = placed(
        echoes.reshape(2 * local_pulses, devices * bins), devices
    )
    relay = across(far_blocks, half)
    pulses = lax.all_to_all(blocks, "rng", split_axis=0, concat_axis=0, tiled=True)
    sends = joined(near_blocks, relay)
    pieces = [across(value, d) if d else value for d, value in enumerate(sends)]
    matrix, own_side = filter_table(fore_flag, angles, local_pulses, sends[0])
    def halos(side, edges, stride):
        rims, out_rims = sorted_rims(side, exchanged(edges[0], 0), exchanged(edges[1], 1))
        return rims, from_partner(out_rims, stride)

    pulses = after(pulses, *pieces[1:4]).reshape(2 * local_pulses * devices, bins - LANES)
    out_inner = inner_image(partner_rows_kernel, angles, matrix, pulses)
    pieces[0] = after(pieces[0], out_inner)
    own_outer, out_outer, *edges = outer_image(own_side, matrix, pieces)
    far = [from_partner(value, 1) for value in (out_outer, out_inner)]
    rims, far_rims = halos(own_side, edges, 1)
    own_kernel = functools.partial(own_rows_kernel, local_pulses)
    own = inner_image(own_kernel, angles, matrix, pulses, (own_outer,))
    tables = merge_tables(0, 1, *settings, out_inner)
    for level in range(levels):
        stride = 2**level
        if level > 0:
            tables = merge_tables(level, stride, *settings, image)
            own, out, edges = split_image(level, image, fore_flag, rim)
            far = [from_partner(value, stride) for value in (out[..., :LANES], out[..., LANES:])]
            rims, far_rims = halos(tables[-1], edges, stride)
        image = merged_image(own, rims, far, far_rims, tables, BF16 if level + 1 < levels else F32)
    return image


def solution(mesh):
    placed_as = (
        P(None, ("sub", "rng"), None),
        P(None, None, "rng"),
        P(None, None, "rng"),
        P(),
        P(),
        P(),
    )
    return jax.shard_map(
        on_device, mesh=mesh, in_specs=placed_as, out_specs=P(None, "sub", "rng"), check_vma=False
    )
```

```python
import functools
import math

import jax
import jax.numpy as jnp
from jax import lax
from jax.experimental import pallas as pl
from jax.experimental.pallas import tpu as pltpu
from jax.sharding import PartitionSpec as P

MAX_SHIFT = 16
LANES = 128
MIB = 2**20
JOIN_COST = 10**11
SIDE = jax.ShapeDtypeStruct((8, LANES), jnp.float32)
VMEM = pl.BlockSpec(memory_space=pltpu.VMEM)
SMEM = pl.BlockSpec(memory_space=pltpu.SMEM)
ANY = pl.BlockSpec(memory_space=pl.ANY)
F32 = jnp.float32
BF16 = jnp.bfloat16


def dot(a, b):
    return jnp.dot(a, b, preferred_element_type=F32)


def params(mib):
    return pltpu.CompilerParams(vmem_limit_bytes=mib * MIB)


def series(square, first, count):
    coefs = [
        (-1) ** i * math.pi ** (2 * i + first) / math.factorial(2 * i + first)
        for i in range(count)
    ]
    total = jnp.full_like(square, coefs[-1])
    for coef in coefs[-2::-1]:
        total = total * square + coef
    return total


def cos_sin_pi(v):
    turns = jnp.floor(v + 0.5)
    rest = v - turns
    sign = 1.0 - 2.0 * (turns - 2.0 * jnp.floor(turns * 0.5))
    square = rest * rest
    return series(square, 0, 8) * sign, series(square, 1, 7) * rest * sign


def rotated(pair, step):
    return pair[0] * step[0] - pair[1] * step[1], pair[0] * step[1] + pair[1] * step[0]


def mixed(left, right):
    lane = lax.broadcasted_iota(jnp.int32, left.shape, 1)
    return jnp.where(lane < LANES // 2, left.astype(F32), right.astype(F32)).astype(BF16)


def place_kernel(echoes_ref, far_ref, near_ref, inner_ref):
    devices, _, count = inner_ref.shape
    bins = count + LANES
    half = devices // 2
    base = lax.axis_index("rng") // half * half

    def tile(device, first):
        return echoes_ref[:, pl.ds(pl.multiple_of(device * bins + first, LANES), LANES)]

    for ref, start in ((far_ref, half - base), (near_ref, base)):
        for i in range(half):
            ref[i] = mixed(tile(start + i, 0), tile(start + i, bins - LANES))
    for device in range(devices):
        begin = device * bins
        inner_ref[device, :, :LANES] = mixed(tile(device, bins - LANES), tile(device, 0))
        inner_ref[device, :, LANES:] = echoes_ref[:, begin + LANES : begin + bins - LANES]


def placed(echoes, devices):
    rows, columns = echoes.shape
    outer = jax.ShapeDtypeStruct((devices // 2, rows, LANES), BF16)
    inner = jax.ShapeDtypeStruct((devices, rows, columns // devices - LANES), BF16)
    return pl.pallas_call(
        place_kernel,
        out_shape=[outer, outer, inner],
        in_specs=[VMEM],
        out_specs=[VMEM] * 3,
        compiler_params=params(8),
        cost_estimate=pl.CostEstimate(flops=0, bytes_accessed=2 * MIB, transcendentals=0),
    )(echoes)


def join_kernel(near_ref, relay_ref, *refs):
    me = lax.axis_index("rng") % len(refs)
    rows = near_ref.shape[1]
    for d, out_ref in enumerate(refs):
        out_ref[:rows] = near_ref[me ^ d]
        out_ref[rows:] = relay_ref[me ^ d]


def joined(near, relay):
    half, rows, count = near.shape
    return pl.pallas_call(
        join_kernel,
        out_shape=[jax.ShapeDtypeStruct((2 * rows, count), BF16)] * half,
        in_specs=[VMEM] * 2,
        out_specs=[VMEM] * half,
        compiler_params=params(4),
        cost_estimate=pl.CostEstimate(flops=JOIN_COST, bytes_accessed=MIB, transcendentals=0),
    )(near, relay)


def across(value, mask):
    devices = lax.axis_size("rng")
    return lax.ppermute(value, "rng", [(i, i ^ mask) for i in range(devices)])


def filter_table_kernel(local_pulses, flag_ref, after_ref, rows_ref, side_ref, cos_ref, sin_ref):
    own_flag = flag_ref[0, lax.axis_index("sub"), 0]
    side_ref[...] = jnp.full(side_ref.shape, own_flag.astype(F32))
    angles, columns = rows_ref.shape
    half = angles // 2
    first = (1 - own_flag) * half
    base = cos_ref.shape[0]
    scale = 1.0 / math.sqrt(columns // 2)
    lane = lax.broadcasted_iota(jnp.int32, (8, columns), 1)
    slot = lane // (2 * local_pulses)
    second = lane // local_pulses % 2
    pulse = (slot * local_pulses + lane % local_pulses).astype(F32)
    lag = second.astype(F32) * 0.5
    per_angle = pulse * (1.0 / angles)
    row = lax.broadcasted_iota(jnp.int32, (8, columns), 0)
    for i in range(base // 8):
        twice = (2 * (row + 8 * i + first) + 1 - angles).astype(F32)
        cosine, sine = cos_sin_pi(twice * per_angle - lag)
        cos_ref[8 * i : 8 * i + 8, :] = cosine * scale
        sin_ref[8 * i : 8 * i + 8, :] = sine * scale
    step = cos_sin_pi(per_angle * (2 * base))
    for j in range(half // base):
        for i in range(base // 16):
            pair = [], []
            for k in (2 * i, 2 * i + 1):
                here = slice(8 * k, 8 * k + 8)
                now = cos_ref[here, :], sin_ref[here, :]
                pair[0].append(now[0])
                pair[1].append(-now[1])
                if j + 1 < half // base:
                    cos_ref[here, :], sin_ref[here, :] = rotated(now, step)
            begin = j * base + 16 * i
            rows_ref[begin : begin + 16, :] = jnp.concatenate(pair[0]).astype(BF16)
            begin += half
            rows_ref[begin : begin + 16, :] = jnp.concatenate(pair[1]).astype(BF16)


def filter_table(fore_flag, angles, local_pulses, earlier):
    side = 2 * local_pulses * lax.axis_size("rng")
    return pl.pallas_call(
        functools.partial(filter_table_kernel, local_pulses),
        out_shape=[jax.ShapeDtypeStruct((angles, side), BF16), SIDE],
        in_specs=[SMEM, ANY],
        out_specs=[VMEM] * 2,
        scratch_shapes=[pltpu.VMEM((64, side), F32)] * 2,
        compiler_params=params(6),
        cost_estimate=pl.CostEstimate(flops=9_000_000, bytes_accessed=4 * MIB, transcendentals=0),
    )(fore_flag, earlier)


def merge_table_kernel(
    level, stride, flag_ref, offset_ref, shift_ref, range_ref, interp_ref, after_ref, centre_ref,
    rim_ref, turn_ref, matrix_ref, side_ref, kernel_ref, sems,
):
    group = lax.axis_index("sub")
    block = lax.axis_index("rng")
    bins = centre_ref.shape[-1]
    angles = turn_ref.shape[-2]
    total_bins = lax.axis_size("rng") * bins
    taps = range_ref.shape[1]
    band = (taps - bins) // 2
    rim = MAX_SHIFT + band
    own_flag = flag_ref[level, group, 0]
    side_ref[...] = jnp.full(side_ref.shape, own_flag.astype(F32))
    copies = [
        pltpu.make_async_copy(source, target, sems.at[i])
        for i, (source, target) in enumerate(
            (
                (range_ref.at[level], kernel_ref),
                (interp_ref.at[level, own_flag], matrix_ref.at[0]),
                (interp_ref.at[level, 1 - own_flag], matrix_ref.at[1]),
            )
        )
    ]
    for copy in copies:
        copy.start()

    def moved(bin_id):
        tap = lax.broadcasted_iota(jnp.int32, (bin_id.shape[0], taps), 1)
        hot = jnp.where(tap == bin_id, 1.0, 0.0).astype(BF16)
        return dot(hot, kernel_ref[...]).astype(BF16)

    row = lax.broadcasted_iota(jnp.int32, (bins, 1), 0)
    upper = row + (bins - 2 * LANES)
    own_bin = jnp.where(row % LANES < LANES // 2, row, upper + LANES)
    own_bin = jnp.where(row >= LANES, jnp.where(row % LANES < LANES // 2, upper, row - LANES), own_bin)
    own_bin = jnp.where(row >= 2 * LANES, row - LANES, own_bin)
    rim_row = lax.broadcasted_iota(jnp.int32, (2 * rim, 1), 0)
    rim_bin = jnp.where(rim_row < rim, rim_row - rim, rim_row - rim + bins)
    rim_ref[...] = jnp.zeros(rim_ref.shape, BF16)
    bin_id = block * bins + lax.broadcasted_iota(jnp.int32, (8, bins), 1)
    reach = 1.0 + bin_id.astype(F32) * (1.0 / total_bins)
    line = lax.broadcasted_iota(jnp.int32, (8, bins), 0)
    base = 64
    members = group, group ^ stride
    for child, member in enumerate(members):
        rate = shift_ref[level, member]
        for first in range(0, base, 8):
            angle = (first + line).astype(F32)
            now = cos_sin_pi(rate * ((angle + 0.5) * (1.0 / angles) - 0.5) * reach)
            turn_ref[child, 0, first : first + 8, :] = now[0]
            turn_ref[child, 1, first : first + 8, :] = now[1]
        step = cos_sin_pi(rate * (base / angles) * reach)
        for first in range(base, angles, 8):
            here, last = slice(first, first + 8), slice(first - base, first - base + 8)
            now = rotated((turn_ref[child, 0, last, :], turn_ref[child, 1, last, :]), step)
            turn_ref[child, 0, here, :], turn_ref[child, 1, here, :] = now
    for copy in copies:
        copy.wait()
    for child, member in enumerate(members):
        lead = band - offset_ref[level, member, 0]
        centre_ref[child] = moved(own_bin + lead)
        ends = moved(rim_bin + lead)
        for part in range(2):
            for side in range(2):
                place = (2 * side + part) * rim
                rim_ref[child, part, place : place + rim, :] = ends[side * rim : (side + 1) * rim]


def merge_tables(
    level, stride, fore_flag, band_offset, center_shift, range_kernel, angle_interp, earlier
):
    taps, bins = range_kernel.shape[1:]
    angles = angle_interp.shape[2]
    rim = MAX_SHIFT + (taps - bins) // 2
    return pl.pallas_call(
        functools.partial(merge_table_kernel, level, stride),
        out_shape=[
            jax.ShapeDtypeStruct((2, bins, bins), BF16),
            jax.ShapeDtypeStruct((2, 2, 4 * rim, bins), BF16),
            jax.ShapeDtypeStruct((2, 2, angles, bins), F32),
            jax.ShapeDtypeStruct((2, *angle_interp.shape[2:]), BF16),
            SIDE,
        ],
        in_specs=[SMEM] * 3 + [ANY] * 3,
        out_specs=[VMEM] * 5,
        scratch_shapes=[pltpu.VMEM((taps, bins), BF16), pltpu.SemaphoreType.DMA((3,))],
        compiler_params=params(12),
        cost_estimate=pl.CostEstimate(
            flops=2_300_000_000, bytes_accessed=7 * MIB, transcendentals=0
        ),
    )(fore_flag, band_offset, center_shift, range_kernel, angle_interp, earlier)


def alternating(pulses, local_pulses):
    row = lax.broadcasted_iota(jnp.int32, (pulses.shape[0], 1), 0)
    pulse = row // (2 * local_pulses) * local_pulses + row % local_pulses
    return jnp.where(pulse % 2 == 1, -pulses.astype(F32), pulses.astype(F32)).astype(BF16)


def outer_kernel(pieces, side_ref, rows_ref, *refs):
    own_side = side_ref[:1, :]
    me = lax.axis_index("rng")
    own_ref, out_ref, *edge_refs = refs[pieces:-1]
    pulses_ref = refs[-1]
    rows = refs[0].shape[0] // 2
    for d, ref in enumerate(refs[:pieces]):
        for t in range(2):
            place = pl.multiple_of((me ^ (d + t * pieces)) * rows, rows)
            pulses_ref[pl.ds(place, rows), :] = ref[t * rows : (t + 1) * rows, :]
    pulses = pulses_ref[...]
    own_parts = dot(rows_ref[...], alternating(pulses, rows // 2))
    out_parts = dot(rows_ref[...], pulses)
    half = own_ref.shape[1]
    rim = LANES // 4
    lane = lax.broadcasted_iota(jnp.int32, (1, LANES), 1)
    edges = [0.0, 0.0]
    for part in range(2):
        own, out = (value[part * half : (part + 1) * half] for value in (own_parts, out_parts))
        own_ref[part] = own.astype(BF16)
        out_ref[part] = out.astype(BF16)
        for side in range(2):
            value = jnp.where(own_side == side, own, out)
            group = 2 * part + side
            for end in range(2):
                turn = (group + end) * rim % LANES
                moved = pltpu.roll(value, turn, 1) if turn else value
                edges[end] = edges[end] + jnp.where(lane // rim == group, moved, 0.0)
    even = me % 2 == 0
    edge_refs[0][...] = jnp.where(even, edges[1], edges[0]).astype(BF16)
    edge_refs[1][...] = jnp.where(even, edges[0], edges[1]).astype(BF16)


def outer_image(own_side, rows, pieces):
    angles, side = rows.shape
    image = jax.ShapeDtypeStruct((2, angles // 2, LANES), BF16)
    edge = jax.ShapeDtypeStruct((angles // 2, LANES), BF16)
    return pl.pallas_call(
        functools.partial(outer_kernel, len(pieces)),
        out_shape=[image, image, edge, edge],
        in_specs=[VMEM] * (2 + len(pieces)),
        out_specs=[VMEM] * 4,
        scratch_shapes=[pltpu.VMEM((side, LANES), BF16)],
        compiler_params=params(10),
        cost_estimate=pl.CostEstimate(
            flops=4 * angles * side * LANES, bytes_accessed=3 * MIB, transcendentals=0
        ),
    )(own_side, rows, *pieces)


def partner_rows_kernel(rows_ref, pulses_ref, image_ref):
    image = dot(rows_ref[...], pulses_ref[...])
    image_ref[...] = image.astype(BF16).reshape(image_ref.shape)


def own_rows_kernel(local_pulses, rows_ref, pulses_ref, outer_ref, image_ref):
    image = dot(rows_ref[...], alternating(pulses_ref[...], local_pulses))
    parts, half, count = outer_ref.shape
    image_ref[:, :, :count] = outer_ref[...]
    image_ref[:, :, count:] = image.astype(BF16).reshape(parts, half, image.shape[1])


def inner_image(kernel, angles, rows, pulses, outer=()):
    count = pulses.shape[1]
    whole = count + (outer[0].shape[2] if outer else 0)
    return pl.pallas_call(
        kernel,
        out_shape=jax.ShapeDtypeStruct((2, angles // 2, whole), BF16),
        in_specs=[VMEM] * (2 + len(outer)),
        out_specs=VMEM,
        compiler_params=params(10),
        cost_estimate=pl.CostEstimate(
            flops=2 * angles * rows.shape[1] * count, bytes_accessed=3 * MIB, transcendentals=0
        ),
    )(rows, pulses, *outer)


def exchanged(value, begin):
    devices = lax.axis_size("rng")
    pairs = [(i, (i + 1) % devices) for i in range(begin, devices, 2)]
    return lax.ppermute(value, "rng", pairs + [(j, i) for i, j in pairs])


def rims_kernel(side_ref, first_ref, second_ref, own_ref, out_ref):
    own_side = side_ref[:1, :]
    rim = LANES // 4
    me, devices = lax.axis_index("rng"), lax.axis_size("rng")
    even = me % 2 == 0
    first, second = first_ref[...].astype(F32), second_ref[...].astype(F32)
    below = jnp.where(me == 0, 0.0, jnp.where(even, second, first))
    above = jnp.where(me == devices - 1, 0.0, jnp.where(even, first, second))
    group = lax.broadcasted_iota(jnp.int32, (1, LANES), 1) // rim
    packed = [0.0, 0.0]
    for end, value in enumerate((below, above)):
        for part in range(2):
            place = 2 * end + part
            for side in range(2):
                turn = (place - (2 * part + side)) * rim % LANES
                moved = pltpu.roll(value, turn, 1) if turn else value
                packed[side] = packed[side] + jnp.where(group == place, moved, 0.0)
    own_ref[...] = jnp.where(own_side == 0, packed[0], packed[1]).astype(BF16)
    out_ref[...] = jnp.where(own_side == 0, packed[1], packed[0]).astype(BF16)


def sorted_rims(own_side, first, second):
    return pl.pallas_call(
        rims_kernel,
        out_shape=[jax.ShapeDtypeStruct(first.shape, BF16)] * 2,
        in_specs=[VMEM] * 3,
        out_specs=[VMEM] * 2,
        compiler_params=params(4),
        cost_estimate=pl.CostEstimate(flops=1_000_000, bytes_accessed=MIB // 4, transcendentals=0),
    )(own_side, first, second)


def resampled(image, rims_ref, centre_ref, rim_ref, value_ref, child):
    parts, half, bins = image.shape
    value_ref[...] = dot(image.reshape(parts * half, bins), centre_ref[child])
    rims = rims_ref[...]
    return [
        (value_ref[part * half : (part + 1) * half, :] + dot(rims, rim_ref[child, part])).astype(BF16)
        for part in range(parts)
    ]


def early_kernel(
    own_ref, rims_ref, centre_ref, rim_ref, matrix_ref, turn_ref, merged_ref, value_ref
):
    rows = resampled(own_ref[...], rims_ref, centre_ref, rim_ref, value_ref, 0)
    merged_ref[0], merged_ref[1] = rotated(
        (dot(matrix_ref[0], rows[0]), dot(matrix_ref[0], rows[1])), (turn_ref[0, 0], turn_ref[0, 1])
    )


def late_kernel(
    far_outer, far_inner, rims_ref, merged_ref, centre_ref, rim_ref, matrix_ref, turn_ref, out_ref,
    buffer, value_ref, sems,
):
    image = jnp.concatenate([far_outer[...], far_inner[...]], axis=2)
    rows = resampled(image, rims_ref, centre_ref, rim_ref, value_ref, 1)
    parts = len(rows)
    block = LANES
    copies = []
    for first in range(0, matrix_ref.shape[1], 2 * block):
        matrix = matrix_ref[1, first : first + 2 * block]
        terms = dot(matrix, rows[0]), dot(matrix, rows[1])
        for step in range(2):
            here = slice(first + step * block, first + (step + 1) * block)
            there = slice(step * block, (step + 1) * block)
            turned = rotated(
                (terms[0][there], terms[1][there]), (turn_ref[1, 0, here], turn_ref[1, 1, here])
            )
            for part in range(parts):
                buffer[part, here] = (merged_ref[part, here] + turned[part]).astype(buffer.dtype)
            copy = pltpu.make_async_copy(
                buffer.at[:, here], out_ref.at[:, here], sems.at[len(copies)]
            )
            copy.start()
            copies.append(copy)
    for copy in copies:
        copy.wait()


def merged_image(own, rims, far, far_rims, tables, dtype):
    centre, rim, turn, matrices, _ = tables
    angles, bins = turn.shape[-2:]
    cost = pl.CostEstimate(flops=4 * angles * bins * bins, bytes_accessed=8 * MIB, transcendentals=0)
    value = pltpu.VMEM((angles, bins), F32)
    merged = pl.pallas_call(
        early_kernel,
        out_shape=jax.ShapeDtypeStruct((2, angles, bins), F32),
        in_specs=[VMEM] * 6,
        out_specs=VMEM,
        scratch_shapes=[value],
        compiler_params=params(16),
        cost_estimate=cost,
    )(own, rims, centre, rim, matrices, turn)
    return pl.pallas_call(
        late_kernel,
        out_shape=jax.ShapeDtypeStruct((2, angles, bins), dtype),
        in_specs=[VMEM] * 8,
        out_specs=ANY,
        scratch_shapes=[
            pltpu.VMEM((2, angles, bins), dtype),
            value,
            pltpu.SemaphoreType.DMA((angles // LANES,)),
        ],
        compiler_params=params(16),
        cost_estimate=cost,
    )(*far, far_rims, merged, centre, rim, matrices, turn)


def after(value, *earlier):
    return lax.optimization_barrier((value, *earlier))[0]


def from_partner(value, stride):
    pairs = [(source, source ^ stride) for source in range(lax.axis_size("sub"))]
    return lax.ppermute(value, "sub", pairs)


def split_image(level, image, fore_flag, rim):
    angles, bins = image.shape[1:]
    half, step = angles // 2, LANES // 2
    own_flag = fore_flag[level, lax.axis_index("sub"), 0]
    sides = image.reshape(2, 2, half, bins)

    def pieces(side):
        rows = lax.dynamic_index_in_dim(sides, side, 1, keepdims=False)
        ends = [rows[..., :step], rows[..., -step:]]
        rest = [rows[..., -2 * step : -step], rows[..., step : -2 * step]]
        return jnp.concatenate(ends + rest, axis=-1)

    def packed(edge):
        return edge.transpose(2, 0, 1, 3).reshape(half, 4 * rim)

    low, high = packed(sides[..., :rim]), packed(sides[..., -rim:])
    even = lax.axis_index("rng") % 2 == 0
    edges = jnp.where(even, high, low), jnp.where(even, low, high)
    return pieces(own_flag), pieces(1 - own_flag), edges


def on_device(echoes, fore_flag, band_offset, angle_interp, range_kernel, center_shift):
    devices = lax.axis_size("rng")
    half = devices // 2
    local_pulses = echoes.shape[1]
    bins = echoes.shape[2] // devices
    angles = angle_interp.shape[2]
    rim = MAX_SHIFT + (range_kernel.shape[1] - bins) // 2
    levels = range_kernel.shape[0]
    settings = (fore_flag, band_offset, center_shift, range_kernel, angle_interp)

    far_blocks, near_blocks, blocks = placed(
        echoes.reshape(2 * local_pulses, devices * bins), devices
    )
    relay = across(far_blocks, half)
    pulses = lax.all_to_all(blocks, "rng", split_axis=0, concat_axis=0, tiled=True)
    sends = joined(near_blocks, relay)
    pieces = [across(value, d) if d else value for d, value in enumerate(sends)]
    matrix, own_side = filter_table(fore_flag, angles, local_pulses, sends[0])
    def halos(side, edges, stride):
        rims, out_rims = sorted_rims(side, exchanged(edges[0], 0), exchanged(edges[1], 1))
        return rims, from_partner(out_rims, stride)

    pulses = after(pulses, *pieces[1:]).reshape(2 * local_pulses * devices, bins - LANES)
    out_inner = inner_image(partner_rows_kernel, angles, matrix, pulses)
    pieces[0] = after(pieces[0], out_inner)
    own_outer, out_outer, *edges = outer_image(own_side, matrix, pieces)
    far = [from_partner(value, 1) for value in (out_outer, out_inner)]
    rims, far_rims = halos(own_side, edges, 1)
    own_kernel = functools.partial(own_rows_kernel, local_pulses)
    own = inner_image(own_kernel, angles, matrix, pulses, (own_outer,))
    tables = merge_tables(0, 1, *settings, own)
    for level in range(levels):
        stride = 2**level
        if level > 0:
            tables = merge_tables(level, stride, *settings, image)
            own, out, edges = split_image(level, image, fore_flag, rim)
            far = [from_partner(value, stride) for value in (out[..., :LANES], out[..., LANES:])]
            rims, far_rims = halos(tables[-1], edges, stride)
        image = merged_image(own, rims, far, far_rims, tables, BF16 if level + 1 < levels else F32)
    return image


def solution(mesh):
    placed_as = (
        P(None, ("sub", "rng"), None),
        P(None, None, "rng"),
        P(None, None, "rng"),
        P(),
        P(),
        P(),
    )
    return jax.shard_map(
        on_device, mesh=mesh, in_specs=placed_as, out_specs=P(None, "sub", "rng"), check_vma=False
    )
```

```python
import functools
import math

import jax
import jax.numpy as jnp
from jax import lax
from jax.experimental import pallas as pl
from jax.experimental.pallas import tpu as pltpu
from jax.sharding import PartitionSpec as P

MAX_SHIFT = 16
LANES = 128
MIB = 2**20
JOIN_COST = 10**11
SIDE = jax.ShapeDtypeStruct((8, LANES), jnp.float32)
VMEM = pl.BlockSpec(memory_space=pltpu.VMEM)
SMEM = pl.BlockSpec(memory_space=pltpu.SMEM)
ANY = pl.BlockSpec(memory_space=pl.ANY)
F32 = jnp.float32
BF16 = jnp.bfloat16


def dot(a, b):
    return jnp.dot(a, b, preferred_element_type=F32)


def params(mib):
    return pltpu.CompilerParams(vmem_limit_bytes=mib * MIB)


def series(square, first, count):
    coefs = [
        (-1) ** i * math.pi ** (2 * i + first) / math.factorial(2 * i + first)
        for i in range(count)
    ]
    total = jnp.full_like(square, coefs[-1])
    for coef in coefs[-2::-1]:
        total = total * square + coef
    return total


def cos_sin_pi(v):
    turns = jnp.floor(v + 0.5)
    rest = v - turns
    sign = 1.0 - 2.0 * (turns - 2.0 * jnp.floor(turns * 0.5))
    square = rest * rest
    return series(square, 0, 8) * sign, series(square, 1, 7) * rest * sign


def rotated(pair, step):
    return pair[0] * step[0] - pair[1] * step[1], pair[0] * step[1] + pair[1] * step[0]


def mixed(left, right):
    lane = lax.broadcasted_iota(jnp.int32, left.shape, 1)
    return jnp.where(lane < LANES // 2, left.astype(F32), right.astype(F32)).astype(BF16)


def place_kernel(echoes_ref, far_ref, near_ref, inner_ref):
    devices, _, count = inner_ref.shape
    bins = count + LANES
    half = devices // 2
    base = lax.axis_index("rng") // half * half

    def tile(device, first):
        return echoes_ref[:, pl.ds(pl.multiple_of(device * bins + first, LANES), LANES)]

    for ref, start in ((far_ref, half - base), (near_ref, base)):
        for i in range(half):
            ref[i] = mixed(tile(start + i, 0), tile(start + i, bins - LANES))
    for device in range(devices):
        begin = device * bins
        inner_ref[device, :, :LANES] = mixed(tile(device, bins - LANES), tile(device, 0))
        inner_ref[device, :, LANES:] = echoes_ref[:, begin + LANES : begin + bins - LANES]


def placed(echoes, devices):
    rows, columns = echoes.shape
    outer = jax.ShapeDtypeStruct((devices // 2, rows, LANES), BF16)
    inner = jax.ShapeDtypeStruct((devices, rows, columns // devices - LANES), BF16)
    return pl.pallas_call(
        place_kernel,
        out_shape=[outer, outer, inner],
        in_specs=[VMEM],
        out_specs=[VMEM] * 3,
        compiler_params=params(8),
        cost_estimate=pl.CostEstimate(flops=0, bytes_accessed=2 * MIB, transcendentals=0),
    )(echoes)


def join_kernel(near_ref, relay_ref, *refs):
    me = lax.axis_index("rng") % len(refs)
    rows = near_ref.shape[1]
    for d, out_ref in enumerate(refs):
        out_ref[:rows] = near_ref[me ^ d]
        out_ref[rows:] = relay_ref[me ^ d]


def joined(near, relay):
    half, rows, count = near.shape
    return pl.pallas_call(
        join_kernel,
        out_shape=[jax.ShapeDtypeStruct((2 * rows, count), BF16)] * half,
        in_specs=[VMEM] * 2,
        out_specs=[VMEM] * half,
        compiler_params=params(4),
        cost_estimate=pl.CostEstimate(flops=JOIN_COST, bytes_accessed=MIB, transcendentals=0),
    )(near, relay)


def across(value, mask):
    devices = lax.axis_size("rng")
    return lax.ppermute(value, "rng", [(i, i ^ mask) for i in range(devices)])


def filter_table_kernel(local_pulses, flag_ref, after_ref, rows_ref, side_ref, cos_ref, sin_ref):
    own_flag = flag_ref[0, lax.axis_index("sub"), 0]
    side_ref[...] = jnp.full(side_ref.shape, own_flag.astype(F32))
    angles, columns = rows_ref.shape
    half = angles // 2
    first = (1 - own_flag) * half
    base = cos_ref.shape[0]
    scale = 1.0 / math.sqrt(columns // 2)
    lane = lax.broadcasted_iota(jnp.int32, (8, columns), 1)
    slot = lane // (2 * local_pulses)
    second = lane // local_pulses % 2
    pulse = (slot * local_pulses + lane % local_pulses).astype(F32)
    lag = second.astype(F32) * 0.5
    per_angle = pulse * (1.0 / angles)
    row = lax.broadcasted_iota(jnp.int32, (8, columns), 0)
    for i in range(base // 8):
        twice = (2 * (row + 8 * i + first) + 1 - angles).astype(F32)
        cosine, sine = cos_sin_pi(twice * per_angle - lag)
        cos_ref[8 * i : 8 * i + 8, :] = cosine * scale
        sin_ref[8 * i : 8 * i + 8, :] = sine * scale
    step = cos_sin_pi(per_angle * (2 * base))
    for j in range(half // base):
        for i in range(base // 16):
            pair = [], []
            for k in (2 * i, 2 * i + 1):
                here = slice(8 * k, 8 * k + 8)
                now = cos_ref[here, :], sin_ref[here, :]
                pair[0].append(now[0])
                pair[1].append(-now[1])
                if j + 1 < half // base:
                    cos_ref[here, :], sin_ref[here, :] = rotated(now, step)
            begin = j * base + 16 * i
            rows_ref[begin : begin + 16, :] = jnp.concatenate(pair[0]).astype(BF16)
            begin += half
            rows_ref[begin : begin + 16, :] = jnp.concatenate(pair[1]).astype(BF16)


def filter_table(fore_flag, angles, local_pulses, earlier):
    side = 2 * local_pulses * lax.axis_size("rng")
    return pl.pallas_call(
        functools.partial(filter_table_kernel, local_pulses),
        out_shape=[jax.ShapeDtypeStruct((angles, side), BF16), SIDE],
        in_specs=[SMEM, ANY],
        out_specs=[VMEM] * 2,
        scratch_shapes=[pltpu.VMEM((64, side), F32)] * 2,
        compiler_params=params(6),
        cost_estimate=pl.CostEstimate(flops=9_000_000, bytes_accessed=4 * MIB, transcendentals=0),
    )(fore_flag, earlier)


def merge_table_kernel(
    level, stride, flag_ref, offset_ref, shift_ref, range_ref, interp_ref, after_ref, centre_ref,
    rim_ref, turn_ref, matrix_ref, side_ref, kernel_ref, sems,
):
    group = lax.axis_index("sub")
    block = lax.axis_index("rng")
    bins = centre_ref.shape[-1]
    angles = turn_ref.shape[-2]
    total_bins = lax.axis_size("rng") * bins
    taps = range_ref.shape[1]
    band = (taps - bins) // 2
    rim = MAX_SHIFT + band
    own_flag = flag_ref[level, group, 0]
    side_ref[...] = jnp.full(side_ref.shape, own_flag.astype(F32))
    copies = [
        pltpu.make_async_copy(source, target, sems.at[i])
        for i, (source, target) in enumerate(
            (
                (range_ref.at[level], kernel_ref),
                (interp_ref.at[level, own_flag], matrix_ref.at[0]),
                (interp_ref.at[level, 1 - own_flag], matrix_ref.at[1]),
            )
        )
    ]
    for copy in copies:
        copy.start()

    def moved(bin_id):
        tap = lax.broadcasted_iota(jnp.int32, (bin_id.shape[0], taps), 1)
        hot = jnp.where(tap == bin_id, 1.0, 0.0).astype(BF16)
        return dot(hot, kernel_ref[...]).astype(BF16)

    row = lax.broadcasted_iota(jnp.int32, (bins, 1), 0)
    upper = row + (bins - 2 * LANES)
    own_bin = jnp.where(row % LANES < LANES // 2, row, upper + LANES)
    own_bin = jnp.where(row >= LANES, jnp.where(row % LANES < LANES // 2, upper, row - LANES), own_bin)
    own_bin = jnp.where(row >= 2 * LANES, row - LANES, own_bin)
    rim_row = lax.broadcasted_iota(jnp.int32, (2 * rim, 1), 0)
    rim_bin = jnp.where(rim_row < rim, rim_row - rim, rim_row - rim + bins)
    rim_ref[...] = jnp.zeros(rim_ref.shape, BF16)
    bin_id = block * bins + lax.broadcasted_iota(jnp.int32, (8, bins), 1)
    reach = 1.0 + bin_id.astype(F32) * (1.0 / total_bins)
    line = lax.broadcasted_iota(jnp.int32, (8, bins), 0)
    base = 64
    members = group, group ^ stride
    for child, member in enumerate(members):
        rate = shift_ref[level, member]
        for first in range(0, base, 8):
            angle = (first + line).astype(F32)
            now = cos_sin_pi(rate * ((angle + 0.5) * (1.0 / angles) - 0.5) * reach)
            turn_ref[child, 0, first : first + 8, :] = now[0]
            turn_ref[child, 1, first : first + 8, :] = now[1]
        step = cos_sin_pi(rate * (base / angles) * reach)
        for first in range(base, angles, 8):
            here, last = slice(first, first + 8), slice(first - base, first - base + 8)
            now = rotated((turn_ref[child, 0, last, :], turn_ref[child, 1, last, :]), step)
            turn_ref[child, 0, here, :], turn_ref[child, 1, here, :] = now
    for copy in copies:
        copy.wait()
    for child, member in enumerate(members):
        lead = band - offset_ref[level, member, 0]
        centre_ref[child] = moved(own_bin + lead)
        ends = moved(rim_bin + lead)
        for part in range(2):
            for side in range(2):
                place = (2 * side + part) * rim
                rim_ref[child, part, place : place + rim, :] = ends[side * rim : (side + 1) * rim]


def merge_tables(
    level, stride, fore_flag, band_offset, center_shift, range_kernel, angle_interp, earlier
):
    taps, bins = range_kernel.shape[1:]
    angles = angle_interp.shape[2]
    rim = MAX_SHIFT + (taps - bins) // 2
    return pl.pallas_call(
        functools.partial(merge_table_kernel, level, stride),
        out_shape=[
            jax.ShapeDtypeStruct((2, bins, bins), BF16),
            jax.ShapeDtypeStruct((2, 2, 4 * rim, bins), BF16),
            jax.ShapeDtypeStruct((2, 2, angles, bins), F32),
            jax.ShapeDtypeStruct((2, *angle_interp.shape[2:]), BF16),
            SIDE,
        ],
        in_specs=[SMEM] * 3 + [ANY] * 3,
        out_specs=[VMEM] * 5,
        scratch_shapes=[pltpu.VMEM((taps, bins), BF16), pltpu.SemaphoreType.DMA((3,))],
        compiler_params=params(12),
        cost_estimate=pl.CostEstimate(
            flops=2_300_000_000, bytes_accessed=7 * MIB, transcendentals=0
        ),
    )(fore_flag, band_offset, center_shift, range_kernel, angle_interp, earlier)


def alternating(pulses, local_pulses):
    row = lax.broadcasted_iota(jnp.int32, (pulses.shape[0], 1), 0)
    pulse = row // (2 * local_pulses) * local_pulses + row % local_pulses
    return jnp.where(pulse % 2 == 1, -pulses.astype(F32), pulses.astype(F32)).astype(BF16)


def outer_kernel(pieces, side_ref, rows_ref, *refs):
    own_side = side_ref[:1, :]
    me = lax.axis_index("rng")
    own_ref, out_ref, *edge_refs = refs[pieces:-1]
    pulses_ref = refs[-1]
    rows = refs[0].shape[0] // 2
    for d, ref in enumerate(refs[:pieces]):
        for t in range(2):
            place = pl.multiple_of((me ^ (d + t * pieces)) * rows, rows)
            pulses_ref[pl.ds(place, rows), :] = ref[t * rows : (t + 1) * rows, :]
    pulses = pulses_ref[...]
    own_parts = dot(rows_ref[...], alternating(pulses, rows // 2))
    out_parts = dot(rows_ref[...], pulses)
    half = own_ref.shape[1]
    rim = LANES // 4
    lane = lax.broadcasted_iota(jnp.int32, (1, LANES), 1)
    edges = [0.0, 0.0]
    for part in range(2):
        own, out = (value[part * half : (part + 1) * half] for value in (own_parts, out_parts))
        own_ref[part] = own.astype(BF16)
        out_ref[part] = out.astype(BF16)
        for side in range(2):
            value = jnp.where(own_side == side, own, out)
            group = 2 * part + side
            for end in range(2):
                turn = (group + end) * rim % LANES
                moved = pltpu.roll(value, turn, 1) if turn else value
                edges[end] = edges[end] + jnp.where(lane // rim == group, moved, 0.0)
    even = me % 2 == 0
    edge_refs[0][...] = jnp.where(even, edges[1], edges[0]).astype(BF16)
    edge_refs[1][...] = jnp.where(even, edges[0], edges[1]).astype(BF16)


def outer_image(own_side, rows, pieces):
    angles, side = rows.shape
    image = jax.ShapeDtypeStruct((2, angles // 2, LANES), BF16)
    edge = jax.ShapeDtypeStruct((angles // 2, LANES), BF16)
    return pl.pallas_call(
        functools.partial(outer_kernel, len(pieces)),
        out_shape=[image, image, edge, edge],
        in_specs=[VMEM] * (2 + len(pieces)),
        out_specs=[VMEM] * 4,
        scratch_shapes=[pltpu.VMEM((side, LANES), BF16)],
        compiler_params=params(10),
        cost_estimate=pl.CostEstimate(
            flops=4 * angles * side * LANES, bytes_accessed=3 * MIB, transcendentals=0
        ),
    )(own_side, rows, *pieces)


def partner_rows_kernel(rows_ref, pulses_ref, image_ref):
    image = dot(rows_ref[...], pulses_ref[...])
    image_ref[...] = image.astype(BF16).reshape(image_ref.shape)


def own_rows_kernel(local_pulses, rows_ref, pulses_ref, outer_ref, image_ref):
    image = dot(rows_ref[...], alternating(pulses_ref[...], local_pulses))
    parts, half, count = outer_ref.shape
    image_ref[:, :, :count] = outer_ref[...]
    image_ref[:, :, count:] = image.astype(BF16).reshape(parts, half, image.shape[1])


def inner_image(kernel, angles, rows, pulses, outer=()):
    count = pulses.shape[1]
    whole = count + (outer[0].shape[2] if outer else 0)
    return pl.pallas_call(
        kernel,
        out_shape=jax.ShapeDtypeStruct((2, angles // 2, whole), BF16),
        in_specs=[VMEM] * (2 + len(outer)),
        out_specs=VMEM,
        compiler_params=params(10),
        cost_estimate=pl.CostEstimate(
            flops=2 * angles * rows.shape[1] * count, bytes_accessed=3 * MIB, transcendentals=0
        ),
    )(rows, pulses, *outer)


def exchanged(value, begin):
    devices = lax.axis_size("rng")
    pairs = [(i, (i + 1) % devices) for i in range(begin, devices, 2)]
    return lax.ppermute(value, "rng", pairs + [(j, i) for i, j in pairs])


def rims_kernel(side_ref, first_ref, second_ref, own_ref, out_ref):
    own_side = side_ref[:1, :]
    rim = LANES // 4
    me, devices = lax.axis_index("rng"), lax.axis_size("rng")
    even = me % 2 == 0
    first, second = first_ref[...].astype(F32), second_ref[...].astype(F32)
    below = jnp.where(me == 0, 0.0, jnp.where(even, second, first))
    above = jnp.where(me == devices - 1, 0.0, jnp.where(even, first, second))
    group = lax.broadcasted_iota(jnp.int32, (1, LANES), 1) // rim
    packed = [0.0, 0.0]
    for end, value in enumerate((below, above)):
        for part in range(2):
            place = 2 * end + part
            for side in range(2):
                turn = (place - (2 * part + side)) * rim % LANES
                moved = pltpu.roll(value, turn, 1) if turn else value
                packed[side] = packed[side] + jnp.where(group == place, moved, 0.0)
    own_ref[...] = jnp.where(own_side == 0, packed[0], packed[1]).astype(BF16)
    out_ref[...] = jnp.where(own_side == 0, packed[1], packed[0]).astype(BF16)


def sorted_rims(own_side, first, second):
    return pl.pallas_call(
        rims_kernel,
        out_shape=[jax.ShapeDtypeStruct(first.shape, BF16)] * 2,
        in_specs=[VMEM] * 3,
        out_specs=[VMEM] * 2,
        compiler_params=params(4),
        cost_estimate=pl.CostEstimate(flops=1_000_000, bytes_accessed=MIB // 4, transcendentals=0),
    )(own_side, first, second)


def resampled(image, rims_ref, centre_ref, rim_ref, value_ref, child):
    parts, half, bins = image.shape
    value_ref[...] = dot(image.reshape(parts * half, bins), centre_ref[child])
    rims = rims_ref[...]
    return [
        (value_ref[part * half : (part + 1) * half, :] + dot(rims, rim_ref[child, part])).astype(BF16)
        for part in range(parts)
    ]


def early_kernel(
    own_ref, rims_ref, centre_ref, rim_ref, matrix_ref, turn_ref, merged_ref, value_ref
):
    rows = resampled(own_ref[...], rims_ref, centre_ref, rim_ref, value_ref, 0)
    merged_ref[0], merged_ref[1] = rotated(
        (dot(matrix_ref[0], rows[0]), dot(matrix_ref[0], rows[1])), (turn_ref[0, 0], turn_ref[0, 1])
    )


def late_kernel(
    far_outer, far_inner, rims_ref, merged_ref, centre_ref, rim_ref, matrix_ref, turn_ref, out_ref,
    buffer, value_ref, sems,
):
    image = jnp.concatenate([far_outer[...], far_inner[...]], axis=2)
    rows = resampled(image, rims_ref, centre_ref, rim_ref, value_ref, 1)
    parts = len(rows)
    block = LANES
    copies = []
    for first in range(0, matrix_ref.shape[1], 2 * block):
        matrix = matrix_ref[1, first : first + 2 * block]
        terms = dot(matrix, rows[0]), dot(matrix, rows[1])
        for step in range(2):
            here = slice(first + step * block, first + (step + 1) * block)
            there = slice(step * block, (step + 1) * block)
            turned = rotated(
                (terms[0][there], terms[1][there]), (turn_ref[1, 0, here], turn_ref[1, 1, here])
            )
            for part in range(parts):
                buffer[part, here] = (merged_ref[part, here] + turned[part]).astype(buffer.dtype)
            copy = pltpu.make_async_copy(
                buffer.at[:, here], out_ref.at[:, here], sems.at[len(copies)]
            )
            copy.start()
            copies.append(copy)
    for copy in copies:
        copy.wait()


def merged_image(own, rims, far, far_rims, tables, dtype):
    centre, rim, turn, matrices, _ = tables
    angles, bins = turn.shape[-2:]
    cost = pl.CostEstimate(flops=4 * angles * bins * bins, bytes_accessed=8 * MIB, transcendentals=0)
    value = pltpu.VMEM((angles, bins), F32)
    merged = pl.pallas_call(
        early_kernel,
        out_shape=jax.ShapeDtypeStruct((2, angles, bins), F32),
        in_specs=[VMEM] * 6,
        out_specs=VMEM,
        scratch_shapes=[value],
        compiler_params=params(16),
        cost_estimate=cost,
    )(own, rims, centre, rim, matrices, turn)
    return pl.pallas_call(
        late_kernel,
        out_shape=jax.ShapeDtypeStruct((2, angles, bins), dtype),
        in_specs=[VMEM] * 8,
        out_specs=ANY,
        scratch_shapes=[
            pltpu.VMEM((2, angles, bins), dtype),
            value,
            pltpu.SemaphoreType.DMA((angles // LANES,)),
        ],
        compiler_params=params(16),
        cost_estimate=cost,
    )(*far, far_rims, merged, centre, rim, matrices, turn)


def after(value, *earlier):
    return lax.optimization_barrier((value, *earlier))[0]


def from_partner(value, stride):
    pairs = [(source, source ^ stride) for source in range(lax.axis_size("sub"))]
    return lax.ppermute(value, "sub", pairs)


def split_image(level, image, fore_flag, rim):
    angles, bins = image.shape[1:]
    half, step = angles // 2, LANES // 2
    own_flag = fore_flag[level, lax.axis_index("sub"), 0]
    sides = image.reshape(2, 2, half, bins)

    def pieces(side):
        rows = lax.dynamic_index_in_dim(sides, side, 1, keepdims=False)
        ends = [rows[..., :step], rows[..., -step:]]
        rest = [rows[..., -2 * step : -step], rows[..., step : -2 * step]]
        return jnp.concatenate(ends + rest, axis=-1)

    def packed(edge):
        return edge.transpose(2, 0, 1, 3).reshape(half, 4 * rim)

    low, high = packed(sides[..., :rim]), packed(sides[..., -rim:])
    even = lax.axis_index("rng") % 2 == 0
    edges = jnp.where(even, high, low), jnp.where(even, low, high)
    return pieces(own_flag), pieces(1 - own_flag), edges


def on_device(echoes, fore_flag, band_offset, angle_interp, range_kernel, center_shift):
    devices = lax.axis_size("rng")
    half = devices // 2
    local_pulses = echoes.shape[1]
    bins = echoes.shape[2] // devices
    angles = angle_interp.shape[2]
    rim = MAX_SHIFT + (range_kernel.shape[1] - bins) // 2
    levels = range_kernel.shape[0]
    settings = (fore_flag, band_offset, center_shift, range_kernel, angle_interp)

    far_blocks, near_blocks, blocks = placed(
        echoes.reshape(2 * local_pulses, devices * bins), devices
    )
    relay = across(far_blocks, half)
    pulses = lax.all_to_all(blocks, "rng", split_axis=0, concat_axis=0, tiled=True)
    sends = joined(near_blocks, relay)
    pieces = [across(value, d) if d else value for d, value in enumerate(sends)]
    matrix, own_side = filter_table(fore_flag, angles, local_pulses, sends[0])
    def halos(side, edges, stride):
        rims, out_rims = sorted_rims(side, exchanged(edges[0], 0), exchanged(edges[1], 1))
        return rims, from_partner(out_rims, stride)

    pulses = after(pulses, *pieces[1:]).reshape(2 * local_pulses * devices, bins - LANES)
    out_inner = inner_image(partner_rows_kernel, angles, matrix, pulses)
    pieces[0] = after(pieces[0], out_inner)
    own_outer, out_outer, *edges = outer_image(own_side, matrix, pieces)
    far = [from_partner(value, 1) for value in (out_outer, out_inner)]
    own_kernel = functools.partial(own_rows_kernel, local_pulses)
    own = inner_image(own_kernel, angles, matrix, pulses, (own_outer,))
    tables = merge_tables(0, 1, *settings, own)
    edges[1] = after(edges[1], tables[0])
    rims, far_rims = halos(own_side, edges, 1)
    for level in range(levels):
        stride = 2**level
        if level > 0:
            tables = merge_tables(level, stride, *settings, image)
            own, out, edges = split_image(level, image, fore_flag, rim)
            far = [from_partner(value, stride) for value in (out[..., :LANES], out[..., LANES:])]
            rims, far_rims = halos(tables[-1], edges, stride)
        image = merged_image(own, rims, far, far_rims, tables, BF16 if level + 1 < levels else F32)
    return image


def solution(mesh):
    placed_as = (
        P(None, ("sub", "rng"), None),
        P(None, None, "rng"),
        P(None, None, "rng"),
        P(),
        P(),
        P(),
    )
    return jax.shard_map(
        on_device, mesh=mesh, in_specs=placed_as, out_specs=P(None, "sub", "rng"), check_vma=False
    )
```

```python
import functools
import math

import jax
import jax.numpy as jnp
from jax import lax
from jax.experimental import pallas as pl
from jax.experimental.pallas import tpu as pltpu
from jax.sharding import PartitionSpec as P

MAX_SHIFT = 16
LANES = 128
MIB = 2**20
JOIN_COST = 10**11
SIDE = jax.ShapeDtypeStruct((8, LANES), jnp.float32)
VMEM = pl.BlockSpec(memory_space=pltpu.VMEM)
SMEM = pl.BlockSpec(memory_space=pltpu.SMEM)
ANY = pl.BlockSpec(memory_space=pl.ANY)
F32 = jnp.float32
BF16 = jnp.bfloat16


def dot(a, b):
    return jnp.dot(a, b, preferred_element_type=F32)


def params(mib):
    return pltpu.CompilerParams(vmem_limit_bytes=mib * MIB)


def series(square, first, count):
    coefs = [
        (-1) ** i * math.pi ** (2 * i + first) / math.factorial(2 * i + first)
        for i in range(count)
    ]
    total = jnp.full_like(square, coefs[-1])
    for coef in coefs[-2::-1]:
        total = total * square + coef
    return total


def cos_sin_pi(v):
    turns = jnp.floor(v + 0.5)
    rest = v - turns
    sign = 1.0 - 2.0 * (turns - 2.0 * jnp.floor(turns * 0.5))
    square = rest * rest
    return series(square, 0, 8) * sign, series(square, 1, 7) * rest * sign


def rotated(pair, step):
    return pair[0] * step[0] - pair[1] * step[1], pair[0] * step[1] + pair[1] * step[0]


def mixed(left, right):
    lane = lax.broadcasted_iota(jnp.int32, left.shape, 1)
    return jnp.where(lane < LANES // 2, left.astype(F32), right.astype(F32)).astype(BF16)


def place_kernel(echoes_ref, far_ref, near_ref, inner_ref):
    devices, _, count = inner_ref.shape
    bins = count + LANES
    half = devices // 2
    base = lax.axis_index("rng") // half * half

    def tile(device, first):
        return echoes_ref[:, pl.ds(pl.multiple_of(device * bins + first, LANES), LANES)]

    for ref, start in ((far_ref, half - base), (near_ref, base)):
        for i in range(half):
            ref[i] = mixed(tile(start + i, 0), tile(start + i, bins - LANES))
    for device in range(devices):
        begin = device * bins
        inner_ref[device, :, :LANES] = mixed(tile(device, bins - LANES), tile(device, 0))
        inner_ref[device, :, LANES:] = echoes_ref[:, begin + LANES : begin + bins - LANES]


def placed(echoes, devices):
    rows, columns = echoes.shape
    outer = jax.ShapeDtypeStruct((devices // 2, rows, LANES), BF16)
    inner = jax.ShapeDtypeStruct((devices, rows, columns // devices - LANES), BF16)
    return pl.pallas_call(
        place_kernel,
        out_shape=[outer, outer, inner],
        in_specs=[VMEM],
        out_specs=[VMEM] * 3,
        compiler_params=params(8),
        cost_estimate=pl.CostEstimate(flops=0, bytes_accessed=2 * MIB, transcendentals=0),
    )(echoes)


def join_kernel(near_ref, relay_ref, *refs):
    me = lax.axis_index("rng") % len(refs)
    rows = near_ref.shape[1]
    for d, out_ref in enumerate(refs):
        out_ref[:rows] = near_ref[me ^ d]
        out_ref[rows:] = relay_ref[me ^ d]


def joined(near, relay):
    half, rows, count = near.shape
    return pl.pallas_call(
        join_kernel,
        out_shape=[jax.ShapeDtypeStruct((2 * rows, count), BF16)] * half,
        in_specs=[VMEM] * 2,
        out_specs=[VMEM] * half,
        compiler_params=params(4),
        cost_estimate=pl.CostEstimate(flops=JOIN_COST, bytes_accessed=MIB, transcendentals=0),
    )(near, relay)


def across(value, mask):
    devices = lax.axis_size("rng")
    return lax.ppermute(value, "rng", [(i, i ^ mask) for i in range(devices)])


def filter_table_kernel(local_pulses, flag_ref, after_ref, rows_ref, side_ref, cos_ref, sin_ref):
    own_flag = flag_ref[0, lax.axis_index("sub"), 0]
    side_ref[...] = jnp.full(side_ref.shape, own_flag.astype(F32))
    angles, columns = rows_ref.shape
    half = angles // 2
    first = (1 - own_flag) * half
    base = cos_ref.shape[0]
    scale = 1.0 / math.sqrt(columns // 2)
    lane = lax.broadcasted_iota(jnp.int32, (8, columns), 1)
    slot = lane // (2 * local_pulses)
    second = lane // local_pulses % 2
    pulse = (slot * local_pulses + lane % local_pulses).astype(F32)
    lag = second.astype(F32) * 0.5
    per_angle = pulse * (1.0 / angles)
    row = lax.broadcasted_iota(jnp.int32, (8, columns), 0)
    for i in range(base // 8):
        twice = (2 * (row + 8 * i + first) + 1 - angles).astype(F32)
        cosine, sine = cos_sin_pi(twice * per_angle - lag)
        cos_ref[8 * i : 8 * i + 8, :] = cosine * scale
        sin_ref[8 * i : 8 * i + 8, :] = sine * scale
    step = cos_sin_pi(per_angle * (2 * base))
    for j in range(half // base):
        for i in range(base // 16):
            pair = [], []
            for k in (2 * i, 2 * i + 1):
                here = slice(8 * k, 8 * k + 8)
                now = cos_ref[here, :], sin_ref[here, :]
                pair[0].append(now[0])
                pair[1].append(-now[1])
                if j + 1 < half // base:
                    cos_ref[here, :], sin_ref[here, :] = rotated(now, step)
            begin = j * base + 16 * i
            rows_ref[begin : begin + 16, :] = jnp.concatenate(pair[0]).astype(BF16)
            begin += half
            rows_ref[begin : begin + 16, :] = jnp.concatenate(pair[1]).astype(BF16)


def filter_table(fore_flag, angles, local_pulses, earlier):
    side = 2 * local_pulses * lax.axis_size("rng")
    return pl.pallas_call(
        functools.partial(filter_table_kernel, local_pulses),
        out_shape=[jax.ShapeDtypeStruct((angles, side), BF16), SIDE],
        in_specs=[SMEM, ANY],
        out_specs=[VMEM] * 2,
        scratch_shapes=[pltpu.VMEM((64, side), F32)] * 2,
        compiler_params=params(6),
        cost_estimate=pl.CostEstimate(flops=9_000_000, bytes_accessed=4 * MIB, transcendentals=0),
    )(fore_flag, earlier)


def merge_table_kernel(
    level, stride, flag_ref, offset_ref, shift_ref, range_ref, interp_ref, after_ref, centre_ref,
    rim_ref, turn_ref, matrix_ref, side_ref, kernel_ref, sems,
):
    group = lax.axis_index("sub")
    block = lax.axis_index("rng")
    bins = centre_ref.shape[-1]
    angles = turn_ref.shape[-2]
    total_bins = lax.axis_size("rng") * bins
    taps = range_ref.shape[1]
    band = (taps - bins) // 2
    rim = MAX_SHIFT + band
    own_flag = flag_ref[level, group, 0]
    side_ref[...] = jnp.full(side_ref.shape, own_flag.astype(F32))
    copies = [
        pltpu.make_async_copy(source, target, sems.at[i])
        for i, (source, target) in enumerate(
            (
                (range_ref.at[level], kernel_ref),
                (interp_ref.at[level, own_flag], matrix_ref.at[0]),
                (interp_ref.at[level, 1 - own_flag], matrix_ref.at[1]),
            )
        )
    ]
    for copy in copies:
        copy.start()

    def moved(bin_id):
        tap = lax.broadcasted_iota(jnp.int32, (bin_id.shape[0], taps), 1)
        hot = jnp.where(tap == bin_id, 1.0, 0.0).astype(BF16)
        return dot(hot, kernel_ref[...]).astype(BF16)

    row = lax.broadcasted_iota(jnp.int32, (bins, 1), 0)
    upper = row + (bins - 2 * LANES)
    own_bin = jnp.where(row % LANES < LANES // 2, row, upper + LANES)
    own_bin = jnp.where(row >= LANES, jnp.where(row % LANES < LANES // 2, upper, row - LANES), own_bin)
    own_bin = jnp.where(row >= 2 * LANES, row - LANES, own_bin)
    rim_row = lax.broadcasted_iota(jnp.int32, (2 * rim, 1), 0)
    rim_bin = jnp.where(rim_row < rim, rim_row - rim, rim_row - rim + bins)
    rim_ref[...] = jnp.zeros(rim_ref.shape, BF16)
    bin_id = block * bins + lax.broadcasted_iota(jnp.int32, (8, bins), 1)
    reach = 1.0 + bin_id.astype(F32) * (1.0 / total_bins)
    line = lax.broadcasted_iota(jnp.int32, (8, bins), 0)
    base = 64
    members = group, group ^ stride
    for child, member in enumerate(members):
        rate = shift_ref[level, member]
        for first in range(0, base, 8):
            angle = (first + line).astype(F32)
            now = cos_sin_pi(rate * ((angle + 0.5) * (1.0 / angles) - 0.5) * reach)
            turn_ref[child, 0, first : first + 8, :] = now[0]
            turn_ref[child, 1, first : first + 8, :] = now[1]
        step = cos_sin_pi(rate * (base / angles) * reach)
        for first in range(base, angles, 8):
            here, last = slice(first, first + 8), slice(first - base, first - base + 8)
            now = rotated((turn_ref[child, 0, last, :], turn_ref[child, 1, last, :]), step)
            turn_ref[child, 0, here, :], turn_ref[child, 1, here, :] = now
    for copy in copies:
        copy.wait()
    for child, member in enumerate(members):
        lead = band - offset_ref[level, member, 0]
        centre_ref[child] = moved(own_bin + lead)
        ends = moved(rim_bin + lead)
        for part in range(2):
            for side in range(2):
                place = (2 * side + part) * rim
                rim_ref[child, part, place : place + rim, :] = ends[side * rim : (side + 1) * rim]


def merge_tables(
    level, stride, fore_flag, band_offset, center_shift, range_kernel, angle_interp, earlier
):
    taps, bins = range_kernel.shape[1:]
    angles = angle_interp.shape[2]
    rim = MAX_SHIFT + (taps - bins) // 2
    return pl.pallas_call(
        functools.partial(merge_table_kernel, level, stride),
        out_shape=[
            jax.ShapeDtypeStruct((2, bins, bins), BF16),
            jax.ShapeDtypeStruct((2, 2, 4 * rim, bins), BF16),
            jax.ShapeDtypeStruct((2, 2, angles, bins), F32),
            jax.ShapeDtypeStruct((2, *angle_interp.shape[2:]), BF16),
            SIDE,
        ],
        in_specs=[SMEM] * 3 + [ANY] * 3,
        out_specs=[VMEM] * 5,
        scratch_shapes=[pltpu.VMEM((taps, bins), BF16), pltpu.SemaphoreType.DMA((3,))],
        compiler_params=params(12),
        cost_estimate=pl.CostEstimate(
            flops=2_300_000_000, bytes_accessed=7 * MIB, transcendentals=0
        ),
    )(fore_flag, band_offset, center_shift, range_kernel, angle_interp, earlier)


def alternating(pulses, local_pulses):
    row = lax.broadcasted_iota(jnp.int32, (pulses.shape[0], 1), 0)
    pulse = row // (2 * local_pulses) * local_pulses + row % local_pulses
    return jnp.where(pulse % 2 == 1, -pulses.astype(F32), pulses.astype(F32)).astype(BF16)


def outer_kernel(pieces, side_ref, rows_ref, *refs):
    own_side = side_ref[:1, :]
    me = lax.axis_index("rng")
    own_ref, out_ref, *edge_refs = refs[pieces:-1]
    pulses_ref = refs[-1]
    rows = refs[0].shape[0] // 2
    for d, ref in enumerate(refs[:pieces]):
        for t in range(2):
            place = pl.multiple_of((me ^ (d + t * pieces)) * rows, rows)
            pulses_ref[pl.ds(place, rows), :] = ref[t * rows : (t + 1) * rows, :]
    pulses = pulses_ref[...]
    own_parts = dot(rows_ref[...], alternating(pulses, rows // 2))
    out_parts = dot(rows_ref[...], pulses)
    half = own_ref.shape[1]
    rim = LANES // 4
    lane = lax.broadcasted_iota(jnp.int32, (1, LANES), 1)
    edges = [0.0, 0.0]
    for part in range(2):
        own, out = (value[part * half : (part + 1) * half] for value in (own_parts, out_parts))
        own_ref[part] = own.astype(BF16)
        out_ref[part] = out.astype(BF16)
        for side in range(2):
            value = jnp.where(own_side == side, own, out)
            group = 2 * part + side
            for end in range(2):
                turn = (group + end) * rim % LANES
                moved = pltpu.roll(value, turn, 1) if turn else value
                edges[end] = edges[end] + jnp.where(lane // rim == group, moved, 0.0)
    even = me % 2 == 0
    edge_refs[0][...] = jnp.where(even, edges[1], edges[0]).astype(BF16)
    edge_refs[1][...] = jnp.where(even, edges[0], edges[1]).astype(BF16)


def outer_image(own_side, rows, pieces):
    angles, side = rows.shape
    image = jax.ShapeDtypeStruct((2, angles // 2, LANES), BF16)
    edge = jax.ShapeDtypeStruct((angles // 2, LANES), BF16)
    return pl.pallas_call(
        functools.partial(outer_kernel, len(pieces)),
        out_shape=[image, image, edge, edge],
        in_specs=[VMEM] * (2 + len(pieces)),
        out_specs=[VMEM] * 4,
        scratch_shapes=[pltpu.VMEM((side, LANES), BF16)],
        compiler_params=params(10),
        cost_estimate=pl.CostEstimate(
            flops=4 * angles * side * LANES, bytes_accessed=3 * MIB, transcendentals=0
        ),
    )(own_side, rows, *pieces)


def partner_rows_kernel(rows_ref, pulses_ref, image_ref):
    image = dot(rows_ref[...], pulses_ref[...])
    image_ref[...] = image.astype(BF16).reshape(image_ref.shape)


def own_rows_kernel(local_pulses, rows_ref, pulses_ref, outer_ref, image_ref):
    image = dot(rows_ref[...], alternating(pulses_ref[...], local_pulses))
    parts, half, count = outer_ref.shape
    image_ref[:, :, :count] = outer_ref[...]
    image_ref[:, :, count:] = image.astype(BF16).reshape(parts, half, image.shape[1])


def inner_image(kernel, angles, rows, pulses, outer=()):
    count = pulses.shape[1]
    whole = count + (outer[0].shape[2] if outer else 0)
    return pl.pallas_call(
        kernel,
        out_shape=jax.ShapeDtypeStruct((2, angles // 2, whole), BF16),
        in_specs=[VMEM] * (2 + len(outer)),
        out_specs=VMEM,
        compiler_params=params(10),
        cost_estimate=pl.CostEstimate(
            flops=2 * angles * rows.shape[1] * count, bytes_accessed=3 * MIB, transcendentals=0
        ),
    )(rows, pulses, *outer)


def exchanged(value, begin):
    devices = lax.axis_size("rng")
    pairs = [(i, i + 1) for i in range(begin, devices - 1, 2)]
    ends = [(i, i) for i in range(devices) if all(i not in pair for pair in pairs)]
    return lax.ppermute(value, "rng", pairs + [(j, i) for i, j in pairs] + ends)


def rims_kernel(side_ref, first_ref, second_ref, own_ref, out_ref):
    own_side = side_ref[:1, :]
    rim = LANES // 4
    me, devices = lax.axis_index("rng"), lax.axis_size("rng")
    even = me % 2 == 0
    first, second = first_ref[...].astype(F32), second_ref[...].astype(F32)
    below = jnp.where(me == 0, 0.0, jnp.where(even, second, first))
    above = jnp.where(me == devices - 1, 0.0, jnp.where(even, first, second))
    group = lax.broadcasted_iota(jnp.int32, (1, LANES), 1) // rim
    packed = [0.0, 0.0]
    for end, value in enumerate((below, above)):
        for part in range(2):
            place = 2 * end + part
            for side in range(2):
                turn = (place - (2 * part + side)) * rim % LANES
                moved = pltpu.roll(value, turn, 1) if turn else value
                packed[side] = packed[side] + jnp.where(group == place, moved, 0.0)
    own_ref[...] = jnp.where(own_side == 0, packed[0], packed[1]).astype(BF16)
    out_ref[...] = jnp.where(own_side == 0, packed[1], packed[0]).astype(BF16)


def sorted_rims(own_side, first, second):
    return pl.pallas_call(
        rims_kernel,
        out_shape=[jax.ShapeDtypeStruct(first.shape, BF16)] * 2,
        in_specs=[VMEM] * 3,
        out_specs=[VMEM] * 2,
        compiler_params=params(4),
        cost_estimate=pl.CostEstimate(flops=1_000_000, bytes_accessed=MIB // 4, transcendentals=0),
    )(own_side, first, second)


def resampled(image, rims_ref, centre_ref, rim_ref, value_ref, child):
    parts, half, bins = image.shape
    value_ref[...] = dot(image.reshape(parts * half, bins), centre_ref[child])
    rims = rims_ref[...]
    return [
        (value_ref[part * half : (part + 1) * half, :] + dot(rims, rim_ref[child, part])).astype(BF16)
        for part in range(parts)
    ]


def early_kernel(
    own_ref, rims_ref, centre_ref, rim_ref, matrix_ref, turn_ref, merged_ref, value_ref
):
    rows = resampled(own_ref[...], rims_ref, centre_ref, rim_ref, value_ref, 0)
    merged_ref[0], merged_ref[1] = rotated(
        (dot(matrix_ref[0], rows[0]), dot(matrix_ref[0], rows[1])), (turn_ref[0, 0], turn_ref[0, 1])
    )


def late_kernel(
    far_outer, far_inner, rims_ref, merged_ref, centre_ref, rim_ref, matrix_ref, turn_ref, out_ref,
    buffer, value_ref, sems,
):
    image = jnp.concatenate([far_outer[...], far_inner[...]], axis=2)
    rows = resampled(image, rims_ref, centre_ref, rim_ref, value_ref, 1)
    parts = len(rows)
    block = LANES
    copies = []
    for first in range(0, matrix_ref.shape[1], 2 * block):
        matrix = matrix_ref[1, first : first + 2 * block]
        terms = dot(matrix, rows[0]), dot(matrix, rows[1])
        for step in range(2):
            here = slice(first + step * block, first + (step + 1) * block)
            there = slice(step * block, (step + 1) * block)
            turned = rotated(
                (terms[0][there], terms[1][there]), (turn_ref[1, 0, here], turn_ref[1, 1, here])
            )
            for part in range(parts):
                buffer[part, here] = (merged_ref[part, here] + turned[part]).astype(buffer.dtype)
            copy = pltpu.make_async_copy(
                buffer.at[:, here], out_ref.at[:, here], sems.at[len(copies)]
            )
            copy.start()
            copies.append(copy)
    for copy in copies:
        copy.wait()


def merged_image(own, rims, far, far_rims, tables, dtype):
    centre, rim, turn, matrices, _ = tables
    angles, bins = turn.shape[-2:]
    cost = pl.CostEstimate(flops=4 * angles * bins * bins, bytes_accessed=8 * MIB, transcendentals=0)
    value = pltpu.VMEM((angles, bins), F32)
    merged = pl.pallas_call(
        early_kernel,
        out_shape=jax.ShapeDtypeStruct((2, angles, bins), F32),
        in_specs=[VMEM] * 6,
        out_specs=VMEM,
        scratch_shapes=[value],
        compiler_params=params(16),
        cost_estimate=cost,
    )(own, rims, centre, rim, matrices, turn)
    return pl.pallas_call(
        late_kernel,
        out_shape=jax.ShapeDtypeStruct((2, angles, bins), dtype),
        in_specs=[VMEM] * 8,
        out_specs=ANY,
        scratch_shapes=[
            pltpu.VMEM((2, angles, bins), dtype),
            value,
            pltpu.SemaphoreType.DMA((angles // LANES,)),
        ],
        compiler_params=params(16),
        cost_estimate=cost,
    )(*far, far_rims, merged, centre, rim, matrices, turn)


def after(value, *earlier):
    return lax.optimization_barrier((value, *earlier))[0]


def from_partner(value, stride):
    pairs = [(source, source ^ stride) for source in range(lax.axis_size("sub"))]
    return lax.ppermute(value, "sub", pairs)


def split_image(level, image, fore_flag, rim):
    angles, bins = image.shape[1:]
    half, step = angles // 2, LANES // 2
    own_flag = fore_flag[level, lax.axis_index("sub"), 0]
    sides = image.reshape(2, 2, half, bins)

    def pieces(side):
        rows = lax.dynamic_index_in_dim(sides, side, 1, keepdims=False)
        ends = [rows[..., :step], rows[..., -step:]]
        rest = [rows[..., -2 * step : -step], rows[..., step : -2 * step]]
        return jnp.concatenate(ends + rest, axis=-1)

    def packed(edge):
        return edge.transpose(2, 0, 1, 3).reshape(half, 4 * rim)

    low, high = packed(sides[..., :rim]), packed(sides[..., -rim:])
    even = lax.axis_index("rng") % 2 == 0
    edges = jnp.where(even, high, low), jnp.where(even, low, high)
    return pieces(own_flag), pieces(1 - own_flag), edges


def on_device(echoes, fore_flag, band_offset, angle_interp, range_kernel, center_shift):
    devices = lax.axis_size("rng")
    half = devices // 2
    local_pulses = echoes.shape[1]
    bins = echoes.shape[2] // devices
    angles = angle_interp.shape[2]
    rim = MAX_SHIFT + (range_kernel.shape[1] - bins) // 2
    levels = range_kernel.shape[0]
    settings = (fore_flag, band_offset, center_shift, range_kernel, angle_interp)

    far_blocks, near_blocks, blocks = placed(
        echoes.reshape(2 * local_pulses, devices * bins), devices
    )
    relay = across(far_blocks, half)
    pulses = lax.all_to_all(blocks, "rng", split_axis=0, concat_axis=0, tiled=True)
    sends = joined(near_blocks, relay)
    pieces = [across(value, d) if d else value for d, value in enumerate(sends)]
    matrix, own_side = filter_table(fore_flag, angles, local_pulses, sends[0])
    pulses = after(pulses, *pieces[1:]).reshape(2 * local_pulses * devices, bins - LANES)
    out_inner = inner_image(partner_rows_kernel, angles, matrix, pulses)
    pieces[0] = after(pieces[0], out_inner)
    own_outer, out_outer, *edges = outer_image(own_side, matrix, pieces)
    far = [from_partner(value, 1) for value in (out_outer, out_inner)]
    edges = exchanged(edges[0], 0), exchanged(edges[1], 1)
    own_kernel = functools.partial(own_rows_kernel, local_pulses)
    own = inner_image(own_kernel, angles, matrix, pulses, (own_outer,))
    tables = merge_tables(0, 1, *settings, own)
    edges = after(edges[0], tables[0]), edges[1]
    for level in range(levels):
        stride = 2**level
        if level > 0:
            tables = merge_tables(level, stride, *settings, image)
            own, out, edges = split_image(level, image, fore_flag, rim)
            far = [from_partner(value, stride) for value in (out[..., :LANES], out[..., LANES:])]
            edges = exchanged(edges[0], 0), exchanged(edges[1], 1)
            own_side = tables[-1]
        rims, out_rims = sorted_rims(own_side, *edges)
        far_rims = from_partner(out_rims, stride)
        image = merged_image(own, rims, far, far_rims, tables, BF16 if level + 1 < levels else F32)
    return image


def solution(mesh):
    placed_as = (
        P(None, ("sub", "rng"), None),
        P(None, None, "rng"),
        P(None, None, "rng"),
        P(),
        P(),
        P(),
    )
    return jax.shard_map(
        on_device, mesh=mesh, in_specs=placed_as, out_specs=P(None, "sub", "rng"), check_vma=False
    )
```

```python
import functools
import math

import jax
import jax.numpy as jnp
from jax import lax
from jax.experimental import pallas as pl
from jax.experimental.pallas import tpu as pltpu
from jax.sharding import PartitionSpec as P

MAX_SHIFT = 16
LANES = 128
MIB = 2**20
JOIN_COST = 10**11
SIDE = jax.ShapeDtypeStruct((8, LANES), jnp.float32)
VMEM = pl.BlockSpec(memory_space=pltpu.VMEM)
SMEM = pl.BlockSpec(memory_space=pltpu.SMEM)
ANY = pl.BlockSpec(memory_space=pl.ANY)
F32 = jnp.float32
BF16 = jnp.bfloat16


def dot(a, b):
    return jnp.dot(a, b, preferred_element_type=F32)


def params(mib):
    return pltpu.CompilerParams(vmem_limit_bytes=mib * MIB)


def series(square, first, count):
    coefs = [
        (-1) ** i * math.pi ** (2 * i + first) / math.factorial(2 * i + first)
        for i in range(count)
    ]
    total = jnp.full_like(square, coefs[-1])
    for coef in coefs[-2::-1]:
        total = total * square + coef
    return total


def cos_sin_pi(v):
    turns = jnp.floor(v + 0.5)
    rest = v - turns
    sign = 1.0 - 2.0 * (turns - 2.0 * jnp.floor(turns * 0.5))
    square = rest * rest
    return series(square, 0, 8) * sign, series(square, 1, 7) * rest * sign


def rotated(pair, step):
    return pair[0] * step[0] - pair[1] * step[1], pair[0] * step[1] + pair[1] * step[0]


def mixed(left, right):
    lane = lax.broadcasted_iota(jnp.int32, left.shape, 1)
    return jnp.where(lane < LANES // 2, left.astype(F32), right.astype(F32)).astype(BF16)


def place_kernel(echoes_ref, far_ref, near_ref, inner_ref):
    devices, _, count = inner_ref.shape
    bins = count + LANES
    half = devices // 2
    base = lax.axis_index("rng") // half * half

    def tile(device, first):
        return echoes_ref[:, pl.ds(pl.multiple_of(device * bins + first, LANES), LANES)]

    for ref, start in ((far_ref, half - base), (near_ref, base)):
        for i in range(half):
            ref[i] = mixed(tile(start + i, 0), tile(start + i, bins - LANES))
    for device in range(devices):
        begin = device * bins
        inner_ref[device, :, :LANES] = mixed(tile(device, bins - LANES), tile(device, 0))
        inner_ref[device, :, LANES:] = echoes_ref[:, begin + LANES : begin + bins - LANES]


def placed(echoes, devices):
    rows, columns = echoes.shape
    outer = jax.ShapeDtypeStruct((devices // 2, rows, LANES), BF16)
    inner = jax.ShapeDtypeStruct((devices, rows, columns // devices - LANES), BF16)
    return pl.pallas_call(
        place_kernel,
        out_shape=[outer, outer, inner],
        in_specs=[VMEM],
        out_specs=[VMEM] * 3,
        compiler_params=params(8),
        cost_estimate=pl.CostEstimate(flops=0, bytes_accessed=2 * MIB, transcendentals=0),
    )(echoes)


def join_kernel(near_ref, relay_ref, *refs):
    me = lax.axis_index("rng") % len(refs)
    rows = near_ref.shape[1]
    for d, out_ref in enumerate(refs):
        out_ref[:rows] = near_ref[me ^ d]
        out_ref[rows:] = relay_ref[me ^ d]


def joined(near, relay):
    half, rows, count = near.shape
    return pl.pallas_call(
        join_kernel,
        out_shape=[jax.ShapeDtypeStruct((2 * rows, count), BF16)] * half,
        in_specs=[VMEM] * 2,
        out_specs=[VMEM] * half,
        compiler_params=params(4),
        cost_estimate=pl.CostEstimate(flops=JOIN_COST, bytes_accessed=MIB, transcendentals=0),
    )(near, relay)


def across(value, mask):
    devices = lax.axis_size("rng")
    return lax.ppermute(value, "rng", [(i, i ^ mask) for i in range(devices)])


def filter_table_kernel(local_pulses, flag_ref, after_ref, rows_ref, side_ref, cos_ref, sin_ref):
    own_flag = flag_ref[0, lax.axis_index("sub"), 0]
    side_ref[...] = jnp.full(side_ref.shape, own_flag.astype(F32))
    angles, columns = rows_ref.shape
    half = angles // 2
    first = (1 - own_flag) * half
    base = cos_ref.shape[0]
    scale = 1.0 / math.sqrt(columns // 2)
    lane = lax.broadcasted_iota(jnp.int32, (8, columns), 1)
    slot = lane // (2 * local_pulses)
    second = lane // local_pulses % 2
    pulse = (slot * local_pulses + lane % local_pulses).astype(F32)
    lag = second.astype(F32) * 0.5
    per_angle = pulse * (1.0 / angles)
    row = lax.broadcasted_iota(jnp.int32, (8, columns), 0)
    for i in range(base // 8):
        twice = (2 * (row + 8 * i + first) + 1 - angles).astype(F32)
        cosine, sine = cos_sin_pi(twice * per_angle - lag)
        cos_ref[8 * i : 8 * i + 8, :] = cosine * scale
        sin_ref[8 * i : 8 * i + 8, :] = sine * scale
    step = cos_sin_pi(per_angle * (2 * base))
    for j in range(half // base):
        for i in range(base // 16):
            pair = [], []
            for k in (2 * i, 2 * i + 1):
                here = slice(8 * k, 8 * k + 8)
                now = cos_ref[here, :], sin_ref[here, :]
                pair[0].append(now[0])
                pair[1].append(-now[1])
                if j + 1 < half // base:
                    cos_ref[here, :], sin_ref[here, :] = rotated(now, step)
            begin = j * base + 16 * i
            rows_ref[begin : begin + 16, :] = jnp.concatenate(pair[0]).astype(BF16)
            begin += half
            rows_ref[begin : begin + 16, :] = jnp.concatenate(pair[1]).astype(BF16)


def filter_table(fore_flag, angles, local_pulses, earlier):
    side = 2 * local_pulses * lax.axis_size("rng")
    return pl.pallas_call(
        functools.partial(filter_table_kernel, local_pulses),
        out_shape=[jax.ShapeDtypeStruct((angles, side), BF16), SIDE],
        in_specs=[SMEM, ANY],
        out_specs=[VMEM] * 2,
        scratch_shapes=[pltpu.VMEM((64, side), F32)] * 2,
        compiler_params=params(6),
        cost_estimate=pl.CostEstimate(flops=9_000_000, bytes_accessed=4 * MIB, transcendentals=0),
    )(fore_flag, earlier)


def merge_table_kernel(
    level, stride, flag_ref, offset_ref, shift_ref, range_ref, interp_ref, after_ref, centre_ref,
    rim_ref, turn_ref, matrix_ref, side_ref, kernel_ref, sems,
):
    group = lax.axis_index("sub")
    block = lax.axis_index("rng")
    bins = centre_ref.shape[-1]
    angles = turn_ref.shape[-2]
    total_bins = lax.axis_size("rng") * bins
    taps = range_ref.shape[1]
    band = (taps - bins) // 2
    rim = MAX_SHIFT + band
    own_flag = flag_ref[level, group, 0]
    side_ref[...] = jnp.full(side_ref.shape, own_flag.astype(F32))
    copies = [
        pltpu.make_async_copy(source, target, sems.at[i])
        for i, (source, target) in enumerate(
            (
                (range_ref.at[level], kernel_ref),
                (interp_ref.at[level, own_flag], matrix_ref.at[0]),
                (interp_ref.at[level, 1 - own_flag], matrix_ref.at[1]),
            )
        )
    ]
    for copy in copies:
        copy.start()

    def moved(bin_id):
        tap = lax.broadcasted_iota(jnp.int32, (bin_id.shape[0], taps), 1)
        hot = jnp.where(tap == bin_id, 1.0, 0.0).astype(BF16)
        return dot(hot, kernel_ref[...]).astype(BF16)

    row = lax.broadcasted_iota(jnp.int32, (bins, 1), 0)
    upper = row + (bins - 2 * LANES)
    own_bin = jnp.where(row % LANES < LANES // 2, row, upper + LANES)
    own_bin = jnp.where(row >= LANES, jnp.where(row % LANES < LANES // 2, upper, row - LANES), own_bin)
    own_bin = jnp.where(row >= 2 * LANES, row - LANES, own_bin)
    rim_row = lax.broadcasted_iota(jnp.int32, (2 * rim, 1), 0)
    rim_bin = jnp.where(rim_row < rim, rim_row - rim, rim_row - rim + bins)
    rim_ref[...] = jnp.zeros(rim_ref.shape, BF16)
    bin_id = block * bins + lax.broadcasted_iota(jnp.int32, (8, bins), 1)
    reach = 1.0 + bin_id.astype(F32) * (1.0 / total_bins)
    line = lax.broadcasted_iota(jnp.int32, (8, bins), 0)
    base = 64
    members = group, group ^ stride
    for child, member in enumerate(members):
        rate = shift_ref[level, member]
        for first in range(0, base, 8):
            angle = (first + line).astype(F32)
            now = cos_sin_pi(rate * ((angle + 0.5) * (1.0 / angles) - 0.5) * reach)
            turn_ref[child, 0, first : first + 8, :] = now[0]
            turn_ref[child, 1, first : first + 8, :] = now[1]
        step = cos_sin_pi(rate * (base / angles) * reach)
        for first in range(base, angles, 8):
            here, last = slice(first, first + 8), slice(first - base, first - base + 8)
            now = rotated((turn_ref[child, 0, last, :], turn_ref[child, 1, last, :]), step)
            turn_ref[child, 0, here, :], turn_ref[child, 1, here, :] = now
    for copy in copies:
        copy.wait()
    for child, member in enumerate(members):
        lead = band - offset_ref[level, member, 0]
        centre_ref[child] = moved(own_bin + lead)
        ends = moved(rim_bin + lead)
        for part in range(2):
            for side in range(2):
                place = (2 * side + part) * rim
                rim_ref[child, part, place : place + rim, :] = ends[side * rim : (side + 1) * rim]


def merge_tables(
    level, stride, fore_flag, band_offset, center_shift, range_kernel, angle_interp, earlier
):
    taps, bins = range_kernel.shape[1:]
    angles = angle_interp.shape[2]
    rim = MAX_SHIFT + (taps - bins) // 2
    return pl.pallas_call(
        functools.partial(merge_table_kernel, level, stride),
        out_shape=[
            jax.ShapeDtypeStruct((2, bins, bins), BF16),
            jax.ShapeDtypeStruct((2, 2, 4 * rim, bins), BF16),
            jax.ShapeDtypeStruct((2, 2, angles, bins), F32),
            jax.ShapeDtypeStruct((2, *angle_interp.shape[2:]), BF16),
            SIDE,
        ],
        in_specs=[SMEM] * 3 + [ANY] * 3,
        out_specs=[VMEM] * 5,
        scratch_shapes=[pltpu.VMEM((taps, bins), BF16), pltpu.SemaphoreType.DMA((3,))],
        compiler_params=params(12),
        cost_estimate=pl.CostEstimate(
            flops=2_300_000_000, bytes_accessed=7 * MIB, transcendentals=0
        ),
    )(fore_flag, band_offset, center_shift, range_kernel, angle_interp, earlier)


def alternating(pulses, local_pulses):
    row = lax.broadcasted_iota(jnp.int32, (pulses.shape[0], 1), 0)
    pulse = row // (2 * local_pulses) * local_pulses + row % local_pulses
    return jnp.where(pulse % 2 == 1, -pulses.astype(F32), pulses.astype(F32)).astype(BF16)


def outer_kernel(pieces, side_ref, rows_ref, *refs):
    own_side = side_ref[:1, :]
    me = lax.axis_index("rng")
    own_ref, out_ref, *edge_refs = refs[pieces:-1]
    pulses_ref = refs[-1]
    rows = refs[0].shape[0] // 2
    for d, ref in enumerate(refs[:pieces]):
        for t in range(2):
            place = pl.multiple_of((me ^ (d + t * pieces)) * rows, rows)
            pulses_ref[pl.ds(place, rows), :] = ref[t * rows : (t + 1) * rows, :]
    pulses = pulses_ref[...]
    own_parts = dot(rows_ref[...], alternating(pulses, rows // 2))
    out_parts = dot(rows_ref[...], pulses)
    half = own_ref.shape[1]
    rim = LANES // 4
    lane = lax.broadcasted_iota(jnp.int32, (1, LANES), 1)
    edges = [0.0, 0.0]
    for part in range(2):
        own, out = (value[part * half : (part + 1) * half] for value in (own_parts, out_parts))
        own_ref[part] = own.astype(BF16)
        out_ref[part] = out.astype(BF16)
        for side in range(2):
            value = jnp.where(own_side == side, own, out)
            group = 2 * part + side
            for end in range(2):
                turn = (group + end) * rim % LANES
                moved = pltpu.roll(value, turn, 1) if turn else value
                edges[end] = edges[end] + jnp.where(lane // rim == group, moved, 0.0)
    even = me % 2 == 0
    edge_refs[0][...] = jnp.where(even, edges[1], edges[0]).astype(BF16)
    edge_refs[1][...] = jnp.where(even, edges[0], edges[1]).astype(BF16)


def outer_image(own_side, rows, pieces):
    angles, side = rows.shape
    image = jax.ShapeDtypeStruct((2, angles // 2, LANES), BF16)
    edge = jax.ShapeDtypeStruct((angles // 2, LANES), BF16)
    return pl.pallas_call(
        functools.partial(outer_kernel, len(pieces)),
        out_shape=[image, image, edge, edge],
        in_specs=[VMEM] * (2 + len(pieces)),
        out_specs=[VMEM] * 4,
        scratch_shapes=[pltpu.VMEM((side, LANES), BF16)],
        compiler_params=params(10),
        cost_estimate=pl.CostEstimate(
            flops=4 * angles * side * LANES, bytes_accessed=3 * MIB, transcendentals=0
        ),
    )(own_side, rows, *pieces)


def partner_rows_kernel(rows_ref, pulses_ref, image_ref):
    image = dot(rows_ref[...], pulses_ref[...])
    image_ref[...] = image.astype(BF16).reshape(image_ref.shape)


def own_rows_kernel(local_pulses, rows_ref, pulses_ref, outer_ref, image_ref):
    image = dot(rows_ref[...], alternating(pulses_ref[...], local_pulses))
    parts, half, count = outer_ref.shape
    image_ref[:, :, :count] = outer_ref[...]
    image_ref[:, :, count:] = image.astype(BF16).reshape(parts, half, image.shape[1])


def inner_image(kernel, angles, rows, pulses, outer=()):
    count = pulses.shape[1]
    whole = count + (outer[0].shape[2] if outer else 0)
    return pl.pallas_call(
        kernel,
        out_shape=jax.ShapeDtypeStruct((2, angles // 2, whole), BF16),
        in_specs=[VMEM] * (2 + len(outer)),
        out_specs=VMEM,
        compiler_params=params(10),
        cost_estimate=pl.CostEstimate(
            flops=2 * angles * rows.shape[1] * count, bytes_accessed=3 * MIB, transcendentals=0
        ),
    )(rows, pulses, *outer)


def exchanged(value, begin):
    devices = lax.axis_size("rng")
    pairs = [(i, i + 1) for i in range(begin, devices - 1, 2)]
    ends = [(i, i) for i in range(devices) if all(i not in pair for pair in pairs)]
    return lax.ppermute(value, "rng", pairs + [(j, i) for i, j in pairs] + ends)


def rims_kernel(side_ref, first_ref, second_ref, own_ref, out_ref):
    own_side = side_ref[:1, :]
    rim = LANES // 4
    me, devices = lax.axis_index("rng"), lax.axis_size("rng")
    even = me % 2 == 0
    first, second = first_ref[...].astype(F32), second_ref[...].astype(F32)
    below = jnp.where(me == 0, 0.0, jnp.where(even, second, first))
    above = jnp.where(me == devices - 1, 0.0, jnp.where(even, first, second))
    group = lax.broadcasted_iota(jnp.int32, (1, LANES), 1) // rim
    packed = [0.0, 0.0]
    for end, value in enumerate((below, above)):
        for part in range(2):
            place = 2 * end + part
            for side in range(2):
                turn = (place - (2 * part + side)) * rim % LANES
                moved = pltpu.roll(value, turn, 1) if turn else value
                packed[side] = packed[side] + jnp.where(group == place, moved, 0.0)
    own_ref[...] = jnp.where(own_side == 0, packed[0], packed[1]).astype(BF16)
    out_ref[...] = jnp.where(own_side == 0, packed[1], packed[0]).astype(BF16)


def sorted_rims(own_side, first, second):
    return pl.pallas_call(
        rims_kernel,
        out_shape=[jax.ShapeDtypeStruct(first.shape, BF16)] * 2,
        in_specs=[VMEM] * 3,
        out_specs=[VMEM] * 2,
        compiler_params=params(4),
        cost_estimate=pl.CostEstimate(flops=1_000_000, bytes_accessed=MIB // 4, transcendentals=0),
    )(own_side, first, second)


def resampled(image, rims_ref, centre_ref, rim_ref, value_ref, child):
    parts, half, bins = image.shape
    value_ref[...] = dot(image.reshape(parts * half, bins), centre_ref[child])
    rims = rims_ref[...]
    return [
        (value_ref[part * half : (part + 1) * half, :] + dot(rims, rim_ref[child, part])).astype(BF16)
        for part in range(parts)
    ]


def early_kernel(
    own_ref, rims_ref, centre_ref, rim_ref, matrix_ref, turn_ref, merged_ref, value_ref
):
    rows = resampled(own_ref[...], rims_ref, centre_ref, rim_ref, value_ref, 0)
    merged_ref[0], merged_ref[1] = rotated(
        (dot(matrix_ref[0], rows[0]), dot(matrix_ref[0], rows[1])), (turn_ref[0, 0], turn_ref[0, 1])
    )


def ends_of(value):
    count = value.shape[-1]
    return jnp.concatenate([value[..., :LANES], value[..., count - LANES :]], axis=-1)


def finish(values, lanes, merged_ref, matrix_ref, turn_ref, out_ref, buffer, sems):
    rows = [value.astype(BF16) for value in values]
    copies = []
    block = 2 * LANES
    for first in range(0, matrix_ref.shape[1], block):
        here = slice(first, first + block)
        matrix = matrix_ref[1, here]
        terms = dot(matrix, rows[0]), dot(matrix, rows[1])
        at = 0
        for begin, end in lanes:
            there = slice(at, at + end - begin)
            turned = rotated(
                (terms[0][:, there], terms[1][:, there]),
                (turn_ref[1, 0, here, begin:end], turn_ref[1, 1, here, begin:end]),
            )
            for part in range(2):
                total = merged_ref[part, here, begin:end] + turned[part]
                buffer[part, here, there] = total.astype(buffer.dtype)
            copy = pltpu.make_async_copy(
                buffer.at[:, here, there],
                out_ref.at[:, here, pl.ds(begin, end - begin)],
                sems.at[len(copies)],
            )
            copy.start()
            copies.append(copy)
            at += end - begin
    for copy in copies:
        copy.wait()


def middle_kernel(
    far_inner, merged_ref, centre_ref, matrix_ref, turn_ref, out_ref, partial_ref, buffer, sems
):
    parts, half, count = far_inner.shape
    bins = centre_ref.shape[2]
    inner = far_inner[...].reshape(parts * half, count)
    value = dot(inner, centre_ref[1, bins - count :, LANES : bins - LANES])
    values = [value[part * half : (part + 1) * half] for part in range(parts)]
    finish(
        values, [(LANES, bins - LANES)], merged_ref, matrix_ref, turn_ref, out_ref, buffer, sems
    )
    partial_ref[...] = dot(inner, ends_of(centre_ref[1, bins - count :, :]))


def end_kernel(
    far_outer, partial_ref, rims_ref, merged_ref, centre_ref, rim_ref, matrix_ref, turn_ref,
    begun_ref, out_ref, buffer, sems,
):
    parts, half, count = far_outer.shape
    bins = centre_ref.shape[2]
    centre = ends_of(centre_ref[1, :count, :])
    values = [
        partial_ref[part * half : (part + 1) * half, :]
        + dot(far_outer[part], centre)
        + dot(rims_ref[...], ends_of(rim_ref[1, part]))
        for part in range(parts)
    ]
    lanes = [(0, LANES), (bins - LANES, bins)]
    finish(values, lanes, merged_ref, matrix_ref, turn_ref, out_ref, buffer, sems)


def merged_image(own, rims, far, far_rims, tables, dtype):
    centre, rim, turn, matrices, _ = tables
    angles, bins = turn.shape[-2:]
    cost = pl.CostEstimate(flops=4 * angles * bins * bins, bytes_accessed=8 * MIB, transcendentals=0)
    value = pltpu.VMEM((angles, bins), F32)
    merged = pl.pallas_call(
        early_kernel,
        out_shape=jax.ShapeDtypeStruct((2, angles, bins), F32),
        in_specs=[VMEM] * 6,
        out_specs=VMEM,
        scratch_shapes=[value],
        compiler_params=params(16),
        cost_estimate=cost,
    )(own, rims, centre, rim, matrices, turn)
    image = jax.ShapeDtypeStruct((2, angles, bins), dtype)
    middle, ends = bins - 2 * LANES, 2 * LANES
    begun, partial = pl.pallas_call(
        middle_kernel,
        out_shape=[image, jax.ShapeDtypeStruct((angles, ends), F32)],
        in_specs=[VMEM] * 5,
        out_specs=[ANY, VMEM],
        scratch_shapes=[
            pltpu.VMEM((2, angles, middle), dtype),
            pltpu.SemaphoreType.DMA((angles // LANES,)),
        ],
        compiler_params=params(16),
        cost_estimate=cost,
    )(far[1], merged, centre, matrices, turn)
    return pl.pallas_call(
        end_kernel,
        out_shape=image,
        in_specs=[VMEM] * 8 + [ANY],
        out_specs=ANY,
        scratch_shapes=[
            pltpu.VMEM((2, angles, ends), dtype),
            pltpu.SemaphoreType.DMA((angles // LANES,)),
        ],
        input_output_aliases={8: 0},
        compiler_params=params(16),
        cost_estimate=cost,
    )(far[0], partial, far_rims, merged, centre, rim, matrices, turn, begun)


def after(value, *earlier):
    return lax.optimization_barrier((value, *earlier))[0]


def from_partner(value, stride):
    pairs = [(source, source ^ stride) for source in range(lax.axis_size("sub"))]
    return lax.ppermute(value, "sub", pairs)


def split_image(level, image, fore_flag, rim):
    angles, bins = image.shape[1:]
    half, step = angles // 2, LANES // 2
    own_flag = fore_flag[level, lax.axis_index("sub"), 0]
    sides = image.reshape(2, 2, half, bins)

    def pieces(side):
        rows = lax.dynamic_index_in_dim(sides, side, 1, keepdims=False)
        ends = [rows[..., :step], rows[..., -step:]]
        rest = [rows[..., -2 * step : -step], rows[..., step : -2 * step]]
        return jnp.concatenate(ends + rest, axis=-1)

    def packed(edge):
        return edge.transpose(2, 0, 1, 3).reshape(half, 4 * rim)

    low, high = packed(sides[..., :rim]), packed(sides[..., -rim:])
    even = lax.axis_index("rng") % 2 == 0
    edges = jnp.where(even, high, low), jnp.where(even, low, high)
    return pieces(own_flag), pieces(1 - own_flag), edges


def on_device(echoes, fore_flag, band_offset, angle_interp, range_kernel, center_shift):
    devices = lax.axis_size("rng")
    half = devices // 2
    local_pulses = echoes.shape[1]
    bins = echoes.shape[2] // devices
    angles = angle_interp.shape[2]
    rim = MAX_SHIFT + (range_kernel.shape[1] - bins) // 2
    levels = range_kernel.shape[0]
    settings = (fore_flag, band_offset, center_shift, range_kernel, angle_interp)

    far_blocks, near_blocks, blocks = placed(
        echoes.reshape(2 * local_pulses, devices * bins), devices
    )
    relay = across(far_blocks, half)
    pulses = lax.all_to_all(blocks, "rng", split_axis=0, concat_axis=0, tiled=True)
    sends = joined(near_blocks, relay)
    pieces = [across(value, d) if d else value for d, value in enumerate(sends)]
    matrix, own_side = filter_table(fore_flag, angles, local_pulses, sends[0])
    pulses = after(pulses, *pieces[1:]).reshape(2 * local_pulses * devices, bins - LANES)
    out_inner = inner_image(partner_rows_kernel, angles, matrix, pulses)
    pieces[0] = after(pieces[0], out_inner)
    own_outer, out_outer, *edges = outer_image(own_side, matrix, pieces)
    far = [from_partner(value, 1) for value in (out_outer, out_inner)]
    edges = exchanged(edges[0], 0), exchanged(edges[1], 1)
    own_kernel = functools.partial(own_rows_kernel, local_pulses)
    own = inner_image(own_kernel, angles, matrix, pulses, (own_outer,))
    tables = merge_tables(0, 1, *settings, own)
    edges = after(edges[0], tables[0]), edges[1]
    for level in range(levels):
        stride = 2**level
        if level > 0:
            tables = merge_tables(level, stride, *settings, image)
            own, out, edges = split_image(level, image, fore_flag, rim)
            far = [from_partner(value, stride) for value in (out[..., :LANES], out[..., LANES:])]
            edges = exchanged(edges[0], 0), exchanged(edges[1], 1)
            own_side = tables[-1]
        rims, out_rims = sorted_rims(own_side, *edges)
        far_rims = from_partner(out_rims, stride)
        image = merged_image(own, rims, far, far_rims, tables, BF16 if level + 1 < levels else F32)
    return image


def solution(mesh):
    placed_as = (
        P(None, ("sub", "rng"), None),
        P(None, None, "rng"),
        P(None, None, "rng"),
        P(),
        P(),
        P(),
    )
    return jax.shard_map(
        on_device, mesh=mesh, in_specs=placed_as, out_specs=P(None, "sub", "rng"), check_vma=False
    )
```

```python
import functools
import math

import jax
import jax.numpy as jnp
from jax import lax
from jax.experimental import pallas as pl
from jax.experimental.pallas import tpu as pltpu
from jax.sharding import PartitionSpec as P

MAX_SHIFT = 16
LANES = 128
MIB = 2**20
JOIN_COST = 10**11
SIDE = jax.ShapeDtypeStruct((8, LANES), jnp.float32)
VMEM = pl.BlockSpec(memory_space=pltpu.VMEM)
SMEM = pl.BlockSpec(memory_space=pltpu.SMEM)
ANY = pl.BlockSpec(memory_space=pl.ANY)
F32 = jnp.float32
BF16 = jnp.bfloat16


def dot(a, b):
    return jnp.dot(a, b, preferred_element_type=F32)


def params(mib):
    return pltpu.CompilerParams(vmem_limit_bytes=mib * MIB)


def series(square, first, count):
    coefs = [
        (-1) ** i * math.pi ** (2 * i + first) / math.factorial(2 * i + first)
        for i in range(count)
    ]
    total = jnp.full_like(square, coefs[-1])
    for coef in coefs[-2::-1]:
        total = total * square + coef
    return total


def cos_sin_pi(v):
    turns = jnp.floor(v + 0.5)
    rest = v - turns
    sign = 1.0 - 2.0 * (turns - 2.0 * jnp.floor(turns * 0.5))
    square = rest * rest
    return series(square, 0, 8) * sign, series(square, 1, 7) * rest * sign


def rotated(pair, step):
    return pair[0] * step[0] - pair[1] * step[1], pair[0] * step[1] + pair[1] * step[0]


def mixed(left, right):
    lane = lax.broadcasted_iota(jnp.int32, left.shape, 1)
    return jnp.where(lane < LANES // 2, left.astype(F32), right.astype(F32)).astype(BF16)


def place_kernel(echoes_ref, far_ref, near_ref, inner_ref):
    devices, _, count = inner_ref.shape
    bins = count + LANES
    half = devices // 2
    base = lax.axis_index("rng") // half * half

    def tile(device, first):
        return echoes_ref[:, pl.ds(pl.multiple_of(device * bins + first, LANES), LANES)]

    for ref, start in ((far_ref, half - base), (near_ref, base)):
        for i in range(half):
            ref[i] = mixed(tile(start + i, 0), tile(start + i, bins - LANES))
    for device in range(devices):
        begin = device * bins
        inner_ref[device, :, :LANES] = mixed(tile(device, bins - LANES), tile(device, 0))
        inner_ref[device, :, LANES:] = echoes_ref[:, begin + LANES : begin + bins - LANES]


def placed(echoes, devices):
    rows, columns = echoes.shape
    outer = jax.ShapeDtypeStruct((devices // 2, rows, LANES), BF16)
    inner = jax.ShapeDtypeStruct((devices, rows, columns // devices - LANES), BF16)
    return pl.pallas_call(
        place_kernel,
        out_shape=[outer, outer, inner],
        in_specs=[VMEM],
        out_specs=[VMEM] * 3,
        compiler_params=params(8),
        cost_estimate=pl.CostEstimate(flops=0, bytes_accessed=2 * MIB, transcendentals=0),
    )(echoes)


def join_kernel(near_ref, relay_ref, *refs):
    me = lax.axis_index("rng") % len(refs)
    rows = near_ref.shape[1]
    for d, out_ref in enumerate(refs):
        out_ref[:rows] = near_ref[me ^ d]
        out_ref[rows:] = relay_ref[me ^ d]


def joined(near, relay):
    half, rows, count = near.shape
    return pl.pallas_call(
        join_kernel,
        out_shape=[jax.ShapeDtypeStruct((2 * rows, count), BF16)] * half,
        in_specs=[VMEM] * 2,
        out_specs=[VMEM] * half,
        compiler_params=params(4),
        cost_estimate=pl.CostEstimate(flops=JOIN_COST, bytes_accessed=MIB, transcendentals=0),
    )(near, relay)


def across(value, mask):
    devices = lax.axis_size("rng")
    return lax.ppermute(value, "rng", [(i, i ^ mask) for i in range(devices)])


def filter_table_kernel(local_pulses, flag_ref, after_ref, rows_ref, side_ref, cos_ref, sin_ref):
    own_flag = flag_ref[0, lax.axis_index("sub"), 0]
    side_ref[...] = jnp.full(side_ref.shape, own_flag.astype(F32))
    angles, columns = rows_ref.shape
    half = angles // 2
    first = (1 - own_flag) * half
    base = cos_ref.shape[0]
    scale = 1.0 / math.sqrt(columns // 2)
    lane = lax.broadcasted_iota(jnp.int32, (8, columns), 1)
    slot = lane // (2 * local_pulses)
    second = lane // local_pulses % 2
    pulse = (slot * local_pulses + lane % local_pulses).astype(F32)
    lag = second.astype(F32) * 0.5
    per_angle = pulse * (1.0 / angles)
    row = lax.broadcasted_iota(jnp.int32, (8, columns), 0)
    for i in range(base // 8):
        twice = (2 * (row + 8 * i + first) + 1 - angles).astype(F32)
        cosine, sine = cos_sin_pi(twice * per_angle - lag)
        cos_ref[8 * i : 8 * i + 8, :] = cosine * scale
        sin_ref[8 * i : 8 * i + 8, :] = sine * scale
    step = cos_sin_pi(per_angle * (2 * base))
    for j in range(half // base):
        for i in range(base // 16):
            pair = [], []
            for k in (2 * i, 2 * i + 1):
                here = slice(8 * k, 8 * k + 8)
                now = cos_ref[here, :], sin_ref[here, :]
                pair[0].append(now[0])
                pair[1].append(-now[1])
                if j + 1 < half // base:
                    cos_ref[here, :], sin_ref[here, :] = rotated(now, step)
            begin = j * base + 16 * i
            rows_ref[begin : begin + 16, :] = jnp.concatenate(pair[0]).astype(BF16)
            begin += half
            rows_ref[begin : begin + 16, :] = jnp.concatenate(pair[1]).astype(BF16)


def filter_table(fore_flag, angles, local_pulses, earlier):
    side = 2 * local_pulses * lax.axis_size("rng")
    return pl.pallas_call(
        functools.partial(filter_table_kernel, local_pulses),
        out_shape=[jax.ShapeDtypeStruct((angles, side), BF16), SIDE],
        in_specs=[SMEM, ANY],
        out_specs=[VMEM] * 2,
        scratch_shapes=[pltpu.VMEM((64, side), F32)] * 2,
        compiler_params=params(6),
        cost_estimate=pl.CostEstimate(flops=9_000_000, bytes_accessed=4 * MIB, transcendentals=0),
    )(fore_flag, earlier)


def merge_table_kernel(
    level, stride, flag_ref, offset_ref, shift_ref, range_ref, interp_ref, after_ref, centre_ref,
    rim_ref, turn_ref, matrix_ref, side_ref, kernel_ref, sems,
):
    group = lax.axis_index("sub")
    block = lax.axis_index("rng")
    bins = centre_ref.shape[-1]
    angles = turn_ref.shape[-2]
    total_bins = lax.axis_size("rng") * bins
    taps = range_ref.shape[1]
    band = (taps - bins) // 2
    rim = MAX_SHIFT + band
    own_flag = flag_ref[level, group, 0]
    side_ref[...] = jnp.full(side_ref.shape, own_flag.astype(F32))
    copies = [
        pltpu.make_async_copy(source, target, sems.at[i])
        for i, (source, target) in enumerate(
            (
                (range_ref.at[level], kernel_ref),
                (interp_ref.at[level, own_flag], matrix_ref.at[0]),
                (interp_ref.at[level, 1 - own_flag], matrix_ref.at[1]),
            )
        )
    ]
    for copy in copies:
        copy.start()

    def moved(bin_id):
        tap = lax.broadcasted_iota(jnp.int32, (bin_id.shape[0], taps), 1)
        hot = jnp.where(tap == bin_id, 1.0, 0.0).astype(BF16)
        return dot(hot, kernel_ref[...]).astype(BF16)

    row = lax.broadcasted_iota(jnp.int32, (bins, 1), 0)
    upper = row + (bins - 2 * LANES)
    own_bin = jnp.where(row % LANES < LANES // 2, row, upper + LANES)
    own_bin = jnp.where(row >= LANES, jnp.where(row % LANES < LANES // 2, upper, row - LANES), own_bin)
    own_bin = jnp.where(row >= 2 * LANES, row - LANES, own_bin)
    rim_row = lax.broadcasted_iota(jnp.int32, (2 * rim, 1), 0)
    rim_bin = jnp.where(rim_row < rim, rim_row - rim, rim_row - rim + bins)
    rim_ref[...] = jnp.zeros(rim_ref.shape, BF16)
    bin_id = block * bins + lax.broadcasted_iota(jnp.int32, (8, bins), 1)
    reach = 1.0 + bin_id.astype(F32) * (1.0 / total_bins)
    line = lax.broadcasted_iota(jnp.int32, (8, bins), 0)
    base = 64
    members = group, group ^ stride
    for child, member in enumerate(members):
        rate = shift_ref[level, member]
        for first in range(0, base, 8):
            angle = (first + line).astype(F32)
            now = cos_sin_pi(rate * ((angle + 0.5) * (1.0 / angles) - 0.5) * reach)
            turn_ref[child, 0, first : first + 8, :] = now[0]
            turn_ref[child, 1, first : first + 8, :] = now[1]
        step = cos_sin_pi(rate * (base / angles) * reach)
        for first in range(base, angles, 8):
            here, last = slice(first, first + 8), slice(first - base, first - base + 8)
            now = rotated((turn_ref[child, 0, last, :], turn_ref[child, 1, last, :]), step)
            turn_ref[child, 0, here, :], turn_ref[child, 1, here, :] = now
    for copy in copies:
        copy.wait()
    for child, member in enumerate(members):
        lead = band - offset_ref[level, member, 0]
        centre_ref[child] = moved(own_bin + lead)
        ends = moved(rim_bin + lead)
        for part in range(2):
            for side in range(2):
                place = (2 * side + part) * rim
                rim_ref[child, part, place : place + rim, :] = ends[side * rim : (side + 1) * rim]


def merge_tables(
    level, stride, fore_flag, band_offset, center_shift, range_kernel, angle_interp, earlier
):
    taps, bins = range_kernel.shape[1:]
    angles = angle_interp.shape[2]
    rim = MAX_SHIFT + (taps - bins) // 2
    return pl.pallas_call(
        functools.partial(merge_table_kernel, level, stride),
        out_shape=[
            jax.ShapeDtypeStruct((2, bins, bins), BF16),
            jax.ShapeDtypeStruct((2, 2, 4 * rim, bins), BF16),
            jax.ShapeDtypeStruct((2, 2, angles, bins), F32),
            jax.ShapeDtypeStruct((2, *angle_interp.shape[2:]), BF16),
            SIDE,
        ],
        in_specs=[SMEM] * 3 + [ANY] * 3,
        out_specs=[VMEM] * 5,
        scratch_shapes=[pltpu.VMEM((taps, bins), BF16), pltpu.SemaphoreType.DMA((3,))],
        compiler_params=params(12),
        cost_estimate=pl.CostEstimate(
            flops=2_300_000_000, bytes_accessed=7 * MIB, transcendentals=0
        ),
    )(fore_flag, band_offset, center_shift, range_kernel, angle_interp, earlier)


def alternating(pulses, local_pulses):
    row = lax.broadcasted_iota(jnp.int32, (pulses.shape[0], 1), 0)
    pulse = row // (2 * local_pulses) * local_pulses + row % local_pulses
    return jnp.where(pulse % 2 == 1, -pulses.astype(F32), pulses.astype(F32)).astype(BF16)


def outer_kernel(pieces, side_ref, rows_ref, *refs):
    own_side = side_ref[:1, :]
    me = lax.axis_index("rng")
    own_ref, *sent_refs = refs[pieces : pieces + 4]
    pulses_ref, *held_refs, sems = refs[pieces + 4 :]
    copies = [
        pltpu.make_async_copy(held, sent, sems.at[i])
        for i, (held, sent) in enumerate(zip(held_refs, sent_refs))
    ]
    rows = refs[0].shape[0] // 2
    for d, ref in enumerate(refs[:pieces]):
        for t in range(2):
            place = pl.multiple_of((me ^ (d + t * pieces)) * rows, rows)
            pulses_ref[pl.ds(place, rows), :] = ref[t * rows : (t + 1) * rows, :]
    pulses = pulses_ref[...]
    half = own_ref.shape[1]
    out_parts = dot(rows_ref[...], pulses)
    for part in range(2):
        held_refs[0][part] = out_parts[part * half : (part + 1) * half].astype(BF16)
    copies[0].start()
    own_parts = dot(rows_ref[...], alternating(pulses, rows // 2))
    rim = LANES // 4
    lane = lax.broadcasted_iota(jnp.int32, (1, LANES), 1)
    edges = [0.0, 0.0]
    for part in range(2):
        own, out = (value[part * half : (part + 1) * half] for value in (own_parts, out_parts))
        for side in range(2):
            value = jnp.where(own_side == side, own, out)
            group = 2 * part + side
            for end in range(2):
                turn = (group + end) * rim % LANES
                moved = pltpu.roll(value, turn, 1) if turn else value
                edges[end] = edges[end] + jnp.where(lane // rim == group, moved, 0.0)
    even = me % 2 == 0
    held_refs[1][...] = jnp.where(even, edges[1], edges[0]).astype(BF16)
    held_refs[2][...] = jnp.where(even, edges[0], edges[1]).astype(BF16)
    copies[1].start()
    copies[2].start()
    for part in range(2):
        own_ref[part] = own_parts[part * half : (part + 1) * half].astype(BF16)
    for copy in copies:
        copy.wait()


def outer_image(own_side, rows, pieces):
    angles, side = rows.shape
    image = jax.ShapeDtypeStruct((2, angles // 2, LANES), BF16)
    edge = jax.ShapeDtypeStruct((angles // 2, LANES), BF16)
    return pl.pallas_call(
        functools.partial(outer_kernel, len(pieces)),
        out_shape=[image, image, edge, edge],
        in_specs=[VMEM] * (2 + len(pieces)),
        out_specs=[VMEM] + [ANY] * 3,
        scratch_shapes=[
            pltpu.VMEM((side, LANES), BF16),
            *(pltpu.VMEM(value.shape, BF16) for value in (image, edge, edge)),
            pltpu.SemaphoreType.DMA((3,)),
        ],
        compiler_params=params(10),
        cost_estimate=pl.CostEstimate(
            flops=4 * angles * side * LANES, bytes_accessed=3 * MIB, transcendentals=0
        ),
    )(own_side, rows, *pieces)


def partner_rows_kernel(rows_ref, pulses_ref, image_ref):
    image = dot(rows_ref[...], pulses_ref[...])
    image_ref[...] = image.astype(BF16).reshape(image_ref.shape)


def own_rows_kernel(local_pulses, rows_ref, pulses_ref, outer_ref, image_ref):
    image = dot(rows_ref[...], alternating(pulses_ref[...], local_pulses))
    parts, half, count = outer_ref.shape
    image_ref[:, :, :count] = outer_ref[...]
    image_ref[:, :, count:] = image.astype(BF16).reshape(parts, half, image.shape[1])


def inner_image(kernel, angles, rows, pulses, outer=()):
    count = pulses.shape[1]
    whole = count + (outer[0].shape[2] if outer else 0)
    return pl.pallas_call(
        kernel,
        out_shape=jax.ShapeDtypeStruct((2, angles // 2, whole), BF16),
        in_specs=[VMEM] * (2 + len(outer)),
        out_specs=VMEM,
        compiler_params=params(10),
        cost_estimate=pl.CostEstimate(
            flops=2 * angles * rows.shape[1] * count, bytes_accessed=3 * MIB, transcendentals=0
        ),
    )(rows, pulses, *outer)


def exchanged(value, begin):
    devices = lax.axis_size("rng")
    pairs = [(i, i + 1) for i in range(begin, devices - 1, 2)]
    ends = [(i, i) for i in range(devices) if all(i not in pair for pair in pairs)]
    return lax.ppermute(value, "rng", pairs + [(j, i) for i, j in pairs] + ends)


def rims_kernel(side_ref, first_ref, second_ref, own_ref, out_ref):
    own_side = side_ref[:1, :]
    rim = LANES // 4
    me, devices = lax.axis_index("rng"), lax.axis_size("rng")
    even = me % 2 == 0
    first, second = first_ref[...].astype(F32), second_ref[...].astype(F32)
    below = jnp.where(me == 0, 0.0, jnp.where(even, second, first))
    above = jnp.where(me == devices - 1, 0.0, jnp.where(even, first, second))
    group = lax.broadcasted_iota(jnp.int32, (1, LANES), 1) // rim
    packed = [0.0, 0.0]
    for end, value in enumerate((below, above)):
        for part in range(2):
            place = 2 * end + part
            for side in range(2):
                turn = (place - (2 * part + side)) * rim % LANES
                moved = pltpu.roll(value, turn, 1) if turn else value
                packed[side] = packed[side] + jnp.where(group == place, moved, 0.0)
    own_ref[...] = jnp.where(own_side == 0, packed[0], packed[1]).astype(BF16)
    out_ref[...] = jnp.where(own_side == 0, packed[1], packed[0]).astype(BF16)


def sorted_rims(own_side, first, second):
    return pl.pallas_call(
        rims_kernel,
        out_shape=[jax.ShapeDtypeStruct(first.shape, BF16)] * 2,
        in_specs=[VMEM] * 3,
        out_specs=[VMEM] * 2,
        compiler_params=params(4),
        cost_estimate=pl.CostEstimate(flops=1_000_000, bytes_accessed=MIB // 4, transcendentals=0),
    )(own_side, first, second)


def resampled(image, rims_ref, centre_ref, rim_ref, value_ref, child):
    parts, half, bins = image.shape
    value_ref[...] = dot(image.reshape(parts * half, bins), centre_ref[child])
    rims = rims_ref[...]
    return [
        (value_ref[part * half : (part + 1) * half, :] + dot(rims, rim_ref[child, part])).astype(BF16)
        for part in range(parts)
    ]


def early_kernel(
    own_ref, rims_ref, centre_ref, rim_ref, matrix_ref, turn_ref, merged_ref, value_ref
):
    rows = resampled(own_ref[...], rims_ref, centre_ref, rim_ref, value_ref, 0)
    merged_ref[0], merged_ref[1] = rotated(
        (dot(matrix_ref[0], rows[0]), dot(matrix_ref[0], rows[1])), (turn_ref[0, 0], turn_ref[0, 1])
    )


def ends_of(value):
    count = value.shape[-1]
    return jnp.concatenate([value[..., :LANES], value[..., count - LANES :]], axis=-1)


def finish(values, lanes, merged_ref, matrix_ref, turn_ref, out_ref, buffer, sems):
    rows = [value.astype(BF16) for value in values]
    copies = []
    block = 2 * LANES
    for first in range(0, matrix_ref.shape[1], block):
        here = slice(first, first + block)
        matrix = matrix_ref[1, here]
        terms = dot(matrix, rows[0]), dot(matrix, rows[1])
        at = 0
        for begin, end in lanes:
            there = slice(at, at + end - begin)
            turned = rotated(
                (terms[0][:, there], terms[1][:, there]),
                (turn_ref[1, 0, here, begin:end], turn_ref[1, 1, here, begin:end]),
            )
            for part in range(2):
                total = merged_ref[part, here, begin:end] + turned[part]
                buffer[part, here, there] = total.astype(buffer.dtype)
            copy = pltpu.make_async_copy(
                buffer.at[:, here, there],
                out_ref.at[:, here, pl.ds(begin, end - begin)],
                sems.at[len(copies)],
            )
            copy.start()
            copies.append(copy)
            at += end - begin
    for copy in copies:
        copy.wait()


def middle_kernel(
    far_inner, merged_ref, centre_ref, matrix_ref, turn_ref, out_ref, partial_ref, buffer, sems
):
    parts, half, count = far_inner.shape
    bins = centre_ref.shape[2]
    inner = far_inner[...].reshape(parts * half, count)
    value = dot(inner, centre_ref[1, bins - count :, LANES : bins - LANES])
    values = [value[part * half : (part + 1) * half] for part in range(parts)]
    finish(
        values, [(LANES, bins - LANES)], merged_ref, matrix_ref, turn_ref, out_ref, buffer, sems
    )
    partial_ref[...] = dot(inner, ends_of(centre_ref[1, bins - count :, :]))


def end_kernel(
    far_outer, partial_ref, rims_ref, merged_ref, centre_ref, rim_ref, matrix_ref, turn_ref,
    begun_ref, out_ref, buffer, sems,
):
    parts, half, count = far_outer.shape
    bins = centre_ref.shape[2]
    centre = ends_of(centre_ref[1, :count, :])
    values = [
        partial_ref[part * half : (part + 1) * half, :]
        + dot(far_outer[part], centre)
        + dot(rims_ref[...], ends_of(rim_ref[1, part]))
        for part in range(parts)
    ]
    lanes = [(0, LANES), (bins - LANES, bins)]
    finish(values, lanes, merged_ref, matrix_ref, turn_ref, out_ref, buffer, sems)


def merged_image(own, rims, far, far_rims, tables, dtype):
    centre, rim, turn, matrices, _ = tables
    angles, bins = turn.shape[-2:]
    cost = pl.CostEstimate(flops=4 * angles * bins * bins, bytes_accessed=8 * MIB, transcendentals=0)
    value = pltpu.VMEM((angles, bins), F32)
    merged = pl.pallas_call(
        early_kernel,
        out_shape=jax.ShapeDtypeStruct((2, angles, bins), F32),
        in_specs=[VMEM] * 6,
        out_specs=VMEM,
        scratch_shapes=[value],
        compiler_params=params(16),
        cost_estimate=cost,
    )(own, rims, centre, rim, matrices, turn)
    image = jax.ShapeDtypeStruct((2, angles, bins), dtype)
    middle, ends = bins - 2 * LANES, 2 * LANES
    begun, partial = pl.pallas_call(
        middle_kernel,
        out_shape=[image, jax.ShapeDtypeStruct((angles, ends), F32)],
        in_specs=[VMEM] * 5,
        out_specs=[ANY, VMEM],
        scratch_shapes=[
            pltpu.VMEM((2, angles, middle), dtype),
            pltpu.SemaphoreType.DMA((angles // LANES,)),
        ],
        compiler_params=params(16),
        cost_estimate=cost,
    )(far[1], merged, centre, matrices, turn)
    return pl.pallas_call(
        end_kernel,
        out_shape=image,
        in_specs=[VMEM] * 8 + [ANY],
        out_specs=ANY,
        scratch_shapes=[
            pltpu.VMEM((2, angles, ends), dtype),
            pltpu.SemaphoreType.DMA((angles // LANES,)),
        ],
        input_output_aliases={8: 0},
        compiler_params=params(16),
        cost_estimate=cost,
    )(far[0], partial, far_rims, merged, centre, rim, matrices, turn, begun)


def after(value, *earlier):
    return lax.optimization_barrier((value, *earlier))[0]


def from_partner(value, stride):
    pairs = [(source, source ^ stride) for source in range(lax.axis_size("sub"))]
    return lax.ppermute(value, "sub", pairs)


def split_image(level, image, fore_flag, rim):
    angles, bins = image.shape[1:]
    half, step = angles // 2, LANES // 2
    own_flag = fore_flag[level, lax.axis_index("sub"), 0]
    sides = image.reshape(2, 2, half, bins)

    def pieces(side):
        rows = lax.dynamic_index_in_dim(sides, side, 1, keepdims=False)
        ends = [rows[..., :step], rows[..., -step:]]
        rest = [rows[..., -2 * step : -step], rows[..., step : -2 * step]]
        return jnp.concatenate(ends + rest, axis=-1)

    def packed(edge):
        return edge.transpose(2, 0, 1, 3).reshape(half, 4 * rim)

    low, high = packed(sides[..., :rim]), packed(sides[..., -rim:])
    even = lax.axis_index("rng") % 2 == 0
    edges = jnp.where(even, high, low), jnp.where(even, low, high)
    return pieces(own_flag), pieces(1 - own_flag), edges


def on_device(echoes, fore_flag, band_offset, angle_interp, range_kernel, center_shift):
    devices = lax.axis_size("rng")
    half = devices // 2
    local_pulses = echoes.shape[1]
    bins = echoes.shape[2] // devices
    angles = angle_interp.shape[2]
    rim = MAX_SHIFT + (range_kernel.shape[1] - bins) // 2
    levels = range_kernel.shape[0]
    settings = (fore_flag, band_offset, center_shift, range_kernel, angle_interp)

    far_blocks, near_blocks, blocks = placed(
        echoes.reshape(2 * local_pulses, devices * bins), devices
    )
    relay = across(far_blocks, half)
    pulses = lax.all_to_all(blocks, "rng", split_axis=0, concat_axis=0, tiled=True)
    sends = joined(near_blocks, relay)
    pieces = [across(value, d) if d else value for d, value in enumerate(sends)]
    matrix, own_side = filter_table(fore_flag, angles, local_pulses, sends[0])
    own_outer, out_outer, *edges = outer_image(own_side, matrix, pieces)
    pulses = after(pulses, out_outer).reshape(2 * local_pulses * devices, bins - LANES)
    out_inner = inner_image(partner_rows_kernel, angles, matrix, pulses)
    far = [from_partner(value, 1) for value in (out_outer, out_inner)]
    edges = [after(edge, out_inner) for edge in edges]
    edges = exchanged(edges[0], 0), exchanged(edges[1], 1)
    pulses = after(pulses, far[0])
    own_kernel = functools.partial(own_rows_kernel, local_pulses)
    own = inner_image(own_kernel, angles, matrix, pulses, (own_outer,))
    tables = merge_tables(0, 1, *settings, own)
    edges = after(edges[0], tables[0]), edges[1]
    for level in range(levels):
        stride = 2**level
        if level > 0:
            tables = merge_tables(level, stride, *settings, image)
            own, out, edges = split_image(level, image, fore_flag, rim)
            far = [from_partner(value, stride) for value in (out[..., :LANES], out[..., LANES:])]
            edges = exchanged(edges[0], 0), exchanged(edges[1], 1)
            own_side = tables[-1]
        rims, out_rims = sorted_rims(own_side, *edges)
        far_rims = from_partner(out_rims, stride)
        image = merged_image(own, rims, far, far_rims, tables, BF16 if level + 1 < levels else F32)
    return image


def solution(mesh):
    placed_as = (
        P(None, ("sub", "rng"), None),
        P(None, None, "rng"),
        P(None, None, "rng"),
        P(),
        P(),
        P(),
    )
    return jax.shard_map(
        on_device, mesh=mesh, in_specs=placed_as, out_specs=P(None, "sub", "rng"), check_vma=False
    )
```

```python
import functools
import math

import jax
import jax.numpy as jnp
from jax import lax
from jax.experimental import pallas as pl
from jax.experimental.pallas import tpu as pltpu
from jax.sharding import PartitionSpec as P

MAX_SHIFT = 16
LANES = 128
MIB = 2**20
JOIN_COST = 10**11
SIDE = jax.ShapeDtypeStruct((8, LANES), jnp.float32)
VMEM = pl.BlockSpec(memory_space=pltpu.VMEM)
SMEM = pl.BlockSpec(memory_space=pltpu.SMEM)
ANY = pl.BlockSpec(memory_space=pl.ANY)
F32 = jnp.float32
BF16 = jnp.bfloat16


def dot(a, b):
    return jnp.dot(a, b, preferred_element_type=F32)


def params(mib):
    return pltpu.CompilerParams(vmem_limit_bytes=mib * MIB)


def series(square, first, count):
    coefs = [
        (-1) ** i * math.pi ** (2 * i + first) / math.factorial(2 * i + first)
        for i in range(count)
    ]
    total = jnp.full_like(square, coefs[-1])
    for coef in coefs[-2::-1]:
        total = total * square + coef
    return total


def cos_sin_pi(v):
    turns = jnp.floor(v + 0.5)
    rest = v - turns
    sign = 1.0 - 2.0 * (turns - 2.0 * jnp.floor(turns * 0.5))
    square = rest * rest
    return series(square, 0, 8) * sign, series(square, 1, 7) * rest * sign


def rotated(pair, step):
    return pair[0] * step[0] - pair[1] * step[1], pair[0] * step[1] + pair[1] * step[0]


def mixed(left, right):
    lane = lax.broadcasted_iota(jnp.int32, left.shape, 1)
    return jnp.where(lane < LANES // 2, left.astype(F32), right.astype(F32)).astype(BF16)


def place_kernel(echoes_ref, far_ref, near_ref, inner_ref):
    devices, _, count = inner_ref.shape
    bins = count + LANES
    half = devices // 2
    base = lax.axis_index("rng") // half * half

    def tile(device, first):
        return echoes_ref[:, pl.ds(pl.multiple_of(device * bins + first, LANES), LANES)]

    for ref, start in ((far_ref, half - base), (near_ref, base)):
        for i in range(half):
            ref[i] = mixed(tile(start + i, 0), tile(start + i, bins - LANES))
    for device in range(devices):
        begin = device * bins
        inner_ref[device, :, :LANES] = mixed(tile(device, bins - LANES), tile(device, 0))
        inner_ref[device, :, LANES:] = echoes_ref[:, begin + LANES : begin + bins - LANES]


def placed(echoes, devices):
    rows, columns = echoes.shape
    outer = jax.ShapeDtypeStruct((devices // 2, rows, LANES), BF16)
    inner = jax.ShapeDtypeStruct((devices, rows, columns // devices - LANES), BF16)
    return pl.pallas_call(
        place_kernel,
        out_shape=[outer, outer, inner],
        in_specs=[VMEM],
        out_specs=[VMEM] * 3,
        compiler_params=params(8),
        cost_estimate=pl.CostEstimate(flops=0, bytes_accessed=2 * MIB, transcendentals=0),
    )(echoes)


def join_kernel(near_ref, relay_ref, *refs):
    me = lax.axis_index("rng") % len(refs)
    rows = near_ref.shape[1]
    for d, out_ref in enumerate(refs):
        out_ref[:rows] = near_ref[me ^ d]
        out_ref[rows:] = relay_ref[me ^ d]


def joined(near, relay):
    half, rows, count = near.shape
    return pl.pallas_call(
        join_kernel,
        out_shape=[jax.ShapeDtypeStruct((2 * rows, count), BF16)] * half,
        in_specs=[VMEM] * 2,
        out_specs=[VMEM] * half,
        compiler_params=params(4),
        cost_estimate=pl.CostEstimate(flops=JOIN_COST, bytes_accessed=MIB, transcendentals=0),
    )(near, relay)


def across(value, mask):
    devices = lax.axis_size("rng")
    return lax.ppermute(value, "rng", [(i, i ^ mask) for i in range(devices)])


def filter_table_kernel(local_pulses, flag_ref, after_ref, rows_ref, side_ref, cos_ref, sin_ref):
    own_flag = flag_ref[0, lax.axis_index("sub"), 0]
    side_ref[...] = jnp.full(side_ref.shape, own_flag.astype(F32))
    angles, columns = rows_ref.shape
    half = angles // 2
    first = (1 - own_flag) * half
    base = cos_ref.shape[0]
    scale = 1.0 / math.sqrt(columns // 2)
    lane = lax.broadcasted_iota(jnp.int32, (8, columns), 1)
    slot = lane // (2 * local_pulses)
    second = lane // local_pulses % 2
    pulse = (slot * local_pulses + lane % local_pulses).astype(F32)
    lag = second.astype(F32) * 0.5
    per_angle = pulse * (1.0 / angles)
    row = lax.broadcasted_iota(jnp.int32, (8, columns), 0)
    for i in range(base // 8):
        twice = (2 * (row + 8 * i + first) + 1 - angles).astype(F32)
        cosine, sine = cos_sin_pi(twice * per_angle - lag)
        cos_ref[8 * i : 8 * i + 8, :] = cosine * scale
        sin_ref[8 * i : 8 * i + 8, :] = sine * scale
    step = cos_sin_pi(per_angle * (2 * base))
    for j in range(half // base):
        for i in range(base // 16):
            pair = [], []
            for k in (2 * i, 2 * i + 1):
                here = slice(8 * k, 8 * k + 8)
                now = cos_ref[here, :], sin_ref[here, :]
                pair[0].append(now[0])
                pair[1].append(-now[1])
                if j + 1 < half // base:
                    cos_ref[here, :], sin_ref[here, :] = rotated(now, step)
            begin = j * base + 16 * i
            rows_ref[begin : begin + 16, :] = jnp.concatenate(pair[0]).astype(BF16)
            begin += half
            rows_ref[begin : begin + 16, :] = jnp.concatenate(pair[1]).astype(BF16)


def filter_table(fore_flag, angles, local_pulses, earlier):
    side = 2 * local_pulses * lax.axis_size("rng")
    return pl.pallas_call(
        functools.partial(filter_table_kernel, local_pulses),
        out_shape=[jax.ShapeDtypeStruct((angles, side), BF16), SIDE],
        in_specs=[SMEM, ANY],
        out_specs=[VMEM] * 2,
        scratch_shapes=[pltpu.VMEM((64, side), F32)] * 2,
        compiler_params=params(6),
        cost_estimate=pl.CostEstimate(flops=9_000_000, bytes_accessed=4 * MIB, transcendentals=0),
    )(fore_flag, earlier)


def merge_table_kernel(
    level, stride, flag_ref, offset_ref, shift_ref, range_ref, interp_ref, after_ref, centre_ref,
    rim_ref, turn_ref, matrix_ref, side_ref, kernel_ref, sems,
):
    group = lax.axis_index("sub")
    block = lax.axis_index("rng")
    bins = centre_ref.shape[-1]
    angles = turn_ref.shape[-2]
    total_bins = lax.axis_size("rng") * bins
    taps = range_ref.shape[1]
    band = (taps - bins) // 2
    rim = MAX_SHIFT + band
    own_flag = flag_ref[level, group, 0]
    side_ref[...] = jnp.full(side_ref.shape, own_flag.astype(F32))
    copies = [
        pltpu.make_async_copy(source, target, sems.at[i])
        for i, (source, target) in enumerate(
            (
                (range_ref.at[level], kernel_ref),
                (interp_ref.at[level, own_flag], matrix_ref.at[0]),
                (interp_ref.at[level, 1 - own_flag], matrix_ref.at[1]),
            )
        )
    ]
    for copy in copies:
        copy.start()

    def moved(bin_id):
        tap = lax.broadcasted_iota(jnp.int32, (bin_id.shape[0], taps), 1)
        hot = jnp.where(tap == bin_id, 1.0, 0.0).astype(BF16)
        return dot(hot, kernel_ref[...]).astype(BF16)

    row = lax.broadcasted_iota(jnp.int32, (bins, 1), 0)
    upper = row + (bins - 2 * LANES)
    own_bin = jnp.where(row % LANES < LANES // 2, row, upper + LANES)
    own_bin = jnp.where(row >= LANES, jnp.where(row % LANES < LANES // 2, upper, row - LANES), own_bin)
    own_bin = jnp.where(row >= 2 * LANES, row - LANES, own_bin)
    rim_row = lax.broadcasted_iota(jnp.int32, (2 * rim, 1), 0)
    rim_bin = jnp.where(rim_row < rim, rim_row - rim, rim_row - rim + bins)
    rim_ref[...] = jnp.zeros(rim_ref.shape, BF16)
    bin_id = block * bins + lax.broadcasted_iota(jnp.int32, (8, bins), 1)
    reach = 1.0 + bin_id.astype(F32) * (1.0 / total_bins)
    line = lax.broadcasted_iota(jnp.int32, (8, bins), 0)
    base = 64
    members = group, group ^ stride
    for child, member in enumerate(members):
        rate = shift_ref[level, member]
        for first in range(0, base, 8):
            angle = (first + line).astype(F32)
            now = cos_sin_pi(rate * ((angle + 0.5) * (1.0 / angles) - 0.5) * reach)
            turn_ref[child, 0, first : first + 8, :] = now[0]
            turn_ref[child, 1, first : first + 8, :] = now[1]
        step = cos_sin_pi(rate * (base / angles) * reach)
        for first in range(base, angles, 8):
            here, last = slice(first, first + 8), slice(first - base, first - base + 8)
            now = rotated((turn_ref[child, 0, last, :], turn_ref[child, 1, last, :]), step)
            turn_ref[child, 0, here, :], turn_ref[child, 1, here, :] = now
    for copy in copies:
        copy.wait()
    for child, member in enumerate(members):
        lead = band - offset_ref[level, member, 0]
        centre_ref[child] = moved(own_bin + lead)
        ends = moved(rim_bin + lead)
        for part in range(2):
            for side in range(2):
                place = (2 * side + part) * rim
                rim_ref[child, part, place : place + rim, :] = ends[side * rim : (side + 1) * rim]


def merge_tables(
    level, stride, fore_flag, band_offset, center_shift, range_kernel, angle_interp, earlier
):
    taps, bins = range_kernel.shape[1:]
    angles = angle_interp.shape[2]
    rim = MAX_SHIFT + (taps - bins) // 2
    return pl.pallas_call(
        functools.partial(merge_table_kernel, level, stride),
        out_shape=[
            jax.ShapeDtypeStruct((2, bins, bins), BF16),
            jax.ShapeDtypeStruct((2, 2, 4 * rim, bins), BF16),
            jax.ShapeDtypeStruct((2, 2, angles, bins), F32),
            jax.ShapeDtypeStruct((2, *angle_interp.shape[2:]), BF16),
            SIDE,
        ],
        in_specs=[SMEM] * 3 + [ANY] * 3,
        out_specs=[VMEM] * 5,
        scratch_shapes=[pltpu.VMEM((taps, bins), BF16), pltpu.SemaphoreType.DMA((3,))],
        compiler_params=params(12),
        cost_estimate=pl.CostEstimate(
            flops=2_300_000_000, bytes_accessed=7 * MIB, transcendentals=0
        ),
    )(fore_flag, band_offset, center_shift, range_kernel, angle_interp, earlier)


def alternating(pulses, local_pulses):
    row = lax.broadcasted_iota(jnp.int32, (pulses.shape[0], 1), 0)
    pulse = row // (2 * local_pulses) * local_pulses + row % local_pulses
    return jnp.where(pulse % 2 == 1, -pulses.astype(F32), pulses.astype(F32)).astype(BF16)


def outer_kernel(pieces, side_ref, rows_ref, *refs):
    own_side = side_ref[:1, :]
    me = lax.axis_index("rng")
    own_ref, out_ref, *edge_refs = refs[pieces:-1]
    pulses_ref = refs[-1]
    rows = refs[0].shape[0] // 2
    for d, ref in enumerate(refs[:pieces]):
        for t in range(2):
            place = pl.multiple_of((me ^ (d + t * pieces)) * rows, rows)
            pulses_ref[pl.ds(place, rows), :] = ref[t * rows : (t + 1) * rows, :]
    pulses = pulses_ref[...]
    own_parts = dot(rows_ref[...], alternating(pulses, rows // 2))
    out_parts = dot(rows_ref[...], pulses)
    half = own_ref.shape[1]
    rim = LANES // 4
    lane = lax.broadcasted_iota(jnp.int32, (1, LANES), 1)
    edges = [0.0, 0.0]
    for part in range(2):
        own, out = (value[part * half : (part + 1) * half] for value in (own_parts, out_parts))
        own_ref[part] = own.astype(BF16)
        out_ref[part] = out.astype(BF16)
        for side in range(2):
            value = jnp.where(own_side == side, own, out)
            group = 2 * part + side
            for end in range(2):
                turn = (group + end) * rim % LANES
                moved = pltpu.roll(value, turn, 1) if turn else value
                edges[end] = edges[end] + jnp.where(lane // rim == group, moved, 0.0)
    even = me % 2 == 0
    edge_refs[0][...] = jnp.where(even, edges[1], edges[0]).astype(BF16)
    edge_refs[1][...] = jnp.where(even, edges[0], edges[1]).astype(BF16)


def outer_image(own_side, rows, pieces):
    angles, side = rows.shape
    image = jax.ShapeDtypeStruct((2, angles // 2, LANES), BF16)
    edge = jax.ShapeDtypeStruct((angles // 2, LANES), BF16)
    return pl.pallas_call(
        functools.partial(outer_kernel, len(pieces)),
        out_shape=[image, image, edge, edge],
        in_specs=[VMEM] * (2 + len(pieces)),
        out_specs=[VMEM] * 4,
        scratch_shapes=[pltpu.VMEM((side, LANES), BF16)],
        compiler_params=params(10),
        cost_estimate=pl.CostEstimate(
            flops=4 * angles * side * LANES, bytes_accessed=3 * MIB, transcendentals=0
        ),
    )(own_side, rows, *pieces)


def partner_rows_kernel(rows_ref, pulses_ref, image_ref):
    image = dot(rows_ref[...], pulses_ref[...])
    image_ref[...] = image.astype(BF16).reshape(image_ref.shape)


def own_rows_kernel(local_pulses, rows_ref, pulses_ref, outer_ref, image_ref):
    image = dot(rows_ref[...], alternating(pulses_ref[...], local_pulses))
    parts, half, count = outer_ref.shape
    image_ref[:, :, :count] = outer_ref[...]
    image_ref[:, :, count:] = image.astype(BF16).reshape(parts, half, image.shape[1])


def inner_image(kernel, angles, rows, pulses, outer=()):
    count = pulses.shape[1]
    whole = count + (outer[0].shape[2] if outer else 0)
    return pl.pallas_call(
        kernel,
        out_shape=jax.ShapeDtypeStruct((2, angles // 2, whole), BF16),
        in_specs=[VMEM] * (2 + len(outer)),
        out_specs=VMEM,
        compiler_params=params(10),
        cost_estimate=pl.CostEstimate(
            flops=2 * angles * rows.shape[1] * count, bytes_accessed=3 * MIB, transcendentals=0
        ),
    )(rows, pulses, *outer)


def exchanged(value, begin):
    devices = lax.axis_size("rng")
    pairs = [(i, i + 1) for i in range(begin, devices - 1, 2)]
    ends = [(i, i) for i in range(devices) if all(i not in pair for pair in pairs)]
    return lax.ppermute(value, "rng", pairs + [(j, i) for i, j in pairs] + ends)


def rims_kernel(side_ref, first_ref, second_ref, own_ref, out_ref):
    own_side = side_ref[:1, :]
    rim = LANES // 4
    me, devices = lax.axis_index("rng"), lax.axis_size("rng")
    even = me % 2 == 0
    first, second = first_ref[...].astype(F32), second_ref[...].astype(F32)
    below = jnp.where(me == 0, 0.0, jnp.where(even, second, first))
    above = jnp.where(me == devices - 1, 0.0, jnp.where(even, first, second))
    group = lax.broadcasted_iota(jnp.int32, (1, LANES), 1) // rim
    packed = [0.0, 0.0]
    for end, value in enumerate((below, above)):
        for part in range(2):
            place = 2 * end + part
            for side in range(2):
                turn = (place - (2 * part + side)) * rim % LANES
                moved = pltpu.roll(value, turn, 1) if turn else value
                packed[side] = packed[side] + jnp.where(group == place, moved, 0.0)
    own_ref[...] = jnp.where(own_side == 0, packed[0], packed[1]).astype(BF16)
    out_ref[...] = jnp.where(own_side == 0, packed[1], packed[0]).astype(BF16)


def sorted_rims(own_side, first, second):
    return pl.pallas_call(
        rims_kernel,
        out_shape=[jax.ShapeDtypeStruct(first.shape, BF16)] * 2,
        in_specs=[VMEM] * 3,
        out_specs=[VMEM] * 2,
        compiler_params=params(4),
        cost_estimate=pl.CostEstimate(flops=1_000_000, bytes_accessed=MIB // 4, transcendentals=0),
    )(own_side, first, second)


def resampled(image, rims_ref, centre_ref, rim_ref, value_ref, child):
    parts, half, bins = image.shape
    value_ref[...] = dot(image.reshape(parts * half, bins), centre_ref[child])
    rims = rims_ref[...]
    return [
        (value_ref[part * half : (part + 1) * half, :] + dot(rims, rim_ref[child, part])).astype(BF16)
        for part in range(parts)
    ]


def early_kernel(
    own_ref, rims_ref, centre_ref, rim_ref, matrix_ref, turn_ref, merged_ref, value_ref
):
    rows = resampled(own_ref[...], rims_ref, centre_ref, rim_ref, value_ref, 0)
    merged_ref[0], merged_ref[1] = rotated(
        (dot(matrix_ref[0], rows[0]), dot(matrix_ref[0], rows[1])), (turn_ref[0, 0], turn_ref[0, 1])
    )


def ends_of(value):
    count = value.shape[-1]
    return jnp.concatenate([value[..., :LANES], value[..., count - LANES :]], axis=-1)


def finish(values, lanes, merged_ref, matrix_ref, turn_ref, out_ref, buffer, sems):
    rows = [value.astype(BF16) for value in values]
    copies = []
    block = 2 * LANES
    for first in range(0, matrix_ref.shape[1], block):
        here = slice(first, first + block)
        matrix = matrix_ref[1, here]
        terms = dot(matrix, rows[0]), dot(matrix, rows[1])
        at = 0
        for begin, end in lanes:
            there = slice(at, at + end - begin)
            turned = rotated(
                (terms[0][:, there], terms[1][:, there]),
                (turn_ref[1, 0, here, begin:end], turn_ref[1, 1, here, begin:end]),
            )
            for part in range(2):
                total = merged_ref[part, here, begin:end] + turned[part]
                buffer[part, here, there] = total.astype(buffer.dtype)
            copy = pltpu.make_async_copy(
                buffer.at[:, here, there],
                out_ref.at[:, here, pl.ds(begin, end - begin)],
                sems.at[len(copies)],
            )
            copy.start()
            copies.append(copy)
            at += end - begin
    for copy in copies:
        copy.wait()


def middle_kernel(
    far_inner, merged_ref, centre_ref, matrix_ref, turn_ref, out_ref, partial_ref, buffer, sems
):
    parts, half, count = far_inner.shape
    bins = centre_ref.shape[2]
    inner = far_inner[...].reshape(parts * half, count)
    value = dot(inner, centre_ref[1, bins - count :, LANES : bins - LANES])
    values = [value[part * half : (part + 1) * half] for part in range(parts)]
    finish(
        values, [(LANES, bins - LANES)], merged_ref, matrix_ref, turn_ref, out_ref, buffer, sems
    )
    partial_ref[...] = dot(inner, ends_of(centre_ref[1, bins - count :, :]))


def end_kernel(
    far_outer, partial_ref, rims_ref, merged_ref, centre_ref, rim_ref, matrix_ref, turn_ref,
    begun_ref, out_ref, buffer, sems,
):
    parts, half, count = far_outer.shape
    bins = centre_ref.shape[2]
    centre = ends_of(centre_ref[1, :count, :])
    values = [
        partial_ref[part * half : (part + 1) * half, :]
        + dot(far_outer[part], centre)
        + dot(rims_ref[...], ends_of(rim_ref[1, part]))
        for part in range(parts)
    ]
    lanes = [(0, LANES), (bins - LANES, bins)]
    finish(values, lanes, merged_ref, matrix_ref, turn_ref, out_ref, buffer, sems)


def merged_image(own, rims, far, far_rims, tables, dtype):
    centre, rim, turn, matrices, _ = tables
    angles, bins = turn.shape[-2:]
    cost = pl.CostEstimate(flops=4 * angles * bins * bins, bytes_accessed=8 * MIB, transcendentals=0)
    value = pltpu.VMEM((angles, bins), F32)
    merged = pl.pallas_call(
        early_kernel,
        out_shape=jax.ShapeDtypeStruct((2, angles, bins), F32),
        in_specs=[VMEM] * 6,
        out_specs=VMEM,
        scratch_shapes=[value],
        compiler_params=params(16),
        cost_estimate=cost,
    )(own, rims, centre, rim, matrices, turn)
    image = jax.ShapeDtypeStruct((2, angles, bins), dtype)
    middle, ends = bins - 2 * LANES, 2 * LANES
    begun, partial = pl.pallas_call(
        middle_kernel,
        out_shape=[image, jax.ShapeDtypeStruct((angles, ends), F32)],
        in_specs=[VMEM] * 5,
        out_specs=[ANY, VMEM],
        scratch_shapes=[
            pltpu.VMEM((2, angles, middle), dtype),
            pltpu.SemaphoreType.DMA((angles // LANES,)),
        ],
        compiler_params=params(16),
        cost_estimate=cost,
    )(far[1], merged, centre, matrices, turn)
    return pl.pallas_call(
        end_kernel,
        out_shape=image,
        in_specs=[VMEM] * 8 + [ANY],
        out_specs=ANY,
        scratch_shapes=[
            pltpu.VMEM((2, angles, ends), dtype),
            pltpu.SemaphoreType.DMA((angles // LANES,)),
        ],
        input_output_aliases={8: 0},
        compiler_params=params(16),
        cost_estimate=cost,
    )(far[0], partial, far_rims, merged, centre, rim, matrices, turn, begun)


def after(value, *earlier):
    return lax.optimization_barrier((value, *earlier))[0]


def from_partner(value, stride):
    pairs = [(source, source ^ stride) for source in range(lax.axis_size("sub"))]
    return lax.ppermute(value, "sub", pairs)


def split_image(level, image, fore_flag, rim):
    angles, bins = image.shape[1:]
    half, step = angles // 2, LANES // 2
    own_flag = fore_flag[level, lax.axis_index("sub"), 0]
    sides = image.reshape(2, 2, half, bins)

    def pieces(side):
        rows = lax.dynamic_index_in_dim(sides, side, 1, keepdims=False)
        ends = [rows[..., :step], rows[..., -step:]]
        rest = [rows[..., -2 * step : -step], rows[..., step : -2 * step]]
        return jnp.concatenate(ends + rest, axis=-1)

    def packed(edge):
        return edge.transpose(2, 0, 1, 3).reshape(half, 4 * rim)

    low, high = packed(sides[..., :rim]), packed(sides[..., -rim:])
    even = lax.axis_index("rng") % 2 == 0
    edges = jnp.where(even, high, low), jnp.where(even, low, high)
    return pieces(own_flag), pieces(1 - own_flag), edges


def on_device(echoes, fore_flag, band_offset, angle_interp, range_kernel, center_shift):
    devices = lax.axis_size("rng")
    half = devices // 2
    local_pulses = echoes.shape[1]
    bins = echoes.shape[2] // devices
    angles = angle_interp.shape[2]
    rim = MAX_SHIFT + (range_kernel.shape[1] - bins) // 2
    levels = range_kernel.shape[0]
    settings = (fore_flag, band_offset, center_shift, range_kernel, angle_interp)

    far_blocks, near_blocks, blocks = placed(
        echoes.reshape(2 * local_pulses, devices * bins), devices
    )
    relay = across(far_blocks, half)
    pulses = lax.all_to_all(blocks, "rng", split_axis=0, concat_axis=0, tiled=True)
    sends = joined(near_blocks, relay)
    pieces = [across(value, d) if d else value for d, value in enumerate(sends)]
    matrix, own_side = filter_table(fore_flag, angles, local_pulses, sends[0])
    own_outer, out_outer, *edges = outer_image(own_side, matrix, pieces)

    def halos(side, edges, stride):
        rims, out_rims = sorted_rims(side, exchanged(edges[0], 0), exchanged(edges[1], 1))
        return rims, from_partner(out_rims, stride)

    pulses = after(pulses, out_outer).reshape(2 * local_pulses * devices, bins - LANES)
    out_inner = inner_image(partner_rows_kernel, angles, matrix, pulses)
    far = [from_partner(value, 1) for value in (out_outer, out_inner)]
    rims, far_rims = halos(own_side, [after(edge, out_inner) for edge in edges], 1)
    pulses = after(pulses, far[0])
    own_kernel = functools.partial(own_rows_kernel, local_pulses)
    own = inner_image(own_kernel, angles, matrix, pulses, (own_outer,))
    tables = merge_tables(0, 1, *settings, own)
    for level in range(levels):
        stride = 2**level
        if level > 0:
            tables = merge_tables(level, stride, *settings, image)
            own, out, edges = split_image(level, image, fore_flag, rim)
            far = [from_partner(value, stride) for value in (out[..., :LANES], out[..., LANES:])]
            rims, far_rims = halos(tables[-1], edges, stride)
        image = merged_image(own, rims, far, far_rims, tables, BF16 if level + 1 < levels else F32)
    return image


def solution(mesh):
    placed_as = (
        P(None, ("sub", "rng"), None),
        P(None, None, "rng"),
        P(None, None, "rng"),
        P(),
        P(),
        P(),
    )
    return jax.shard_map(
        on_device, mesh=mesh, in_specs=placed_as, out_specs=P(None, "sub", "rng"), check_vma=False
    )
```

```python
import functools
import math

import jax
import jax.numpy as jnp
from jax import lax
from jax.experimental import pallas as pl
from jax.experimental.pallas import tpu as pltpu
from jax.sharding import PartitionSpec as P

MAX_SHIFT = 16
LANES = 128
MIB = 2**20
JOIN_COST = 10**11
SIDE = jax.ShapeDtypeStruct((8, LANES), jnp.float32)
VMEM = pl.BlockSpec(memory_space=pltpu.VMEM)
SMEM = pl.BlockSpec(memory_space=pltpu.SMEM)
ANY = pl.BlockSpec(memory_space=pl.ANY)
F32 = jnp.float32
BF16 = jnp.bfloat16


def dot(a, b):
    return jnp.dot(a, b, preferred_element_type=F32)


def params(mib):
    return pltpu.CompilerParams(vmem_limit_bytes=mib * MIB)


def series(square, first, count):
    coefs = [
        (-1) ** i * math.pi ** (2 * i + first) / math.factorial(2 * i + first)
        for i in range(count)
    ]
    total = jnp.full_like(square, coefs[-1])
    for coef in coefs[-2::-1]:
        total = total * square + coef
    return total


def cos_sin_pi(v):
    turns = jnp.floor(v + 0.5)
    rest = v - turns
    sign = 1.0 - 2.0 * (turns - 2.0 * jnp.floor(turns * 0.5))
    square = rest * rest
    return series(square, 0, 8) * sign, series(square, 1, 7) * rest * sign


def rotated(pair, step):
    return pair[0] * step[0] - pair[1] * step[1], pair[0] * step[1] + pair[1] * step[0]


def mixed(left, right):
    lane = lax.broadcasted_iota(jnp.int32, left.shape, 1)
    return jnp.where(lane < LANES // 2, left.astype(F32), right.astype(F32)).astype(BF16)


def place_kernel(echoes_ref, far_ref, near_ref, inner_ref):
    devices, _, count = inner_ref.shape
    bins = count + LANES
    half = devices // 2
    base = lax.axis_index("rng") // half * half

    def tile(device, first):
        return echoes_ref[:, pl.ds(pl.multiple_of(device * bins + first, LANES), LANES)]

    for ref, start in ((far_ref, half - base), (near_ref, base)):
        for i in range(half):
            ref[i] = mixed(tile(start + i, 0), tile(start + i, bins - LANES))
    for device in range(devices):
        begin = device * bins
        inner_ref[device, :, :LANES] = mixed(tile(device, bins - LANES), tile(device, 0))
        inner_ref[device, :, LANES:] = echoes_ref[:, begin + LANES : begin + bins - LANES]


def placed(echoes, devices):
    rows, columns = echoes.shape
    outer = jax.ShapeDtypeStruct((devices // 2, rows, LANES), BF16)
    inner = jax.ShapeDtypeStruct((devices, rows, columns // devices - LANES), BF16)
    return pl.pallas_call(
        place_kernel,
        out_shape=[outer, outer, inner],
        in_specs=[VMEM],
        out_specs=[VMEM] * 3,
        compiler_params=params(8),
        cost_estimate=pl.CostEstimate(flops=0, bytes_accessed=2 * MIB, transcendentals=0),
    )(echoes)


def join_kernel(near_ref, relay_ref, *refs):
    me = lax.axis_index("rng") % len(refs)
    rows = near_ref.shape[1]
    for d, out_ref in enumerate(refs):
        out_ref[:rows] = near_ref[me ^ d]
        out_ref[rows:] = relay_ref[me ^ d]


def joined(near, relay):
    half, rows, count = near.shape
    return pl.pallas_call(
        join_kernel,
        out_shape=[jax.ShapeDtypeStruct((2 * rows, count), BF16)] * half,
        in_specs=[VMEM] * 2,
        out_specs=[VMEM] * half,
        compiler_params=params(4),
        cost_estimate=pl.CostEstimate(flops=JOIN_COST, bytes_accessed=MIB, transcendentals=0),
    )(near, relay)


def across(value, mask):
    devices = lax.axis_size("rng")
    return lax.ppermute(value, "rng", [(i, i ^ mask) for i in range(devices)])


def filter_table_kernel(local_pulses, flag_ref, after_ref, rows_ref, side_ref, cos_ref, sin_ref):
    own_flag = flag_ref[0, lax.axis_index("sub"), 0]
    side_ref[...] = jnp.full(side_ref.shape, own_flag.astype(F32))
    half, columns = rows_ref.shape
    angles = 2 * half
    first = (1 - own_flag) * half
    base = cos_ref.shape[0]
    scale = 1.0 / math.sqrt(columns // 2)
    lane = lax.broadcasted_iota(jnp.int32, (8, columns), 1)
    slot = lane // (2 * local_pulses)
    second = lane // local_pulses % 2
    pulse = (slot * local_pulses + lane % local_pulses).astype(F32)
    lag = second.astype(F32) * 0.5
    per_angle = pulse * (1.0 / angles)
    row = lax.broadcasted_iota(jnp.int32, (8, columns), 0)
    for i in range(base // 8):
        twice = (2 * (row + 8 * i + first) + 1 - angles).astype(F32)
        cosine, sine = cos_sin_pi(twice * per_angle - lag)
        cos_ref[8 * i : 8 * i + 8, :] = cosine * scale
        sin_ref[8 * i : 8 * i + 8, :] = sine * scale
    step = cos_sin_pi(per_angle * (2 * base))
    for j in range(half // base):
        for i in range(base // 16):
            pair = []
            for k in (2 * i, 2 * i + 1):
                here = slice(8 * k, 8 * k + 8)
                now = cos_ref[here, :], sin_ref[here, :]
                pair.append(now[0])
                if j + 1 < half // base:
                    cos_ref[here, :], sin_ref[here, :] = rotated(now, step)
            begin = j * base + 16 * i
            rows_ref[begin : begin + 16, :] = jnp.concatenate(pair).astype(BF16)


def filter_table(fore_flag, angles, local_pulses, earlier):
    side = 2 * local_pulses * lax.axis_size("rng")
    return pl.pallas_call(
        functools.partial(filter_table_kernel, local_pulses),
        out_shape=[jax.ShapeDtypeStruct((angles // 2, side), BF16), SIDE],
        in_specs=[SMEM, ANY],
        out_specs=[VMEM] * 2,
        scratch_shapes=[pltpu.VMEM((64, side), F32)] * 2,
        compiler_params=params(6),
        cost_estimate=pl.CostEstimate(flops=9_000_000, bytes_accessed=4 * MIB, transcendentals=0),
    )(fore_flag, earlier)


def merge_table_kernel(
    level, stride, flag_ref, offset_ref, shift_ref, range_ref, interp_ref, after_ref, centre_ref,
    rim_ref, turn_ref, matrix_ref, side_ref, kernel_ref, sems,
):
    group = lax.axis_index("sub")
    block = lax.axis_index("rng")
    bins = centre_ref.shape[-1]
    angles = turn_ref.shape[-2]
    total_bins = lax.axis_size("rng") * bins
    taps = range_ref.shape[1]
    band = (taps - bins) // 2
    rim = MAX_SHIFT + band
    own_flag = flag_ref[level, group, 0]
    side_ref[...] = jnp.full(side_ref.shape, own_flag.astype(F32))
    copies = [
        pltpu.make_async_copy(source, target, sems.at[i])
        for i, (source, target) in enumerate(
            (
                (range_ref.at[level], kernel_ref),
                (interp_ref.at[level, own_flag], matrix_ref.at[0]),
                (interp_ref.at[level, 1 - own_flag], matrix_ref.at[1]),
            )
        )
    ]
    for copy in copies:
        copy.start()

    def moved(bin_id):
        tap = lax.broadcasted_iota(jnp.int32, (bin_id.shape[0], taps), 1)
        hot = jnp.where(tap == bin_id, 1.0, 0.0).astype(BF16)
        return dot(hot, kernel_ref[...]).astype(BF16)

    row = lax.broadcasted_iota(jnp.int32, (bins, 1), 0)
    upper = row + (bins - 2 * LANES)
    own_bin = jnp.where(row % LANES < LANES // 2, row, upper + LANES)
    own_bin = jnp.where(row >= LANES, jnp.where(row % LANES < LANES // 2, upper, row - LANES), own_bin)
    own_bin = jnp.where(row >= 2 * LANES, row - LANES, own_bin)
    rim_row = lax.broadcasted_iota(jnp.int32, (2 * rim, 1), 0)
    rim_bin = jnp.where(rim_row < rim, rim_row - rim, rim_row - rim + bins)
    rim_ref[...] = jnp.zeros(rim_ref.shape, BF16)
    bin_id = block * bins + lax.broadcasted_iota(jnp.int32, (8, bins), 1)
    reach = 1.0 + bin_id.astype(F32) * (1.0 / total_bins)
    line = lax.broadcasted_iota(jnp.int32, (8, bins), 0)
    base = 64
    members = group, group ^ stride
    for child, member in enumerate(members):
        rate = shift_ref[level, member]
        for first in range(0, base, 8):
            angle = (first + line).astype(F32)
            now = cos_sin_pi(rate * ((angle + 0.5) * (1.0 / angles) - 0.5) * reach)
            turn_ref[child, 0, first : first + 8, :] = now[0]
            turn_ref[child, 1, first : first + 8, :] = now[1]
        step = cos_sin_pi(rate * (base / angles) * reach)
        for first in range(base, angles, 8):
            here, last = slice(first, first + 8), slice(first - base, first - base + 8)
            now = rotated((turn_ref[child, 0, last, :], turn_ref[child, 1, last, :]), step)
            turn_ref[child, 0, here, :], turn_ref[child, 1, here, :] = now
    for copy in copies:
        copy.wait()
    for child, member in enumerate(members):
        lead = band - offset_ref[level, member, 0]
        centre_ref[child] = moved(own_bin + lead)
        ends = moved(rim_bin + lead)
        for part in range(2):
            for side in range(2):
                place = (2 * side + part) * rim
                rim_ref[child, part, place : place + rim, :] = ends[side * rim : (side + 1) * rim]


def merge_tables(
    level, stride, fore_flag, band_offset, center_shift, range_kernel, angle_interp, earlier
):
    taps, bins = range_kernel.shape[1:]
    angles = angle_interp.shape[2]
    rim = MAX_SHIFT + (taps - bins) // 2
    return pl.pallas_call(
        functools.partial(merge_table_kernel, level, stride),
        out_shape=[
            jax.ShapeDtypeStruct((2, bins, bins), BF16),
            jax.ShapeDtypeStruct((2, 2, 4 * rim, bins), BF16),
            jax.ShapeDtypeStruct((2, 2, angles, bins), F32),
            jax.ShapeDtypeStruct((2, *angle_interp.shape[2:]), BF16),
            SIDE,
        ],
        in_specs=[SMEM] * 3 + [ANY] * 3,
        out_specs=[VMEM] * 5,
        scratch_shapes=[pltpu.VMEM((taps, bins), BF16), pltpu.SemaphoreType.DMA((3,))],
        compiler_params=params(12),
        cost_estimate=pl.CostEstimate(
            flops=2_300_000_000, bytes_accessed=7 * MIB, transcendentals=0
        ),
    )(fore_flag, band_offset, center_shift, range_kernel, angle_interp, earlier)


def alternating(pulses, local_pulses):
    row = lax.broadcasted_iota(jnp.int32, (pulses.shape[0], 1), 0)
    pulse = row // (2 * local_pulses) * local_pulses + row % local_pulses
    return jnp.where(pulse % 2 == 1, -pulses, pulses)


def both_parts(pulses, local_pulses):
    count = pulses.shape[0]
    second = lax.broadcasted_iota(jnp.int32, (count, 1), 0) // local_pulses % 2 == 1
    ahead, behind = pltpu.roll(pulses, count - local_pulses, 0), pltpu.roll(pulses, local_pulses, 0)
    turned = jnp.where(second, -behind, ahead)
    return jnp.concatenate([pulses, turned], axis=1).astype(BF16)


def outer_kernel(pieces, side_ref, rows_ref, *refs):
    own_side = side_ref[:1, :]
    me = lax.axis_index("rng")
    own_ref, out_ref, *edge_refs = refs[pieces:-1]
    pulses_ref = refs[-1]
    rows = refs[0].shape[0] // 2
    for d, ref in enumerate(refs[:pieces]):
        for t in range(2):
            place = pl.multiple_of((me ^ (d + t * pieces)) * rows, rows)
            pulses_ref[pl.ds(place, rows), :] = ref[t * rows : (t + 1) * rows, :]
    pulses = pulses_ref[...]
    pulses = pulses.astype(F32)
    images = [
        dot(rows_ref[...], both_parts(value, rows // 2))
        for value in (alternating(pulses, rows // 2), pulses)
    ]
    half = own_ref.shape[1]
    rim = LANES // 4
    lane = lax.broadcasted_iota(jnp.int32, (1, LANES), 1)
    edges = [0.0, 0.0]
    for part in range(2):
        own, out = (image[:, part * LANES : (part + 1) * LANES] for image in images)
        own_ref[part] = own.astype(BF16)
        out_ref[part] = out.astype(BF16)
        for side in range(2):
            value = jnp.where(own_side == side, own, out)
            group = 2 * part + side
            for end in range(2):
                turn = (group + end) * rim % LANES
                moved = pltpu.roll(value, turn, 1) if turn else value
                edges[end] = edges[end] + jnp.where(lane // rim == group, moved, 0.0)
    even = me % 2 == 0
    edge_refs[0][...] = jnp.where(even, edges[1], edges[0]).astype(BF16)
    edge_refs[1][...] = jnp.where(even, edges[0], edges[1]).astype(BF16)


def outer_image(own_side, rows, pieces):
    half, side = rows.shape
    angles = 2 * half
    image = jax.ShapeDtypeStruct((2, angles // 2, LANES), BF16)
    edge = jax.ShapeDtypeStruct((angles // 2, LANES), BF16)
    return pl.pallas_call(
        functools.partial(outer_kernel, len(pieces)),
        out_shape=[image, image, edge, edge],
        in_specs=[VMEM] * (2 + len(pieces)),
        out_specs=[VMEM] * 4,
        scratch_shapes=[pltpu.VMEM((side, LANES), BF16)],
        compiler_params=params(10),
        cost_estimate=pl.CostEstimate(
            flops=4 * angles * side * LANES, bytes_accessed=3 * MIB, transcendentals=0
        ),
    )(own_side, rows, *pieces)


def partner_rows_kernel(local_pulses, rows_ref, pulses_ref, image_ref):
    count = pulses_ref.shape[1]
    image = dot(rows_ref[...], both_parts(pulses_ref[...].astype(F32), local_pulses))
    for part in range(2):
        image_ref[part] = image[:, part * count : (part + 1) * count].astype(BF16)


def own_rows_kernel(local_pulses, rows_ref, pulses_ref, outer_ref, image_ref):
    inner = pulses_ref.shape[1]
    pulses = alternating(pulses_ref[...].astype(F32), local_pulses)
    image = dot(rows_ref[...], both_parts(pulses, local_pulses))
    count = outer_ref.shape[2]
    image_ref[:, :, :count] = outer_ref[...]
    for part in range(2):
        image_ref[part, :, count:] = image[:, part * inner : (part + 1) * inner].astype(BF16)


def inner_image(kernel, angles, rows, pulses, outer=()):
    count = pulses.shape[1]
    whole = count + (outer[0].shape[2] if outer else 0)
    return pl.pallas_call(
        kernel,
        out_shape=jax.ShapeDtypeStruct((2, angles // 2, whole), BF16),
        in_specs=[VMEM] * (2 + len(outer)),
        out_specs=VMEM,
        compiler_params=params(10),
        cost_estimate=pl.CostEstimate(
            flops=2 * angles * rows.shape[1] * count, bytes_accessed=3 * MIB, transcendentals=0
        ),
    )(rows, pulses, *outer)


def exchanged(value, begin):
    devices = lax.axis_size("rng")
    pairs = [(i, i + 1) for i in range(begin, devices - 1, 2)]
    ends = [(i, i) for i in range(devices) if all(i not in pair for pair in pairs)]
    return lax.ppermute(value, "rng", pairs + [(j, i) for i, j in pairs] + ends)


def rims_kernel(side_ref, first_ref, second_ref, own_ref, out_ref):
    own_side = side_ref[:1, :]
    rim = LANES // 4
    me, devices = lax.axis_index("rng"), lax.axis_size("rng")
    even = me % 2 == 0
    first, second = first_ref[...].astype(F32), second_ref[...].astype(F32)
    below = jnp.where(me == 0, 0.0, jnp.where(even, second, first))
    above = jnp.where(me == devices - 1, 0.0, jnp.where(even, first, second))
    group = lax.broadcasted_iota(jnp.int32, (1, LANES), 1) // rim
    packed = [0.0, 0.0]
    for end, value in enumerate((below, above)):
        for part in range(2):
            place = 2 * end + part
            for side in range(2):
                turn = (place - (2 * part + side)) * rim % LANES
                moved = pltpu.roll(value, turn, 1) if turn else value
                packed[side] = packed[side] + jnp.where(group == place, moved, 0.0)
    own_ref[...] = jnp.where(own_side == 0, packed[0], packed[1]).astype(BF16)
    out_ref[...] = jnp.where(own_side == 0, packed[1], packed[0]).astype(BF16)


def sorted_rims(own_side, first, second):
    return pl.pallas_call(
        rims_kernel,
        out_shape=[jax.ShapeDtypeStruct(first.shape, BF16)] * 2,
        in_specs=[VMEM] * 3,
        out_specs=[VMEM] * 2,
        compiler_params=params(4),
        cost_estimate=pl.CostEstimate(flops=1_000_000, bytes_accessed=MIB // 4, transcendentals=0),
    )(own_side, first, second)


def resampled(image, rims_ref, centre_ref, rim_ref, value_ref, child):
    parts, half, bins = image.shape
    value_ref[...] = dot(image.reshape(parts * half, bins), centre_ref[child])
    rims = rims_ref[...]
    return [
        (value_ref[part * half : (part + 1) * half, :] + dot(rims, rim_ref[child, part])).astype(BF16)
        for part in range(parts)
    ]


def early_kernel(
    own_ref, rims_ref, centre_ref, rim_ref, matrix_ref, turn_ref, merged_ref, value_ref
):
    rows = resampled(own_ref[...], rims_ref, centre_ref, rim_ref, value_ref, 0)
    merged_ref[0], merged_ref[1] = rotated(
        (dot(matrix_ref[0], rows[0]), dot(matrix_ref[0], rows[1])), (turn_ref[0, 0], turn_ref[0, 1])
    )


def ends_of(value):
    count = value.shape[-1]
    return jnp.concatenate([value[..., :LANES], value[..., count - LANES :]], axis=-1)


def finish(values, lanes, merged_ref, matrix_ref, turn_ref, out_ref, buffer, sems):
    rows = [value.astype(BF16) for value in values]
    copies = []
    block = 2 * LANES
    for first in range(0, matrix_ref.shape[1], block):
        here = slice(first, first + block)
        matrix = matrix_ref[1, here]
        terms = dot(matrix, rows[0]), dot(matrix, rows[1])
        at = 0
        for begin, end in lanes:
            there = slice(at, at + end - begin)
            turned = rotated(
                (terms[0][:, there], terms[1][:, there]),
                (turn_ref[1, 0, here, begin:end], turn_ref[1, 1, here, begin:end]),
            )
            for part in range(2):
                total = merged_ref[part, here, begin:end] + turned[part]
                buffer[part, here, there] = total.astype(buffer.dtype)
            copy = pltpu.make_async_copy(
                buffer.at[:, here, there],
                out_ref.at[:, here, pl.ds(begin, end - begin)],
                sems.at[len(copies)],
            )
            copy.start()
            copies.append(copy)
            at += end - begin
    for copy in copies:
        copy.wait()


def middle_kernel(
    far_inner, merged_ref, centre_ref, matrix_ref, turn_ref, out_ref, partial_ref, buffer, sems
):
    parts, half, count = far_inner.shape
    bins = centre_ref.shape[2]
    inner = far_inner[...].reshape(parts * half, count)
    value = dot(inner, centre_ref[1, bins - count :, LANES : bins - LANES])
    values = [value[part * half : (part + 1) * half] for part in range(parts)]
    finish(
        values, [(LANES, bins - LANES)], merged_ref, matrix_ref, turn_ref, out_ref, buffer, sems
    )
    partial_ref[...] = dot(inner, ends_of(centre_ref[1, bins - count :, :]))


def end_kernel(
    far_outer, partial_ref, rims_ref, merged_ref, centre_ref, rim_ref, matrix_ref, turn_ref,
    begun_ref, out_ref, buffer, sems,
):
    parts, half, count = far_outer.shape
    bins = centre_ref.shape[2]
    centre = ends_of(centre_ref[1, :count, :])
    values = [
        partial_ref[part * half : (part + 1) * half, :]
        + dot(far_outer[part], centre)
        + dot(rims_ref[...], ends_of(rim_ref[1, part]))
        for part in range(parts)
    ]
    lanes = [(0, LANES), (bins - LANES, bins)]
    finish(values, lanes, merged_ref, matrix_ref, turn_ref, out_ref, buffer, sems)


def merged_image(own, rims, far, far_rims, tables, dtype):
    centre, rim, turn, matrices, _ = tables
    angles, bins = turn.shape[-2:]
    cost = pl.CostEstimate(flops=4 * angles * bins * bins, bytes_accessed=8 * MIB, transcendentals=0)
    value = pltpu.VMEM((angles, bins), F32)
    merged = pl.pallas_call(
        early_kernel,
        out_shape=jax.ShapeDtypeStruct((2, angles, bins), F32),
        in_specs=[VMEM] * 6,
        out_specs=VMEM,
        scratch_shapes=[value],
        compiler_params=params(16),
        cost_estimate=cost,
    )(own, rims, centre, rim, matrices, turn)
    image = jax.ShapeDtypeStruct((2, angles, bins), dtype)
    middle, ends = bins - 2 * LANES, 2 * LANES
    begun, partial = pl.pallas_call(
        middle_kernel,
        out_shape=[image, jax.ShapeDtypeStruct((angles, ends), F32)],
        in_specs=[VMEM] * 5,
        out_specs=[ANY, VMEM],
        scratch_shapes=[
            pltpu.VMEM((2, angles, middle), dtype),
            pltpu.SemaphoreType.DMA((angles // LANES,)),
        ],
        compiler_params=params(16),
        cost_estimate=cost,
    )(far[1], merged, centre, matrices, turn)
    return pl.pallas_call(
        end_kernel,
        out_shape=image,
        in_specs=[VMEM] * 8 + [ANY],
        out_specs=ANY,
        scratch_shapes=[
            pltpu.VMEM((2, angles, ends), dtype),
            pltpu.SemaphoreType.DMA((angles // LANES,)),
        ],
        input_output_aliases={8: 0},
        compiler_params=params(16),
        cost_estimate=cost,
    )(far[0], partial, far_rims, merged, centre, rim, matrices, turn, begun)


def after(value, *earlier):
    return lax.optimization_barrier((value, *earlier))[0]


def from_partner(value, stride):
    pairs = [(source, source ^ stride) for source in range(lax.axis_size("sub"))]
    return lax.ppermute(value, "sub", pairs)


def split_image(level, image, fore_flag, rim):
    angles, bins = image.shape[1:]
    half, step = angles // 2, LANES // 2
    own_flag = fore_flag[level, lax.axis_index("sub"), 0]
    sides = image.reshape(2, 2, half, bins)

    def pieces(side):
        rows = lax.dynamic_index_in_dim(sides, side, 1, keepdims=False)
        ends = [rows[..., :step], rows[..., -step:]]
        rest = [rows[..., -2 * step : -step], rows[..., step : -2 * step]]
        return jnp.concatenate(ends + rest, axis=-1)

    def packed(edge):
        return edge.transpose(2, 0, 1, 3).reshape(half, 4 * rim)

    low, high = packed(sides[..., :rim]), packed(sides[..., -rim:])
    even = lax.axis_index("rng") % 2 == 0
    edges = jnp.where(even, high, low), jnp.where(even, low, high)
    return pieces(own_flag), pieces(1 - own_flag), edges


def on_device(echoes, fore_flag, band_offset, angle_interp, range_kernel, center_shift):
    devices = lax.axis_size("rng")
    half = devices // 2
    local_pulses = echoes.shape[1]
    bins = echoes.shape[2] // devices
    angles = angle_interp.shape[2]
    rim = MAX_SHIFT + (range_kernel.shape[1] - bins) // 2
    levels = range_kernel.shape[0]
    settings = (fore_flag, band_offset, center_shift, range_kernel, angle_interp)

    far_blocks, near_blocks, blocks = placed(
        echoes.reshape(2 * local_pulses, devices * bins), devices
    )
    relay = across(far_blocks, half)
    pulses = lax.all_to_all(blocks, "rng", split_axis=0, concat_axis=0, tiled=True)
    sends = joined(near_blocks, relay)
    pieces = [across(value, d) if d else value for d, value in enumerate(sends)]
    matrix, own_side = filter_table(fore_flag, angles, local_pulses, sends[0])
    own_outer, out_outer, *edges = outer_image(own_side, matrix, pieces)

    pulses = after(pulses, out_outer).reshape(2 * local_pulses * devices, bins - LANES)
    out_kernel = functools.partial(partner_rows_kernel, local_pulses)
    out_inner = inner_image(out_kernel, angles, matrix, pulses)
    far = [from_partner(value, 1) for value in (out_outer, out_inner)]
    edges = [after(edge, out_inner) for edge in edges]
    edges = exchanged(edges[0], 0), exchanged(edges[1], 1)
    pulses = after(pulses, far[0], *edges)
    own_kernel = functools.partial(own_rows_kernel, local_pulses)
    own = inner_image(own_kernel, angles, matrix, pulses, (own_outer,))
    rims, out_rims = sorted_rims(own_side, *edges)
    tables = merge_tables(0, 1, *settings, after(out_rims, own))
    for level in range(levels):
        stride = 2**level
        if level > 0:
            tables = merge_tables(level, stride, *settings, image)
            own, out, edges = split_image(level, image, fore_flag, rim)
            far = [from_partner(value, stride) for value in (out[..., :LANES], out[..., LANES:])]
            edges = exchanged(edges[0], 0), exchanged(edges[1], 1)
            rims, out_rims = sorted_rims(tables[-1], *edges)
        far_rims = from_partner(out_rims, stride)
        image = merged_image(own, rims, far, far_rims, tables, BF16 if level + 1 < levels else F32)
    return image


def solution(mesh):
    placed_as = (
        P(None, ("sub", "rng"), None),
        P(None, None, "rng"),
        P(None, None, "rng"),
        P(),
        P(),
        P(),
    )
    return jax.shard_map(
        on_device, mesh=mesh, in_specs=placed_as, out_specs=P(None, "sub", "rng"), check_vma=False
    )
```

```python
import functools
import math

import jax
import jax.numpy as jnp
from jax import lax
from jax.experimental import pallas as pl
from jax.experimental.pallas import tpu as pltpu
from jax.sharding import PartitionSpec as P

MAX_SHIFT = 16
LANES = 128
MIB = 2**20
JOIN_COST = 10**11
SIDE = jax.ShapeDtypeStruct((8, LANES), jnp.float32)
VMEM = pl.BlockSpec(memory_space=pltpu.VMEM)
SMEM = pl.BlockSpec(memory_space=pltpu.SMEM)
ANY = pl.BlockSpec(memory_space=pl.ANY)
F32 = jnp.float32
BF16 = jnp.bfloat16


def dot(a, b):
    return jnp.dot(a, b, preferred_element_type=F32)


def params(mib):
    return pltpu.CompilerParams(vmem_limit_bytes=mib * MIB)


def series(square, first, count):
    coefs = [
        (-1) ** i * math.pi ** (2 * i + first) / math.factorial(2 * i + first)
        for i in range(count)
    ]
    total = jnp.full_like(square, coefs[-1])
    for coef in coefs[-2::-1]:
        total = total * square + coef
    return total


def cos_sin_pi(v):
    turns = jnp.floor(v + 0.5)
    rest = v - turns
    sign = 1.0 - 2.0 * (turns - 2.0 * jnp.floor(turns * 0.5))
    square = rest * rest
    return series(square, 0, 8) * sign, series(square, 1, 7) * rest * sign


def rotated(pair, step):
    return pair[0] * step[0] - pair[1] * step[1], pair[0] * step[1] + pair[1] * step[0]


def mixed(left, right):
    lane = lax.broadcasted_iota(jnp.int32, left.shape, 1)
    return jnp.where(lane < LANES // 2, left.astype(F32), right.astype(F32)).astype(BF16)


def place_kernel(echoes_ref, far_ref, near_ref, inner_ref):
    devices, _, count = inner_ref.shape
    bins = count + LANES
    half = devices // 2
    base = lax.axis_index("rng") // half * half

    def tile(device, first):
        return echoes_ref[:, pl.ds(pl.multiple_of(device * bins + first, LANES), LANES)]

    for ref, start in ((far_ref, half - base), (near_ref, base)):
        for i in range(half):
            ref[i] = mixed(tile(start + i, 0), tile(start + i, bins - LANES))
    for device in range(devices):
        begin = device * bins
        inner_ref[device, :, :LANES] = mixed(tile(device, bins - LANES), tile(device, 0))
        inner_ref[device, :, LANES:] = echoes_ref[:, begin + LANES : begin + bins - LANES]


def placed(echoes, devices):
    rows, columns = echoes.shape
    outer = jax.ShapeDtypeStruct((devices // 2, rows, LANES), BF16)
    inner = jax.ShapeDtypeStruct((devices, rows, columns // devices - LANES), BF16)
    return pl.pallas_call(
        place_kernel,
        out_shape=[outer, outer, inner],
        in_specs=[VMEM],
        out_specs=[VMEM] * 3,
        compiler_params=params(8),
        cost_estimate=pl.CostEstimate(flops=0, bytes_accessed=2 * MIB, transcendentals=0),
    )(echoes)


def join_kernel(near_ref, relay_ref, *refs):
    me = lax.axis_index("rng") % len(refs)
    rows = near_ref.shape[1]
    for d, out_ref in enumerate(refs):
        out_ref[:rows] = near_ref[me ^ d]
        out_ref[rows:] = relay_ref[me ^ d]


def joined(near, relay):
    half, rows, count = near.shape
    return pl.pallas_call(
        join_kernel,
        out_shape=[jax.ShapeDtypeStruct((2 * rows, count), BF16)] * half,
        in_specs=[VMEM] * 2,
        out_specs=[VMEM] * half,
        compiler_params=params(4),
        cost_estimate=pl.CostEstimate(flops=JOIN_COST, bytes_accessed=MIB, transcendentals=0),
    )(near, relay)


def across(value, mask):
    devices = lax.axis_size("rng")
    return lax.ppermute(value, "rng", [(i, i ^ mask) for i in range(devices)])


def filter_table_kernel(local_pulses, flag_ref, after_ref, rows_ref, side_ref, cos_ref, sin_ref):
    own_flag = flag_ref[0, lax.axis_index("sub"), 0]
    side_ref[...] = jnp.full(side_ref.shape, own_flag.astype(F32))
    half, columns = rows_ref.shape
    angles = 2 * half
    first = (1 - own_flag) * half
    base = cos_ref.shape[0]
    scale = 1.0 / math.sqrt(columns // 2)
    lane = lax.broadcasted_iota(jnp.int32, (8, columns), 1)
    slot = lane // (2 * local_pulses)
    second = lane // local_pulses % 2
    pulse = (slot * local_pulses + lane % local_pulses).astype(F32)
    lag = second.astype(F32) * 0.5
    per_angle = pulse * (1.0 / angles)
    row = lax.broadcasted_iota(jnp.int32, (8, columns), 0)
    for i in range(base // 8):
        twice = (2 * (row + 8 * i + first) + 1 - angles).astype(F32)
        cosine, sine = cos_sin_pi(twice * per_angle - lag)
        cos_ref[8 * i : 8 * i + 8, :] = cosine * scale
        sin_ref[8 * i : 8 * i + 8, :] = sine * scale
    step = cos_sin_pi(per_angle * (2 * base))
    for j in range(half // base):
        for i in range(base // 16):
            pair = []
            for k in (2 * i, 2 * i + 1):
                here = slice(8 * k, 8 * k + 8)
                now = cos_ref[here, :], sin_ref[here, :]
                pair.append(now[0])
                if j + 1 < half // base:
                    cos_ref[here, :], sin_ref[here, :] = rotated(now, step)
            begin = j * base + 16 * i
            rows_ref[begin : begin + 16, :] = jnp.concatenate(pair).astype(BF16)


def filter_table(fore_flag, angles, local_pulses, earlier):
    side = 2 * local_pulses * lax.axis_size("rng")
    return pl.pallas_call(
        functools.partial(filter_table_kernel, local_pulses),
        out_shape=[jax.ShapeDtypeStruct((angles // 2, side), BF16), SIDE],
        in_specs=[SMEM, ANY],
        out_specs=[VMEM] * 2,
        scratch_shapes=[pltpu.VMEM((64, side), F32)] * 2,
        compiler_params=params(6),
        cost_estimate=pl.CostEstimate(flops=9_000_000, bytes_accessed=4 * MIB, transcendentals=0),
    )(fore_flag, earlier)


def merge_table_kernel(
    level, stride, flag_ref, offset_ref, shift_ref, range_ref, interp_ref, after_ref, centre_ref,
    rim_ref, turn_ref, matrix_ref, side_ref, kernel_ref, sems,
):
    group = lax.axis_index("sub")
    block = lax.axis_index("rng")
    bins = centre_ref.shape[-1]
    angles = turn_ref.shape[-2]
    total_bins = lax.axis_size("rng") * bins
    taps = range_ref.shape[1]
    band = (taps - bins) // 2
    rim = MAX_SHIFT + band
    own_flag = flag_ref[level, group, 0]
    side_ref[...] = jnp.full(side_ref.shape, own_flag.astype(F32))
    copies = [
        pltpu.make_async_copy(source, target, sems.at[i])
        for i, (source, target) in enumerate(
            (
                (range_ref.at[level], kernel_ref),
                (interp_ref.at[level, own_flag], matrix_ref.at[0]),
                (interp_ref.at[level, 1 - own_flag], matrix_ref.at[1]),
            )
        )
    ]
    for copy in copies:
        copy.start()

    def moved(bin_id):
        tap = lax.broadcasted_iota(jnp.int32, (bin_id.shape[0], taps), 1)
        hot = jnp.where(tap == bin_id, 1.0, 0.0).astype(BF16)
        return dot(hot, kernel_ref[...]).astype(BF16)

    row = lax.broadcasted_iota(jnp.int32, (bins, 1), 0)
    upper = row + (bins - 2 * LANES)
    own_bin = jnp.where(row % LANES < LANES // 2, row, upper + LANES)
    own_bin = jnp.where(row >= LANES, jnp.where(row % LANES < LANES // 2, upper, row - LANES), own_bin)
    own_bin = jnp.where(row >= 2 * LANES, row - LANES, own_bin)
    rim_row = lax.broadcasted_iota(jnp.int32, (2 * rim, 1), 0)
    rim_bin = jnp.where(rim_row < rim, rim_row - rim, rim_row - rim + bins)
    rim_ref[...] = jnp.zeros(rim_ref.shape, BF16)
    bin_id = block * bins + lax.broadcasted_iota(jnp.int32, (8, bins), 1)
    reach = 1.0 + bin_id.astype(F32) * (1.0 / total_bins)
    line = lax.broadcasted_iota(jnp.int32, (8, bins), 0)
    base = 64
    members = group, group ^ stride
    for child, member in enumerate(members):
        rate = shift_ref[level, member]
        for first in range(0, base, 8):
            angle = (first + line).astype(F32)
            now = cos_sin_pi(rate * ((angle + 0.5) * (1.0 / angles) - 0.5) * reach)
            turn_ref[child, 0, first : first + 8, :] = now[0]
            turn_ref[child, 1, first : first + 8, :] = now[1]
        step = cos_sin_pi(rate * (base / angles) * reach)
        for first in range(base, angles, 8):
            here, last = slice(first, first + 8), slice(first - base, first - base + 8)
            now = rotated((turn_ref[child, 0, last, :], turn_ref[child, 1, last, :]), step)
            turn_ref[child, 0, here, :], turn_ref[child, 1, here, :] = now
    for copy in copies:
        copy.wait()
    for child, member in enumerate(members):
        lead = band - offset_ref[level, member, 0]
        centre_ref[child] = moved(own_bin + lead)
        ends = moved(rim_bin + lead)
        for part in range(2):
            for side in range(2):
                place = (2 * side + part) * rim
                rim_ref[child, part, place : place + rim, :] = ends[side * rim : (side + 1) * rim]


def merge_tables(
    level, stride, fore_flag, band_offset, center_shift, range_kernel, angle_interp, earlier
):
    taps, bins = range_kernel.shape[1:]
    angles = angle_interp.shape[2]
    rim = MAX_SHIFT + (taps - bins) // 2
    return pl.pallas_call(
        functools.partial(merge_table_kernel, level, stride),
        out_shape=[
            jax.ShapeDtypeStruct((2, bins, bins), BF16),
            jax.ShapeDtypeStruct((2, 2, 4 * rim, bins), BF16),
            jax.ShapeDtypeStruct((2, 2, angles, bins), F32),
            jax.ShapeDtypeStruct((2, *angle_interp.shape[2:]), BF16),
            SIDE,
        ],
        in_specs=[SMEM] * 3 + [ANY] * 3,
        out_specs=[VMEM] * 5,
        scratch_shapes=[pltpu.VMEM((taps, bins), BF16), pltpu.SemaphoreType.DMA((3,))],
        compiler_params=params(12),
        cost_estimate=pl.CostEstimate(
            flops=2_300_000_000, bytes_accessed=7 * MIB, transcendentals=0
        ),
    )(fore_flag, band_offset, center_shift, range_kernel, angle_interp, earlier)


def alternating(pulses, local_pulses):
    row = lax.broadcasted_iota(jnp.int32, (pulses.shape[0], 1), 0)
    pulse = row // (2 * local_pulses) * local_pulses + row % local_pulses
    return jnp.where(pulse % 2 == 1, -pulses, pulses)


def both_parts(pulses, local_pulses):
    count = pulses.shape[0]
    second = lax.broadcasted_iota(jnp.int32, (count, 1), 0) // local_pulses % 2 == 1
    ahead, behind = pltpu.roll(pulses, count - local_pulses, 0), pltpu.roll(pulses, local_pulses, 0)
    turned = jnp.where(second, -behind, ahead)
    return jnp.concatenate([pulses, turned], axis=1).astype(BF16)


def outer_kernel(pieces, side_ref, rows_ref, *refs):
    own_side = side_ref[:1, :]
    me = lax.axis_index("rng")
    own_ref, out_ref, *edge_refs = refs[pieces:-1]
    pulses_ref = refs[-1]
    rows = refs[0].shape[0] // 2
    for d, ref in enumerate(refs[:pieces]):
        for t in range(2):
            place = pl.multiple_of((me ^ (d + t * pieces)) * rows, rows)
            pulses_ref[pl.ds(place, rows), :] = ref[t * rows : (t + 1) * rows, :]
    pulses = pulses_ref[...]
    pulses = pulses.astype(F32)
    images = [
        dot(rows_ref[...], both_parts(value, rows // 2))
        for value in (alternating(pulses, rows // 2), pulses)
    ]
    half = own_ref.shape[1]
    rim = LANES // 4
    lane = lax.broadcasted_iota(jnp.int32, (1, LANES), 1)
    edges = [0.0, 0.0]
    for part in range(2):
        own, out = (image[:, part * LANES : (part + 1) * LANES] for image in images)
        own_ref[part] = own.astype(BF16)
        out_ref[part] = out.astype(BF16)
        for side in range(2):
            value = jnp.where(own_side == side, own, out)
            group = 2 * part + side
            for end in range(2):
                turn = (group + end) * rim % LANES
                moved = pltpu.roll(value, turn, 1) if turn else value
                edges[end] = edges[end] + jnp.where(lane // rim == group, moved, 0.0)
    even = me % 2 == 0
    edge_refs[0][...] = jnp.where(even, edges[1], edges[0]).astype(BF16)
    edge_refs[1][...] = jnp.where(even, edges[0], edges[1]).astype(BF16)


def outer_image(own_side, rows, pieces):
    half, side = rows.shape
    angles = 2 * half
    image = jax.ShapeDtypeStruct((2, angles // 2, LANES), BF16)
    edge = jax.ShapeDtypeStruct((angles // 2, LANES), BF16)
    return pl.pallas_call(
        functools.partial(outer_kernel, len(pieces)),
        out_shape=[image, image, edge, edge],
        in_specs=[VMEM] * (2 + len(pieces)),
        out_specs=[VMEM] * 4,
        scratch_shapes=[pltpu.VMEM((side, LANES), BF16)],
        compiler_params=params(10),
        cost_estimate=pl.CostEstimate(
            flops=4 * angles * side * LANES, bytes_accessed=3 * MIB, transcendentals=0
        ),
    )(own_side, rows, *pieces)


def partner_rows_kernel(local_pulses, rows_ref, pulses_ref, image_ref):
    count = pulses_ref.shape[1]
    image = dot(rows_ref[...], both_parts(pulses_ref[...].astype(F32), local_pulses))
    for part in range(2):
        image_ref[part] = image[:, part * count : (part + 1) * count].astype(BF16)


def own_rows_kernel(local_pulses, rows_ref, pulses_ref, outer_ref, image_ref):
    inner = pulses_ref.shape[1]
    pulses = alternating(pulses_ref[...].astype(F32), local_pulses)
    image = dot(rows_ref[...], both_parts(pulses, local_pulses))
    count = outer_ref.shape[2]
    image_ref[:, :, :count] = outer_ref[...]
    for part in range(2):
        image_ref[part, :, count:] = image[:, part * inner : (part + 1) * inner].astype(BF16)


def inner_image(kernel, angles, rows, pulses, outer=()):
    count = pulses.shape[1]
    whole = count + (outer[0].shape[2] if outer else 0)
    return pl.pallas_call(
        kernel,
        out_shape=jax.ShapeDtypeStruct((2, angles // 2, whole), BF16),
        in_specs=[VMEM] * (2 + len(outer)),
        out_specs=VMEM,
        compiler_params=params(10),
        cost_estimate=pl.CostEstimate(
            flops=2 * angles * rows.shape[1] * count, bytes_accessed=3 * MIB, transcendentals=0
        ),
    )(rows, pulses, *outer)


def exchanged(value, begin):
    devices = lax.axis_size("rng")
    pairs = [(i, i + 1) for i in range(begin, devices - 1, 2)]
    ends = [(i, i) for i in range(devices) if all(i not in pair for pair in pairs)]
    return lax.ppermute(value, "rng", pairs + [(j, i) for i, j in pairs] + ends)


def rims_kernel(side_ref, first_ref, second_ref, own_ref, out_ref):
    own_side = side_ref[:1, :]
    rim = LANES // 4
    me, devices = lax.axis_index("rng"), lax.axis_size("rng")
    even = me % 2 == 0
    first, second = first_ref[...].astype(F32), second_ref[...].astype(F32)
    below = jnp.where(me == 0, 0.0, jnp.where(even, second, first))
    above = jnp.where(me == devices - 1, 0.0, jnp.where(even, first, second))
    group = lax.broadcasted_iota(jnp.int32, (1, LANES), 1) // rim
    packed = [0.0, 0.0]
    for end, value in enumerate((below, above)):
        for part in range(2):
            place = 2 * end + part
            for side in range(2):
                turn = (place - (2 * part + side)) * rim % LANES
                moved = pltpu.roll(value, turn, 1) if turn else value
                packed[side] = packed[side] + jnp.where(group == place, moved, 0.0)
    own_ref[...] = jnp.where(own_side == 0, packed[0], packed[1]).astype(BF16)
    out_ref[...] = jnp.where(own_side == 0, packed[1], packed[0]).astype(BF16)


def sorted_rims(own_side, first, second):
    return pl.pallas_call(
        rims_kernel,
        out_shape=[jax.ShapeDtypeStruct(first.shape, BF16)] * 2,
        in_specs=[VMEM] * 3,
        out_specs=[VMEM] * 2,
        compiler_params=params(4),
        cost_estimate=pl.CostEstimate(flops=1_000_000, bytes_accessed=MIB // 4, transcendentals=0),
    )(own_side, first, second)


def resampled(image, rims_ref, centre_ref, rim_ref, value_ref, child):
    parts, half, bins = image.shape
    value_ref[...] = dot(image.reshape(parts * half, bins), centre_ref[child])
    rims = rims_ref[...]
    return [
        (value_ref[part * half : (part + 1) * half, :] + dot(rims, rim_ref[child, part])).astype(BF16)
        for part in range(parts)
    ]


def early_kernel(
    own_ref, rims_ref, centre_ref, rim_ref, matrix_ref, turn_ref, merged_ref, value_ref
):
    rows = resampled(own_ref[...], rims_ref, centre_ref, rim_ref, value_ref, 0)
    merged_ref[0], merged_ref[1] = rotated(
        (dot(matrix_ref[0], rows[0]), dot(matrix_ref[0], rows[1])), (turn_ref[0, 0], turn_ref[0, 1])
    )


def ends_of(value):
    count = value.shape[-1]
    return jnp.concatenate([value[..., :LANES], value[..., count - LANES :]], axis=-1)


def finish(values, lanes, merged_ref, matrix_ref, turn_ref, out_ref, buffer, sems):
    rows = [value.astype(BF16) for value in values]
    copies = []
    block = 2 * LANES
    for first in range(0, matrix_ref.shape[1], block):
        here = slice(first, first + block)
        matrix = matrix_ref[1, here]
        terms = dot(matrix, rows[0]), dot(matrix, rows[1])
        at = 0
        for begin, end in lanes:
            there = slice(at, at + end - begin)
            turned = rotated(
                (terms[0][:, there], terms[1][:, there]),
                (turn_ref[1, 0, here, begin:end], turn_ref[1, 1, here, begin:end]),
            )
            for part in range(2):
                total = merged_ref[part, here, begin:end] + turned[part]
                buffer[part, here, there] = total.astype(buffer.dtype)
            copy = pltpu.make_async_copy(
                buffer.at[:, here, there],
                out_ref.at[:, here, pl.ds(begin, end - begin)],
                sems.at[len(copies)],
            )
            copy.start()
            copies.append(copy)
            at += end - begin
    for copy in copies:
        copy.wait()


def middle_kernel(
    far_inner, merged_ref, centre_ref, matrix_ref, turn_ref, out_ref, partial_ref, buffer, sems
):
    parts, half, count = far_inner.shape
    bins = centre_ref.shape[2]
    inner = far_inner[...].reshape(parts * half, count)
    value = dot(inner, centre_ref[1, bins - count :, LANES : bins - LANES])
    values = [value[part * half : (part + 1) * half] for part in range(parts)]
    finish(
        values, [(LANES, bins - LANES)], merged_ref, matrix_ref, turn_ref, out_ref, buffer, sems
    )
    partial_ref[...] = dot(inner, ends_of(centre_ref[1, bins - count :, :]))


def end_kernel(
    far_outer, partial_ref, rims_ref, merged_ref, centre_ref, rim_ref, matrix_ref, turn_ref,
    begun_ref, out_ref, buffer, sems,
):
    parts, half, count = far_outer.shape
    bins = centre_ref.shape[2]
    centre = ends_of(centre_ref[1, :count, :])
    values = [
        partial_ref[part * half : (part + 1) * half, :]
        + dot(far_outer[part], centre)
        + dot(rims_ref[...], ends_of(rim_ref[1, part]))
        for part in range(parts)
    ]
    lanes = [(0, LANES), (bins - LANES, bins)]
    finish(values, lanes, merged_ref, matrix_ref, turn_ref, out_ref, buffer, sems)


def merged_image(own, rims, far, far_rims, tables, dtype):
    centre, rim, turn, matrices, _ = tables
    angles, bins = turn.shape[-2:]
    cost = pl.CostEstimate(flops=4 * angles * bins * bins, bytes_accessed=8 * MIB, transcendentals=0)
    value = pltpu.VMEM((angles, bins), F32)
    merged = pl.pallas_call(
        early_kernel,
        out_shape=jax.ShapeDtypeStruct((2, angles, bins), F32),
        in_specs=[VMEM] * 6,
        out_specs=VMEM,
        scratch_shapes=[value],
        compiler_params=params(16),
        cost_estimate=cost,
    )(own, rims, centre, rim, matrices, turn)
    image = jax.ShapeDtypeStruct((2, angles, bins), dtype)
    middle, ends = bins - 2 * LANES, 2 * LANES
    begun, partial = pl.pallas_call(
        middle_kernel,
        out_shape=[image, jax.ShapeDtypeStruct((angles, ends), F32)],
        in_specs=[VMEM] * 5,
        out_specs=[ANY, VMEM],
        scratch_shapes=[
            pltpu.VMEM((2, angles, middle), dtype),
            pltpu.SemaphoreType.DMA((angles // LANES,)),
        ],
        compiler_params=params(16),
        cost_estimate=cost,
    )(far[1], merged, centre, matrices, turn)
    return pl.pallas_call(
        end_kernel,
        out_shape=image,
        in_specs=[VMEM] * 8 + [ANY],
        out_specs=ANY,
        scratch_shapes=[
            pltpu.VMEM((2, angles, ends), dtype),
            pltpu.SemaphoreType.DMA((angles // LANES,)),
        ],
        input_output_aliases={8: 0},
        compiler_params=params(16),
        cost_estimate=cost,
    )(far[0], partial, far_rims, merged, centre, rim, matrices, turn, begun)


def after(value, *earlier):
    return lax.optimization_barrier((value, *earlier))[0]


def from_partner(value, stride):
    pairs = [(source, source ^ stride) for source in range(lax.axis_size("sub"))]
    return lax.ppermute(value, "sub", pairs)


def split_image(level, image, fore_flag, rim):
    angles, bins = image.shape[1:]
    half, step = angles // 2, LANES // 2
    own_flag = fore_flag[level, lax.axis_index("sub"), 0]
    sides = image.reshape(2, 2, half, bins)

    def pieces(side):
        rows = lax.dynamic_index_in_dim(sides, side, 1, keepdims=False)
        ends = [rows[..., :step], rows[..., -step:]]
        rest = [rows[..., -2 * step : -step], rows[..., step : -2 * step]]
        return jnp.concatenate(ends + rest, axis=-1)

    def packed(edge):
        return edge.transpose(2, 0, 1, 3).reshape(half, 4 * rim)

    low, high = packed(sides[..., :rim]), packed(sides[..., -rim:])
    even = lax.axis_index("rng") % 2 == 0
    edges = jnp.where(even, high, low), jnp.where(even, low, high)
    return pieces(own_flag), pieces(1 - own_flag), edges


def on_device(echoes, fore_flag, band_offset, angle_interp, range_kernel, center_shift):
    devices = lax.axis_size("rng")
    half = devices // 2
    local_pulses = echoes.shape[1]
    bins = echoes.shape[2] // devices
    angles = angle_interp.shape[2]
    rim = MAX_SHIFT + (range_kernel.shape[1] - bins) // 2
    levels = range_kernel.shape[0]
    settings = (fore_flag, band_offset, center_shift, range_kernel, angle_interp)

    far_blocks, near_blocks, blocks = placed(
        echoes.reshape(2 * local_pulses, devices * bins), devices
    )
    relay = across(far_blocks, half)
    pulses = lax.all_to_all(blocks, "rng", split_axis=0, concat_axis=0, tiled=True)
    sends = joined(near_blocks, relay)
    pieces = [across(value, d) if d else value for d, value in enumerate(sends)]
    matrix, own_side = filter_table(fore_flag, angles, local_pulses, sends[0])
    own_outer, out_outer, *edges = outer_image(own_side, matrix, pieces)

    pulses = after(pulses, out_outer).reshape(2 * local_pulses * devices, bins - LANES)
    out_kernel = functools.partial(partner_rows_kernel, local_pulses)
    out_inner = inner_image(out_kernel, angles, matrix, pulses)
    far = [from_partner(value, 1) for value in (out_outer, out_inner)]
    edges = [after(edge, out_inner) for edge in edges]
    edges = exchanged(edges[0], 0), exchanged(edges[1], 1)
    pulses = after(pulses, far[0])
    own_kernel = functools.partial(own_rows_kernel, local_pulses)
    own = inner_image(own_kernel, angles, matrix, pulses, (own_outer,))
    tables = merge_tables(0, 1, *settings, after(own_side, far[0]))
    rims, out_rims = sorted_rims(own_side, after(edges[0], tables[0]), edges[1])
    for level in range(levels):
        stride = 2**level
        if level > 0:
            tables = merge_tables(level, stride, *settings, image)
            own, out, edges = split_image(level, image, fore_flag, rim)
            far = [from_partner(value, stride) for value in (out[..., :LANES], out[..., LANES:])]
            edges = exchanged(edges[0], 0), exchanged(edges[1], 1)
            rims, out_rims = sorted_rims(tables[-1], *edges)
        far_rims = from_partner(out_rims, stride)
        image = merged_image(own, rims, far, far_rims, tables, BF16 if level + 1 < levels else F32)
    return image


def solution(mesh):
    placed_as = (
        P(None, ("sub", "rng"), None),
        P(None, None, "rng"),
        P(None, None, "rng"),
        P(),
        P(),
        P(),
    )
    return jax.shard_map(
        on_device, mesh=mesh, in_specs=placed_as, out_specs=P(None, "sub", "rng"), check_vma=False
    )
```

```python
import functools
import math

import jax
import jax.numpy as jnp
from jax import lax
from jax.experimental import pallas as pl
from jax.experimental.pallas import tpu as pltpu
from jax.sharding import PartitionSpec as P

MAX_SHIFT = 16
LANES = 128
MIB = 2**20
JOIN_COST = 10**11
SIDE = jax.ShapeDtypeStruct((8, LANES), jnp.float32)
VMEM = pl.BlockSpec(memory_space=pltpu.VMEM)
SMEM = pl.BlockSpec(memory_space=pltpu.SMEM)
ANY = pl.BlockSpec(memory_space=pl.ANY)
F32 = jnp.float32
BF16 = jnp.bfloat16


def dot(a, b):
    return jnp.dot(a, b, preferred_element_type=F32)


def params(mib):
    return pltpu.CompilerParams(vmem_limit_bytes=mib * MIB)


def series(square, first, count):
    coefs = [
        (-1) ** i * math.pi ** (2 * i + first) / math.factorial(2 * i + first)
        for i in range(count)
    ]
    total = jnp.full_like(square, coefs[-1])
    for coef in coefs[-2::-1]:
        total = total * square + coef
    return total


def cos_sin_pi(v):
    turns = jnp.floor(v + 0.5)
    rest = v - turns
    sign = 1.0 - 2.0 * (turns - 2.0 * jnp.floor(turns * 0.5))
    square = rest * rest
    return series(square, 0, 8) * sign, series(square, 1, 7) * rest * sign


def rotated(pair, step):
    return pair[0] * step[0] - pair[1] * step[1], pair[0] * step[1] + pair[1] * step[0]


def mixed(left, right):
    lane = lax.broadcasted_iota(jnp.int32, left.shape, 1)
    return jnp.where(lane < LANES // 2, left.astype(F32), right.astype(F32)).astype(BF16)


def place_kernel(echoes_ref, far_ref, near_ref, inner_ref):
    devices, _, count = inner_ref.shape
    bins = count + LANES
    half = devices // 2
    base = lax.axis_index("rng") // half * half

    def tile(device, first):
        return echoes_ref[:, pl.ds(pl.multiple_of(device * bins + first, LANES), LANES)]

    for ref, start in ((far_ref, half - base), (near_ref, base)):
        for i in range(half):
            ref[i] = mixed(tile(start + i, 0), tile(start + i, bins - LANES))
    for device in range(devices):
        begin = device * bins
        inner_ref[device, :, :LANES] = mixed(tile(device, bins - LANES), tile(device, 0))
        inner_ref[device, :, LANES:] = echoes_ref[:, begin + LANES : begin + bins - LANES]


def placed(echoes, devices):
    rows, columns = echoes.shape
    outer = jax.ShapeDtypeStruct((devices // 2, rows, LANES), BF16)
    inner = jax.ShapeDtypeStruct((devices, rows, columns // devices - LANES), BF16)
    return pl.pallas_call(
        place_kernel,
        out_shape=[outer, outer, inner],
        in_specs=[VMEM],
        out_specs=[VMEM] * 3,
        compiler_params=params(8),
        cost_estimate=pl.CostEstimate(flops=0, bytes_accessed=2 * MIB, transcendentals=0),
    )(echoes)


def join_kernel(near_ref, relay_ref, *refs):
    me = lax.axis_index("rng") % len(refs)
    rows = near_ref.shape[1]
    for d, out_ref in enumerate(refs):
        out_ref[:rows] = near_ref[me ^ d]
        out_ref[rows:] = relay_ref[me ^ d]


def joined(near, relay):
    half, rows, count = near.shape
    return pl.pallas_call(
        join_kernel,
        out_shape=[jax.ShapeDtypeStruct((2 * rows, count), BF16)] * half,
        in_specs=[VMEM] * 2,
        out_specs=[VMEM] * half,
        compiler_params=params(4),
        cost_estimate=pl.CostEstimate(flops=JOIN_COST, bytes_accessed=MIB, transcendentals=0),
    )(near, relay)


def across(value, mask):
    devices = lax.axis_size("rng")
    return lax.ppermute(value, "rng", [(i, i ^ mask) for i in range(devices)])


def filter_table_kernel(local_pulses, flag_ref, after_ref, rows_ref, side_ref, cos_ref, sin_ref):
    own_flag = flag_ref[0, lax.axis_index("sub"), 0]
    side_ref[...] = jnp.full(side_ref.shape, own_flag.astype(F32))
    half, columns = rows_ref.shape
    angles = 2 * half
    first = (1 - own_flag) * half
    base = cos_ref.shape[0]
    scale = 1.0 / math.sqrt(columns // 2)
    lane = lax.broadcasted_iota(jnp.int32, (8, columns), 1)
    slot = lane // (2 * local_pulses)
    second = lane // local_pulses % 2
    pulse = (slot * local_pulses + lane % local_pulses).astype(F32)
    lag = second.astype(F32) * 0.5
    per_angle = pulse * (1.0 / angles)
    row = lax.broadcasted_iota(jnp.int32, (8, columns), 0)
    for i in range(base // 8):
        twice = (2 * (row + 8 * i + first) + 1 - angles).astype(F32)
        cosine, sine = cos_sin_pi(twice * per_angle - lag)
        cos_ref[8 * i : 8 * i + 8, :] = cosine * scale
        sin_ref[8 * i : 8 * i + 8, :] = sine * scale
    step = cos_sin_pi(per_angle * (2 * base))
    for j in range(half // base):
        for i in range(base // 16):
            pair = []
            for k in (2 * i, 2 * i + 1):
                here = slice(8 * k, 8 * k + 8)
                now = cos_ref[here, :], sin_ref[here, :]
                pair.append(now[0])
                if j + 1 < half // base:
                    cos_ref[here, :], sin_ref[here, :] = rotated(now, step)
            begin = j * base + 16 * i
            rows_ref[begin : begin + 16, :] = jnp.concatenate(pair).astype(BF16)


def filter_table(fore_flag, angles, local_pulses, earlier):
    side = 2 * local_pulses * lax.axis_size("rng")
    return pl.pallas_call(
        functools.partial(filter_table_kernel, local_pulses),
        out_shape=[jax.ShapeDtypeStruct((angles // 2, side), BF16), SIDE],
        in_specs=[SMEM, ANY],
        out_specs=[VMEM] * 2,
        scratch_shapes=[pltpu.VMEM((64, side), F32)] * 2,
        compiler_params=params(6),
        cost_estimate=pl.CostEstimate(flops=9_000_000, bytes_accessed=4 * MIB, transcendentals=0),
    )(fore_flag, earlier)


def merge_table_kernel(
    level, stride, flag_ref, offset_ref, shift_ref, range_ref, interp_ref, after_ref, centre_ref,
    rim_ref, turn_ref, matrix_ref, side_ref, kernel_ref, sems,
):
    group = lax.axis_index("sub")
    block = lax.axis_index("rng")
    bins = centre_ref.shape[-1]
    angles = turn_ref.shape[-2]
    total_bins = lax.axis_size("rng") * bins
    taps = range_ref.shape[1]
    band = (taps - bins) // 2
    rim = MAX_SHIFT + band
    own_flag = flag_ref[level, group, 0]
    side_ref[...] = jnp.full(side_ref.shape, own_flag.astype(F32))
    copies = [
        pltpu.make_async_copy(source, target, sems.at[i])
        for i, (source, target) in enumerate(
            (
                (range_ref.at[level], kernel_ref),
                (interp_ref.at[level, own_flag], matrix_ref.at[0]),
                (interp_ref.at[level, 1 - own_flag], matrix_ref.at[1]),
            )
        )
    ]
    for copy in copies:
        copy.start()

    def moved(bin_id):
        tap = lax.broadcasted_iota(jnp.int32, (bin_id.shape[0], taps), 1)
        hot = jnp.where(tap == bin_id, 1.0, 0.0).astype(BF16)
        return dot(hot, kernel_ref[...]).astype(BF16)

    row = lax.broadcasted_iota(jnp.int32, (bins, 1), 0)
    upper = row + (bins - 2 * LANES)
    own_bin = jnp.where(row % LANES < LANES // 2, row, upper + LANES)
    own_bin = jnp.where(row >= LANES, jnp.where(row % LANES < LANES // 2, upper, row - LANES), own_bin)
    own_bin = jnp.where(row >= 2 * LANES, row - LANES, own_bin)
    rim_row = lax.broadcasted_iota(jnp.int32, (2 * rim, 1), 0)
    rim_bin = jnp.where(rim_row < rim, rim_row - rim, rim_row - rim + bins)
    rim_ref[...] = jnp.zeros(rim_ref.shape, BF16)
    bin_id = block * bins + lax.broadcasted_iota(jnp.int32, (8, bins), 1)
    reach = 1.0 + bin_id.astype(F32) * (1.0 / total_bins)
    line = lax.broadcasted_iota(jnp.int32, (8, bins), 0)
    base = 64
    members = group, group ^ stride
    for child, member in enumerate(members):
        rate = shift_ref[level, member]
        for first in range(0, base, 8):
            angle = (first + line).astype(F32)
            now = cos_sin_pi(rate * ((angle + 0.5) * (1.0 / angles) - 0.5) * reach)
            turn_ref[child, 0, first : first + 8, :] = now[0]
            turn_ref[child, 1, first : first + 8, :] = now[1]
        step = cos_sin_pi(rate * (base / angles) * reach)
        for first in range(base, angles, 8):
            here, last = slice(first, first + 8), slice(first - base, first - base + 8)
            now = rotated((turn_ref[child, 0, last, :], turn_ref[child, 1, last, :]), step)
            turn_ref[child, 0, here, :], turn_ref[child, 1, here, :] = now
    for copy in copies:
        copy.wait()
    for child, member in enumerate(members):
        lead = band - offset_ref[level, member, 0]
        centre_ref[child] = moved(own_bin + lead)
        ends = moved(rim_bin + lead)
        for part in range(2):
            for side in range(2):
                place = (2 * side + part) * rim
                rim_ref[child, part, place : place + rim, :] = ends[side * rim : (side + 1) * rim]


def merge_tables(
    level, stride, fore_flag, band_offset, center_shift, range_kernel, angle_interp, earlier
):
    taps, bins = range_kernel.shape[1:]
    angles = angle_interp.shape[2]
    rim = MAX_SHIFT + (taps - bins) // 2
    return pl.pallas_call(
        functools.partial(merge_table_kernel, level, stride),
        out_shape=[
            jax.ShapeDtypeStruct((2, bins, bins), BF16),
            jax.ShapeDtypeStruct((2, 2, 4 * rim, bins), BF16),
            jax.ShapeDtypeStruct((2, 2, angles, bins), F32),
            jax.ShapeDtypeStruct((2, *angle_interp.shape[2:]), BF16),
            SIDE,
        ],
        in_specs=[SMEM] * 3 + [ANY] * 3,
        out_specs=[VMEM] * 5,
        scratch_shapes=[pltpu.VMEM((taps, bins), BF16), pltpu.SemaphoreType.DMA((3,))],
        compiler_params=params(12),
        cost_estimate=pl.CostEstimate(
            flops=2_300_000_000, bytes_accessed=7 * MIB, transcendentals=0
        ),
    )(fore_flag, band_offset, center_shift, range_kernel, angle_interp, earlier)


def alternating(pulses, local_pulses):
    row = lax.broadcasted_iota(jnp.int32, (pulses.shape[0], 1), 0)
    pulse = row // (2 * local_pulses) * local_pulses + row % local_pulses
    return jnp.where(pulse % 2 == 1, -pulses, pulses)


def both_parts(pulses, local_pulses):
    count = pulses.shape[0]
    second = lax.broadcasted_iota(jnp.int32, (count, 1), 0) // local_pulses % 2 == 1
    ahead, behind = pltpu.roll(pulses, count - local_pulses, 0), pltpu.roll(pulses, local_pulses, 0)
    turned = jnp.where(second, -behind, ahead)
    return jnp.concatenate([pulses, turned], axis=1).astype(BF16)


def outer_kernel(pieces, side_ref, rows_ref, *refs):
    own_side = side_ref[:1, :]
    me = lax.axis_index("rng")
    own_ref, out_ref, *edge_refs = refs[pieces:-1]
    pulses_ref = refs[-1]
    rows = refs[0].shape[0] // 2
    for d, ref in enumerate(refs[:pieces]):
        for t in range(2):
            place = pl.multiple_of((me ^ (d + t * pieces)) * rows, rows)
            pulses_ref[pl.ds(place, rows), :] = ref[t * rows : (t + 1) * rows, :]
    pulses = pulses_ref[...]
    pulses = pulses.astype(F32)
    images = [
        dot(rows_ref[...], both_parts(value, rows // 2))
        for value in (alternating(pulses, rows // 2), pulses)
    ]
    half = own_ref.shape[1]
    rim = LANES // 4
    lane = lax.broadcasted_iota(jnp.int32, (1, LANES), 1)
    edges = [0.0, 0.0]
    for part in range(2):
        own, out = (image[:, part * LANES : (part + 1) * LANES] for image in images)
        own_ref[part] = own.astype(BF16)
        out_ref[part] = out.astype(BF16)
        for side in range(2):
            value = jnp.where(own_side == side, own, out)
            group = 2 * part + side
            for end in range(2):
                turn = (group + end) * rim % LANES
                moved = pltpu.roll(value, turn, 1) if turn else value
                edges[end] = edges[end] + jnp.where(lane // rim == group, moved, 0.0)
    even = me % 2 == 0
    edge_refs[0][...] = jnp.where(even, edges[1], edges[0]).astype(BF16)
    edge_refs[1][...] = jnp.where(even, edges[0], edges[1]).astype(BF16)


def outer_image(own_side, rows, pieces):
    half, side = rows.shape
    angles = 2 * half
    image = jax.ShapeDtypeStruct((2, angles // 2, LANES), BF16)
    edge = jax.ShapeDtypeStruct((angles // 2, LANES), BF16)
    return pl.pallas_call(
        functools.partial(outer_kernel, len(pieces)),
        out_shape=[image, image, edge, edge],
        in_specs=[VMEM] * (2 + len(pieces)),
        out_specs=[VMEM] * 4,
        scratch_shapes=[pltpu.VMEM((side, LANES), BF16)],
        compiler_params=params(10),
        cost_estimate=pl.CostEstimate(
            flops=4 * angles * side * LANES, bytes_accessed=3 * MIB, transcendentals=0
        ),
    )(own_side, rows, *pieces)


def partner_rows_kernel(local_pulses, rows_ref, pulses_ref, image_ref):
    count = pulses_ref.shape[1]
    image = dot(rows_ref[...], both_parts(pulses_ref[...].astype(F32), local_pulses))
    for part in range(2):
        image_ref[part] = image[:, part * count : (part + 1) * count].astype(BF16)


def own_rows_kernel(local_pulses, rows_ref, pulses_ref, outer_ref, image_ref):
    inner = pulses_ref.shape[1]
    pulses = alternating(pulses_ref[...].astype(F32), local_pulses)
    image = dot(rows_ref[...], both_parts(pulses, local_pulses))
    count = outer_ref.shape[2]
    image_ref[:, :, :count] = outer_ref[...]
    for part in range(2):
        image_ref[part, :, count:] = image[:, part * inner : (part + 1) * inner].astype(BF16)


def inner_image(kernel, angles, rows, pulses, outer=()):
    count = pulses.shape[1]
    whole = count + (outer[0].shape[2] if outer else 0)
    return pl.pallas_call(
        kernel,
        out_shape=jax.ShapeDtypeStruct((2, angles // 2, whole), BF16),
        in_specs=[VMEM] * (2 + len(outer)),
        out_specs=VMEM,
        compiler_params=params(10),
        cost_estimate=pl.CostEstimate(
            flops=2 * angles * rows.shape[1] * count, bytes_accessed=3 * MIB, transcendentals=0
        ),
    )(rows, pulses, *outer)


def exchanged(value, begin):
    devices = lax.axis_size("rng")
    pairs = [(i, i + 1) for i in range(begin, devices - 1, 2)]
    ends = [(i, i) for i in range(devices) if all(i not in pair for pair in pairs)]
    return lax.ppermute(value, "rng", pairs + [(j, i) for i, j in pairs] + ends)


def rims_kernel(side_ref, first_ref, second_ref, own_ref, out_ref):
    own_side = side_ref[:1, :]
    rim = LANES // 4
    me, devices = lax.axis_index("rng"), lax.axis_size("rng")
    even = me % 2 == 0
    first, second = first_ref[...].astype(F32), second_ref[...].astype(F32)
    below = jnp.where(me == 0, 0.0, jnp.where(even, second, first))
    above = jnp.where(me == devices - 1, 0.0, jnp.where(even, first, second))
    group = lax.broadcasted_iota(jnp.int32, (1, LANES), 1) // rim
    packed = [0.0, 0.0]
    for end, value in enumerate((below, above)):
        for part in range(2):
            place = 2 * end + part
            for side in range(2):
                turn = (place - (2 * part + side)) * rim % LANES
                moved = pltpu.roll(value, turn, 1) if turn else value
                packed[side] = packed[side] + jnp.where(group == place, moved, 0.0)
    own_ref[...] = jnp.where(own_side == 0, packed[0], packed[1]).astype(BF16)
    out_ref[...] = jnp.where(own_side == 0, packed[1], packed[0]).astype(BF16)


def sorted_rims(own_side, first, second):
    return pl.pallas_call(
        rims_kernel,
        out_shape=[jax.ShapeDtypeStruct(first.shape, BF16)] * 2,
        in_specs=[VMEM] * 3,
        out_specs=[VMEM] * 2,
        compiler_params=params(4),
        cost_estimate=pl.CostEstimate(flops=1_000_000, bytes_accessed=MIB // 4, transcendentals=0),
    )(own_side, first, second)


def resampled(image, rims_ref, centre_ref, rim_ref, value_ref, child):
    parts, half, bins = image.shape
    value_ref[...] = dot(image.reshape(parts * half, bins), centre_ref[child])
    rims = rims_ref[...]
    return [
        (value_ref[part * half : (part + 1) * half, :] + dot(rims, rim_ref[child, part])).astype(BF16)
        for part in range(parts)
    ]


def early_kernel(
    own_ref, rims_ref, centre_ref, rim_ref, matrix_ref, turn_ref, merged_ref, value_ref
):
    rows = resampled(own_ref[...], rims_ref, centre_ref, rim_ref, value_ref, 0)
    merged_ref[0], merged_ref[1] = rotated(
        (dot(matrix_ref[0], rows[0]), dot(matrix_ref[0], rows[1])), (turn_ref[0, 0], turn_ref[0, 1])
    )


def ends_of(value):
    count = value.shape[-1]
    return jnp.concatenate([value[..., :LANES], value[..., count - LANES :]], axis=-1)


def finish(values, lanes, merged_ref, matrix_ref, turn_ref, out_ref, buffer, sems):
    rows = [value.astype(BF16) for value in values]
    copies = []
    block = 2 * LANES
    for first in range(0, matrix_ref.shape[1], block):
        here = slice(first, first + block)
        matrix = matrix_ref[1, here]
        terms = dot(matrix, rows[0]), dot(matrix, rows[1])
        at = 0
        for begin, end in lanes:
            there = slice(at, at + end - begin)
            turned = rotated(
                (terms[0][:, there], terms[1][:, there]),
                (turn_ref[1, 0, here, begin:end], turn_ref[1, 1, here, begin:end]),
            )
            for part in range(2):
                total = merged_ref[part, here, begin:end] + turned[part]
                buffer[part, here, there] = total.astype(buffer.dtype)
            copy = pltpu.make_async_copy(
                buffer.at[:, here, there],
                out_ref.at[:, here, pl.ds(begin, end - begin)],
                sems.at[len(copies)],
            )
            copy.start()
            copies.append(copy)
            at += end - begin
    for copy in copies:
        copy.wait()


def middle_kernel(
    far_inner, merged_ref, centre_ref, matrix_ref, turn_ref, out_ref, partial_ref, buffer, sems
):
    parts, half, count = far_inner.shape
    bins = centre_ref.shape[2]
    inner = far_inner[...].reshape(parts * half, count)
    value = dot(inner, centre_ref[1, bins - count :, LANES : bins - LANES])
    values = [value[part * half : (part + 1) * half] for part in range(parts)]
    finish(
        values, [(LANES, bins - LANES)], merged_ref, matrix_ref, turn_ref, out_ref, buffer, sems
    )
    partial_ref[...] = dot(inner, ends_of(centre_ref[1, bins - count :, :]))


def end_kernel(
    far_outer, partial_ref, rims_ref, merged_ref, centre_ref, rim_ref, matrix_ref, turn_ref,
    begun_ref, out_ref, buffer, sems,
):
    parts, half, count = far_outer.shape
    bins = centre_ref.shape[2]
    centre = ends_of(centre_ref[1, :count, :])
    values = [
        partial_ref[part * half : (part + 1) * half, :]
        + dot(far_outer[part], centre)
        + dot(rims_ref[...], ends_of(rim_ref[1, part]))
        for part in range(parts)
    ]
    lanes = [(0, LANES), (bins - LANES, bins)]
    finish(values, lanes, merged_ref, matrix_ref, turn_ref, out_ref, buffer, sems)


def merged_image(own, rims, far, far_rims, tables, dtype):
    centre, rim, turn, matrices, _ = tables
    angles, bins = turn.shape[-2:]
    cost = pl.CostEstimate(flops=4 * angles * bins * bins, bytes_accessed=8 * MIB, transcendentals=0)
    value = pltpu.VMEM((angles, bins), F32)
    merged = pl.pallas_call(
        early_kernel,
        out_shape=jax.ShapeDtypeStruct((2, angles, bins), F32),
        in_specs=[VMEM] * 6,
        out_specs=VMEM,
        scratch_shapes=[value],
        compiler_params=params(16),
        cost_estimate=cost,
    )(own, rims, centre, rim, matrices, turn)
    image = jax.ShapeDtypeStruct((2, angles, bins), dtype)
    middle, ends = bins - 2 * LANES, 2 * LANES
    begun, partial = pl.pallas_call(
        middle_kernel,
        out_shape=[image, jax.ShapeDtypeStruct((angles, ends), F32)],
        in_specs=[VMEM] * 5,
        out_specs=[ANY, VMEM],
        scratch_shapes=[
            pltpu.VMEM((2, angles, middle), dtype),
            pltpu.SemaphoreType.DMA((angles // LANES,)),
        ],
        compiler_params=params(16),
        cost_estimate=cost,
    )(far[1], merged, centre, matrices, turn)
    return pl.pallas_call(
        end_kernel,
        out_shape=image,
        in_specs=[VMEM] * 8 + [ANY],
        out_specs=ANY,
        scratch_shapes=[
            pltpu.VMEM((2, angles, ends), dtype),
            pltpu.SemaphoreType.DMA((angles // LANES,)),
        ],
        input_output_aliases={8: 0},
        compiler_params=params(16),
        cost_estimate=cost,
    )(far[0], partial, far_rims, merged, centre, rim, matrices, turn, begun)


def after(value, *earlier):
    return lax.optimization_barrier((value, *earlier))[0]


def from_partner(value, stride):
    pairs = [(source, source ^ stride) for source in range(lax.axis_size("sub"))]
    return lax.ppermute(value, "sub", pairs)


def split_image(level, image, fore_flag, rim):
    angles, bins = image.shape[1:]
    half, step = angles // 2, LANES // 2
    own_flag = fore_flag[level, lax.axis_index("sub"), 0]
    sides = image.reshape(2, 2, half, bins)

    def pieces(side):
        rows = lax.dynamic_index_in_dim(sides, side, 1, keepdims=False)
        ends = [rows[..., :step], rows[..., -step:]]
        rest = [rows[..., -2 * step : -step], rows[..., step : -2 * step]]
        return jnp.concatenate(ends + rest, axis=-1)

    def packed(edge):
        return edge.transpose(2, 0, 1, 3).reshape(half, 4 * rim)

    low, high = packed(sides[..., :rim]), packed(sides[..., -rim:])
    even = lax.axis_index("rng") % 2 == 0
    edges = jnp.where(even, high, low), jnp.where(even, low, high)
    return pieces(own_flag), pieces(1 - own_flag), edges


def on_device(echoes, fore_flag, band_offset, angle_interp, range_kernel, center_shift):
    devices = lax.axis_size("rng")
    half = devices // 2
    local_pulses = echoes.shape[1]
    bins = echoes.shape[2] // devices
    angles = angle_interp.shape[2]
    rim = MAX_SHIFT + (range_kernel.shape[1] - bins) // 2
    levels = range_kernel.shape[0]
    settings = (fore_flag, band_offset, center_shift, range_kernel, angle_interp)

    far_blocks, near_blocks, blocks = placed(
        echoes.reshape(2 * local_pulses, devices * bins), devices
    )
    relay = across(far_blocks, half)
    pulses = lax.all_to_all(blocks, "rng", split_axis=0, concat_axis=0, tiled=True)
    sends = joined(near_blocks, relay)
    pieces = [across(value, d) if d else value for d, value in enumerate(sends)]
    matrix, own_side = filter_table(fore_flag, angles, local_pulses, sends[0])
    own_outer, out_outer, *edges = outer_image(own_side, matrix, pieces)

    pulses = after(pulses, out_outer).reshape(2 * local_pulses * devices, bins - LANES)
    out_kernel = functools.partial(partner_rows_kernel, local_pulses)
    out_inner = inner_image(out_kernel, angles, matrix, pulses)
    far = [from_partner(value, 1) for value in (out_outer, out_inner)]
    edges = [after(edge, out_inner) for edge in edges]
    edges = exchanged(edges[0], 0), exchanged(edges[1], 1)
    pulses = after(pulses, far[0])
    own_kernel = functools.partial(own_rows_kernel, local_pulses)
    own = inner_image(own_kernel, angles, matrix, pulses, (own_outer,))
    rims, out_rims = sorted_rims(own_side, *edges)
    tables = merge_tables(0, 1, *settings, after(out_rims, own))
    for level in range(levels):
        stride = 2**level
        if level > 0:
            tables = merge_tables(level, stride, *settings, image)
            own, out, edges = split_image(level, image, fore_flag, rim)
            far = [from_partner(value, stride) for value in (out[..., :LANES], out[..., LANES:])]
            edges = exchanged(edges[0], 0), exchanged(edges[1], 1)
            rims, out_rims = sorted_rims(tables[-1], *edges)
        far_rims = from_partner(out_rims, stride)
        image = merged_image(own, rims, far, far_rims, tables, BF16 if level + 1 < levels else F32)
    return image


def solution(mesh):
    placed_as = (
        P(None, ("sub", "rng"), None),
        P(None, None, "rng"),
        P(None, None, "rng"),
        P(),
        P(),
        P(),
    )
    return jax.shard_map(
        on_device, mesh=mesh, in_specs=placed_as, out_specs=P(None, "sub", "rng"), check_vma=False
    )
```

```python
import functools
import math

import jax
import jax.numpy as jnp
from jax import lax
from jax.experimental import pallas as pl
from jax.experimental.pallas import tpu as pltpu
from jax.sharding import PartitionSpec as P

MAX_SHIFT = 16
LANES = 128
MIB = 2**20
JOIN_COST = 10**11
SIDE = jax.ShapeDtypeStruct((8, LANES), jnp.float32)
VMEM = pl.BlockSpec(memory_space=pltpu.VMEM)
SMEM = pl.BlockSpec(memory_space=pltpu.SMEM)
ANY = pl.BlockSpec(memory_space=pl.ANY)
F32 = jnp.float32
BF16 = jnp.bfloat16


def dot(a, b):
    return jnp.dot(a, b, preferred_element_type=F32)


def params(mib):
    return pltpu.CompilerParams(vmem_limit_bytes=mib * MIB)


def series(square, first, count):
    coefs = [
        (-1) ** i * math.pi ** (2 * i + first) / math.factorial(2 * i + first)
        for i in range(count)
    ]
    total = jnp.full_like(square, coefs[-1])
    for coef in coefs[-2::-1]:
        total = total * square + coef
    return total


def cos_sin_pi(v):
    turns = jnp.floor(v + 0.5)
    rest = v - turns
    sign = 1.0 - 2.0 * (turns - 2.0 * jnp.floor(turns * 0.5))
    square = rest * rest
    return series(square, 0, 8) * sign, series(square, 1, 7) * rest * sign


def rotated(pair, step):
    return pair[0] * step[0] - pair[1] * step[1], pair[0] * step[1] + pair[1] * step[0]


def mixed(left, right):
    lane = lax.broadcasted_iota(jnp.int32, left.shape, 1)
    return jnp.where(lane < LANES // 2, left.astype(F32), right.astype(F32)).astype(BF16)


def place_kernel(echoes_ref, far_ref, near_ref, inner_ref):
    devices, _, count = inner_ref.shape
    bins = count + LANES
    half = devices // 2
    base = lax.axis_index("rng") // half * half

    def tile(device, first):
        return echoes_ref[:, pl.ds(pl.multiple_of(device * bins + first, LANES), LANES)]

    for ref, start in ((far_ref, half - base), (near_ref, base)):
        for i in range(half):
            ref[i] = mixed(tile(start + i, 0), tile(start + i, bins - LANES))
    for device in range(devices):
        begin = device * bins
        inner_ref[device, :, :LANES] = mixed(tile(device, bins - LANES), tile(device, 0))
        inner_ref[device, :, LANES:] = echoes_ref[:, begin + LANES : begin + bins - LANES]


def placed(echoes, devices):
    rows, columns = echoes.shape
    outer = jax.ShapeDtypeStruct((devices // 2, rows, LANES), BF16)
    inner = jax.ShapeDtypeStruct((devices, rows, columns // devices - LANES), BF16)
    return pl.pallas_call(
        place_kernel,
        out_shape=[outer, outer, inner],
        in_specs=[VMEM],
        out_specs=[VMEM] * 3,
        compiler_params=params(8),
        cost_estimate=pl.CostEstimate(flops=0, bytes_accessed=2 * MIB, transcendentals=0),
    )(echoes)


def join_kernel(near_ref, relay_ref, *refs):
    me = lax.axis_index("rng") % len(refs)
    rows = near_ref.shape[1]
    for d, out_ref in enumerate(refs):
        out_ref[:rows] = near_ref[me ^ d]
        out_ref[rows:] = relay_ref[me ^ d]


def joined(near, relay):
    half, rows, count = near.shape
    return pl.pallas_call(
        join_kernel,
        out_shape=[jax.ShapeDtypeStruct((2 * rows, count), BF16)] * half,
        in_specs=[VMEM] * 2,
        out_specs=[VMEM] * half,
        compiler_params=params(4),
        cost_estimate=pl.CostEstimate(flops=JOIN_COST, bytes_accessed=MIB, transcendentals=0),
    )(near, relay)


def across(value, mask):
    devices = lax.axis_size("rng")
    return lax.ppermute(value, "rng", [(i, i ^ mask) for i in range(devices)])


def filter_table_kernel(local_pulses, flag_ref, after_ref, rows_ref, side_ref, cos_ref, sin_ref):
    own_flag = flag_ref[0, lax.axis_index("sub"), 0]
    side_ref[...] = jnp.full(side_ref.shape, own_flag.astype(F32))
    half, columns = rows_ref.shape
    angles = 2 * half
    first = (1 - own_flag) * half
    base = cos_ref.shape[0]
    scale = 1.0 / math.sqrt(columns // 2)
    lane = lax.broadcasted_iota(jnp.int32, (8, columns), 1)
    slot = lane // (2 * local_pulses)
    second = lane // local_pulses % 2
    pulse = (slot * local_pulses + lane % local_pulses).astype(F32)
    lag = second.astype(F32) * 0.5
    per_angle = pulse * (1.0 / angles)
    row = lax.broadcasted_iota(jnp.int32, (8, columns), 0)
    for i in range(base // 8):
        twice = (2 * (row + 8 * i + first) + 1 - angles).astype(F32)
        cosine, sine = cos_sin_pi(twice * per_angle - lag)
        cos_ref[8 * i : 8 * i + 8, :] = cosine * scale
        sin_ref[8 * i : 8 * i + 8, :] = sine * scale
    step = cos_sin_pi(per_angle * (2 * base))
    for j in range(half // base):
        for i in range(base // 16):
            pair = []
            for k in (2 * i, 2 * i + 1):
                here = slice(8 * k, 8 * k + 8)
                now = cos_ref[here, :], sin_ref[here, :]
                pair.append(now[0])
                if j + 1 < half // base:
                    cos_ref[here, :], sin_ref[here, :] = rotated(now, step)
            begin = j * base + 16 * i
            rows_ref[begin : begin + 16, :] = jnp.concatenate(pair).astype(BF16)


def filter_table(fore_flag, angles, local_pulses, earlier):
    side = 2 * local_pulses * lax.axis_size("rng")
    return pl.pallas_call(
        functools.partial(filter_table_kernel, local_pulses),
        out_shape=[jax.ShapeDtypeStruct((angles // 2, side), BF16), SIDE],
        in_specs=[SMEM, ANY],
        out_specs=[VMEM] * 2,
        scratch_shapes=[pltpu.VMEM((64, side), F32)] * 2,
        compiler_params=params(6),
        cost_estimate=pl.CostEstimate(flops=9_000_000, bytes_accessed=4 * MIB, transcendentals=0),
    )(fore_flag, earlier)


def merge_table_kernel(
    level, stride, flag_ref, offset_ref, shift_ref, range_ref, interp_ref, after_ref, centre_ref,
    rim_ref, turn_ref, matrix_ref, side_ref, kernel_ref, sems,
):
    group = lax.axis_index("sub")
    block = lax.axis_index("rng")
    bins = centre_ref.shape[-1]
    angles = turn_ref.shape[-2]
    total_bins = lax.axis_size("rng") * bins
    taps = range_ref.shape[1]
    band = (taps - bins) // 2
    rim = MAX_SHIFT + band
    own_flag = flag_ref[level, group, 0]
    side_ref[...] = jnp.full(side_ref.shape, own_flag.astype(F32))
    copies = [
        pltpu.make_async_copy(source, target, sems.at[i])
        for i, (source, target) in enumerate(
            (
                (range_ref.at[level], kernel_ref),
                (interp_ref.at[level, own_flag], matrix_ref.at[0]),
                (interp_ref.at[level, 1 - own_flag], matrix_ref.at[1]),
            )
        )
    ]
    for copy in copies:
        copy.start()

    def moved(bin_id):
        tap = lax.broadcasted_iota(jnp.int32, (bin_id.shape[0], taps), 1)
        hot = jnp.where(tap == bin_id, 1.0, 0.0).astype(BF16)
        return dot(hot, kernel_ref[...]).astype(BF16)

    piece = LANES // 2
    starts = [0, bins - piece, bins - 2 * piece, piece, *range(2 * piece, bins - 2 * piece, piece)]
    line_bin = lax.broadcasted_iota(jnp.int32, (piece, 1), 0)
    line_tap = lax.broadcasted_iota(jnp.int32, (piece, piece + taps - bins), 1)
    rim_row = lax.broadcasted_iota(jnp.int32, (2 * rim, 1), 0)
    rim_bin = jnp.where(rim_row < rim, rim_row - rim, rim_row - rim + bins)
    rim_ref[...] = jnp.zeros(rim_ref.shape, BF16)
    bin_id = block * bins + lax.broadcasted_iota(jnp.int32, (8, bins), 1)
    reach = 1.0 + bin_id.astype(F32) * (1.0 / total_bins)
    line = lax.broadcasted_iota(jnp.int32, (8, bins), 0)
    base = 64
    members = group, group ^ stride
    for child, member in enumerate(members):
        rate = shift_ref[level, member]
        for first in range(0, base, 8):
            angle = (first + line).astype(F32)
            now = cos_sin_pi(rate * ((angle + 0.5) * (1.0 / angles) - 0.5) * reach)
            turn_ref[child, 0, first : first + 8, :] = now[0]
            turn_ref[child, 1, first : first + 8, :] = now[1]
        step = cos_sin_pi(rate * (base / angles) * reach)
        for first in range(base, angles, 8):
            here, last = slice(first, first + 8), slice(first - base, first - base + 8)
            now = rotated((turn_ref[child, 0, last, :], turn_ref[child, 1, last, :]), step)
            turn_ref[child, 0, here, :], turn_ref[child, 1, here, :] = now
    for copy in copies:
        copy.wait()
    for child, member in enumerate(members):
        lead = band - offset_ref[level, member, 0]
        hot = jnp.where(line_tap == line_bin + lead, 1.0, 0.0).astype(BF16)
        for i, start in enumerate(starts):
            some = kernel_ref[start : start + piece + taps - bins, :]
            centre_ref[child, i * piece : (i + 1) * piece, :] = dot(hot, some).astype(BF16)
        ends = moved(rim_bin + lead)
        for part in range(2):
            for side in range(2):
                place = (2 * side + part) * rim
                rim_ref[child, part, place : place + rim, :] = ends[side * rim : (side + 1) * rim]


def merge_tables(
    level, stride, fore_flag, band_offset, center_shift, range_kernel, angle_interp, earlier
):
    taps, bins = range_kernel.shape[1:]
    angles = angle_interp.shape[2]
    rim = MAX_SHIFT + (taps - bins) // 2
    return pl.pallas_call(
        functools.partial(merge_table_kernel, level, stride),
        out_shape=[
            jax.ShapeDtypeStruct((2, bins, bins), BF16),
            jax.ShapeDtypeStruct((2, 2, 4 * rim, bins), BF16),
            jax.ShapeDtypeStruct((2, 2, angles, bins), F32),
            jax.ShapeDtypeStruct((2, *angle_interp.shape[2:]), BF16),
            SIDE,
        ],
        in_specs=[SMEM] * 3 + [ANY] * 3,
        out_specs=[VMEM] * 5,
        scratch_shapes=[pltpu.VMEM((taps, bins), BF16), pltpu.SemaphoreType.DMA((3,))],
        compiler_params=params(12),
        cost_estimate=pl.CostEstimate(
            flops=2_300_000_000, bytes_accessed=7 * MIB, transcendentals=0
        ),
    )(fore_flag, band_offset, center_shift, range_kernel, angle_interp, earlier)


def alternating(pulses, local_pulses):
    row = lax.broadcasted_iota(jnp.int32, (pulses.shape[0], 1), 0)
    pulse = row // (2 * local_pulses) * local_pulses + row % local_pulses
    return jnp.where(pulse % 2 == 1, -pulses, pulses)


def both_parts(pulses, local_pulses):
    count = pulses.shape[0]
    second = lax.broadcasted_iota(jnp.int32, (count, 1), 0) // local_pulses % 2 == 1
    ahead, behind = pltpu.roll(pulses, count - local_pulses, 0), pltpu.roll(pulses, local_pulses, 0)
    turned = jnp.where(second, -behind, ahead)
    return jnp.concatenate([pulses, turned], axis=1).astype(BF16)


def outer_kernel(pieces, side_ref, rows_ref, *refs):
    own_side = side_ref[:1, :]
    me = lax.axis_index("rng")
    own_ref, out_ref, *edge_refs = refs[pieces:-1]
    pulses_ref = refs[-1]
    rows = refs[0].shape[0] // 2
    for d, ref in enumerate(refs[:pieces]):
        for t in range(2):
            place = pl.multiple_of((me ^ (d + t * pieces)) * rows, rows)
            pulses_ref[pl.ds(place, rows), :] = ref[t * rows : (t + 1) * rows, :]
    pulses = pulses_ref[...]
    pulses = pulses.astype(F32)
    images = [
        dot(rows_ref[...], both_parts(value, rows // 2))
        for value in (alternating(pulses, rows // 2), pulses)
    ]
    half = own_ref.shape[1]
    rim = LANES // 4
    lane = lax.broadcasted_iota(jnp.int32, (1, LANES), 1)
    edges = [0.0, 0.0]
    for part in range(2):
        own, out = (image[:, part * LANES : (part + 1) * LANES] for image in images)
        own_ref[part] = own.astype(BF16)
        out_ref[part] = out.astype(BF16)
        for side in range(2):
            value = jnp.where(own_side == side, own, out)
            group = 2 * part + side
            for end in range(2):
                turn = (group + end) * rim % LANES
                moved = pltpu.roll(value, turn, 1) if turn else value
                edges[end] = edges[end] + jnp.where(lane // rim == group, moved, 0.0)
    even = me % 2 == 0
    edge_refs[0][...] = jnp.where(even, edges[1], edges[0]).astype(BF16)
    edge_refs[1][...] = jnp.where(even, edges[0], edges[1]).astype(BF16)


def outer_image(own_side, rows, pieces):
    half, side = rows.shape
    angles = 2 * half
    image = jax.ShapeDtypeStruct((2, angles // 2, LANES), BF16)
    edge = jax.ShapeDtypeStruct((angles // 2, LANES), BF16)
    return pl.pallas_call(
        functools.partial(outer_kernel, len(pieces)),
        out_shape=[image, image, edge, edge],
        in_specs=[VMEM] * (2 + len(pieces)),
        out_specs=[VMEM] * 4,
        scratch_shapes=[pltpu.VMEM((side, LANES), BF16)],
        compiler_params=params(10),
        cost_estimate=pl.CostEstimate(
            flops=4 * angles * side * LANES, bytes_accessed=3 * MIB, transcendentals=0
        ),
    )(own_side, rows, *pieces)


def partner_rows_kernel(local_pulses, rows_ref, pulses_ref, image_ref):
    count = pulses_ref.shape[1]
    image = dot(rows_ref[...], both_parts(pulses_ref[...].astype(F32), local_pulses))
    for part in range(2):
        image_ref[part] = image[:, part * count : (part + 1) * count].astype(BF16)


def own_rows_kernel(local_pulses, rows_ref, pulses_ref, outer_ref, image_ref):
    inner = pulses_ref.shape[1]
    pulses = alternating(pulses_ref[...].astype(F32), local_pulses)
    image = dot(rows_ref[...], both_parts(pulses, local_pulses))
    count = outer_ref.shape[2]
    image_ref[:, :, :count] = outer_ref[...]
    for part in range(2):
        image_ref[part, :, count:] = image[:, part * inner : (part + 1) * inner].astype(BF16)


def inner_image(kernel, angles, rows, pulses, outer=()):
    count = pulses.shape[1]
    whole = count + (outer[0].shape[2] if outer else 0)
    return pl.pallas_call(
        kernel,
        out_shape=jax.ShapeDtypeStruct((2, angles // 2, whole), BF16),
        in_specs=[VMEM] * (2 + len(outer)),
        out_specs=VMEM,
        compiler_params=params(10),
        cost_estimate=pl.CostEstimate(
            flops=2 * angles * rows.shape[1] * count, bytes_accessed=3 * MIB, transcendentals=0
        ),
    )(rows, pulses, *outer)


def exchanged(value, begin):
    devices = lax.axis_size("rng")
    pairs = [(i, i + 1) for i in range(begin, devices - 1, 2)]
    ends = [(i, i) for i in range(devices) if all(i not in pair for pair in pairs)]
    return lax.ppermute(value, "rng", pairs + [(j, i) for i, j in pairs] + ends)


def rims_kernel(side_ref, first_ref, second_ref, own_ref, out_ref):
    own_side = side_ref[:1, :]
    rim = LANES // 4
    me, devices = lax.axis_index("rng"), lax.axis_size("rng")
    even = me % 2 == 0
    first, second = first_ref[...].astype(F32), second_ref[...].astype(F32)
    below = jnp.where(me == 0, 0.0, jnp.where(even, second, first))
    above = jnp.where(me == devices - 1, 0.0, jnp.where(even, first, second))
    group = lax.broadcasted_iota(jnp.int32, (1, LANES), 1) // rim
    packed = [0.0, 0.0]
    for end, value in enumerate((below, above)):
        for part in range(2):
            place = 2 * end + part
            for side in range(2):
                turn = (place - (2 * part + side)) * rim % LANES
                moved = pltpu.roll(value, turn, 1) if turn else value
                packed[side] = packed[side] + jnp.where(group == place, moved, 0.0)
    own_ref[...] = jnp.where(own_side == 0, packed[0], packed[1]).astype(BF16)
    out_ref[...] = jnp.where(own_side == 0, packed[1], packed[0]).astype(BF16)


def sorted_rims(own_side, first, second):
    return pl.pallas_call(
        rims_kernel,
        out_shape=[jax.ShapeDtypeStruct(first.shape, BF16)] * 2,
        in_specs=[VMEM] * 3,
        out_specs=[VMEM] * 2,
        compiler_params=params(4),
        cost_estimate=pl.CostEstimate(flops=1_000_000, bytes_accessed=MIB // 4, transcendentals=0),
    )(own_side, first, second)


def resampled(image, rims_ref, centre_ref, rim_ref, value_ref, child):
    parts, half, bins = image.shape
    value_ref[...] = dot(image.reshape(parts * half, bins), centre_ref[child])
    rims = rims_ref[...]
    return [
        (value_ref[part * half : (part + 1) * half, :] + dot(rims, rim_ref[child, part])).astype(BF16)
        for part in range(parts)
    ]


def early_kernel(
    own_ref, rims_ref, centre_ref, rim_ref, matrix_ref, turn_ref, merged_ref, value_ref
):
    rows = resampled(own_ref[...], rims_ref, centre_ref, rim_ref, value_ref, 0)
    merged_ref[0], merged_ref[1] = rotated(
        (dot(matrix_ref[0], rows[0]), dot(matrix_ref[0], rows[1])), (turn_ref[0, 0], turn_ref[0, 1])
    )


def late_kernel(
    far_outer, far_inner, rims_ref, merged_ref, centre_ref, rim_ref, matrix_ref, turn_ref, out_ref,
    buffer, value_ref, sems,
):
    image = jnp.concatenate([far_outer[...], far_inner[...]], axis=2)
    rows = resampled(image, rims_ref, centre_ref, rim_ref, value_ref, 1)
    parts = len(rows)
    block = LANES
    copies = []
    for first in range(0, matrix_ref.shape[1], 2 * block):
        matrix = matrix_ref[1, first : first + 2 * block]
        terms = dot(matrix, rows[0]), dot(matrix, rows[1])
        for step in range(2):
            here = slice(first + step * block, first + (step + 1) * block)
            there = slice(step * block, (step + 1) * block)
            turned = rotated(
                (terms[0][there], terms[1][there]), (turn_ref[1, 0, here], turn_ref[1, 1, here])
            )
            for part in range(parts):
                buffer[part, here] = (merged_ref[part, here] + turned[part]).astype(buffer.dtype)
            copy = pltpu.make_async_copy(
                buffer.at[:, here], out_ref.at[:, here], sems.at[len(copies)]
            )
            copy.start()
            copies.append(copy)
    for copy in copies:
        copy.wait()


def merged_image(own, rims, far, far_rims, tables, dtype):
    centre, rim, turn, matrices, _ = tables
    angles, bins = turn.shape[-2:]
    cost = pl.CostEstimate(flops=4 * angles * bins * bins, bytes_accessed=8 * MIB, transcendentals=0)
    value = pltpu.VMEM((angles, bins), F32)
    merged = pl.pallas_call(
        early_kernel,
        out_shape=jax.ShapeDtypeStruct((2, angles, bins), F32),
        in_specs=[VMEM] * 6,
        out_specs=VMEM,
        scratch_shapes=[value],
        compiler_params=params(16),
        cost_estimate=cost,
    )(own, rims, centre, rim, matrices, turn)
    return pl.pallas_call(
        late_kernel,
        out_shape=jax.ShapeDtypeStruct((2, angles, bins), dtype),
        in_specs=[VMEM] * 8,
        out_specs=ANY,
        scratch_shapes=[
            pltpu.VMEM((2, angles, bins), dtype),
            value,
            pltpu.SemaphoreType.DMA((angles // LANES,)),
        ],
        compiler_params=params(16),
        cost_estimate=cost,
    )(*far, far_rims, merged, centre, rim, matrices, turn)


def after(value, *earlier):
    return lax.optimization_barrier((value, *earlier))[0]


def from_partner(value, stride):
    pairs = [(source, source ^ stride) for source in range(lax.axis_size("sub"))]
    return lax.ppermute(value, "sub", pairs)


def split_image(level, image, fore_flag, rim):
    angles, bins = image.shape[1:]
    half, step = angles // 2, LANES // 2
    own_flag = fore_flag[level, lax.axis_index("sub"), 0]
    sides = image.reshape(2, 2, half, bins)

    def pieces(side):
        rows = lax.dynamic_index_in_dim(sides, side, 1, keepdims=False)
        ends = [rows[..., :step], rows[..., -step:]]
        rest = [rows[..., -2 * step : -step], rows[..., step : -2 * step]]
        return jnp.concatenate(ends + rest, axis=-1)

    def packed(edge):
        return edge.transpose(2, 0, 1, 3).reshape(half, 4 * rim)

    low, high = packed(sides[..., :rim]), packed(sides[..., -rim:])
    even = lax.axis_index("rng") % 2 == 0
    edges = jnp.where(even, high, low), jnp.where(even, low, high)
    return pieces(own_flag), pieces(1 - own_flag), edges


def on_device(echoes, fore_flag, band_offset, angle_interp, range_kernel, center_shift):
    devices = lax.axis_size("rng")
    half = devices // 2
    local_pulses = echoes.shape[1]
    bins = echoes.shape[2] // devices
    angles = angle_interp.shape[2]
    rim = MAX_SHIFT + (range_kernel.shape[1] - bins) // 2
    levels = range_kernel.shape[0]
    settings = (fore_flag, band_offset, center_shift, range_kernel, angle_interp)

    far_blocks, near_blocks, blocks = placed(
        echoes.reshape(2 * local_pulses, devices * bins), devices
    )
    relay = across(far_blocks, half)
    pulses = lax.all_to_all(blocks, "rng", split_axis=0, concat_axis=0, tiled=True)
    sends = joined(near_blocks, relay)
    pieces = [across(value, d) if d else value for d, value in enumerate(sends)]
    matrix, own_side = filter_table(fore_flag, angles, local_pulses, sends[0])
    own_outer, out_outer, *edges = outer_image(own_side, matrix, pieces)

    pulses = after(pulses, out_outer).reshape(2 * local_pulses * devices, bins - LANES)
    out_kernel = functools.partial(partner_rows_kernel, local_pulses)
    out_inner = inner_image(out_kernel, angles, matrix, pulses)
    far = [from_partner(value, 1) for value in (out_outer, out_inner)]
    edges = [after(edge, out_inner) for edge in edges]
    edges = exchanged(edges[0], 0), exchanged(edges[1], 1)
    pulses = after(pulses, far[0])
    own_kernel = functools.partial(own_rows_kernel, local_pulses)
    own = inner_image(own_kernel, angles, matrix, pulses, (own_outer,))
    rims, out_rims = sorted_rims(own_side, *edges)
    tables = merge_tables(0, 1, *settings, after(out_rims, own))
    for level in range(levels):
        stride = 2**level
        if level > 0:
            tables = merge_tables(level, stride, *settings, image)
            own, out, edges = split_image(level, image, fore_flag, rim)
            far = [from_partner(value, stride) for value in (out[..., :LANES], out[..., LANES:])]
            edges = exchanged(edges[0], 0), exchanged(edges[1], 1)
            rims, out_rims = sorted_rims(tables[-1], *edges)
        far_rims = from_partner(out_rims, stride)
        image = merged_image(own, rims, far, far_rims, tables, BF16 if level + 1 < levels else F32)
    return image


def solution(mesh):
    placed_as = (
        P(None, ("sub", "rng"), None),
        P(None, None, "rng"),
        P(None, None, "rng"),
        P(),
        P(),
        P(),
    )
    return jax.shard_map(
        on_device, mesh=mesh, in_specs=placed_as, out_specs=P(None, "sub", "rng"), check_vma=False
    )
```

```python
import functools
import math

import jax
import jax.numpy as jnp
from jax import lax
from jax.experimental import pallas as pl
from jax.experimental.pallas import tpu as pltpu
from jax.sharding import PartitionSpec as P

MAX_SHIFT = 16
LANES = 128
MIB = 2**20
JOIN_COST = 10**11
SIDE = jax.ShapeDtypeStruct((8, LANES), jnp.float32)
VMEM = pl.BlockSpec(memory_space=pltpu.VMEM)
SMEM = pl.BlockSpec(memory_space=pltpu.SMEM)
ANY = pl.BlockSpec(memory_space=pl.ANY)
F32 = jnp.float32
BF16 = jnp.bfloat16


def dot(a, b):
    return jnp.dot(a, b, preferred_element_type=F32)


def params(mib):
    return pltpu.CompilerParams(vmem_limit_bytes=mib * MIB)


def series(square, first, count):
    coefs = [
        (-1) ** i * math.pi ** (2 * i + first) / math.factorial(2 * i + first)
        for i in range(count)
    ]
    total = jnp.full_like(square, coefs[-1])
    for coef in coefs[-2::-1]:
        total = total * square + coef
    return total


def cos_sin_pi(v):
    turns = jnp.floor(v + 0.5)
    rest = v - turns
    sign = 1.0 - 2.0 * (turns - 2.0 * jnp.floor(turns * 0.5))
    square = rest * rest
    return series(square, 0, 8) * sign, series(square, 1, 7) * rest * sign


def rotated(pair, step):
    return pair[0] * step[0] - pair[1] * step[1], pair[0] * step[1] + pair[1] * step[0]


def mixed(left, right):
    lane = lax.broadcasted_iota(jnp.int32, left.shape, 1)
    return jnp.where(lane < LANES // 2, left.astype(F32), right.astype(F32)).astype(BF16)


def place_kernel(echoes_ref, far_ref, near_ref, inner_ref):
    devices, _, count = inner_ref.shape
    bins = count + LANES
    half = devices // 2
    base = lax.axis_index("rng") // half * half

    def tile(device, first):
        return echoes_ref[:, pl.ds(pl.multiple_of(device * bins + first, LANES), LANES)]

    for ref, start in ((far_ref, half - base), (near_ref, base)):
        for i in range(half):
            ref[i] = mixed(tile(start + i, 0), tile(start + i, bins - LANES))
    for device in range(devices):
        begin = device * bins
        inner_ref[device, :, :LANES] = mixed(tile(device, bins - LANES), tile(device, 0))
        inner_ref[device, :, LANES:] = echoes_ref[:, begin + LANES : begin + bins - LANES]


def placed(echoes, devices):
    rows, columns = echoes.shape
    outer = jax.ShapeDtypeStruct((devices // 2, rows, LANES), BF16)
    inner = jax.ShapeDtypeStruct((devices, rows, columns // devices - LANES), BF16)
    return pl.pallas_call(
        place_kernel,
        out_shape=[outer, outer, inner],
        in_specs=[VMEM],
        out_specs=[VMEM] * 3,
        compiler_params=params(8),
        cost_estimate=pl.CostEstimate(flops=0, bytes_accessed=2 * MIB, transcendentals=0),
    )(echoes)


def join_kernel(near_ref, relay_ref, *refs):
    me = lax.axis_index("rng") % len(refs)
    rows = near_ref.shape[1]
    for d, out_ref in enumerate(refs):
        out_ref[:rows] = near_ref[me ^ d]
        out_ref[rows:] = relay_ref[me ^ d]


def joined(near, relay):
    half, rows, count = near.shape
    return pl.pallas_call(
        join_kernel,
        out_shape=[jax.ShapeDtypeStruct((2 * rows, count), BF16)] * half,
        in_specs=[VMEM] * 2,
        out_specs=[VMEM] * half,
        compiler_params=params(4),
        cost_estimate=pl.CostEstimate(flops=JOIN_COST, bytes_accessed=MIB, transcendentals=0),
    )(near, relay)


def across(value, mask):
    devices = lax.axis_size("rng")
    return lax.ppermute(value, "rng", [(i, i ^ mask) for i in range(devices)])


def filter_table_kernel(local_pulses, flag_ref, after_ref, rows_ref, side_ref, cos_ref, sin_ref):
    own_flag = flag_ref[0, lax.axis_index("sub"), 0]
    side_ref[...] = jnp.full(side_ref.shape, own_flag.astype(F32))
    half, columns = rows_ref.shape
    angles = 2 * half
    first = (1 - own_flag) * half
    base = cos_ref.shape[0]
    scale = 1.0 / math.sqrt(columns // 2)
    lane = lax.broadcasted_iota(jnp.int32, (8, columns), 1)
    slot = lane // (2 * local_pulses)
    second = lane // local_pulses % 2
    pulse = (slot * local_pulses + lane % local_pulses).astype(F32)
    lag = second.astype(F32) * 0.5
    per_angle = pulse * (1.0 / angles)
    row = lax.broadcasted_iota(jnp.int32, (8, columns), 0)
    for i in range(base // 8):
        twice = (2 * (row + 8 * i + first) + 1 - angles).astype(F32)
        cosine, sine = cos_sin_pi(twice * per_angle - lag)
        cos_ref[8 * i : 8 * i + 8, :] = cosine * scale
        sin_ref[8 * i : 8 * i + 8, :] = sine * scale
    step = cos_sin_pi(per_angle * (2 * base))
    for j in range(half // base):
        for i in range(base // 16):
            pair = []
            for k in (2 * i, 2 * i + 1):
                here = slice(8 * k, 8 * k + 8)
                now = cos_ref[here, :], sin_ref[here, :]
                pair.append(now[0])
                if j + 1 < half // base:
                    cos_ref[here, :], sin_ref[here, :] = rotated(now, step)
            begin = j * base + 16 * i
            rows_ref[begin : begin + 16, :] = jnp.concatenate(pair).astype(BF16)


def filter_table(fore_flag, angles, local_pulses, earlier):
    side = 2 * local_pulses * lax.axis_size("rng")
    return pl.pallas_call(
        functools.partial(filter_table_kernel, local_pulses),
        out_shape=[jax.ShapeDtypeStruct((angles // 2, side), BF16), SIDE],
        in_specs=[SMEM, ANY],
        out_specs=[VMEM] * 2,
        scratch_shapes=[pltpu.VMEM((64, side), F32)] * 2,
        compiler_params=params(6),
        cost_estimate=pl.CostEstimate(flops=9_000_000, bytes_accessed=4 * MIB, transcendentals=0),
    )(fore_flag, earlier)


def merge_table_kernel(
    level, stride, flag_ref, offset_ref, shift_ref, range_ref, interp_ref, after_ref, centre_ref,
    rim_ref, turn_ref, matrix_ref, side_ref, kernel_ref, sems,
):
    group = lax.axis_index("sub")
    block = lax.axis_index("rng")
    bins = centre_ref.shape[-1]
    angles = turn_ref.shape[-2]
    total_bins = lax.axis_size("rng") * bins
    taps = range_ref.shape[1]
    band = (taps - bins) // 2
    rim = MAX_SHIFT + band
    own_flag = flag_ref[level, group, 0]
    side_ref[...] = jnp.full(side_ref.shape, own_flag.astype(F32))
    copies = [
        pltpu.make_async_copy(source, target, sems.at[i])
        for i, (source, target) in enumerate(
            (
                (range_ref.at[level], kernel_ref),
                (interp_ref.at[level, own_flag], matrix_ref.at[0]),
                (interp_ref.at[level, 1 - own_flag], matrix_ref.at[1]),
            )
        )
    ]
    for copy in copies:
        copy.start()

    def moved(bin_id):
        tap = lax.broadcasted_iota(jnp.int32, (bin_id.shape[0], taps), 1)
        hot = jnp.where(tap == bin_id, 1.0, 0.0).astype(BF16)
        return dot(hot, kernel_ref[...]).astype(BF16)

    piece = LANES // 2
    starts = [0, bins - piece, bins - 2 * piece, piece, *range(2 * piece, bins - 2 * piece, piece)]
    line_bin = lax.broadcasted_iota(jnp.int32, (piece, 1), 0)
    line_tap = lax.broadcasted_iota(jnp.int32, (piece, piece + taps - bins), 1)
    rim_row = lax.broadcasted_iota(jnp.int32, (2 * rim, 1), 0)
    rim_bin = jnp.where(rim_row < rim, rim_row - rim, rim_row - rim + bins)
    rim_ref[...] = jnp.zeros(rim_ref.shape, BF16)
    bin_id = block * bins + lax.broadcasted_iota(jnp.int32, (8, bins), 1)
    reach = 1.0 + bin_id.astype(F32) * (1.0 / total_bins)
    line = lax.broadcasted_iota(jnp.int32, (8, bins), 0)
    base = 64
    members = group, group ^ stride
    for child, member in enumerate(members):
        rate = shift_ref[level, member]
        for first in range(0, base, 8):
            angle = (first + line).astype(F32)
            now = cos_sin_pi(rate * ((angle + 0.5) * (1.0 / angles) - 0.5) * reach)
            turn_ref[child, 0, first : first + 8, :] = now[0]
            turn_ref[child, 1, first : first + 8, :] = now[1]
        step = cos_sin_pi(rate * (base / angles) * reach)
        for first in range(base, angles, 8):
            here, last = slice(first, first + 8), slice(first - base, first - base + 8)
            now = rotated((turn_ref[child, 0, last, :], turn_ref[child, 1, last, :]), step)
            turn_ref[child, 0, here, :], turn_ref[child, 1, here, :] = now
    for copy in copies:
        copy.wait()
    for child, member in enumerate(members):
        lead = band - offset_ref[level, member, 0]
        hot = jnp.where(line_tap == line_bin + lead, 1.0, 0.0).astype(BF16)
        for i, start in enumerate(starts):
            some = kernel_ref[start : start + piece + taps - bins, :]
            centre_ref[child, i * piece : (i + 1) * piece, :] = dot(hot, some).astype(BF16)
        ends = moved(rim_bin + lead)
        for part in range(2):
            for side in range(2):
                place = (2 * side + part) * rim
                rim_ref[child, part, place : place + rim, :] = ends[side * rim : (side + 1) * rim]


def merge_tables(
    level, stride, fore_flag, band_offset, center_shift, range_kernel, angle_interp, earlier
):
    taps, bins = range_kernel.shape[1:]
    angles = angle_interp.shape[2]
    rim = MAX_SHIFT + (taps - bins) // 2
    return pl.pallas_call(
        functools.partial(merge_table_kernel, level, stride),
        out_shape=[
            jax.ShapeDtypeStruct((2, bins, bins), BF16),
            jax.ShapeDtypeStruct((2, 2, 4 * rim, bins), BF16),
            jax.ShapeDtypeStruct((2, 2, angles, bins), F32),
            jax.ShapeDtypeStruct((2, *angle_interp.shape[2:]), BF16),
            SIDE,
        ],
        in_specs=[SMEM] * 3 + [ANY] * 3,
        out_specs=[VMEM] * 5,
        scratch_shapes=[pltpu.VMEM((taps, bins), BF16), pltpu.SemaphoreType.DMA((3,))],
        compiler_params=params(12),
        cost_estimate=pl.CostEstimate(
            flops=2_300_000_000, bytes_accessed=7 * MIB, transcendentals=0
        ),
    )(fore_flag, band_offset, center_shift, range_kernel, angle_interp, earlier)


def alternating(pulses, local_pulses):
    row = lax.broadcasted_iota(jnp.int32, (pulses.shape[0], 1), 0)
    pulse = row // (2 * local_pulses) * local_pulses + row % local_pulses
    return jnp.where(pulse % 2 == 1, -pulses, pulses)


def both_parts(pulses, local_pulses):
    count = pulses.shape[0]
    second = lax.broadcasted_iota(jnp.int32, (count, 1), 0) // local_pulses % 2 == 1
    ahead, behind = pltpu.roll(pulses, count - local_pulses, 0), pltpu.roll(pulses, local_pulses, 0)
    turned = jnp.where(second, -behind, ahead)
    return jnp.concatenate([pulses, turned], axis=1).astype(BF16)


def outer_kernel(order, side_ref, rows_ref, *refs):
    own_side = side_ref[:1, :]
    me = lax.axis_index("rng")
    pieces = len(order)
    own_ref, out_ref, *edge_refs = refs[pieces:-1]
    pulses_ref = refs[-1]
    rows = refs[0].shape[0] // 2
    for d, ref in zip(order, refs[:pieces]):
        for t in range(2):
            place = pl.multiple_of((me ^ (d + t * pieces)) * rows, rows)
            pulses_ref[pl.ds(place, rows), :] = ref[t * rows : (t + 1) * rows, :]
    pulses = pulses_ref[...]
    pulses = pulses.astype(F32)
    images = [
        dot(rows_ref[...], both_parts(value, rows // 2))
        for value in (alternating(pulses, rows // 2), pulses)
    ]
    half = own_ref.shape[1]
    rim = LANES // 4
    lane = lax.broadcasted_iota(jnp.int32, (1, LANES), 1)
    edges = [0.0, 0.0]
    for part in range(2):
        own, out = (image[:, part * LANES : (part + 1) * LANES] for image in images)
        own_ref[part] = own.astype(BF16)
        out_ref[part] = out.astype(BF16)
        for side in range(2):
            value = jnp.where(own_side == side, own, out)
            group = 2 * part + side
            for end in range(2):
                turn = (group + end) * rim % LANES
                moved = pltpu.roll(value, turn, 1) if turn else value
                edges[end] = edges[end] + jnp.where(lane // rim == group, moved, 0.0)
    even = me % 2 == 0
    edge_refs[0][...] = jnp.where(even, edges[1], edges[0]).astype(BF16)
    edge_refs[1][...] = jnp.where(even, edges[0], edges[1]).astype(BF16)


def outer_image(own_side, rows, pieces):
    half, side = rows.shape
    middle = len(pieces) // 2
    order = [0, 1, 2, *range(middle, len(pieces)), *range(3, middle)]
    angles = 2 * half
    image = jax.ShapeDtypeStruct((2, angles // 2, LANES), BF16)
    edge = jax.ShapeDtypeStruct((angles // 2, LANES), BF16)
    return pl.pallas_call(
        functools.partial(outer_kernel, order),
        out_shape=[image, image, edge, edge],
        in_specs=[VMEM] * (2 + len(pieces)),
        out_specs=[VMEM] * 4,
        scratch_shapes=[pltpu.VMEM((side, LANES), BF16)],
        compiler_params=params(10),
        cost_estimate=pl.CostEstimate(
            flops=4 * angles * side * LANES, bytes_accessed=3 * MIB, transcendentals=0
        ),
    )(own_side, rows, *(pieces[d] for d in order))


def partner_rows_kernel(local_pulses, rows_ref, pulses_ref, image_ref):
    count = pulses_ref.shape[1]
    image = dot(rows_ref[...], both_parts(pulses_ref[...].astype(F32), local_pulses))
    for part in range(2):
        image_ref[part] = image[:, part * count : (part + 1) * count].astype(BF16)


def own_rows_kernel(local_pulses, rows_ref, pulses_ref, outer_ref, image_ref):
    inner = pulses_ref.shape[1]
    pulses = alternating(pulses_ref[...].astype(F32), local_pulses)
    image = dot(rows_ref[...], both_parts(pulses, local_pulses))
    count = outer_ref.shape[2]
    image_ref[:, :, :count] = outer_ref[...]
    for part in range(2):
        image_ref[part, :, count:] = image[:, part * inner : (part + 1) * inner].astype(BF16)


def inner_image(kernel, angles, rows, pulses, outer=()):
    count = pulses.shape[1]
    whole = count + (outer[0].shape[2] if outer else 0)
    return pl.pallas_call(
        kernel,
        out_shape=jax.ShapeDtypeStruct((2, angles // 2, whole), BF16),
        in_specs=[VMEM] * (2 + len(outer)),
        out_specs=VMEM,
        compiler_params=params(10),
        cost_estimate=pl.CostEstimate(
            flops=2 * angles * rows.shape[1] * count, bytes_accessed=3 * MIB, transcendentals=0
        ),
    )(rows, pulses, *outer)


def exchanged(value, begin):
    devices = lax.axis_size("rng")
    pairs = [(i, i + 1) for i in range(begin, devices - 1, 2)]
    ends = [(i, i) for i in range(devices) if all(i not in pair for pair in pairs)]
    return lax.ppermute(value, "rng", pairs + [(j, i) for i, j in pairs] + ends)


def rims_kernel(side_ref, first_ref, second_ref, own_ref, out_ref):
    own_side = side_ref[:1, :]
    rim = LANES // 4
    me, devices = lax.axis_index("rng"), lax.axis_size("rng")
    even = me % 2 == 0
    first, second = first_ref[...].astype(F32), second_ref[...].astype(F32)
    below = jnp.where(me == 0, 0.0, jnp.where(even, second, first))
    above = jnp.where(me == devices - 1, 0.0, jnp.where(even, first, second))
    group = lax.broadcasted_iota(jnp.int32, (1, LANES), 1) // rim
    packed = [0.0, 0.0]
    for end, value in enumerate((below, above)):
        for part in range(2):
            place = 2 * end + part
            for side in range(2):
                turn = (place - (2 * part + side)) * rim % LANES
                moved = pltpu.roll(value, turn, 1) if turn else value
                packed[side] = packed[side] + jnp.where(group == place, moved, 0.0)
    own_ref[...] = jnp.where(own_side == 0, packed[0], packed[1]).astype(BF16)
    out_ref[...] = jnp.where(own_side == 0, packed[1], packed[0]).astype(BF16)


def sorted_rims(own_side, first, second):
    return pl.pallas_call(
        rims_kernel,
        out_shape=[jax.ShapeDtypeStruct(first.shape, BF16)] * 2,
        in_specs=[VMEM] * 3,
        out_specs=[VMEM] * 2,
        compiler_params=params(4),
        cost_estimate=pl.CostEstimate(flops=1_000_000, bytes_accessed=MIB // 4, transcendentals=0),
    )(own_side, first, second)


def resampled(image, rims_ref, centre_ref, rim_ref, value_ref, child):
    parts, half, bins = image.shape
    value_ref[...] = dot(image.reshape(parts * half, bins), centre_ref[child])
    rims = rims_ref[...]
    return [
        (value_ref[part * half : (part + 1) * half, :] + dot(rims, rim_ref[child, part])).astype(BF16)
        for part in range(parts)
    ]


def early_kernel(
    own_ref, rims_ref, centre_ref, rim_ref, matrix_ref, turn_ref, merged_ref, value_ref
):
    rows = resampled(own_ref[...], rims_ref, centre_ref, rim_ref, value_ref, 0)
    merged_ref[0], merged_ref[1] = rotated(
        (dot(matrix_ref[0], rows[0]), dot(matrix_ref[0], rows[1])), (turn_ref[0, 0], turn_ref[0, 1])
    )


def late_kernel(
    far_outer, far_inner, rims_ref, merged_ref, centre_ref, rim_ref, matrix_ref, turn_ref, out_ref,
    buffer, value_ref, sems,
):
    image = jnp.concatenate([far_outer[...], far_inner[...]], axis=2)
    rows = resampled(image, rims_ref, centre_ref, rim_ref, value_ref, 1)
    parts = len(rows)
    block = LANES
    copies = []
    for first in range(0, matrix_ref.shape[1], 2 * block):
        matrix = matrix_ref[1, first : first + 2 * block]
        terms = dot(matrix, rows[0]), dot(matrix, rows[1])
        for step in range(2):
            here = slice(first + step * block, first + (step + 1) * block)
            there = slice(step * block, (step + 1) * block)
            turned = rotated(
                (terms[0][there], terms[1][there]), (turn_ref[1, 0, here], turn_ref[1, 1, here])
            )
            for part in range(parts):
                buffer[part, here] = (merged_ref[part, here] + turned[part]).astype(buffer.dtype)
            copy = pltpu.make_async_copy(
                buffer.at[:, here], out_ref.at[:, here], sems.at[len(copies)]
            )
            copy.start()
            copies.append(copy)
    for copy in copies:
        copy.wait()


def merged_image(own, rims, far, far_rims, tables, dtype):
    centre, rim, turn, matrices, _ = tables
    angles, bins = turn.shape[-2:]
    cost = pl.CostEstimate(flops=4 * angles * bins * bins, bytes_accessed=8 * MIB, transcendentals=0)
    value = pltpu.VMEM((angles, bins), F32)
    merged = pl.pallas_call(
        early_kernel,
        out_shape=jax.ShapeDtypeStruct((2, angles, bins), F32),
        in_specs=[VMEM] * 6,
        out_specs=VMEM,
        scratch_shapes=[value],
        compiler_params=params(16),
        cost_estimate=cost,
    )(own, rims, centre, rim, matrices, turn)
    return pl.pallas_call(
        late_kernel,
        out_shape=jax.ShapeDtypeStruct((2, angles, bins), dtype),
        in_specs=[VMEM] * 8,
        out_specs=ANY,
        scratch_shapes=[
            pltpu.VMEM((2, angles, bins), dtype),
            value,
            pltpu.SemaphoreType.DMA((angles // LANES,)),
        ],
        compiler_params=params(16),
        cost_estimate=cost,
    )(*far, far_rims, merged, centre, rim, matrices, turn)


def after(value, *earlier):
    return lax.optimization_barrier((value, *earlier))[0]


def from_partner(value, stride):
    pairs = [(source, source ^ stride) for source in range(lax.axis_size("sub"))]
    return lax.ppermute(value, "sub", pairs)


def split_image(level, image, fore_flag, rim):
    angles, bins = image.shape[1:]
    half, step = angles // 2, LANES // 2
    own_flag = fore_flag[level, lax.axis_index("sub"), 0]
    sides = image.reshape(2, 2, half, bins)

    def pieces(side):
        rows = lax.dynamic_index_in_dim(sides, side, 1, keepdims=False)
        ends = [rows[..., :step], rows[..., -step:]]
        rest = [rows[..., -2 * step : -step], rows[..., step : -2 * step]]
        return jnp.concatenate(ends + rest, axis=-1)

    def packed(edge):
        return edge.transpose(2, 0, 1, 3).reshape(half, 4 * rim)

    low, high = packed(sides[..., :rim]), packed(sides[..., -rim:])
    even = lax.axis_index("rng") % 2 == 0
    edges = jnp.where(even, high, low), jnp.where(even, low, high)
    return pieces(own_flag), pieces(1 - own_flag), edges


def on_device(echoes, fore_flag, band_offset, angle_interp, range_kernel, center_shift):
    devices = lax.axis_size("rng")
    half = devices // 2
    local_pulses = echoes.shape[1]
    bins = echoes.shape[2] // devices
    angles = angle_interp.shape[2]
    rim = MAX_SHIFT + (range_kernel.shape[1] - bins) // 2
    levels = range_kernel.shape[0]
    settings = (fore_flag, band_offset, center_shift, range_kernel, angle_interp)

    far_blocks, near_blocks, blocks = placed(
        echoes.reshape(2 * local_pulses, devices * bins), devices
    )
    relay = across(far_blocks, half)
    pulses = lax.all_to_all(blocks, "rng", split_axis=0, concat_axis=0, tiled=True)
    sends = joined(near_blocks, relay)
    pieces = [across(value, d) if d else value for d, value in enumerate(sends)]
    matrix, own_side = filter_table(fore_flag, angles, local_pulses, sends[0])
    own_outer, out_outer, *edges = outer_image(own_side, matrix, pieces)

    pulses = after(pulses, out_outer).reshape(2 * local_pulses * devices, bins - LANES)
    out_kernel = functools.partial(partner_rows_kernel, local_pulses)
    out_inner = inner_image(out_kernel, angles, matrix, pulses)
    far = [from_partner(value, 1) for value in (out_outer, out_inner)]
    edges = [after(edge, out_inner) for edge in edges]
    edges = exchanged(edges[0], 0), exchanged(edges[1], 1)
    pulses = after(pulses, far[0])
    own_kernel = functools.partial(own_rows_kernel, local_pulses)
    own = inner_image(own_kernel, angles, matrix, pulses, (own_outer,))
    rims, out_rims = sorted_rims(own_side, *edges)
    tables = merge_tables(0, 1, *settings, after(out_rims, own))
    for level in range(levels):
        stride = 2**level
        if level > 0:
            tables = merge_tables(level, stride, *settings, image)
            own, out, edges = split_image(level, image, fore_flag, rim)
            far = [from_partner(value, stride) for value in (out[..., :LANES], out[..., LANES:])]
            edges = exchanged(edges[0], 0), exchanged(edges[1], 1)
            rims, out_rims = sorted_rims(tables[-1], *edges)
        far_rims = from_partner(out_rims, stride)
        image = merged_image(own, rims, far, far_rims, tables, BF16 if level + 1 < levels else F32)
    return image


def solution(mesh):
    placed_as = (
        P(None, ("sub", "rng"), None),
        P(None, None, "rng"),
        P(None, None, "rng"),
        P(),
        P(),
        P(),
    )
    return jax.shard_map(
        on_device, mesh=mesh, in_specs=placed_as, out_specs=P(None, "sub", "rng"), check_vma=False
    )
```

```python
import functools
import math

import jax
import jax.numpy as jnp
from jax import lax
from jax.experimental import pallas as pl
from jax.experimental.pallas import tpu as pltpu
from jax.sharding import PartitionSpec as P

MAX_SHIFT = 16
LANES = 128
MIB = 2**20
JOIN_COST = 10**11
SIDE = jax.ShapeDtypeStruct((8, LANES), jnp.float32)
VMEM = pl.BlockSpec(memory_space=pltpu.VMEM)
SMEM = pl.BlockSpec(memory_space=pltpu.SMEM)
ANY = pl.BlockSpec(memory_space=pl.ANY)
F32 = jnp.float32
BF16 = jnp.bfloat16


def dot(a, b):
    return jnp.dot(a, b, preferred_element_type=F32)


def params(mib):
    return pltpu.CompilerParams(vmem_limit_bytes=mib * MIB)


def series(square, first, count):
    coefs = [
        (-1) ** i * math.pi ** (2 * i + first) / math.factorial(2 * i + first)
        for i in range(count)
    ]
    total = jnp.full_like(square, coefs[-1])
    for coef in coefs[-2::-1]:
        total = total * square + coef
    return total


def cos_sin_pi(v):
    turns = jnp.floor(v + 0.5)
    rest = v - turns
    sign = 1.0 - 2.0 * (turns - 2.0 * jnp.floor(turns * 0.5))
    square = rest * rest
    return series(square, 0, 8) * sign, series(square, 1, 7) * rest * sign


def rotated(pair, step):
    return pair[0] * step[0] - pair[1] * step[1], pair[0] * step[1] + pair[1] * step[0]


def mixed(left, right):
    lane = lax.broadcasted_iota(jnp.int32, left.shape, 1)
    return jnp.where(lane < LANES // 2, left.astype(F32), right.astype(F32)).astype(BF16)


def place_kernel(echoes_ref, far_ref, near_ref, inner_ref):
    devices, _, count = inner_ref.shape
    bins = count + LANES
    half = devices // 2
    base = lax.axis_index("rng") // half * half

    def tile(device, first):
        return echoes_ref[:, pl.ds(pl.multiple_of(device * bins + first, LANES), LANES)]

    for ref, start in ((far_ref, half - base), (near_ref, base)):
        for i in range(half):
            ref[i] = mixed(tile(start + i, 0), tile(start + i, bins - LANES))
    for device in range(devices):
        begin = device * bins
        inner_ref[device, :, :LANES] = mixed(tile(device, bins - LANES), tile(device, 0))
        inner_ref[device, :, LANES:] = echoes_ref[:, begin + LANES : begin + bins - LANES]


def placed(echoes, devices):
    rows, columns = echoes.shape
    outer = jax.ShapeDtypeStruct((devices // 2, rows, LANES), BF16)
    inner = jax.ShapeDtypeStruct((devices, rows, columns // devices - LANES), BF16)
    return pl.pallas_call(
        place_kernel,
        out_shape=[outer, outer, inner],
        in_specs=[VMEM],
        out_specs=[VMEM] * 3,
        compiler_params=params(8),
        cost_estimate=pl.CostEstimate(flops=0, bytes_accessed=2 * MIB, transcendentals=0),
    )(echoes)


def join_kernel(near_ref, relay_ref, *refs):
    me = lax.axis_index("rng") % len(refs)
    rows = near_ref.shape[1]
    for d, out_ref in enumerate(refs):
        out_ref[:rows] = near_ref[me ^ d]
        out_ref[rows:] = relay_ref[me ^ d]


def joined(near, relay):
    half, rows, count = near.shape
    return pl.pallas_call(
        join_kernel,
        out_shape=[jax.ShapeDtypeStruct((2 * rows, count), BF16)] * half,
        in_specs=[VMEM] * 2,
        out_specs=[VMEM] * half,
        compiler_params=params(4),
        cost_estimate=pl.CostEstimate(flops=JOIN_COST, bytes_accessed=MIB, transcendentals=0),
    )(near, relay)


def across(value, mask):
    devices = lax.axis_size("rng")
    return lax.ppermute(value, "rng", [(i, i ^ mask) for i in range(devices)])


def filter_table_kernel(local_pulses, flag_ref, after_ref, rows_ref, side_ref, cos_ref, sin_ref):
    own_flag = flag_ref[0, lax.axis_index("sub"), 0]
    side_ref[...] = jnp.full(side_ref.shape, own_flag.astype(F32))
    half, columns = rows_ref.shape
    angles = 2 * half
    first = (1 - own_flag) * half
    base = cos_ref.shape[0]
    scale = 1.0 / math.sqrt(columns // 2)
    lane = lax.broadcasted_iota(jnp.int32, (8, columns), 1)
    slot = lane // (2 * local_pulses)
    second = lane // local_pulses % 2
    pulse = (slot * local_pulses + lane % local_pulses).astype(F32)
    lag = second.astype(F32) * 0.5
    per_angle = pulse * (1.0 / angles)
    row = lax.broadcasted_iota(jnp.int32, (8, columns), 0)
    for i in range(base // 8):
        twice = (2 * (row + 8 * i + first) + 1 - angles).astype(F32)
        cosine, sine = cos_sin_pi(twice * per_angle - lag)
        cos_ref[8 * i : 8 * i + 8, :] = cosine * scale
        sin_ref[8 * i : 8 * i + 8, :] = sine * scale
    step = cos_sin_pi(per_angle * (2 * base))
    for j in range(half // base):
        for i in range(base // 16):
            pair = []
            for k in (2 * i, 2 * i + 1):
                here = slice(8 * k, 8 * k + 8)
                now = cos_ref[here, :], sin_ref[here, :]
                pair.append(now[0])
                if j + 1 < half // base:
                    cos_ref[here, :], sin_ref[here, :] = rotated(now, step)
            begin = j * base + 16 * i
            rows_ref[begin : begin + 16, :] = jnp.concatenate(pair).astype(BF16)


def filter_table(fore_flag, angles, local_pulses, earlier):
    side = 2 * local_pulses * lax.axis_size("rng")
    return pl.pallas_call(
        functools.partial(filter_table_kernel, local_pulses),
        out_shape=[jax.ShapeDtypeStruct((angles // 2, side), BF16), SIDE],
        in_specs=[SMEM, ANY],
        out_specs=[VMEM] * 2,
        scratch_shapes=[pltpu.VMEM((64, side), F32)] * 2,
        compiler_params=params(6),
        cost_estimate=pl.CostEstimate(flops=9_000_000, bytes_accessed=4 * MIB, transcendentals=0),
    )(fore_flag, earlier)


def merge_table_kernel(
    level, stride, flag_ref, offset_ref, shift_ref, range_ref, interp_ref, after_ref, centre_ref,
    rim_ref, turn_ref, matrix_ref, side_ref, kernel_ref, sems,
):
    group = lax.axis_index("sub")
    block = lax.axis_index("rng")
    bins = centre_ref.shape[-1]
    angles = turn_ref.shape[-2]
    total_bins = lax.axis_size("rng") * bins
    taps = range_ref.shape[1]
    band = (taps - bins) // 2
    rim = MAX_SHIFT + band
    own_flag = flag_ref[level, group, 0]
    side_ref[...] = jnp.full(side_ref.shape, own_flag.astype(F32))
    copies = [
        pltpu.make_async_copy(source, target, sems.at[i])
        for i, (source, target) in enumerate(
            (
                (range_ref.at[level], kernel_ref),
                (interp_ref.at[level, own_flag], matrix_ref.at[0]),
                (interp_ref.at[level, 1 - own_flag], matrix_ref.at[1]),
            )
        )
    ]
    for copy in copies:
        copy.start()

    def moved(bin_id):
        tap = lax.broadcasted_iota(jnp.int32, (bin_id.shape[0], taps), 1)
        hot = jnp.where(tap == bin_id, 1.0, 0.0).astype(BF16)
        return dot(hot, kernel_ref[...]).astype(BF16)

    piece = LANES // 2
    starts = [0, bins - piece, bins - 2 * piece, piece, *range(2 * piece, bins - 2 * piece, piece)]
    line_bin = lax.broadcasted_iota(jnp.int32, (piece, 1), 0)
    line_tap = lax.broadcasted_iota(jnp.int32, (piece, piece + taps - bins), 1)
    rim_row = lax.broadcasted_iota(jnp.int32, (2 * rim, 1), 0)
    rim_bin = jnp.where(rim_row < rim, rim_row - rim, rim_row - rim + bins)
    rim_ref[...] = jnp.zeros(rim_ref.shape, BF16)
    bin_id = block * bins + lax.broadcasted_iota(jnp.int32, (8, bins), 1)
    reach = 1.0 + bin_id.astype(F32) * (1.0 / total_bins)
    line = lax.broadcasted_iota(jnp.int32, (8, bins), 0)
    base = 64
    members = group, group ^ stride
    for child, member in enumerate(members):
        rate = shift_ref[level, member]
        for first in range(0, base, 8):
            angle = (first + line).astype(F32)
            now = cos_sin_pi(rate * ((angle + 0.5) * (1.0 / angles) - 0.5) * reach)
            turn_ref[child, 0, first : first + 8, :] = now[0]
            turn_ref[child, 1, first : first + 8, :] = now[1]
        step = cos_sin_pi(rate * (base / angles) * reach)
        for first in range(base, angles, 8):
            here, last = slice(first, first + 8), slice(first - base, first - base + 8)
            now = rotated((turn_ref[child, 0, last, :], turn_ref[child, 1, last, :]), step)
            turn_ref[child, 0, here, :], turn_ref[child, 1, here, :] = now
    for copy in copies:
        copy.wait()
    for child, member in enumerate(members):
        lead = band - offset_ref[level, member, 0]
        hot = jnp.where(line_tap == line_bin + lead, 1.0, 0.0).astype(BF16)
        for i, start in enumerate(starts):
            some = kernel_ref[start : start + piece + taps - bins, :]
            centre_ref[child, i * piece : (i + 1) * piece, :] = dot(hot, some).astype(BF16)
        ends = moved(rim_bin + lead)
        for part in range(2):
            for side in range(2):
                place = (2 * side + part) * rim
                rim_ref[child, part, place : place + rim, :] = ends[side * rim : (side + 1) * rim]


def merge_tables(
    level, stride, fore_flag, band_offset, center_shift, range_kernel, angle_interp, earlier
):
    taps, bins = range_kernel.shape[1:]
    angles = angle_interp.shape[2]
    rim = MAX_SHIFT + (taps - bins) // 2
    return pl.pallas_call(
        functools.partial(merge_table_kernel, level, stride),
        out_shape=[
            jax.ShapeDtypeStruct((2, bins, bins), BF16),
            jax.ShapeDtypeStruct((2, 2, 4 * rim, bins), BF16),
            jax.ShapeDtypeStruct((2, 2, angles, bins), F32),
            jax.ShapeDtypeStruct((2, *angle_interp.shape[2:]), BF16),
            SIDE,
        ],
        in_specs=[SMEM] * 3 + [ANY] * 3,
        out_specs=[VMEM] * 5,
        scratch_shapes=[pltpu.VMEM((taps, bins), BF16), pltpu.SemaphoreType.DMA((3,))],
        compiler_params=params(12),
        cost_estimate=pl.CostEstimate(
            flops=2_300_000_000, bytes_accessed=7 * MIB, transcendentals=0
        ),
    )(fore_flag, band_offset, center_shift, range_kernel, angle_interp, earlier)


def alternating(pulses, local_pulses):
    row = lax.broadcasted_iota(jnp.int32, (pulses.shape[0], 1), 0)
    pulse = row // (2 * local_pulses) * local_pulses + row % local_pulses
    return jnp.where(pulse % 2 == 1, -pulses, pulses)


def both_parts(pulses, local_pulses):
    count = pulses.shape[0]
    second = lax.broadcasted_iota(jnp.int32, (count, 1), 0) // local_pulses % 2 == 1
    ahead, behind = pltpu.roll(pulses, count - local_pulses, 0), pltpu.roll(pulses, local_pulses, 0)
    turned = jnp.where(second, -behind, ahead)
    return jnp.concatenate([pulses, turned], axis=1).astype(BF16)


def outer_kernel(pieces, side_ref, rows_ref, *refs):
    own_side = side_ref[:1, :]
    me = lax.axis_index("rng")
    own_ref, out_ref, *edge_refs = refs[pieces:-1]
    pulses_ref = refs[-1]
    rows = refs[0].shape[0] // 2
    for d, ref in enumerate(refs[:pieces]):
        for t in range(2):
            place = pl.multiple_of((me ^ (d + t * pieces)) * rows, rows)
            pulses_ref[pl.ds(place, rows), :] = ref[t * rows : (t + 1) * rows, :]
    pulses = pulses_ref[...]
    pulses = pulses.astype(F32)
    images = [
        dot(rows_ref[...], both_parts(value, rows // 2))
        for value in (alternating(pulses, rows // 2), pulses)
    ]
    half = own_ref.shape[1]
    rim = LANES // 4
    lane = lax.broadcasted_iota(jnp.int32, (1, LANES), 1)
    edges = [0.0, 0.0]
    for part in range(2):
        own, out = (image[:, part * LANES : (part + 1) * LANES] for image in images)
        own_ref[part] = own.astype(BF16)
        out_ref[part] = out.astype(BF16)
        for side in range(2):
            value = jnp.where(own_side == side, own, out)
            group = 2 * part + side
            for end in range(2):
                turn = (group + end) * rim % LANES
                moved = pltpu.roll(value, turn, 1) if turn else value
                edges[end] = edges[end] + jnp.where(lane // rim == group, moved, 0.0)
    even = me % 2 == 0
    edge_refs[0][...] = jnp.where(even, edges[1], edges[0]).astype(BF16)
    edge_refs[1][...] = jnp.where(even, edges[0], edges[1]).astype(BF16)


def outer_image(own_side, rows, pieces):
    half, side = rows.shape
    angles = 2 * half
    image = jax.ShapeDtypeStruct((2, angles // 2, LANES), BF16)
    edge = jax.ShapeDtypeStruct((angles // 2, LANES), BF16)
    return pl.pallas_call(
        functools.partial(outer_kernel, len(pieces)),
        out_shape=[image, image, edge, edge],
        in_specs=[VMEM] * (2 + len(pieces)),
        out_specs=[VMEM] * 4,
        scratch_shapes=[pltpu.VMEM((side, LANES), BF16)],
        compiler_params=params(10),
        cost_estimate=pl.CostEstimate(
            flops=4 * angles * side * LANES, bytes_accessed=3 * MIB, transcendentals=0
        ),
    )(own_side, rows, *pieces)


def partner_rows_kernel(local_pulses, rows_ref, pulses_ref, image_ref):
    count = pulses_ref.shape[1]
    image = dot(rows_ref[...], both_parts(pulses_ref[...].astype(F32), local_pulses))
    for part in range(2):
        image_ref[part] = image[:, part * count : (part + 1) * count].astype(BF16)


def own_rows_kernel(local_pulses, rows_ref, pulses_ref, outer_ref, image_ref):
    inner = pulses_ref.shape[1]
    pulses = alternating(pulses_ref[...].astype(F32), local_pulses)
    image = dot(rows_ref[...], both_parts(pulses, local_pulses))
    count = outer_ref.shape[2]
    image_ref[:, :, :count] = outer_ref[...]
    for part in range(2):
        image_ref[part, :, count:] = image[:, part * inner : (part + 1) * inner].astype(BF16)


def inner_image(kernel, angles, rows, pulses, outer=()):
    count = pulses.shape[1]
    whole = count + (outer[0].shape[2] if outer else 0)
    return pl.pallas_call(
        kernel,
        out_shape=jax.ShapeDtypeStruct((2, angles // 2, whole), BF16),
        in_specs=[VMEM] * (2 + len(outer)),
        out_specs=VMEM,
        compiler_params=params(10),
        cost_estimate=pl.CostEstimate(
            flops=2 * angles * rows.shape[1] * count, bytes_accessed=3 * MIB, transcendentals=0
        ),
    )(rows, pulses, *outer)


def exchanged(value, begin):
    devices = lax.axis_size("rng")
    pairs = [(i, i + 1) for i in range(begin, devices - 1, 2)]
    ends = [(i, i) for i in range(devices) if all(i not in pair for pair in pairs)]
    return lax.ppermute(value, "rng", pairs + [(j, i) for i, j in pairs] + ends)


def rims_kernel(side_ref, first_ref, second_ref, own_ref, out_ref):
    own_side = side_ref[:1, :]
    rim = LANES // 4
    me, devices = lax.axis_index("rng"), lax.axis_size("rng")
    even = me % 2 == 0
    first, second = first_ref[...].astype(F32), second_ref[...].astype(F32)
    below = jnp.where(me == 0, 0.0, jnp.where(even, second, first))
    above = jnp.where(me == devices - 1, 0.0, jnp.where(even, first, second))
    group = lax.broadcasted_iota(jnp.int32, (1, LANES), 1) // rim
    packed = [0.0, 0.0]
    for end, value in enumerate((below, above)):
        for part in range(2):
            place = 2 * end + part
            for side in range(2):
                turn = (place - (2 * part + side)) * rim % LANES
                moved = pltpu.roll(value, turn, 1) if turn else value
                packed[side] = packed[side] + jnp.where(group == place, moved, 0.0)
    own_ref[...] = jnp.where(own_side == 0, packed[0], packed[1]).astype(BF16)
    out_ref[...] = jnp.where(own_side == 0, packed[1], packed[0]).astype(BF16)


def sorted_rims(own_side, first, second):
    return pl.pallas_call(
        rims_kernel,
        out_shape=[jax.ShapeDtypeStruct(first.shape, BF16)] * 2,
        in_specs=[VMEM] * 3,
        out_specs=[VMEM] * 2,
        compiler_params=params(4),
        cost_estimate=pl.CostEstimate(flops=1_000_000, bytes_accessed=MIB // 4, transcendentals=0),
    )(own_side, first, second)


def resampled(image, rims_ref, centre_ref, rim_ref, value_ref, child):
    parts, half, bins = image.shape
    value_ref[...] = dot(image.reshape(parts * half, bins), centre_ref[child])
    rims = rims_ref[...]
    return [
        (value_ref[part * half : (part + 1) * half, :] + dot(rims, rim_ref[child, part])).astype(BF16)
        for part in range(parts)
    ]


def early_kernel(
    own_ref, rims_ref, centre_ref, rim_ref, matrix_ref, turn_ref, merged_ref, value_ref
):
    rows = resampled(own_ref[...], rims_ref, centre_ref, rim_ref, value_ref, 0)
    merged_ref[0], merged_ref[1] = rotated(
        (dot(matrix_ref[0], rows[0]), dot(matrix_ref[0], rows[1])), (turn_ref[0, 0], turn_ref[0, 1])
    )


def late_kernel(
    far_outer, far_inner, rims_ref, merged_ref, centre_ref, rim_ref, matrix_ref, turn_ref, out_ref,
    buffer, value_ref, sems,
):
    image = jnp.concatenate([far_outer[...], far_inner[...]], axis=2)
    rows = resampled(image, rims_ref, centre_ref, rim_ref, value_ref, 1)
    parts = len(rows)
    block = LANES
    copies = []
    for first in range(0, matrix_ref.shape[1], block):
        here = slice(first, first + block)
        matrix = matrix_ref[1, here]
        turned = rotated(
            (dot(matrix, rows[0]), dot(matrix, rows[1])),
            (turn_ref[1, 0, here], turn_ref[1, 1, here]),
        )
        for part in range(parts):
            buffer[part, here] = (merged_ref[part, here] + turned[part]).astype(buffer.dtype)
        copy = pltpu.make_async_copy(buffer.at[:, here], out_ref.at[:, here], sems.at[len(copies)])
        copy.start()
        copies.append(copy)
    for copy in copies:
        copy.wait()


def merged_image(own, rims, far, far_rims, tables, dtype):
    centre, rim, turn, matrices, _ = tables
    angles, bins = turn.shape[-2:]
    cost = pl.CostEstimate(flops=4 * angles * bins * bins, bytes_accessed=8 * MIB, transcendentals=0)
    value = pltpu.VMEM((angles, bins), F32)
    merged = pl.pallas_call(
        early_kernel,
        out_shape=jax.ShapeDtypeStruct((2, angles, bins), F32),
        in_specs=[VMEM] * 6,
        out_specs=VMEM,
        scratch_shapes=[value],
        compiler_params=params(16),
        cost_estimate=cost,
    )(own, rims, centre, rim, matrices, turn)
    return pl.pallas_call(
        late_kernel,
        out_shape=jax.ShapeDtypeStruct((2, angles, bins), dtype),
        in_specs=[VMEM] * 8,
        out_specs=ANY,
        scratch_shapes=[
            pltpu.VMEM((2, angles, bins), dtype),
            value,
            pltpu.SemaphoreType.DMA((angles // LANES,)),
        ],
        compiler_params=params(16),
        cost_estimate=cost,
    )(*far, far_rims, merged, centre, rim, matrices, turn)


def after(value, *earlier):
    return lax.optimization_barrier((value, *earlier))[0]


def from_partner(value, stride):
    pairs = [(source, source ^ stride) for source in range(lax.axis_size("sub"))]
    return lax.ppermute(value, "sub", pairs)


def split_image(level, image, fore_flag, rim):
    angles, bins = image.shape[1:]
    half, step = angles // 2, LANES // 2
    own_flag = fore_flag[level, lax.axis_index("sub"), 0]
    sides = image.reshape(2, 2, half, bins)

    def pieces(side):
        rows = lax.dynamic_index_in_dim(sides, side, 1, keepdims=False)
        ends = [rows[..., :step], rows[..., -step:]]
        rest = [rows[..., -2 * step : -step], rows[..., step : -2 * step]]
        return jnp.concatenate(ends + rest, axis=-1)

    def packed(edge):
        return edge.transpose(2, 0, 1, 3).reshape(half, 4 * rim)

    low, high = packed(sides[..., :rim]), packed(sides[..., -rim:])
    even = lax.axis_index("rng") % 2 == 0
    edges = jnp.where(even, high, low), jnp.where(even, low, high)
    return pieces(own_flag), pieces(1 - own_flag), edges


def on_device(echoes, fore_flag, band_offset, angle_interp, range_kernel, center_shift):
    devices = lax.axis_size("rng")
    half = devices // 2
    local_pulses = echoes.shape[1]
    bins = echoes.shape[2] // devices
    angles = angle_interp.shape[2]
    rim = MAX_SHIFT + (range_kernel.shape[1] - bins) // 2
    levels = range_kernel.shape[0]
    settings = (fore_flag, band_offset, center_shift, range_kernel, angle_interp)

    far_blocks, near_blocks, blocks = placed(
        echoes.reshape(2 * local_pulses, devices * bins), devices
    )
    relay = across(far_blocks, half)
    pulses = lax.all_to_all(blocks, "rng", split_axis=0, concat_axis=0, tiled=True)
    sends = joined(near_blocks, relay)
    pieces = [across(value, d) if d else value for d, value in enumerate(sends)]
    matrix, own_side = filter_table(fore_flag, angles, local_pulses, sends[0])
    own_outer, out_outer, *edges = outer_image(own_side, matrix, pieces)

    pulses = after(pulses, out_outer).reshape(2 * local_pulses * devices, bins - LANES)
    out_kernel = functools.partial(partner_rows_kernel, local_pulses)
    out_inner = inner_image(out_kernel, angles, matrix, pulses)
    far = [from_partner(value, 1) for value in (out_outer, out_inner)]
    edges = [after(edge, out_inner) for edge in edges]
    edges = exchanged(edges[0], 0), exchanged(edges[1], 1)
    pulses = after(pulses, far[0])
    own_kernel = functools.partial(own_rows_kernel, local_pulses)
    own = inner_image(own_kernel, angles, matrix, pulses, (own_outer,))
    rims, out_rims = sorted_rims(own_side, *edges)
    tables = merge_tables(0, 1, *settings, after(out_rims, own))
    for level in range(levels):
        stride = 2**level
        if level > 0:
            tables = merge_tables(level, stride, *settings, image)
            own, out, edges = split_image(level, image, fore_flag, rim)
            far = [from_partner(value, stride) for value in (out[..., :LANES], out[..., LANES:])]
            edges = exchanged(edges[0], 0), exchanged(edges[1], 1)
            rims, out_rims = sorted_rims(tables[-1], *edges)
        far_rims = from_partner(out_rims, stride)
        image = merged_image(own, rims, far, far_rims, tables, BF16 if level + 1 < levels else F32)
    return image


def solution(mesh):
    placed_as = (
        P(None, ("sub", "rng"), None),
        P(None, None, "rng"),
        P(None, None, "rng"),
        P(),
        P(),
        P(),
    )
    return jax.shard_map(
        on_device, mesh=mesh, in_specs=placed_as, out_specs=P(None, "sub", "rng"), check_vma=False
    )
```

```python
import functools
import math

import jax
import jax.numpy as jnp
from jax import lax
from jax.experimental import pallas as pl
from jax.experimental.pallas import tpu as pltpu
from jax.sharding import PartitionSpec as P

MAX_SHIFT = 16
LANES = 128
MIB = 2**20
JOIN_COST = 10**11
SIDE = jax.ShapeDtypeStruct((8, LANES), jnp.float32)
VMEM = pl.BlockSpec(memory_space=pltpu.VMEM)
SMEM = pl.BlockSpec(memory_space=pltpu.SMEM)
ANY = pl.BlockSpec(memory_space=pl.ANY)
F32 = jnp.float32
BF16 = jnp.bfloat16


def dot(a, b):
    return jnp.dot(a, b, preferred_element_type=F32)


def params(mib):
    return pltpu.CompilerParams(vmem_limit_bytes=mib * MIB)


def series(square, first, count):
    coefs = [
        (-1) ** i * math.pi ** (2 * i + first) / math.factorial(2 * i + first)
        for i in range(count)
    ]
    total = jnp.full_like(square, coefs[-1])
    for coef in coefs[-2::-1]:
        total = total * square + coef
    return total


def cos_sin_pi(v):
    turns = jnp.floor(v + 0.5)
    rest = v - turns
    sign = 1.0 - 2.0 * (turns - 2.0 * jnp.floor(turns * 0.5))
    square = rest * rest
    return series(square, 0, 8) * sign, series(square, 1, 7) * rest * sign


def rotated(pair, step):
    return pair[0] * step[0] - pair[1] * step[1], pair[0] * step[1] + pair[1] * step[0]


def mixed(left, right):
    lane = lax.broadcasted_iota(jnp.int32, left.shape, 1)
    return jnp.where(lane < LANES // 2, left.astype(F32), right.astype(F32)).astype(BF16)


def place_kernel(echoes_ref, far_ref, near_ref, inner_ref):
    devices, _, count = inner_ref.shape
    bins = count + LANES
    half = devices // 2
    base = lax.axis_index("rng") // half * half

    def tile(device, first):
        return echoes_ref[:, pl.ds(pl.multiple_of(device * bins + first, LANES), LANES)]

    for ref, start in ((far_ref, half - base), (near_ref, base)):
        for i in range(half):
            ref[i] = mixed(tile(start + i, 0), tile(start + i, bins - LANES))
    for device in range(devices):
        begin = device * bins
        inner_ref[device, :, :LANES] = mixed(tile(device, bins - LANES), tile(device, 0))
        inner_ref[device, :, LANES:] = echoes_ref[:, begin + LANES : begin + bins - LANES]


def placed(echoes, devices):
    rows, columns = echoes.shape
    outer = jax.ShapeDtypeStruct((devices // 2, rows, LANES), BF16)
    inner = jax.ShapeDtypeStruct((devices, rows, columns // devices - LANES), BF16)
    return pl.pallas_call(
        place_kernel,
        out_shape=[outer, outer, inner],
        in_specs=[VMEM],
        out_specs=[VMEM] * 3,
        compiler_params=params(8),
        cost_estimate=pl.CostEstimate(flops=0, bytes_accessed=2 * MIB, transcendentals=0),
    )(echoes)


def join_kernel(near_ref, relay_ref, *refs):
    me = lax.axis_index("rng") % len(refs)
    rows = near_ref.shape[1]
    for d, out_ref in enumerate(refs):
        out_ref[:rows] = near_ref[me ^ d]
        out_ref[rows:] = relay_ref[me ^ d]


def joined(near, relay):
    half, rows, count = near.shape
    return pl.pallas_call(
        join_kernel,
        out_shape=[jax.ShapeDtypeStruct((2 * rows, count), BF16)] * half,
        in_specs=[VMEM] * 2,
        out_specs=[VMEM] * half,
        compiler_params=params(4),
        cost_estimate=pl.CostEstimate(flops=JOIN_COST, bytes_accessed=MIB, transcendentals=0),
    )(near, relay)


def across(value, mask):
    devices = lax.axis_size("rng")
    return lax.ppermute(value, "rng", [(i, i ^ mask) for i in range(devices)])


def filter_table_kernel(local_pulses, flag_ref, after_ref, rows_ref, side_ref, cos_ref, sin_ref):
    own_flag = flag_ref[0, lax.axis_index("sub"), 0]
    side_ref[...] = jnp.full(side_ref.shape, own_flag.astype(F32))
    half, columns = rows_ref.shape
    angles = 2 * half
    first = (1 - own_flag) * half
    base = cos_ref.shape[0]
    scale = 1.0 / math.sqrt(columns // 2)
    lane = lax.broadcasted_iota(jnp.int32, (8, columns), 1)
    slot = lane // (2 * local_pulses)
    second = lane // local_pulses % 2
    pulse = (slot * local_pulses + lane % local_pulses).astype(F32)
    lag = second.astype(F32) * 0.5
    per_angle = pulse * (1.0 / angles)
    row = lax.broadcasted_iota(jnp.int32, (8, columns), 0)
    for i in range(base // 8):
        twice = (2 * (row + 8 * i + first) + 1 - angles).astype(F32)
        cosine, sine = cos_sin_pi(twice * per_angle - lag)
        cos_ref[8 * i : 8 * i + 8, :] = cosine * scale
        sin_ref[8 * i : 8 * i + 8, :] = sine * scale
    step = cos_sin_pi(per_angle * (2 * base))
    for j in range(half // base):
        for i in range(base // 16):
            pair = []
            for k in (2 * i, 2 * i + 1):
                here = slice(8 * k, 8 * k + 8)
                now = cos_ref[here, :], sin_ref[here, :]
                pair.append(now[0])
                if j + 1 < half // base:
                    cos_ref[here, :], sin_ref[here, :] = rotated(now, step)
            begin = j * base + 16 * i
            rows_ref[begin : begin + 16, :] = jnp.concatenate(pair).astype(BF16)


def filter_table(fore_flag, angles, local_pulses, earlier):
    side = 2 * local_pulses * lax.axis_size("rng")
    return pl.pallas_call(
        functools.partial(filter_table_kernel, local_pulses),
        out_shape=[jax.ShapeDtypeStruct((angles // 2, side), BF16), SIDE],
        in_specs=[SMEM, ANY],
        out_specs=[VMEM] * 2,
        scratch_shapes=[pltpu.VMEM((64, side), F32)] * 2,
        compiler_params=params(6),
        cost_estimate=pl.CostEstimate(flops=9_000_000, bytes_accessed=4 * MIB, transcendentals=0),
    )(fore_flag, earlier)


def merge_table_kernel(
    level, stride, flag_ref, offset_ref, shift_ref, range_ref, interp_ref, after_ref, centre_ref,
    rim_ref, turn_ref, matrix_ref, side_ref, kernel_ref, sems,
):
    group = lax.axis_index("sub")
    block = lax.axis_index("rng")
    bins = centre_ref.shape[-1]
    angles = turn_ref.shape[-2]
    total_bins = lax.axis_size("rng") * bins
    taps = range_ref.shape[1]
    band = (taps - bins) // 2
    rim = MAX_SHIFT + band
    own_flag = flag_ref[level, group, 0]
    side_ref[...] = jnp.full(side_ref.shape, own_flag.astype(F32))
    copies = [
        pltpu.make_async_copy(source, target, sems.at[i])
        for i, (source, target) in enumerate(
            (
                (range_ref.at[level], kernel_ref),
                (interp_ref.at[level, own_flag], matrix_ref.at[0]),
                (interp_ref.at[level, 1 - own_flag], matrix_ref.at[1]),
            )
        )
    ]
    for copy in copies:
        copy.start()

    def moved(bin_id):
        tap = lax.broadcasted_iota(jnp.int32, (bin_id.shape[0], taps), 1)
        hot = jnp.where(tap == bin_id, 1.0, 0.0).astype(BF16)
        return dot(hot, kernel_ref[...]).astype(BF16)

    piece = LANES // 2
    starts = [0, bins - piece, bins - 2 * piece, piece, *range(2 * piece, bins - 2 * piece, piece)]
    line_bin = lax.broadcasted_iota(jnp.int32, (piece, 1), 0)
    line_tap = lax.broadcasted_iota(jnp.int32, (piece, piece + taps - bins), 1)
    rim_row = lax.broadcasted_iota(jnp.int32, (2 * rim, 1), 0)
    rim_bin = jnp.where(rim_row < rim, rim_row - rim, rim_row - rim + bins)
    rim_ref[...] = jnp.zeros(rim_ref.shape, BF16)
    bin_id = block * bins + lax.broadcasted_iota(jnp.int32, (8, bins), 1)
    reach = 1.0 + bin_id.astype(F32) * (1.0 / total_bins)
    line = lax.broadcasted_iota(jnp.int32, (8, bins), 0)
    base = 64
    members = group, group ^ stride
    for child, member in enumerate(members):
        rate = shift_ref[level, member]
        for first in range(0, base, 8):
            angle = (first + line).astype(F32)
            now = cos_sin_pi(rate * ((angle + 0.5) * (1.0 / angles) - 0.5) * reach)
            turn_ref[child, 0, first : first + 8, :] = now[0]
            turn_ref[child, 1, first : first + 8, :] = now[1]
        step = cos_sin_pi(rate * (base / angles) * reach)
        for first in range(base, angles, 8):
            here, last = slice(first, first + 8), slice(first - base, first - base + 8)
            now = rotated((turn_ref[child, 0, last, :], turn_ref[child, 1, last, :]), step)
            turn_ref[child, 0, here, :], turn_ref[child, 1, here, :] = now
    for copy in copies:
        copy.wait()
    for child, member in enumerate(members):
        lead = band - offset_ref[level, member, 0]
        hot = jnp.where(line_tap == line_bin + lead, 1.0, 0.0).astype(BF16)
        for i, start in enumerate(starts):
            some = kernel_ref[start : start + piece + taps - bins, :]
            centre_ref[child, i * piece : (i + 1) * piece, :] = dot(hot, some).astype(BF16)
        ends = moved(rim_bin + lead)
        for part in range(2):
            for side in range(2):
                place = (2 * side + part) * rim
                rim_ref[child, part, place : place + rim, :] = ends[side * rim : (side + 1) * rim]


def merge_tables(
    level, stride, fore_flag, band_offset, center_shift, range_kernel, angle_interp, earlier
):
    taps, bins = range_kernel.shape[1:]
    angles = angle_interp.shape[2]
    rim = MAX_SHIFT + (taps - bins) // 2
    return pl.pallas_call(
        functools.partial(merge_table_kernel, level, stride),
        out_shape=[
            jax.ShapeDtypeStruct((2, bins, bins), BF16),
            jax.ShapeDtypeStruct((2, 2, 4 * rim, bins), BF16),
            jax.ShapeDtypeStruct((2, 2, angles, bins), F32),
            jax.ShapeDtypeStruct((2, *angle_interp.shape[2:]), BF16),
            SIDE,
        ],
        in_specs=[SMEM] * 3 + [ANY] * 3,
        out_specs=[VMEM] * 5,
        scratch_shapes=[pltpu.VMEM((taps, bins), BF16), pltpu.SemaphoreType.DMA((3,))],
        compiler_params=params(12),
        cost_estimate=pl.CostEstimate(
            flops=2_300_000_000, bytes_accessed=7 * MIB, transcendentals=0
        ),
    )(fore_flag, band_offset, center_shift, range_kernel, angle_interp, earlier)


def alternating(pulses, local_pulses):
    row = lax.broadcasted_iota(jnp.int32, (pulses.shape[0], 1), 0)
    pulse = row // (2 * local_pulses) * local_pulses + row % local_pulses
    return jnp.where(pulse % 2 == 1, -pulses, pulses)


def both_parts(pulses, local_pulses):
    count = pulses.shape[0]
    second = lax.broadcasted_iota(jnp.int32, (count, 1), 0) // local_pulses % 2 == 1
    ahead, behind = pltpu.roll(pulses, count - local_pulses, 0), pltpu.roll(pulses, local_pulses, 0)
    turned = jnp.where(second, -behind, ahead)
    return jnp.concatenate([pulses, turned], axis=1).astype(BF16)


def outer_kernel(pieces, side_ref, rows_ref, *refs):
    own_side = side_ref[:1, :]
    me = lax.axis_index("rng")
    own_ref, out_ref, *edge_refs = refs[pieces:-1]
    pulses_ref = refs[-1]
    rows = refs[0].shape[0] // 2
    for d, ref in enumerate(refs[:pieces]):
        for t in range(2):
            place = pl.multiple_of((me ^ (d + t * pieces)) * rows, rows)
            pulses_ref[pl.ds(place, rows), :] = ref[t * rows : (t + 1) * rows, :]
    pulses = pulses_ref[...]
    pulses = pulses.astype(F32)
    images = [
        dot(rows_ref[...], both_parts(value, rows // 2))
        for value in (alternating(pulses, rows // 2), pulses)
    ]
    half = own_ref.shape[1]
    rim = LANES // 4
    lane = lax.broadcasted_iota(jnp.int32, (1, LANES), 1)
    edges = [0.0, 0.0]
    for part in range(2):
        own, out = (image[:, part * LANES : (part + 1) * LANES] for image in images)
        own_ref[part] = own.astype(BF16)
        out_ref[part] = out.astype(BF16)
        for side in range(2):
            value = jnp.where(own_side == side, own, out)
            group = 2 * part + side
            for end in range(2):
                turn = (group + end) * rim % LANES
                moved = pltpu.roll(value, turn, 1) if turn else value
                edges[end] = edges[end] + jnp.where(lane // rim == group, moved, 0.0)
    even = me % 2 == 0
    edge_refs[0][...] = jnp.where(even, edges[1], edges[0]).astype(BF16)
    edge_refs[1][...] = jnp.where(even, edges[0], edges[1]).astype(BF16)


def outer_image(own_side, rows, pieces):
    half, side = rows.shape
    angles = 2 * half
    image = jax.ShapeDtypeStruct((2, angles // 2, LANES), BF16)
    edge = jax.ShapeDtypeStruct((angles // 2, LANES), BF16)
    return pl.pallas_call(
        functools.partial(outer_kernel, len(pieces)),
        out_shape=[image, image, edge, edge],
        in_specs=[VMEM] * (2 + len(pieces)),
        out_specs=[VMEM] * 4,
        scratch_shapes=[pltpu.VMEM((side, LANES), BF16)],
        compiler_params=params(10),
        cost_estimate=pl.CostEstimate(
            flops=4 * angles * side * LANES, bytes_accessed=3 * MIB, transcendentals=0
        ),
    )(own_side, rows, *pieces)


def partner_rows_kernel(local_pulses, rows_ref, pulses_ref, image_ref):
    count = pulses_ref.shape[1]
    image = dot(rows_ref[...], both_parts(pulses_ref[...].astype(F32), local_pulses))
    for part in range(2):
        image_ref[part] = image[:, part * count : (part + 1) * count].astype(BF16)


def own_rows_kernel(local_pulses, rows_ref, pulses_ref, outer_ref, image_ref):
    inner = pulses_ref.shape[1]
    pulses = alternating(pulses_ref[...].astype(F32), local_pulses)
    image = dot(rows_ref[...], both_parts(pulses, local_pulses))
    count = outer_ref.shape[2]
    image_ref[:, :, :count] = outer_ref[...]
    for part in range(2):
        image_ref[part, :, count:] = image[:, part * inner : (part + 1) * inner].astype(BF16)


def inner_image(kernel, angles, rows, pulses, outer=()):
    count = pulses.shape[1]
    whole = count + (outer[0].shape[2] if outer else 0)
    return pl.pallas_call(
        kernel,
        out_shape=jax.ShapeDtypeStruct((2, angles // 2, whole), BF16),
        in_specs=[VMEM] * (2 + len(outer)),
        out_specs=VMEM,
        compiler_params=params(10),
        cost_estimate=pl.CostEstimate(
            flops=2 * angles * rows.shape[1] * count, bytes_accessed=3 * MIB, transcendentals=0
        ),
    )(rows, pulses, *outer)


def exchanged(value, begin):
    devices = lax.axis_size("rng")
    pairs = [(i, i + 1) for i in range(begin, devices - 1, 2)]
    ends = [(i, i) for i in range(devices) if all(i not in pair for pair in pairs)]
    return lax.ppermute(value, "rng", pairs + [(j, i) for i, j in pairs] + ends)


def rims_kernel(side_ref, first_ref, second_ref, own_ref, out_ref):
    own_side = side_ref[:1, :]
    rim = LANES // 4
    me, devices = lax.axis_index("rng"), lax.axis_size("rng")
    even = me % 2 == 0
    first, second = first_ref[...].astype(F32), second_ref[...].astype(F32)
    below = jnp.where(me == 0, 0.0, jnp.where(even, second, first))
    above = jnp.where(me == devices - 1, 0.0, jnp.where(even, first, second))
    group = lax.broadcasted_iota(jnp.int32, (1, LANES), 1) // rim
    packed = [0.0, 0.0]
    for end, value in enumerate((below, above)):
        for part in range(2):
            place = 2 * end + part
            for side in range(2):
                turn = (place - (2 * part + side)) * rim % LANES
                moved = pltpu.roll(value, turn, 1) if turn else value
                packed[side] = packed[side] + jnp.where(group == place, moved, 0.0)
    own_ref[...] = jnp.where(own_side == 0, packed[0], packed[1]).astype(BF16)
    out_ref[...] = jnp.where(own_side == 0, packed[1], packed[0]).astype(BF16)


def sorted_rims(own_side, first, second):
    return pl.pallas_call(
        rims_kernel,
        out_shape=[jax.ShapeDtypeStruct(first.shape, BF16)] * 2,
        in_specs=[VMEM] * 3,
        out_specs=[VMEM] * 2,
        compiler_params=params(4),
        cost_estimate=pl.CostEstimate(flops=1_000_000, bytes_accessed=MIB // 4, transcendentals=0),
    )(own_side, first, second)


def resampled(image, rims_ref, centre_ref, rim_ref, value_ref, child):
    parts, half, bins = image.shape
    rims = rims_ref[...]
    return [
        (dot(image[part], centre_ref[child]) + dot(rims, rim_ref[child, part])).astype(BF16)
        for part in range(parts)
    ]


def early_kernel(
    own_ref, rims_ref, centre_ref, rim_ref, matrix_ref, turn_ref, merged_ref, value_ref
):
    rows = resampled(own_ref[...], rims_ref, centre_ref, rim_ref, value_ref, 0)
    merged_ref[0], merged_ref[1] = rotated(
        (dot(matrix_ref[0], rows[0]), dot(matrix_ref[0], rows[1])), (turn_ref[0, 0], turn_ref[0, 1])
    )


def late_kernel(
    far_outer, far_inner, rims_ref, merged_ref, centre_ref, rim_ref, matrix_ref, turn_ref, out_ref,
    buffer, value_ref, sems,
):
    image = jnp.concatenate([far_outer[...], far_inner[...]], axis=2)
    rows = resampled(image, rims_ref, centre_ref, rim_ref, value_ref, 1)
    parts = len(rows)
    block = LANES
    copies = []
    for first in range(0, matrix_ref.shape[1], 2 * block):
        matrix = matrix_ref[1, first : first + 2 * block]
        terms = dot(matrix, rows[0]), dot(matrix, rows[1])
        for step in range(2):
            here = slice(first + step * block, first + (step + 1) * block)
            there = slice(step * block, (step + 1) * block)
            turned = rotated(
                (terms[0][there], terms[1][there]), (turn_ref[1, 0, here], turn_ref[1, 1, here])
            )
            for part in range(parts):
                buffer[part, here] = (merged_ref[part, here] + turned[part]).astype(buffer.dtype)
            copy = pltpu.make_async_copy(
                buffer.at[:, here], out_ref.at[:, here], sems.at[len(copies)]
            )
            copy.start()
            copies.append(copy)
    for copy in copies:
        copy.wait()


def merged_image(own, rims, far, far_rims, tables, dtype):
    centre, rim, turn, matrices, _ = tables
    angles, bins = turn.shape[-2:]
    cost = pl.CostEstimate(flops=4 * angles * bins * bins, bytes_accessed=8 * MIB, transcendentals=0)
    value = pltpu.VMEM((angles, bins), F32)
    merged = pl.pallas_call(
        early_kernel,
        out_shape=jax.ShapeDtypeStruct((2, angles, bins), F32),
        in_specs=[VMEM] * 6,
        out_specs=VMEM,
        scratch_shapes=[value],
        compiler_params=params(16),
        cost_estimate=cost,
    )(own, rims, centre, rim, matrices, turn)
    return pl.pallas_call(
        late_kernel,
        out_shape=jax.ShapeDtypeStruct((2, angles, bins), dtype),
        in_specs=[VMEM] * 8,
        out_specs=ANY,
        scratch_shapes=[
            pltpu.VMEM((2, angles, bins), dtype),
            value,
            pltpu.SemaphoreType.DMA((angles // LANES,)),
        ],
        compiler_params=params(16),
        cost_estimate=cost,
    )(*far, far_rims, merged, centre, rim, matrices, turn)


def after(value, *earlier):
    return lax.optimization_barrier((value, *earlier))[0]


def from_partner(value, stride):
    pairs = [(source, source ^ stride) for source in range(lax.axis_size("sub"))]
    return lax.ppermute(value, "sub", pairs)


def split_image(level, image, fore_flag, rim):
    angles, bins = image.shape[1:]
    half, step = angles // 2, LANES // 2
    own_flag = fore_flag[level, lax.axis_index("sub"), 0]
    sides = image.reshape(2, 2, half, bins)

    def pieces(side):
        rows = lax.dynamic_index_in_dim(sides, side, 1, keepdims=False)
        ends = [rows[..., :step], rows[..., -step:]]
        rest = [rows[..., -2 * step : -step], rows[..., step : -2 * step]]
        return jnp.concatenate(ends + rest, axis=-1)

    def packed(edge):
        return edge.transpose(2, 0, 1, 3).reshape(half, 4 * rim)

    low, high = packed(sides[..., :rim]), packed(sides[..., -rim:])
    even = lax.axis_index("rng") % 2 == 0
    edges = jnp.where(even, high, low), jnp.where(even, low, high)
    return pieces(own_flag), pieces(1 - own_flag), edges


def on_device(echoes, fore_flag, band_offset, angle_interp, range_kernel, center_shift):
    devices = lax.axis_size("rng")
    half = devices // 2
    local_pulses = echoes.shape[1]
    bins = echoes.shape[2] // devices
    angles = angle_interp.shape[2]
    rim = MAX_SHIFT + (range_kernel.shape[1] - bins) // 2
    levels = range_kernel.shape[0]
    settings = (fore_flag, band_offset, center_shift, range_kernel, angle_interp)

    far_blocks, near_blocks, blocks = placed(
        echoes.reshape(2 * local_pulses, devices * bins), devices
    )
    relay = across(far_blocks, half)
    pulses = lax.all_to_all(blocks, "rng", split_axis=0, concat_axis=0, tiled=True)
    sends = joined(near_blocks, relay)
    pieces = [across(value, d) if d else value for d, value in enumerate(sends)]
    matrix, own_side = filter_table(fore_flag, angles, local_pulses, sends[0])
    own_outer, out_outer, *edges = outer_image(own_side, matrix, pieces)

    pulses = after(pulses, out_outer).reshape(2 * local_pulses * devices, bins - LANES)
    out_kernel = functools.partial(partner_rows_kernel, local_pulses)
    out_inner = inner_image(out_kernel, angles, matrix, pulses)
    far = [from_partner(value, 1) for value in (out_outer, out_inner)]
    edges = [after(edge, out_inner) for edge in edges]
    edges = exchanged(edges[0], 0), exchanged(edges[1], 1)
    pulses = after(pulses, far[0])
    own_kernel = functools.partial(own_rows_kernel, local_pulses)
    own = inner_image(own_kernel, angles, matrix, pulses, (own_outer,))
    rims, out_rims = sorted_rims(own_side, *edges)
    tables = merge_tables(0, 1, *settings, after(out_rims, own))
    for level in range(levels):
        stride = 2**level
        if level > 0:
            tables = merge_tables(level, stride, *settings, image)
            own, out, edges = split_image(level, image, fore_flag, rim)
            far = [from_partner(value, stride) for value in (out[..., :LANES], out[..., LANES:])]
            edges = exchanged(edges[0], 0), exchanged(edges[1], 1)
            rims, out_rims = sorted_rims(tables[-1], *edges)
        far_rims = from_partner(out_rims, stride)
        image = merged_image(own, rims, far, far_rims, tables, BF16 if level + 1 < levels else F32)
    return image


def solution(mesh):
    placed_as = (
        P(None, ("sub", "rng"), None),
        P(None, None, "rng"),
        P(None, None, "rng"),
        P(),
        P(),
        P(),
    )
    return jax.shard_map(
        on_device, mesh=mesh, in_specs=placed_as, out_specs=P(None, "sub", "rng"), check_vma=False
    )
```
